32 devices in a mesh: grp: 4 (over y, core), dev: 8 (over z, x).
Axes of the slice: x: 2, y: 2, z: 4, core: 2. Of those that a mesh axis runs over, the one named last changes fastest.
Arguments:
- suffix_queries: bfloat16 [4096, 2048], P(('grp', 'dev')), may hold values from -12 to 12
- suffix_keys: bfloat16 [4096, 2048], P(('grp', 'dev')), may hold values from -12 to 12
- suffix_values: bfloat16 [4096, 2048], P(('grp', 'dev')), may hold values from -6 to 6
- layer_input: bfloat16 [4096, 2048], P(('grp', 'dev')), may hold values from -6 to 6
- suffix_lengths: int32 [32, 4], P(('grp', 'dev')), may hold values from 1 to 64, as said below
- request_group: int32 [32, 4], P(('grp', 'dev')), may hold values from 0 to 3, as said below
- prefix_keys: bfloat16 [4, 4096, 2048], P('grp', None, 'dev'), may hold values from -12 to 12
- prefix_values: bfloat16 [4, 4096, 2048], P('grp', None, 'dev'), may hold values from -6 to 6
- up_weight: bfloat16 [2048, 8192], P(None, ('grp', 'dev')), may hold values from -0.125 to 0.125
- up_bias: bfloat16 [8192], P(('grp', 'dev')), may hold values from -3 to 3
- down_weight: bfloat16 [8192, 2048], P(('grp', 'dev')), may hold values from -0.0625 to 0.0625
- down_bias: float32 [2048], replicated, may hold values from -3 to 3
- attn_gain: float32 [2048], replicated, may hold values from 0.5 to 1.5
- attn_shift: float32 [2048], replicated, may hold values from -2 to 2
- out_gain: float32 [2048], replicated, may hold values from 0.5 to 1.5
- out_shift: float32 [2048], replicated, may hold values from -2 to 2
Outputs:
- layer_output: bfloat16 [4096, 2048], P(('grp', 'dev'))
The draws below stay inside these ranges and needn't reach their ends.
Inputs may be any that keep to these rules, and one draw needn't show every extreme that they name: `suffix_lengths`: each row lists one device's 4 requests in slot order; they fill its 128 slots exactly, and at least one of them has 64 tokens. `request_group`: the 4 requests of one row name every prefix exactly once.
All inputs are finite; a program needn't handle non-finite values.
Results may differ from the reference program's by a relative error of at most 0.014.
Values may be sent and summed in bfloat16 or wider, within the bound.
No kernel may reach another device: no remote copies, remote signals or barrier semaphores. Data moves between devices by JAX's collectives and lax.ppermute only.
A program may use at most 128 MiB of HBM per device.

```python
import jax
import jax.numpy as jnp
from jax import lax

D = 2048
HEADS = 16
HD = 128
FF = 8192
PLEN = 4096
TOK_DEV = 128
PREFIXES = 4
REQ_DEV = 4
MOST = 64
TOKENS = 4096
N_GRP = 4
N_DEV = 8


def draw_suffix_queries(key, part):
    drawn_draw = 1.5 * jax.random.truncated_normal(jax.random.fold_in(key, 11), -5.0, 5.0, (TOKENS, D), jnp.float32)
    return drawn_draw.astype(jnp.bfloat16)


def draw_suffix_keys(key, part):
    drawn_draw = 1.5 * jax.random.truncated_normal(jax.random.fold_in(key, 17), -5.0, 5.0, (TOKENS, D), jnp.float32)
    return drawn_draw.astype(jnp.bfloat16)


def draw_prefix_keys(key, part):
    drawn_draw = 1.5 * jax.random.truncated_normal(jax.random.fold_in(key, 13), -5.0, 5.0, (PREFIXES, PLEN, D), jnp.float32)
    return drawn_draw.astype(jnp.bfloat16)


def draw_suffix_lengths(key, part):
    row_total = TOKENS // TOK_DEV
    others = REQ_DEV - 1
    extra_total = TOK_DEV - MOST - others

    def one_device(device_key):
        weight_key, step_key, order_key = jax.random.split(device_key, 3)
        weights = jax.random.randint(weight_key, (others,), 1, 9).astype(jnp.int32)
        labels = lax.iota(jnp.int32, others)

        def add_unit(step, filled):
            score_draw = jax.random.randint(jax.random.fold_in(step_key, step), (others,), 0, 1024).astype(jnp.int32)
            score = score_draw * weights * REQ_DEV + labels
            score = jnp.where(filled < MOST, score, -1)
            pick = jnp.argmax(score).astype(jnp.int32)
            return (filled + (labels == pick).astype(jnp.int32)).astype(jnp.int32)
        filled = lax.fori_loop(0, extra_total, add_unit, jnp.ones((others,), jnp.int32))
        pieces = jnp.concatenate([jnp.full((1,), MOST, jnp.int32), filled]).astype(jnp.int32)
        return jnp.take(pieces, jax.random.permutation(order_key, REQ_DEV)).astype(jnp.int32)
    return jax.vmap(one_device)(jax.random.split(key, row_total))


def draw_request_group(key, part):
    row_total = TOKENS // TOK_DEV

    def one_device(device_key):
        return jax.random.permutation(device_key, PREFIXES)[:REQ_DEV].astype(jnp.int32)
    return jax.vmap(one_device)(jax.random.split(key, row_total))


def block_scale(own_key, shape, cuts, least, top_value):
    level, own = 1.0, jax.random.fold_in(own_key, 6)
    for axis_at, shards_of in cuts:
        heights = jnp.exp(jax.random.uniform(jax.random.fold_in(own, axis_at), (shards_of,), jnp.float32, least / len(cuts), top_value / len(cuts)))
        level = level * jnp.repeat(heights, shape[axis_at] // shards_of).reshape([-1 if axis == axis_at else 1 for axis in range(len(shape))])
    return level


def bell_draw(stream_key, shape, deviation, bound, shards=(), held_as=jnp.bfloat16):
    array = jax.random.normal(stream_key, shape, jnp.float32) * deviation
    if len(shards) > 0:
        array = block_scale(stream_key, shape, shards, -0.22, 0.18) * array
    return jnp.clip(array, min=-bound, max=bound).astype(held_as)


def setup_inputs(seed: int = 0) -> dict:
    arg_keys = jax.random.split(jax.random.key(seed), 17)
    suffix_queries = draw_suffix_queries(jax.random.fold_in(arg_keys[16], 71), 0)
    suffix_keys = draw_suffix_keys(jax.random.fold_in(arg_keys[16], 71), 0)
    suffix_values = bell_draw(arg_keys[2], (TOKENS, D), 1.0, 6.0, ((0, 32),))
    layer_input = bell_draw(arg_keys[3], (TOKENS, D), 1.0, 6.0, ((0, 32),))
    suffix_lengths = draw_suffix_lengths(jax.random.fold_in(arg_keys[16], 71), 0)
    request_group = draw_request_group(jax.random.fold_in(arg_keys[16], 71), 0)
    prefix_keys = draw_prefix_keys(jax.random.fold_in(arg_keys[16], 71), 0)
    prefix_values = bell_draw(arg_keys[7], (PREFIXES, PLEN, D), 1.0, 6.0, ((0, 4), (2, 8)))
    up_weight = bell_draw(arg_keys[8], (D, FF), D ** -0.5, 0.125, ((1, 32),))
    up_bias = bell_draw(arg_keys[9], (FF,), 0.5, 3.0, ((0, 32),))
    down_weight = bell_draw(arg_keys[10], (FF, D), FF ** -0.5, 0.0625, ((0, 32),))
    down_bias = bell_draw(arg_keys[11], (D,), 0.5, 3.0, (), jnp.float32)
    attn_gain = jnp.clip(1.0 + 0.1 * jax.random.normal(arg_keys[12], (D,), jnp.float32), 0.5, 1.5)
    attn_shift = bell_draw(arg_keys[13], (D,), 0.3, 2.0, (), jnp.float32)
    out_gain = jnp.clip(1.0 + 0.1 * jax.random.normal(arg_keys[14], (D,), jnp.float32), 0.5, 1.5)
    out_shift = bell_draw(arg_keys[15], (D,), 0.3, 2.0, (), jnp.float32)
    return {"suffix_queries": suffix_queries, "suffix_keys": suffix_keys, "suffix_values": suffix_values, "layer_input": layer_input, "suffix_lengths": suffix_lengths, "request_group": request_group, "prefix_keys": prefix_keys, "prefix_values": prefix_values, "up_weight": up_weight, "up_bias": up_bias, "down_weight": down_weight, "down_bias": down_bias, "attn_gain": attn_gain, "attn_shift": attn_shift, "out_gain": out_gain, "out_shift": out_shift}


norm_eps = 1e-12

def layer_norm(summed, norm_gain, norm_shift):
    row_mean = lax.optimization_barrier(jnp.mean(summed, axis=-1, keepdims=True))
    centred = summed - row_mean
    spread = lax.optimization_barrier(jnp.mean(centred * centred, axis=-1, keepdims=True))
    return centred * lax.rsqrt(spread + norm_eps) * norm_gain + norm_shift

def request_layout(lengths, slot_count):
    lengths = lengths.astype(jnp.int32)
    end_points = jnp.cumsum(lengths).astype(jnp.int32)
    starts = (end_points - lengths).astype(jnp.int32)
    positions = lax.iota(jnp.int32, slot_count)
    member = (positions[:, None] >= starts[None, :]) & (positions[:, None] < end_points[None, :])
    slot_ids = lax.iota(jnp.int32, lengths.shape[0])
    segment = lax.optimization_barrier(jnp.sum(jnp.where(member, slot_ids[None, :], 0), axis=1)).astype(jnp.int32)
    return (starts, segment)

def attend_suffix(query_rows, key_rows, value_rows, segment):
    slot_count = query_rows.shape[0]
    query_heads = query_rows.astype(jnp.float32).reshape(slot_count, HEADS, HD)
    key_heads = key_rows.astype(jnp.float32).reshape(slot_count, HEADS, HD)
    value_heads = value_rows.astype(jnp.float32).reshape(slot_count, HEADS, HD)
    scores = jnp.einsum('qhd,khd->hqk', query_heads, key_heads) * HD ** (-0.5)
    positions = lax.iota(jnp.int32, slot_count)
    visible = ((segment[:, None] == segment[None, :]) & (positions[None, :] <= positions[:, None]))[None]
    row_top = lax.optimization_barrier(jnp.max(jnp.where(visible, scores, -jnp.inf), axis=2))
    weights = jnp.where(visible, jnp.exp(scores - row_top[:, :, None]), 0.0)
    row_sum = lax.optimization_barrier(jnp.sum(weights, axis=2))
    rounded = lax.optimization_barrier(weights.astype(jnp.bfloat16)).astype(jnp.float32)
    mixed_sum = jnp.einsum('hqk,khd->qhd', rounded, value_heads)
    return (row_top.T, row_sum.T, mixed_sum)

def merge_parts(far_answer, far_top, far_sum, own_top, own_sum, own_mixed):
    far_top = far_top.astype(jnp.float32)
    far_sum = far_sum.astype(jnp.float32)
    joint_top = jnp.maximum(far_top, own_top)
    far_weight = jnp.exp(far_top - joint_top) * far_sum
    own_weight = jnp.exp(own_top - joint_top)
    numerator = far_weight[:, :, None] * far_answer.astype(jnp.float32) + own_weight[:, :, None] * own_mixed
    return numerator / (far_weight + own_weight * own_sum)[:, :, None]

def reference(suffix_queries, suffix_keys, suffix_values, layer_input, suffix_lengths, request_group, prefix_keys, prefix_values, up_weight, up_bias, down_weight, down_bias, attn_gain, attn_shift, out_gain, out_shift):
    device_total = N_GRP * N_DEV
    anchor = jnp.zeros((), jnp.int32)

    def per_device(stacked):
        query_rows, key_rows, value_rows, input_rows, lengths, groups = stacked
        lengths = lengths.astype(jnp.int32)
        groups = groups.astype(jnp.int32)
        starts, segment = request_layout(lengths, TOK_DEV)
        padded = jnp.concatenate([query_rows, jnp.zeros((MOST, D), query_rows.dtype)], axis=0)
        placed_answer = jnp.zeros((TOK_DEV + MOST, D), jnp.bfloat16)
        placed_top = jnp.zeros((TOK_DEV + MOST, HEADS), jnp.bfloat16)
        placed_sum = jnp.zeros((TOK_DEV + MOST, HEADS), jnp.bfloat16)
        for request in range(REQ_DEV):
            taken = lax.dynamic_slice_in_dim(padded, starts[request], MOST, 0).astype(jnp.float32).reshape(MOST, HEADS, HD)
            cache_keys = lax.dynamic_index_in_dim(prefix_keys, groups[request], 0, keepdims=False).astype(jnp.float32).reshape(PLEN, HEADS, HD)
            cache_values = lax.dynamic_index_in_dim(prefix_values, groups[request], 0, keepdims=False).astype(jnp.float32).reshape(PLEN, HEADS, HD)
            scores = jnp.einsum('qhd,khd->hqk', taken, cache_keys) * HD ** (-0.5)
            row_top = lax.optimization_barrier(jnp.max(scores, axis=2)).astype(jnp.bfloat16)
            weights = jnp.exp(scores - lax.optimization_barrier(row_top).astype(jnp.float32)[:, :, None])
            row_sum = lax.optimization_barrier(jnp.sum(weights, axis=2))
            rounded = lax.optimization_barrier(weights.astype(jnp.bfloat16)).astype(jnp.float32)
            mixed_sum = jnp.einsum('hqk,khd->qhd', rounded, cache_values)
            answer = (mixed_sum / row_sum.T[:, :, None]).astype(jnp.bfloat16).reshape(MOST, D)
            placed_answer = lax.dynamic_update_slice(placed_answer, answer, (starts[request], anchor))
            placed_top = lax.dynamic_update_slice(placed_top, row_top.T, (starts[request], anchor))
            placed_sum = lax.dynamic_update_slice(placed_sum, row_sum.T.astype(jnp.bfloat16), (starts[request], anchor))
        own_top, own_sum, own_mixed = attend_suffix(query_rows, key_rows, value_rows, segment)
        far_answer = placed_answer[:TOK_DEV].reshape(TOK_DEV, HEADS, HD)
        context = merge_parts(far_answer, placed_top[:TOK_DEV], placed_sum[:TOK_DEV], own_top, own_sum, own_mixed)
        hidden_state = layer_norm(input_rows.astype(jnp.float32) + context.reshape(TOK_DEV, D), attn_gain, attn_shift).astype(jnp.bfloat16)
        product = jnp.dot(hidden_state, up_weight, preferred_element_type=jnp.float32)
        activation = jax.nn.gelu(product + up_bias.astype(jnp.float32), approximate=True).astype(jnp.bfloat16)
        mlp_sum = jnp.dot(activation, down_weight, preferred_element_type=jnp.float32)
        return layer_norm(hidden_state.astype(jnp.float32) + mlp_sum + down_bias, out_gain, out_shift).astype(jnp.bfloat16)
    stacked = (suffix_queries.reshape(device_total, TOK_DEV, D), suffix_keys.reshape(device_total, TOK_DEV, D), suffix_values.reshape(device_total, TOK_DEV, D), layer_input.reshape(device_total, TOK_DEV, D), suffix_lengths, request_group)
    outputs = lax.map(per_device, stacked)
    return outputs.reshape(TOKENS, D)
```

```python
import functools
import math

import jax
import jax.numpy as jnp
from jax import lax
from jax.experimental import pallas as pl
from jax.experimental.pallas import tpu as pltpu
from jax.sharding import PartitionSpec as P

HD = 128
LANES = 128
STAT_ROWS = 8
ROW_BLOCK = 256
KEY_CHUNK = 1024

norm_eps = 1e-12
score_scale = HD ** (-0.5)
log2_e = math.log2(math.e)
kernel_vmem = 56 * 1024 * 1024


def layer_norm(summed, norm_gain, norm_shift):
    row_mean = jnp.mean(summed, axis=-1, keepdims=True)
    centred = summed - row_mean
    spread = jnp.mean(centred * centred, axis=-1, keepdims=True)
    return centred * lax.rsqrt(spread + norm_eps) * norm_gain + norm_shift


def vmem_spec():
    return pl.BlockSpec(memory_space=pltpu.VMEM)


def smem_spec():
    return pl.BlockSpec(memory_space=pltpu.SMEM)


def pack_kernel(lengths_ref, groups_ref, query_ref, out_ref, wide_ref):
    request_total = lengths_ref.shape[1]
    _, column_count, capacity, part_width = out_ref.shape
    slot_count = query_ref.shape[0]
    tiles = part_width // LANES
    for tile in range(wide_ref.shape[0]):
        wide_ref[tile, 0:slot_count, :] = query_ref[
            :, tile * LANES : (tile + 1) * LANES
        ].astype(jnp.float32)
        wide_ref[tile, slot_count : slot_count + capacity, :] = jnp.zeros(
            (capacity, LANES), jnp.float32
        )
    start = 0
    for request in range(request_total):
        group = groups_ref[0, request]
        for column in range(column_count):
            for tile in range(tiles):
                rows = wide_ref[column * tiles + tile, pl.ds(start, capacity), :]
                out_ref[group, column, :, tile * LANES : (tile + 1) * LANES] = rows.astype(
                    jnp.bfloat16
                )
        start = start + lengths_ref[0, request]


def pack_queries(lengths, groups, queries, group_count, column_count, capacity):
    slot_count, model_width = queries.shape
    part_width = model_width // column_count
    return pl.pallas_call(
        pack_kernel,
        out_shape=jax.ShapeDtypeStruct(
            (group_count, column_count, capacity, part_width), jnp.bfloat16
        ),
        in_specs=[smem_spec(), smem_spec(), vmem_spec()],
        out_specs=vmem_spec(),
        scratch_shapes=[
            pltpu.VMEM((model_width // LANES, slot_count + capacity, LANES), jnp.float32)
        ],
        compiler_params=pltpu.CompilerParams(vmem_limit_bytes=kernel_vmem),
        name="pack_queries",
    )(lengths, groups, queries)


def far_kernel(
    counts_ref,
    arrived_ref,
    keys_ref,
    values_ref,
    out_ref,
    query_ref,
    answer_ref,
    stat_ref,
    score_ref,
    top_ref,
):
    sources, capacity, part_width = arrived_ref.shape
    local_heads = part_width // HD
    key_total = keys_ref.shape[1]
    chunks = key_total // KEY_CHUNK

    def take(source, offset):
        for head in range(local_heads):
            query_ref[head, pl.ds(offset, capacity), :] = arrived_ref[
                source, :, head * HD : (head + 1) * HD
            ].astype(jnp.float32)
        return offset + counts_ref[source]

    total = lax.fori_loop(0, sources, take, jnp.int32(0))
    blocks = (total + ROW_BLOCK - 1) // ROW_BLOCK
    lane = lax.broadcasted_iota(jnp.int32, (ROW_BLOCK, LANES), 1)

    def block_rows(block):
        return pl.ds(pl.multiple_of(block * ROW_BLOCK, ROW_BLOCK), ROW_BLOCK)

    def load_queries(block, head):
        return query_ref[head, block_rows(block), :].astype(jnp.bfloat16)

    def score_chunk(rows, head, slot, chunk, part_top):
        columns = slice(chunk * KEY_CHUNK, (chunk + 1) * KEY_CHUNK)
        scores = jnp.dot(
            rows,
            keys_ref[head * HD : (head + 1) * HD, columns],
            preferred_element_type=jnp.float32,
        )
        score_ref[slot, :, columns] = scores
        for piece in range(KEY_CHUNK // LANES):
            part = scores[:, piece * LANES : (piece + 1) * LANES]
            part_top = part if part_top is None else jnp.maximum(part_top, part)
        return part_top

    def finish_top(part_top, slot):
        row_top = jnp.max(part_top, axis=1, keepdims=True) * score_scale
        row_top = row_top.astype(jnp.bfloat16).astype(jnp.float32)
        top_ref[slot] = jnp.broadcast_to(row_top, (ROW_BLOCK, LANES))

    def weigh_chunk(head, slot, chunk, shift):
        columns = slice(chunk * KEY_CHUNK, (chunk + 1) * KEY_CHUNK)
        weights = jnp.exp2(score_ref[slot, :, columns] * (score_scale * log2_e) - shift)
        return jnp.dot(
            weights.astype(jnp.bfloat16),
            values_ref[head, columns, :],
            preferred_element_type=jnp.float32,
        )

    def finish_answer(block, head, slot, mixed):
        rows = block_rows(block)
        row_sum = mixed[:, HD:]
        answer_ref[head, rows, :] = mixed[:, :HD] / row_sum
        top = top_ref[slot]
        if head == 0:
            stat_ref[rows, :] = jnp.where(lane == 0, top, row_sum)
        else:
            before = stat_ref[rows, :]
            with_top = jnp.where(lane == head, top, before)
            stat_ref[rows, :] = jnp.where(lane == local_heads + head, row_sum, with_top)

    def slot_of(block, head):
        return (block * local_heads + head) % 2 if local_heads % 2 else head % 2

    first_rows = load_queries(0, 0)
    part_top = None
    for chunk in range(chunks):
        part_top = score_chunk(first_rows, 0, 0, chunk, part_top)
    finish_top(part_top, 0)

    def one_block(block, carry):
        for head in range(local_heads):
            slot = slot_of(block, head)
            if head + 1 < local_heads:
                next_block, next_head = block, head + 1
            else:
                next_block, next_head = jnp.minimum(block + 1, blocks - 1), 0
            next_slot = 1 - slot
            next_rows = load_queries(next_block, next_head)
            shift = top_ref[slot][:, 0:1] * log2_e
            part_top = None
            mixed = None
            for chunk in range(chunks):
                part_top = score_chunk(next_rows, next_head, next_slot, chunk, part_top)
                part = weigh_chunk(head, slot, chunk, shift)
                mixed = part if mixed is None else mixed + part
            finish_answer(block, head, slot, mixed)
            finish_top(part_top, next_slot)
        return carry

    lax.fori_loop(0, blocks, one_block, 0)

    def give(source, offset):
        rows = [answer_ref[head, pl.ds(offset, capacity), :] for head in range(local_heads)]
        turned = jnp.transpose(stat_ref[pl.ds(offset, LANES), :])[:STAT_ROWS, :]
        if part_width > LANES:
            turned = jnp.concatenate(
                [turned, jnp.zeros((STAT_ROWS, part_width - LANES), jnp.float32)], axis=1
            )
        rows = jnp.concatenate(rows, axis=1)
        out_ref[source] = jnp.concatenate([rows, turned], axis=0).astype(jnp.bfloat16)
        return offset + counts_ref[source]

    lax.fori_loop(0, sources, give, jnp.int32(0))


def attend_prefix(counts, arrived, turned_keys, wide_values):
    sources, capacity, part_width = arrived.shape
    local_heads = part_width // HD
    key_total = turned_keys.shape[1]
    row_total = -(-sources * capacity // ROW_BLOCK) * ROW_BLOCK + LANES
    return pl.pallas_call(
        far_kernel,
        out_shape=jax.ShapeDtypeStruct((sources, capacity + STAT_ROWS, part_width), jnp.bfloat16),
        in_specs=[smem_spec(), vmem_spec(), vmem_spec(), vmem_spec()],
        out_specs=vmem_spec(),
        scratch_shapes=[
            pltpu.VMEM((local_heads, row_total, HD), jnp.float32),
            pltpu.VMEM((local_heads, row_total, HD), jnp.float32),
            pltpu.VMEM((row_total, LANES), jnp.float32),
            pltpu.VMEM((2, ROW_BLOCK, key_total), jnp.float32),
            pltpu.VMEM((2, ROW_BLOCK, LANES), jnp.float32),
        ],
        compiler_params=pltpu.CompilerParams(vmem_limit_bytes=kernel_vmem),
        cost_estimate=pl.CostEstimate(
            flops=4 * sources * capacity * key_total * part_width,
            bytes_accessed=8 * key_total * part_width,
            transcendentals=sources * capacity * key_total * local_heads,
        ),
        name="attend_prefix",
    )(counts, arrived, turned_keys, wide_values)


def stat_lane(head, local_heads):
    return (head // local_heads) * STAT_ROWS + head % local_heads


def own_kernel(local_heads, lengths_ref, query_ref, key_ref, value_ref, mixed_ref, top_ref, sum_ref):
    slot_count, model_width = query_ref.shape
    head_count = model_width // HD
    row = lax.broadcasted_iota(jnp.int32, (slot_count, slot_count), 0)
    column = lax.broadcasted_iota(jnp.int32, (slot_count, slot_count), 1)
    row_segment = jnp.zeros((slot_count, slot_count), jnp.int32)
    column_segment = jnp.zeros((slot_count, slot_count), jnp.int32)
    start = 0
    for request in range(lengths_ref.shape[1]):
        start = start + lengths_ref[0, request]
        row_segment = row_segment + (row >= start).astype(jnp.int32)
        column_segment = column_segment + (column >= start).astype(jnp.int32)
    visible = (row_segment == column_segment) & (column <= row)
    lane = lax.broadcasted_iota(jnp.int32, (slot_count, LANES), 1)
    tops = jnp.zeros((slot_count, LANES), jnp.float32)
    sums = jnp.ones((slot_count, LANES), jnp.float32)
    for head in range(head_count):
        columns = slice(head * HD, (head + 1) * HD)
        scores = (
            lax.dot_general(
                query_ref[:, columns],
                key_ref[:, columns],
                (((1,), (1,)), ((), ())),
                preferred_element_type=jnp.float32,
            )
            * score_scale
        )
        top = jnp.max(jnp.where(visible, scores, -jnp.inf), axis=1, keepdims=True)
        weights = jnp.where(visible, jnp.exp(scores - top), 0.0)
        mixed_ref[:, columns] = jnp.dot(
            weights.astype(jnp.bfloat16),
            value_ref[:, columns],
            preferred_element_type=jnp.float32,
        )
        at = stat_lane(head, local_heads)
        tops = jnp.where(lane == at, top, tops)
        sums = jnp.where(lane == at, jnp.sum(weights, axis=1, keepdims=True), sums)
    top_ref[...] = tops
    sum_ref[...] = sums


def attend_suffix(lengths, queries, keys, values, local_heads):
    slot_count, model_width = queries.shape
    stats = jax.ShapeDtypeStruct((slot_count, LANES), jnp.float32)
    return pl.pallas_call(
        functools.partial(own_kernel, local_heads),
        out_shape=(jax.ShapeDtypeStruct((slot_count, model_width), jnp.float32), stats, stats),
        in_specs=[smem_spec()] + [vmem_spec()] * 3,
        out_specs=(vmem_spec(), vmem_spec(), vmem_spec()),
        compiler_params=pltpu.CompilerParams(vmem_limit_bytes=kernel_vmem),
        cost_estimate=pl.CostEstimate(
            flops=40 * slot_count * slot_count * model_width,
            bytes_accessed=8 * slot_count * model_width,
            transcendentals=slot_count * model_width,
        ),
        name="attend_suffix",
    )(lengths, queries, keys, values)


def merge_kernel(
    lengths_ref,
    groups_ref,
    arrived_ref,
    own_mixed_ref,
    own_top_ref,
    own_sum_ref,
    input_ref,
    gain_ref,
    shift_ref,
    hidden_ref,
    far_ref,
    stat_ref,
):
    _, column_count, chunk_rows, part_width = arrived_ref.shape
    slot_count, model_width = input_ref.shape
    capacity = chunk_rows - STAT_ROWS
    local_heads = part_width // HD
    head_count = model_width // HD
    start = 0
    for request in range(lengths_ref.shape[1]):
        group = groups_ref[0, request]
        pieces = []
        for column in range(column_count):
            block = arrived_ref[group, column].astype(jnp.float32)
            for head in range(local_heads):
                far_ref[column * local_heads + head, pl.ds(start, capacity), :] = block[
                    :capacity, head * HD : (head + 1) * HD
                ]
            pieces.append(block[capacity:, :LANES])
        if column_count * STAT_ROWS < LANES:
            pieces.append(jnp.zeros((LANES - column_count * STAT_ROWS, LANES), jnp.float32))
        turned = jnp.transpose(jnp.concatenate(pieces, axis=0))
        stat_ref[pl.ds(start, capacity), :] = turned[:capacity]
        start = start + lengths_ref[0, request]
    far_top = stat_ref[:slot_count, :]
    far_sum = pltpu.roll(far_top, LANES - local_heads, 1)
    own_top = own_top_ref[...]
    joint_top = jnp.maximum(far_top, own_top)
    far_weight = jnp.exp(far_top - joint_top) * far_sum
    own_weight = jnp.exp(own_top - joint_top)
    bottom = far_weight + own_weight * own_sum_ref[...]
    far_weight = far_weight / bottom
    own_weight = own_weight / bottom
    total = jnp.zeros((slot_count, LANES), jnp.float32)
    for head in range(head_count):
        columns = slice(head * HD, (head + 1) * HD)
        at = stat_lane(head, local_heads)
        summed = (
            input_ref[:, columns].astype(jnp.float32)
            + far_weight[:, at : at + 1] * far_ref[head, :slot_count, :]
            + own_weight[:, at : at + 1] * own_mixed_ref[:, columns]
        )
        far_ref[head, :slot_count, :] = summed
        total = total + summed
    row_mean = jnp.sum(total, axis=1, keepdims=True) * (1.0 / model_width)
    total = jnp.zeros((slot_count, LANES), jnp.float32)
    for head in range(head_count):
        centred = far_ref[head, :slot_count, :] - row_mean
        total = total + centred * centred
    spread = jnp.sum(total, axis=1, keepdims=True) * (1.0 / model_width)
    factor = lax.rsqrt(spread + norm_eps)
    for head in range(head_count):
        columns = slice(head * HD, (head + 1) * HD)
        centred = far_ref[head, :slot_count, :] - row_mean
        hidden_ref[:, columns] = (
            centred * factor * gain_ref[:, columns] + shift_ref[:, columns]
        ).astype(jnp.bfloat16)


def merge_parts(lengths, groups, arrived, own_mixed, own_top, own_sum, layer_input, gain, shift):
    slot_count, model_width = layer_input.shape
    capacity = arrived.shape[2] - STAT_ROWS
    return pl.pallas_call(
        merge_kernel,
        out_shape=jax.ShapeDtypeStruct((slot_count, model_width), jnp.bfloat16),
        in_specs=[smem_spec(), smem_spec()] + [vmem_spec()] * 7,
        out_specs=vmem_spec(),
        scratch_shapes=[
            pltpu.VMEM((model_width // HD, slot_count + capacity, HD), jnp.float32),
            pltpu.VMEM((slot_count + capacity, LANES), jnp.float32),
        ],
        compiler_params=pltpu.CompilerParams(vmem_limit_bytes=kernel_vmem),
        name="merge_parts",
    )(
        lengths,
        groups,
        arrived,
        own_mixed,
        own_top,
        own_sum,
        layer_input,
        gain.reshape(1, model_width),
        shift.reshape(1, model_width),
    )


def expand_rows(piece_rows, up_matrix, up_offset):
    product = jnp.dot(piece_rows, up_matrix, preferred_element_type=jnp.float32)
    return jax.nn.gelu(product + up_offset.astype(jnp.float32), approximate=True).astype(
        jnp.bfloat16
    )


def on_device(
    suffix_queries,
    suffix_keys,
    suffix_values,
    layer_input,
    suffix_lengths,
    request_group,
    prefix_keys,
    prefix_values,
    up_weight,
    up_bias,
    down_weight,
    down_bias,
    attn_gain,
    attn_shift,
    out_gain,
    out_shift,
):
    slot_count, model_width = suffix_queries.shape
    group_count = lax.axis_size("grp")
    column_count = lax.axis_size("dev")
    part_width = model_width // column_count
    local_heads = part_width // HD
    capacity = 2 * slot_count // group_count
    sources = group_count * column_count
    request_total = suffix_lengths.shape[1]

    table = lax.all_gather(
        jnp.concatenate([suffix_lengths, request_group], axis=1),
        ("grp", "dev"),
        axis=0,
        tiled=True,
    )
    counts = jnp.sum(
        jnp.where(table[:, request_total:] == lax.axis_index("grp"), table[:, :request_total], 0),
        axis=1,
    )

    outgoing = pack_queries(
        suffix_lengths, request_group, suffix_queries, group_count, column_count, capacity
    )
    arrived = lax.all_to_all(
        outgoing.reshape(sources, capacity, part_width),
        ("grp", "dev"),
        split_axis=0,
        concat_axis=0,
        tiled=True,
    )
    turned_keys = prefix_keys[0].T
    value_heads = prefix_values[0].reshape(-1, local_heads, HD).transpose(1, 0, 2)
    wide_values = jnp.concatenate([value_heads, jnp.ones_like(value_heads)], axis=2)
    answer_part = attend_prefix(counts, arrived, turned_keys, wide_values)
    answer = lax.all_to_all(
        answer_part, ("grp", "dev"), split_axis=0, concat_axis=0, tiled=True
    ).reshape(group_count, column_count, capacity + STAT_ROWS, part_width)
    own_mixed, own_top, own_sum = attend_suffix(
        suffix_lengths, suffix_queries, suffix_keys, suffix_values, local_heads
    )
    hidden_state = merge_parts(
        suffix_lengths,
        request_group,
        answer,
        own_mixed,
        own_top,
        own_sum,
        layer_input,
        attn_gain,
        attn_shift,
    )
    up_slice, bias_slice, down_slice = (
        lax.all_gather(up_weight, "grp", axis=1, tiled=True),
        lax.all_gather(up_bias, "grp", axis=0, tiled=True),
        lax.all_gather(down_weight, "grp", axis=0, tiled=True),
    )
    activation = expand_rows(
        lax.all_gather(hidden_state, "dev", axis=0, tiled=True), up_slice, bias_slice
    )
    mlp_sum = lax.psum_scatter(
        jnp.dot(activation, down_slice, preferred_element_type=jnp.float32).astype(jnp.bfloat16),
        "dev",
        scatter_dimension=0,
        tiled=True,
    ).astype(jnp.float32)
    return layer_norm(
        hidden_state.astype(jnp.float32) + mlp_sum + down_bias, out_gain, out_shift
    ).astype(jnp.bfloat16)


def solution(mesh):
    placed = (
        P(("grp", "dev"), None),
        P(("grp", "dev"), None),
        P(("grp", "dev"), None),
        P(("grp", "dev"), None),
        P(("grp", "dev"), None),
        P(("grp", "dev"), None),
        P("grp", None, "dev"),
        P("grp", None, "dev"),
        P(None, ("grp", "dev")),
        P(("grp", "dev")),
        P(("grp", "dev"), None),
        P(),
        P(),
        P(),
        P(),
        P(),
    )
    return jax.shard_map(
        on_device, mesh=mesh, in_specs=placed, out_specs=P(("grp", "dev"), None), check_vma=False
    )
```

```python
import functools
import math

import jax
import jax.numpy as jnp
from jax import lax
from jax.experimental import pallas as pl
from jax.experimental.pallas import tpu as pltpu
from jax.sharding import PartitionSpec as P

HD = 128
LANES = 128
STAT_ROWS = 8
ROW_BLOCK = 256
KEY_CHUNK = 1024

norm_eps = 1e-12
score_scale = HD ** (-0.5)
log2_e = math.log2(math.e)
kernel_vmem = 56 * 1024 * 1024


def layer_norm(summed, norm_gain, norm_shift):
    row_mean = jnp.mean(summed, axis=-1, keepdims=True)
    centred = summed - row_mean
    spread = jnp.mean(centred * centred, axis=-1, keepdims=True)
    return centred * lax.rsqrt(spread + norm_eps) * norm_gain + norm_shift


def vmem_spec():
    return pl.BlockSpec(memory_space=pltpu.VMEM)


def smem_spec():
    return pl.BlockSpec(memory_space=pltpu.SMEM)


def pack_kernel(lengths_ref, groups_ref, query_ref, out_ref, wide_ref):
    request_total = lengths_ref.shape[1]
    _, column_count, chunk_rows, part_width = out_ref.shape
    capacity = chunk_rows - STAT_ROWS
    slot_count = query_ref.shape[0]
    tiles = part_width // LANES
    for tile in range(wide_ref.shape[0]):
        wide_ref[tile, 0:slot_count, :] = query_ref[
            :, tile * LANES : (tile + 1) * LANES
        ].astype(jnp.float32)
        wide_ref[tile, slot_count : slot_count + capacity, :] = jnp.zeros(
            (capacity, LANES), jnp.float32
        )
    start = 0
    for request in range(request_total):
        group = groups_ref[0, request]
        count = jnp.full((STAT_ROWS, LANES), lengths_ref[0, request], jnp.int32).astype(jnp.float32)
        for column in range(column_count):
            for tile in range(tiles):
                rows = wide_ref[column * tiles + tile, pl.ds(start, capacity), :]
                rows = jnp.concatenate([rows, count], axis=0)
                out_ref[group, column, :, tile * LANES : (tile + 1) * LANES] = rows.astype(
                    jnp.bfloat16
                )
        start = start + lengths_ref[0, request]


def pack_queries(lengths, groups, queries, group_count, column_count, capacity):
    slot_count, model_width = queries.shape
    part_width = model_width // column_count
    return pl.pallas_call(
        pack_kernel,
        out_shape=jax.ShapeDtypeStruct(
            (group_count, column_count, capacity + STAT_ROWS, part_width), jnp.bfloat16
        ),
        in_specs=[smem_spec(), smem_spec(), vmem_spec()],
        out_specs=vmem_spec(),
        scratch_shapes=[
            pltpu.VMEM((model_width // LANES, slot_count + capacity, LANES), jnp.float32)
        ],
        compiler_params=pltpu.CompilerParams(vmem_limit_bytes=kernel_vmem),
        name="pack_queries",
    )(lengths, groups, queries)


def far_kernel(
    counts_ref,
    arrived_ref,
    keys_ref,
    values_ref,
    out_ref,
    query_ref,
    answer_ref,
    stat_ref,
    score_ref,
    top_ref,
):
    sources, chunk_rows, part_width = arrived_ref.shape
    capacity = chunk_rows - STAT_ROWS
    local_heads = part_width // HD
    key_total = keys_ref.shape[1]
    chunks = key_total // KEY_CHUNK

    def take(source, offset):
        for head in range(local_heads):
            rows = arrived_ref[source, :, head * HD : (head + 1) * HD].astype(jnp.float32)
            query_ref[head, pl.ds(offset, capacity), :] = rows[:capacity]
        return offset + counts_ref[source]

    total = lax.fori_loop(0, sources, take, jnp.int32(0))
    blocks = (total + ROW_BLOCK - 1) // ROW_BLOCK
    lane = lax.broadcasted_iota(jnp.int32, (ROW_BLOCK, LANES), 1)

    def block_rows(block):
        return pl.ds(pl.multiple_of(block * ROW_BLOCK, ROW_BLOCK), ROW_BLOCK)

    def load_queries(block, head):
        return query_ref[head, block_rows(block), :].astype(jnp.bfloat16)

    def score_chunk(rows, head, slot, chunk, part_top):
        columns = slice(chunk * KEY_CHUNK, (chunk + 1) * KEY_CHUNK)
        scores = jnp.dot(
            rows,
            keys_ref[head * HD : (head + 1) * HD, columns],
            preferred_element_type=jnp.float32,
        )
        score_ref[slot, :, columns] = scores
        for piece in range(KEY_CHUNK // LANES):
            part = scores[:, piece * LANES : (piece + 1) * LANES]
            part_top = part if part_top is None else jnp.maximum(part_top, part)
        return part_top

    def finish_top(part_top, slot):
        row_top = jnp.max(part_top, axis=1, keepdims=True) * score_scale
        row_top = row_top.astype(jnp.bfloat16).astype(jnp.float32)
        top_ref[slot] = jnp.broadcast_to(row_top, (ROW_BLOCK, LANES))

    def weigh_chunk(head, slot, chunk, shift):
        columns = slice(chunk * KEY_CHUNK, (chunk + 1) * KEY_CHUNK)
        weights = jnp.exp2(score_ref[slot, :, columns] * (score_scale * log2_e) - shift)
        return jnp.dot(
            weights.astype(jnp.bfloat16),
            values_ref[head, columns, :],
            preferred_element_type=jnp.float32,
        )

    def finish_answer(block, head, slot, mixed):
        rows = block_rows(block)
        row_sum = mixed[:, HD:]
        answer_ref[head, rows, :] = mixed[:, :HD] / row_sum
        top = top_ref[slot]
        if head == 0:
            stat_ref[rows, :] = jnp.where(lane == 0, top, row_sum)
        else:
            before = stat_ref[rows, :]
            with_top = jnp.where(lane == head, top, before)
            stat_ref[rows, :] = jnp.where(lane == local_heads + head, row_sum, with_top)

    def slot_of(block, head):
        return (block * local_heads + head) % 2 if local_heads % 2 else head % 2

    first_rows = load_queries(0, 0)
    part_top = None
    for chunk in range(chunks):
        part_top = score_chunk(first_rows, 0, 0, chunk, part_top)
    finish_top(part_top, 0)

    def one_block(block, carry):
        for head in range(local_heads):
            slot = slot_of(block, head)
            if head + 1 < local_heads:
                next_block, next_head = block, head + 1
            else:
                next_block, next_head = jnp.minimum(block + 1, blocks - 1), 0
            next_slot = 1 - slot
            next_rows = load_queries(next_block, next_head)
            shift = top_ref[slot][:, 0:1] * log2_e
            part_top = None
            mixed = None
            for chunk in range(chunks):
                part_top = score_chunk(next_rows, next_head, next_slot, chunk, part_top)
                part = weigh_chunk(head, slot, chunk, shift)
                mixed = part if mixed is None else mixed + part
            finish_answer(block, head, slot, mixed)
            finish_top(part_top, next_slot)
        return carry

    lax.fori_loop(0, blocks, one_block, 0)

    def give(source, offset):
        rows = [answer_ref[head, pl.ds(offset, capacity), :] for head in range(local_heads)]
        turned = jnp.transpose(stat_ref[pl.ds(offset, LANES), :])[:STAT_ROWS, :]
        if part_width > LANES:
            turned = jnp.concatenate(
                [turned, jnp.zeros((STAT_ROWS, part_width - LANES), jnp.float32)], axis=1
            )
        rows = jnp.concatenate(rows, axis=1)
        out_ref[source] = jnp.concatenate([rows, turned], axis=0).astype(jnp.bfloat16)
        return offset + counts_ref[source]

    lax.fori_loop(0, sources, give, jnp.int32(0))


def attend_prefix(counts, arrived, turned_keys, wide_values):
    sources, chunk_rows, part_width = arrived.shape
    capacity = chunk_rows - STAT_ROWS
    local_heads = part_width // HD
    key_total = turned_keys.shape[1]
    row_total = -(-sources * capacity // ROW_BLOCK) * ROW_BLOCK + LANES
    return pl.pallas_call(
        far_kernel,
        out_shape=jax.ShapeDtypeStruct((sources, capacity + STAT_ROWS, part_width), jnp.bfloat16),
        in_specs=[smem_spec(), vmem_spec(), vmem_spec(), vmem_spec()],
        out_specs=vmem_spec(),
        scratch_shapes=[
            pltpu.VMEM((local_heads, row_total, HD), jnp.float32),
            pltpu.VMEM((local_heads, row_total, HD), jnp.float32),
            pltpu.VMEM((row_total, LANES), jnp.float32),
            pltpu.VMEM((2, ROW_BLOCK, key_total), jnp.float32),
            pltpu.VMEM((2, ROW_BLOCK, LANES), jnp.float32),
        ],
        compiler_params=pltpu.CompilerParams(vmem_limit_bytes=kernel_vmem),
        cost_estimate=pl.CostEstimate(
            flops=4 * sources * capacity * key_total * part_width,
            bytes_accessed=8 * key_total * part_width,
            transcendentals=sources * capacity * key_total * local_heads,
        ),
        name="attend_prefix",
    )(counts, arrived, turned_keys, wide_values)


def stat_lane(head, local_heads):
    return (head // local_heads) * STAT_ROWS + head % local_heads


def own_kernel(local_heads, lengths_ref, query_ref, key_ref, value_ref, mixed_ref, top_ref, sum_ref):
    slot_count, model_width = query_ref.shape
    head_count = model_width // HD
    row = lax.broadcasted_iota(jnp.int32, (slot_count, slot_count), 0)
    column = lax.broadcasted_iota(jnp.int32, (slot_count, slot_count), 1)
    row_segment = jnp.zeros((slot_count, slot_count), jnp.int32)
    column_segment = jnp.zeros((slot_count, slot_count), jnp.int32)
    start = 0
    for request in range(lengths_ref.shape[1]):
        start = start + lengths_ref[0, request]
        row_segment = row_segment + (row >= start).astype(jnp.int32)
        column_segment = column_segment + (column >= start).astype(jnp.int32)
    visible = (row_segment == column_segment) & (column <= row)
    lane = lax.broadcasted_iota(jnp.int32, (slot_count, LANES), 1)
    tops = jnp.zeros((slot_count, LANES), jnp.float32)
    sums = jnp.ones((slot_count, LANES), jnp.float32)
    for head in range(head_count):
        columns = slice(head * HD, (head + 1) * HD)
        scores = (
            lax.dot_general(
                query_ref[:, columns],
                key_ref[:, columns],
                (((1,), (1,)), ((), ())),
                preferred_element_type=jnp.float32,
            )
            * score_scale
        )
        top = jnp.max(jnp.where(visible, scores, -jnp.inf), axis=1, keepdims=True)
        weights = jnp.where(visible, jnp.exp(scores - top), 0.0)
        mixed_ref[:, columns] = jnp.dot(
            weights.astype(jnp.bfloat16),
            value_ref[:, columns],
            preferred_element_type=jnp.float32,
        )
        at = stat_lane(head, local_heads)
        tops = jnp.where(lane == at, top, tops)
        sums = jnp.where(lane == at, jnp.sum(weights, axis=1, keepdims=True), sums)
    top_ref[...] = tops
    sum_ref[...] = sums


def attend_suffix(lengths, queries, keys, values, local_heads):
    slot_count, model_width = queries.shape
    stats = jax.ShapeDtypeStruct((slot_count, LANES), jnp.float32)
    return pl.pallas_call(
        functools.partial(own_kernel, local_heads),
        out_shape=(jax.ShapeDtypeStruct((slot_count, model_width), jnp.float32), stats, stats),
        in_specs=[smem_spec()] + [vmem_spec()] * 3,
        out_specs=(vmem_spec(), vmem_spec(), vmem_spec()),
        compiler_params=pltpu.CompilerParams(vmem_limit_bytes=kernel_vmem),
        cost_estimate=pl.CostEstimate(
            flops=40 * slot_count * slot_count * model_width,
            bytes_accessed=8 * slot_count * model_width,
            transcendentals=slot_count * model_width,
        ),
        name="attend_suffix",
    )(lengths, queries, keys, values)


def merge_kernel(
    lengths_ref,
    groups_ref,
    arrived_ref,
    own_mixed_ref,
    own_top_ref,
    own_sum_ref,
    input_ref,
    gain_ref,
    shift_ref,
    hidden_ref,
    far_ref,
    stat_ref,
):
    _, column_count, chunk_rows, part_width = arrived_ref.shape
    slot_count, model_width = input_ref.shape
    capacity = chunk_rows - STAT_ROWS
    local_heads = part_width // HD
    head_count = model_width // HD
    start = 0
    for request in range(lengths_ref.shape[1]):
        group = groups_ref[0, request]
        pieces = []
        for column in range(column_count):
            block = arrived_ref[group, column].astype(jnp.float32)
            for head in range(local_heads):
                far_ref[column * local_heads + head, pl.ds(start, capacity), :] = block[
                    :capacity, head * HD : (head + 1) * HD
                ]
            pieces.append(block[capacity:, :LANES])
        if column_count * STAT_ROWS < LANES:
            pieces.append(jnp.zeros((LANES - column_count * STAT_ROWS, LANES), jnp.float32))
        turned = jnp.transpose(jnp.concatenate(pieces, axis=0))
        stat_ref[pl.ds(start, capacity), :] = turned[:capacity]
        start = start + lengths_ref[0, request]
    far_top = stat_ref[:slot_count, :]
    far_sum = pltpu.roll(far_top, LANES - local_heads, 1)
    own_top = own_top_ref[...]
    joint_top = jnp.maximum(far_top, own_top)
    far_weight = jnp.exp(far_top - joint_top) * far_sum
    own_weight = jnp.exp(own_top - joint_top)
    bottom = far_weight + own_weight * own_sum_ref[...]
    far_weight = far_weight / bottom
    own_weight = own_weight / bottom
    total = jnp.zeros((slot_count, LANES), jnp.float32)
    for head in range(head_count):
        columns = slice(head * HD, (head + 1) * HD)
        at = stat_lane(head, local_heads)
        summed = (
            input_ref[:, columns].astype(jnp.float32)
            + far_weight[:, at : at + 1] * far_ref[head, :slot_count, :]
            + own_weight[:, at : at + 1] * own_mixed_ref[:, columns]
        )
        far_ref[head, :slot_count, :] = summed
        total = total + summed
    row_mean = jnp.sum(total, axis=1, keepdims=True) * (1.0 / model_width)
    total = jnp.zeros((slot_count, LANES), jnp.float32)
    for head in range(head_count):
        centred = far_ref[head, :slot_count, :] - row_mean
        total = total + centred * centred
    spread = jnp.sum(total, axis=1, keepdims=True) * (1.0 / model_width)
    factor = lax.rsqrt(spread + norm_eps)
    for head in range(head_count):
        columns = slice(head * HD, (head + 1) * HD)
        centred = far_ref[head, :slot_count, :] - row_mean
        hidden_ref[:, columns] = (
            centred * factor * gain_ref[:, columns] + shift_ref[:, columns]
        ).astype(jnp.bfloat16)


def merge_parts(lengths, groups, arrived, own_mixed, own_top, own_sum, layer_input, gain, shift):
    slot_count, model_width = layer_input.shape
    capacity = arrived.shape[2] - STAT_ROWS
    return pl.pallas_call(
        merge_kernel,
        out_shape=jax.ShapeDtypeStruct((slot_count, model_width), jnp.bfloat16),
        in_specs=[smem_spec(), smem_spec()] + [vmem_spec()] * 7,
        out_specs=vmem_spec(),
        scratch_shapes=[
            pltpu.VMEM((model_width // HD, slot_count + capacity, HD), jnp.float32),
            pltpu.VMEM((slot_count + capacity, LANES), jnp.float32),
        ],
        compiler_params=pltpu.CompilerParams(vmem_limit_bytes=kernel_vmem),
        name="merge_parts",
    )(
        lengths,
        groups,
        arrived,
        own_mixed,
        own_top,
        own_sum,
        layer_input,
        gain.reshape(1, model_width),
        shift.reshape(1, model_width),
    )


def swap(value, mask):
    total = lax.axis_size("grp") * lax.axis_size("dev")
    return lax.ppermute(value, ("grp", "dev"), [(here, here ^ mask) for here in range(total)])


def spread(block, masks):
    held = {0: block}
    for mask in masks:
        held.update({mask ^ at: swap(held[at], mask) for at in list(held)})
    return held


def mlp_kernel(parts, *refs):
    rows_ref, refs = refs[0], refs[1:]
    ups, downs = refs[:parts], refs[parts : 2 * parts]
    out_ref, up_ref, down_ref, sems = refs[2 * parts :]
    model_width = rows_ref.shape[1]
    copies = []
    for part in range(parts):
        up_copy = pltpu.make_async_copy(ups[part], up_ref.at[part], sems.at[part, 0])
        down_copy = pltpu.make_async_copy(downs[part], down_ref.at[part], sems.at[part, 1])
        up_copy.start()
        down_copy.start()
        copies.append((up_copy, down_copy))
    rows = rows_ref[...]
    total = None
    for part in range(parts):
        copies[part][0].wait()
        product = jnp.dot(
            rows, up_ref[part, :model_width, :], preferred_element_type=jnp.float32
        )
        offset = up_ref[part, model_width:, :].astype(jnp.float32)[0:1]
        activation = jax.nn.gelu(product + offset, approximate=True).astype(jnp.bfloat16)
        copies[part][1].wait()
        term = jnp.dot(activation, down_ref[part], preferred_element_type=jnp.float32)
        total = term if total is None else total + term
    out_ref[...] = total.astype(jnp.bfloat16)


def feed_forward(rows, ups, downs):
    parts = len(ups)
    row_count, model_width = rows.shape
    up_rows, units = ups[0].shape
    return pl.pallas_call(
        functools.partial(mlp_kernel, parts),
        out_shape=jax.ShapeDtypeStruct((row_count, model_width), jnp.bfloat16),
        in_specs=[vmem_spec()] + [pl.BlockSpec(memory_space=pl.ANY)] * (2 * parts),
        out_specs=vmem_spec(),
        scratch_shapes=[
            pltpu.VMEM((parts, up_rows, units), jnp.bfloat16),
            pltpu.VMEM((parts, units, model_width), jnp.bfloat16),
            pltpu.SemaphoreType.DMA((parts, 2)),
        ],
        compiler_params=pltpu.CompilerParams(vmem_limit_bytes=kernel_vmem),
        cost_estimate=pl.CostEstimate(
            flops=4 * row_count * model_width * parts * units,
            bytes_accessed=4 * parts * model_width * units,
            transcendentals=row_count * parts * units,
        ),
        name="feed_forward",
    )(rows, *ups, *downs)


def add_kernel(here_ref, there_ref, out_ref):
    out_ref[...] = (
        here_ref[...].astype(jnp.float32) + there_ref[...].astype(jnp.float32)
    ).astype(jnp.bfloat16)


def add_rows(here, there):
    return pl.pallas_call(
        add_kernel,
        out_shape=jax.ShapeDtypeStruct(here.shape, jnp.bfloat16),
        in_specs=[vmem_spec(), vmem_spec()],
        out_specs=vmem_spec(),
        name="add_rows",
    )(here, there)


def finish_kernel(hidden_ref, own_ref, near_ref, far_ref, bias_ref, gain_ref, shift_ref, out_ref):
    summed = hidden_ref[...].astype(jnp.float32) + (
        own_ref[...].astype(jnp.float32)
        + near_ref[...].astype(jnp.float32)
        + far_ref[...].astype(jnp.float32)
    )
    summed = summed + bias_ref[...]
    out_ref[...] = layer_norm(summed, gain_ref[...], shift_ref[...]).astype(jnp.bfloat16)


def finish_rows(hidden, own, near, far, bias, gain, shift):
    model_width = hidden.shape[1]
    return pl.pallas_call(
        finish_kernel,
        out_shape=jax.ShapeDtypeStruct(hidden.shape, jnp.bfloat16),
        in_specs=[vmem_spec()] * 7,
        out_specs=vmem_spec(),
        compiler_params=pltpu.CompilerParams(vmem_limit_bytes=kernel_vmem),
        name="finish_rows",
    )(
        hidden,
        own,
        near,
        far,
        bias.reshape(1, model_width),
        gain.reshape(1, model_width),
        shift.reshape(1, model_width),
    )


def on_device(
    suffix_queries,
    suffix_keys,
    suffix_values,
    layer_input,
    suffix_lengths,
    request_group,
    prefix_keys,
    prefix_values,
    up_weight,
    up_bias,
    down_weight,
    down_bias,
    attn_gain,
    attn_shift,
    out_gain,
    out_shift,
):
    slot_count, model_width = suffix_queries.shape
    group_count = lax.axis_size("grp")
    column_count = lax.axis_size("dev")
    part_width = model_width // column_count
    local_heads = part_width // HD
    capacity = 2 * slot_count // group_count
    sources = group_count * column_count

    outgoing = pack_queries(
        suffix_lengths, request_group, suffix_queries, group_count, column_count, capacity
    )
    arrived = lax.all_to_all(
        outgoing.reshape(sources, capacity + STAT_ROWS, part_width),
        ("grp", "dev"),
        split_axis=0,
        concat_axis=0,
        tiled=True,
    )
    counts = arrived[:, capacity, 0].astype(jnp.int32)
    turned_keys = prefix_keys[0].T
    value_heads = prefix_values[0].reshape(-1, local_heads, HD).transpose(1, 0, 2)
    wide_values = jnp.concatenate([value_heads, jnp.ones_like(value_heads)], axis=2)
    answer_part = attend_prefix(counts, arrived, turned_keys, wide_values)
    answer = lax.all_to_all(
        answer_part, ("grp", "dev"), split_axis=0, concat_axis=0, tiled=True
    ).reshape(group_count, column_count, capacity + STAT_ROWS, part_width)
    own_mixed, own_top, own_sum = attend_suffix(
        suffix_lengths, suffix_queries, suffix_keys, suffix_values, local_heads
    )
    hidden_state = merge_parts(
        suffix_lengths,
        request_group,
        answer,
        own_mixed,
        own_top,
        own_sum,
        layer_input,
        attn_gain,
        attn_shift,
    )
    near_mask = group_count // 2 * column_count
    far_mask = column_count // 2
    column_masks = [1 << bit for bit in range(far_mask.bit_length() - 1)]
    group_masks = [column_count << bit for bit in range((group_count // 2).bit_length() - 1)]
    bias_rows = jnp.broadcast_to(up_bias[None, :], (16, up_bias.shape[0]))
    ups = spread(jnp.concatenate([up_weight, bias_rows], axis=0), column_masks[::-1] + group_masks)
    downs = spread(down_weight, column_masks + group_masks)
    order = sorted(ups)
    ups = [ups[mask] for mask in order]
    downs = [downs[mask] for mask in order]

    far_hidden = swap(hidden_state, far_mask)
    near_hidden = swap(hidden_state, near_mask)
    cross_hidden = swap(far_hidden, near_mask)
    own_part = feed_forward(hidden_state, ups, downs)
    near_part = feed_forward(near_hidden, ups, downs)
    far_part = feed_forward(far_hidden, ups, downs)
    cross_part = feed_forward(cross_hidden, ups, downs)
    near_sum = swap(near_part, near_mask)
    cross_sum = swap(cross_part, near_mask)
    far_sum = swap(add_rows(far_part, cross_sum), far_mask)
    return finish_rows(
        hidden_state, own_part, near_sum, far_sum, down_bias, out_gain, out_shift
    )


def solution(mesh):
    placed = (
        P(("grp", "dev"), None),
        P(("grp", "dev"), None),
        P(("grp", "dev"), None),
        P(("grp", "dev"), None),
        P(("grp", "dev"), None),
        P(("grp", "dev"), None),
        P("grp", None, "dev"),
        P("grp", None, "dev"),
        P(None, ("grp", "dev")),
        P(("grp", "dev")),
        P(("grp", "dev"), None),
        P(),
        P(),
        P(),
        P(),
        P(),
    )
    return jax.shard_map(
        on_device, mesh=mesh, in_specs=placed, out_specs=P(("grp", "dev"), None), check_vma=False
    )
```

```python
import functools
import math

import jax
import jax.numpy as jnp
from jax import lax
from jax.experimental import pallas as pl
from jax.experimental.pallas import tpu as pltpu
from jax.sharding import PartitionSpec as P

HD = 128
LANES = 128
STAT_ROWS = 8
ROW_BLOCK = 256
KEY_CHUNK = 1024

norm_eps = 1e-12
score_scale = HD ** (-0.5)
log2_e = math.log2(math.e)
kernel_vmem = 56 * 1024 * 1024


def layer_norm(summed, norm_gain, norm_shift):
    row_mean = jnp.mean(summed, axis=-1, keepdims=True)
    centred = summed - row_mean
    spread = jnp.mean(centred * centred, axis=-1, keepdims=True)
    return centred * lax.rsqrt(spread + norm_eps) * norm_gain + norm_shift


def vmem_spec():
    return pl.BlockSpec(memory_space=pltpu.VMEM)


def smem_spec():
    return pl.BlockSpec(memory_space=pltpu.SMEM)


def pack_kernel(lengths_ref, groups_ref, query_ref, out_ref, wide_ref):
    request_total = lengths_ref.shape[1]
    _, column_count, chunk_rows, part_width = out_ref.shape
    capacity = chunk_rows - STAT_ROWS
    slot_count = query_ref.shape[0]
    tiles = part_width // LANES
    for tile in range(wide_ref.shape[0]):
        wide_ref[tile, 0:slot_count, :] = query_ref[
            :, tile * LANES : (tile + 1) * LANES
        ].astype(jnp.float32)
        wide_ref[tile, slot_count : slot_count + capacity, :] = jnp.zeros(
            (capacity, LANES), jnp.float32
        )
    start = 0
    for request in range(request_total):
        group = groups_ref[0, request]
        count = jnp.full((STAT_ROWS, LANES), lengths_ref[0, request], jnp.int32).astype(jnp.float32)
        for column in range(column_count):
            for tile in range(tiles):
                rows = wide_ref[column * tiles + tile, pl.ds(start, capacity), :]
                rows = jnp.concatenate([rows, count], axis=0)
                out_ref[group, column, :, tile * LANES : (tile + 1) * LANES] = rows.astype(
                    jnp.bfloat16
                )
        start = start + lengths_ref[0, request]


def pack_queries(lengths, groups, queries, group_count, column_count, capacity):
    slot_count, model_width = queries.shape
    part_width = model_width // column_count
    return pl.pallas_call(
        pack_kernel,
        out_shape=jax.ShapeDtypeStruct(
            (group_count, column_count, capacity + STAT_ROWS, part_width), jnp.bfloat16
        ),
        in_specs=[smem_spec(), smem_spec(), vmem_spec()],
        out_specs=vmem_spec(),
        scratch_shapes=[
            pltpu.VMEM((model_width // LANES, slot_count + capacity, LANES), jnp.float32)
        ],
        compiler_params=pltpu.CompilerParams(vmem_limit_bytes=kernel_vmem),
        name="pack_queries",
    )(lengths, groups, queries)


def far_kernel(
    counts_ref,
    arrived_ref,
    keys_ref,
    values_ref,
    out_ref,
    query_ref,
    answer_ref,
    stat_ref,
    score_ref,
    top_ref,
):
    sources, chunk_rows, part_width = arrived_ref.shape
    capacity = chunk_rows - STAT_ROWS
    local_heads = part_width // HD
    key_total = keys_ref.shape[1]
    chunks = key_total // KEY_CHUNK

    def take(source, offset):
        for head in range(local_heads):
            rows = arrived_ref[source, :, head * HD : (head + 1) * HD].astype(jnp.float32)
            query_ref[head, pl.ds(offset, capacity), :] = rows[:capacity]
        return offset + counts_ref[source]

    total = lax.fori_loop(0, sources, take, jnp.int32(0))
    blocks = (total + ROW_BLOCK - 1) // ROW_BLOCK
    lane = lax.broadcasted_iota(jnp.int32, (ROW_BLOCK, LANES), 1)

    def block_rows(block):
        return pl.ds(pl.multiple_of(block * ROW_BLOCK, ROW_BLOCK), ROW_BLOCK)

    def load_queries(block, head):
        return query_ref[head, block_rows(block), :].astype(jnp.bfloat16)

    def score_chunk(rows, head, slot, chunk, part_top):
        columns = slice(chunk * KEY_CHUNK, (chunk + 1) * KEY_CHUNK)
        scores = jnp.dot(
            rows,
            keys_ref[head * HD : (head + 1) * HD, columns],
            preferred_element_type=jnp.float32,
        )
        score_ref[slot, :, columns] = scores
        for piece in range(KEY_CHUNK // LANES):
            part = scores[:, piece * LANES : (piece + 1) * LANES]
            part_top = part if part_top is None else jnp.maximum(part_top, part)
        return part_top

    def finish_top(part_top, slot):
        row_top = jnp.max(part_top, axis=1, keepdims=True) * score_scale
        row_top = row_top.astype(jnp.bfloat16).astype(jnp.float32)
        top_ref[slot] = jnp.broadcast_to(row_top, (ROW_BLOCK, LANES))

    def weigh_chunk(head, slot, chunk, shift):
        columns = slice(chunk * KEY_CHUNK, (chunk + 1) * KEY_CHUNK)
        weights = jnp.exp2(score_ref[slot, :, columns] * (score_scale * log2_e) - shift)
        return jnp.dot(
            weights.astype(jnp.bfloat16),
            values_ref[head, columns, :],
            preferred_element_type=jnp.float32,
        )

    def finish_answer(block, head, slot, mixed):
        rows = block_rows(block)
        row_sum = mixed[:, HD:]
        answer_ref[head, rows, :] = mixed[:, :HD] / row_sum
        top = top_ref[slot]
        if head == 0:
            stat_ref[rows, :] = jnp.where(lane == 0, top, row_sum)
        else:
            before = stat_ref[rows, :]
            with_top = jnp.where(lane == head, top, before)
            stat_ref[rows, :] = jnp.where(lane == local_heads + head, row_sum, with_top)

    def slot_of(block, head):
        return (block * local_heads + head) % 2 if local_heads % 2 else head % 2

    first_rows = load_queries(0, 0)
    part_top = None
    for chunk in range(chunks):
        part_top = score_chunk(first_rows, 0, 0, chunk, part_top)
    finish_top(part_top, 0)

    def one_block(block, carry):
        for head in range(local_heads):
            slot = slot_of(block, head)
            if head + 1 < local_heads:
                next_block, next_head = block, head + 1
            else:
                next_block, next_head = jnp.minimum(block + 1, blocks - 1), 0
            next_slot = 1 - slot
            next_rows = load_queries(next_block, next_head)
            shift = top_ref[slot][:, 0:1] * log2_e
            part_top = None
            mixed = None
            for chunk in range(chunks):
                part_top = score_chunk(next_rows, next_head, next_slot, chunk, part_top)
                part = weigh_chunk(head, slot, chunk, shift)
                mixed = part if mixed is None else mixed + part
            finish_answer(block, head, slot, mixed)
            finish_top(part_top, next_slot)
        return carry

    lax.fori_loop(0, blocks, one_block, 0)

    def give(source, offset):
        rows = [answer_ref[head, pl.ds(offset, capacity), :] for head in range(local_heads)]
        turned = jnp.transpose(stat_ref[pl.ds(offset, LANES), :])[:STAT_ROWS, :]
        if part_width > LANES:
            turned = jnp.concatenate(
                [turned, jnp.zeros((STAT_ROWS, part_width - LANES), jnp.float32)], axis=1
            )
        rows = jnp.concatenate(rows, axis=1)
        out_ref[source] = jnp.concatenate([rows, turned], axis=0).astype(jnp.bfloat16)
        return offset + counts_ref[source]

    lax.fori_loop(0, sources, give, jnp.int32(0))


def attend_prefix(counts, arrived, turned_keys, wide_values):
    sources, chunk_rows, part_width = arrived.shape
    capacity = chunk_rows - STAT_ROWS
    local_heads = part_width // HD
    key_total = turned_keys.shape[1]
    row_total = -(-sources * capacity // ROW_BLOCK) * ROW_BLOCK + LANES
    return pl.pallas_call(
        far_kernel,
        out_shape=jax.ShapeDtypeStruct((sources, capacity + STAT_ROWS, part_width), jnp.bfloat16),
        in_specs=[smem_spec(), vmem_spec(), vmem_spec(), vmem_spec()],
        out_specs=vmem_spec(),
        scratch_shapes=[
            pltpu.VMEM((local_heads, row_total, HD), jnp.float32),
            pltpu.VMEM((local_heads, row_total, HD), jnp.float32),
            pltpu.VMEM((row_total, LANES), jnp.float32),
            pltpu.VMEM((2, ROW_BLOCK, key_total), jnp.float32),
            pltpu.VMEM((2, ROW_BLOCK, LANES), jnp.float32),
        ],
        compiler_params=pltpu.CompilerParams(vmem_limit_bytes=kernel_vmem),
        cost_estimate=pl.CostEstimate(
            flops=4 * sources * capacity * key_total * part_width,
            bytes_accessed=8 * key_total * part_width,
            transcendentals=sources * capacity * key_total * local_heads,
        ),
        name="attend_prefix",
    )(counts, arrived, turned_keys, wide_values)


def stat_lane(head, local_heads):
    return (head // local_heads) * STAT_ROWS + head % local_heads


def own_kernel(local_heads, lengths_ref, query_ref, key_ref, value_ref, mixed_ref, top_ref, sum_ref):
    slot_count, model_width = query_ref.shape
    head_count = model_width // HD
    row = lax.broadcasted_iota(jnp.int32, (slot_count, slot_count), 0)
    column = lax.broadcasted_iota(jnp.int32, (slot_count, slot_count), 1)
    row_segment = jnp.zeros((slot_count, slot_count), jnp.int32)
    column_segment = jnp.zeros((slot_count, slot_count), jnp.int32)
    start = 0
    for request in range(lengths_ref.shape[1]):
        start = start + lengths_ref[0, request]
        row_segment = row_segment + (row >= start).astype(jnp.int32)
        column_segment = column_segment + (column >= start).astype(jnp.int32)
    visible = (row_segment == column_segment) & (column <= row)
    lane = lax.broadcasted_iota(jnp.int32, (slot_count, LANES), 1)
    tops = jnp.zeros((slot_count, LANES), jnp.float32)
    sums = jnp.ones((slot_count, LANES), jnp.float32)
    for head in range(head_count):
        columns = slice(head * HD, (head + 1) * HD)
        scores = (
            lax.dot_general(
                query_ref[:, columns],
                key_ref[:, columns],
                (((1,), (1,)), ((), ())),
                preferred_element_type=jnp.float32,
            )
            * score_scale
        )
        top = jnp.max(jnp.where(visible, scores, -jnp.inf), axis=1, keepdims=True)
        weights = jnp.where(visible, jnp.exp(scores - top), 0.0)
        mixed_ref[:, columns] = jnp.dot(
            weights.astype(jnp.bfloat16),
            value_ref[:, columns],
            preferred_element_type=jnp.float32,
        )
        at = stat_lane(head, local_heads)
        tops = jnp.where(lane == at, top, tops)
        sums = jnp.where(lane == at, jnp.sum(weights, axis=1, keepdims=True), sums)
    top_ref[...] = tops
    sum_ref[...] = sums


def attend_suffix(lengths, queries, keys, values, local_heads):
    slot_count, model_width = queries.shape
    stats = jax.ShapeDtypeStruct((slot_count, LANES), jnp.float32)
    return pl.pallas_call(
        functools.partial(own_kernel, local_heads),
        out_shape=(jax.ShapeDtypeStruct((slot_count, model_width), jnp.float32), stats, stats),
        in_specs=[smem_spec()] + [vmem_spec()] * 3,
        out_specs=(vmem_spec(), vmem_spec(), vmem_spec()),
        compiler_params=pltpu.CompilerParams(vmem_limit_bytes=kernel_vmem),
        cost_estimate=pl.CostEstimate(
            flops=40 * slot_count * slot_count * model_width,
            bytes_accessed=8 * slot_count * model_width,
            transcendentals=slot_count * model_width,
        ),
        name="attend_suffix",
    )(lengths, queries, keys, values)


def merge_kernel(
    lengths_ref,
    groups_ref,
    arrived_ref,
    own_mixed_ref,
    own_top_ref,
    own_sum_ref,
    input_ref,
    gain_ref,
    shift_ref,
    hidden_ref,
    far_ref,
    stat_ref,
):
    _, column_count, chunk_rows, part_width = arrived_ref.shape
    slot_count, model_width = input_ref.shape
    capacity = chunk_rows - STAT_ROWS
    local_heads = part_width // HD
    head_count = model_width // HD
    start = 0
    for request in range(lengths_ref.shape[1]):
        group = groups_ref[0, request]
        pieces = []
        for column in range(column_count):
            block = arrived_ref[group, column].astype(jnp.float32)
            for head in range(local_heads):
                far_ref[column * local_heads + head, pl.ds(start, capacity), :] = block[
                    :capacity, head * HD : (head + 1) * HD
                ]
            pieces.append(block[capacity:, :LANES])
        if column_count * STAT_ROWS < LANES:
            pieces.append(jnp.zeros((LANES - column_count * STAT_ROWS, LANES), jnp.float32))
        turned = jnp.transpose(jnp.concatenate(pieces, axis=0))
        stat_ref[pl.ds(start, capacity), :] = turned[:capacity]
        start = start + lengths_ref[0, request]
    far_top = stat_ref[:slot_count, :]
    far_sum = pltpu.roll(far_top, LANES - local_heads, 1)
    own_top = own_top_ref[...]
    joint_top = jnp.maximum(far_top, own_top)
    far_weight = jnp.exp(far_top - joint_top) * far_sum
    own_weight = jnp.exp(own_top - joint_top)
    bottom = far_weight + own_weight * own_sum_ref[...]
    far_weight = far_weight / bottom
    own_weight = own_weight / bottom
    total = jnp.zeros((slot_count, LANES), jnp.float32)
    for head in range(head_count):
        columns = slice(head * HD, (head + 1) * HD)
        at = stat_lane(head, local_heads)
        summed = (
            input_ref[:, columns].astype(jnp.float32)
            + far_weight[:, at : at + 1] * far_ref[head, :slot_count, :]
            + own_weight[:, at : at + 1] * own_mixed_ref[:, columns]
        )
        far_ref[head, :slot_count, :] = summed
        total = total + summed
    row_mean = jnp.sum(total, axis=1, keepdims=True) * (1.0 / model_width)
    total = jnp.zeros((slot_count, LANES), jnp.float32)
    for head in range(head_count):
        centred = far_ref[head, :slot_count, :] - row_mean
        total = total + centred * centred
    spread = jnp.sum(total, axis=1, keepdims=True) * (1.0 / model_width)
    factor = lax.rsqrt(spread + norm_eps)
    for head in range(head_count):
        columns = slice(head * HD, (head + 1) * HD)
        centred = far_ref[head, :slot_count, :] - row_mean
        hidden_ref[:, columns] = (
            centred * factor * gain_ref[:, columns] + shift_ref[:, columns]
        ).astype(jnp.bfloat16)


def merge_parts(lengths, groups, arrived, own_mixed, own_top, own_sum, layer_input, gain, shift):
    slot_count, model_width = layer_input.shape
    capacity = arrived.shape[2] - STAT_ROWS
    return pl.pallas_call(
        merge_kernel,
        out_shape=jax.ShapeDtypeStruct((slot_count, model_width), jnp.bfloat16),
        in_specs=[smem_spec(), smem_spec()] + [vmem_spec()] * 7,
        out_specs=vmem_spec(),
        scratch_shapes=[
            pltpu.VMEM((model_width // HD, slot_count + capacity, HD), jnp.float32),
            pltpu.VMEM((slot_count + capacity, LANES), jnp.float32),
        ],
        compiler_params=pltpu.CompilerParams(vmem_limit_bytes=kernel_vmem),
        name="merge_parts",
    )(
        lengths,
        groups,
        arrived,
        own_mixed,
        own_top,
        own_sum,
        layer_input,
        gain.reshape(1, model_width),
        shift.reshape(1, model_width),
    )


def swap(value, mask):
    total = lax.axis_size("grp") * lax.axis_size("dev")
    return lax.ppermute(value, ("grp", "dev"), [(here, here ^ mask) for here in range(total)])


def complete(held, masks):
    held = dict(held)
    for mask in masks:
        for at in list(held):
            if mask ^ at not in held:
                held[mask ^ at] = swap(held[at], mask)
    return held


def mlp_kernel(parts, *refs):
    rows_ref, refs = refs[0], refs[1:]
    ups, downs = refs[:parts], refs[parts : 2 * parts]
    out_ref, up_ref, down_ref, sems = refs[2 * parts :]
    model_width = rows_ref.shape[1]
    copies = []
    for part in range(parts):
        up_copy = pltpu.make_async_copy(ups[part], up_ref.at[part], sems.at[part, 0])
        down_copy = pltpu.make_async_copy(downs[part], down_ref.at[part], sems.at[part, 1])
        up_copy.start()
        down_copy.start()
        copies.append((up_copy, down_copy))
    rows = rows_ref[...]
    total = None
    for part in range(parts):
        copies[part][0].wait()
        product = jnp.dot(
            rows, up_ref[part, :model_width, :], preferred_element_type=jnp.float32
        )
        offset = up_ref[part, model_width:, :].astype(jnp.float32)[0:1]
        activation = jax.nn.gelu(product + offset, approximate=True).astype(jnp.bfloat16)
        copies[part][1].wait()
        term = jnp.dot(activation, down_ref[part], preferred_element_type=jnp.float32)
        total = term if total is None else total + term
    out_ref[...] = total.astype(jnp.bfloat16)


def feed_forward(rows, ups, downs):
    parts = len(ups)
    row_count, model_width = rows.shape
    up_rows, units = ups[0].shape
    return pl.pallas_call(
        functools.partial(mlp_kernel, parts),
        out_shape=jax.ShapeDtypeStruct((row_count, model_width), jnp.bfloat16),
        in_specs=[vmem_spec()] + [pl.BlockSpec(memory_space=pl.ANY)] * (2 * parts),
        out_specs=vmem_spec(),
        scratch_shapes=[
            pltpu.VMEM((parts, up_rows, units), jnp.bfloat16),
            pltpu.VMEM((parts, units, model_width), jnp.bfloat16),
            pltpu.SemaphoreType.DMA((parts, 2)),
        ],
        compiler_params=pltpu.CompilerParams(vmem_limit_bytes=kernel_vmem),
        cost_estimate=pl.CostEstimate(
            flops=4 * row_count * model_width * parts * units,
            bytes_accessed=4 * parts * model_width * units,
            transcendentals=row_count * parts * units,
        ),
        name="feed_forward",
    )(rows, *ups, *downs)


def add_kernel(here_ref, there_ref, out_ref):
    out_ref[...] = (
        here_ref[...].astype(jnp.float32) + there_ref[...].astype(jnp.float32)
    ).astype(jnp.bfloat16)


def add_rows(here, there):
    return pl.pallas_call(
        add_kernel,
        out_shape=jax.ShapeDtypeStruct(here.shape, jnp.bfloat16),
        in_specs=[vmem_spec(), vmem_spec()],
        out_specs=vmem_spec(),
        name="add_rows",
    )(here, there)


def finish_kernel(hidden_ref, own_ref, near_ref, far_ref, bias_ref, gain_ref, shift_ref, out_ref):
    summed = hidden_ref[...].astype(jnp.float32) + (
        own_ref[...].astype(jnp.float32)
        + near_ref[...].astype(jnp.float32)
        + far_ref[...].astype(jnp.float32)
    )
    summed = summed + bias_ref[...]
    out_ref[...] = layer_norm(summed, gain_ref[...], shift_ref[...]).astype(jnp.bfloat16)


def finish_rows(hidden, own, near, far, bias, gain, shift):
    model_width = hidden.shape[1]
    return pl.pallas_call(
        finish_kernel,
        out_shape=jax.ShapeDtypeStruct(hidden.shape, jnp.bfloat16),
        in_specs=[vmem_spec()] * 7,
        out_specs=vmem_spec(),
        compiler_params=pltpu.CompilerParams(vmem_limit_bytes=kernel_vmem),
        name="finish_rows",
    )(
        hidden,
        own,
        near,
        far,
        bias.reshape(1, model_width),
        gain.reshape(1, model_width),
        shift.reshape(1, model_width),
    )


def on_device(
    suffix_queries,
    suffix_keys,
    suffix_values,
    layer_input,
    suffix_lengths,
    request_group,
    prefix_keys,
    prefix_values,
    up_weight,
    up_bias,
    down_weight,
    down_bias,
    attn_gain,
    attn_shift,
    out_gain,
    out_shift,
):
    slot_count, model_width = suffix_queries.shape
    group_count = lax.axis_size("grp")
    column_count = lax.axis_size("dev")
    part_width = model_width // column_count
    local_heads = part_width // HD
    capacity = 2 * slot_count // group_count
    sources = group_count * column_count

    near_mask = group_count // 2 * column_count
    far_mask = column_count // 2
    column_masks = [1 << bit for bit in range(far_mask.bit_length() - 1)]
    group_masks = [column_count << bit for bit in range((group_count // 2).bit_length() - 1)]

    outgoing = pack_queries(
        suffix_lengths, request_group, suffix_queries, group_count, column_count, capacity
    )
    bias_rows = jnp.broadcast_to(up_bias[None, :], (16, up_bias.shape[0]))
    ups = {0: jnp.concatenate([up_weight, bias_rows], axis=0)}
    downs = {0: down_weight}

    arrived = lax.all_to_all(
        outgoing.reshape(sources, capacity + STAT_ROWS, part_width),
        ("grp", "dev"),
        split_axis=0,
        concat_axis=0,
        tiled=True,
    )
    for mask in column_masks:
        ups[mask] = swap(ups[0], mask)
    arrived, ups, downs = lax.optimization_barrier((arrived, ups, downs))

    counts = arrived[:, capacity, 0].astype(jnp.int32)
    turned_keys = prefix_keys[0].T
    value_heads = prefix_values[0].reshape(-1, local_heads, HD).transpose(1, 0, 2)
    wide_values = jnp.concatenate([value_heads, jnp.ones_like(value_heads)], axis=2)
    answer_part = attend_prefix(counts, arrived, turned_keys, wide_values)
    for mask in column_masks:
        downs[mask] = swap(downs[0], mask)
    answer_part, ups, downs = lax.optimization_barrier((answer_part, ups, downs))

    answer = lax.all_to_all(
        answer_part, ("grp", "dev"), split_axis=0, concat_axis=0, tiled=True
    ).reshape(group_count, column_count, capacity + STAT_ROWS, part_width)
    ups = complete(ups, column_masks[::-1])
    downs = complete(downs, column_masks)
    own_mixed, own_top, own_sum = attend_suffix(
        suffix_lengths, suffix_queries, suffix_keys, suffix_values, local_heads
    )
    answer, ups, downs, own_mixed = lax.optimization_barrier((answer, ups, downs, own_mixed))

    hidden_state = merge_parts(
        suffix_lengths,
        request_group,
        answer,
        own_mixed,
        own_top,
        own_sum,
        layer_input,
        attn_gain,
        attn_shift,
    )

    far_hidden = swap(hidden_state, far_mask)
    near_hidden = swap(hidden_state, near_mask)
    ups = complete(ups, group_masks)
    downs = complete(downs, group_masks)
    order = sorted(ups)
    ups = [ups[mask] for mask in order]
    downs = [downs[mask] for mask in order]
    own_part = feed_forward(hidden_state, ups, downs)
    near_part = feed_forward(near_hidden, ups, downs)
    far_hidden, own_part, near_part = lax.optimization_barrier((far_hidden, own_part, near_part))
    cross_hidden = swap(far_hidden, near_mask)
    near_sum = swap(near_part, near_mask)
    far_part = feed_forward(far_hidden, ups, downs)
    cross_hidden, far_part = lax.optimization_barrier((cross_hidden, far_part))
    cross_part = feed_forward(cross_hidden, ups, downs)
    cross_sum = swap(cross_part, near_mask)
    far_sum = swap(add_rows(far_part, cross_sum), far_mask)
    return finish_rows(
        hidden_state, own_part, near_sum, far_sum, down_bias, out_gain, out_shift
    )


def solution(mesh):
    placed = (
        P(("grp", "dev"), None),
        P(("grp", "dev"), None),
        P(("grp", "dev"), None),
        P(("grp", "dev"), None),
        P(("grp", "dev"), None),
        P(("grp", "dev"), None),
        P("grp", None, "dev"),
        P("grp", None, "dev"),
        P(None, ("grp", "dev")),
        P(("grp", "dev")),
        P(("grp", "dev"), None),
        P(),
        P(),
        P(),
        P(),
        P(),
    )
    return jax.shard_map(
        on_device, mesh=mesh, in_specs=placed, out_specs=P(("grp", "dev"), None), check_vma=False
    )
```

```python
import functools
import math

import jax
import jax.numpy as jnp
from jax import lax
from jax.experimental import pallas as pl
from jax.experimental.pallas import tpu as pltpu
from jax.sharding import PartitionSpec as P

HD = 128
LANES = 128
STAT_ROWS = 8
ROW_BLOCK = 256
KEY_CHUNK = 1024

norm_eps = 1e-12
score_scale = HD ** (-0.5)
log2_e = math.log2(math.e)
mebibyte = 1024 * 1024


def layer_norm(summed, norm_gain, norm_shift):
    row_mean = jnp.mean(summed, axis=-1, keepdims=True)
    centred = summed - row_mean
    spread = jnp.mean(centred * centred, axis=-1, keepdims=True)
    return centred * lax.rsqrt(spread + norm_eps) * norm_gain + norm_shift


def vmem_spec():
    return pl.BlockSpec(memory_space=pltpu.VMEM)


def smem_spec():
    return pl.BlockSpec(memory_space=pltpu.SMEM)


def pack_kernel(lengths_ref, groups_ref, query_ref, out_ref, wide_ref):
    request_total = lengths_ref.shape[1]
    _, column_count, chunk_rows, part_width = out_ref.shape
    capacity = chunk_rows - STAT_ROWS
    slot_count = query_ref.shape[0]
    tiles = part_width // LANES
    for tile in range(wide_ref.shape[0]):
        wide_ref[tile, 0:slot_count, :] = query_ref[
            :, tile * LANES : (tile + 1) * LANES
        ].astype(jnp.float32)
        wide_ref[tile, slot_count : slot_count + capacity, :] = jnp.zeros(
            (capacity, LANES), jnp.float32
        )
    start = 0
    for request in range(request_total):
        group = groups_ref[0, request]
        count = jnp.full((STAT_ROWS, LANES), lengths_ref[0, request], jnp.int32).astype(jnp.float32)
        for column in range(column_count):
            for tile in range(tiles):
                rows = wide_ref[column * tiles + tile, pl.ds(start, capacity), :]
                rows = jnp.concatenate([rows, count], axis=0)
                out_ref[group, column, :, tile * LANES : (tile + 1) * LANES] = rows.astype(
                    jnp.bfloat16
                )
        start = start + lengths_ref[0, request]


def pack_queries(lengths, groups, queries, group_count, column_count, capacity):
    slot_count, model_width = queries.shape
    part_width = model_width // column_count
    return pl.pallas_call(
        pack_kernel,
        out_shape=jax.ShapeDtypeStruct(
            (group_count, column_count, capacity + STAT_ROWS, part_width), jnp.bfloat16
        ),
        in_specs=[smem_spec(), smem_spec(), vmem_spec()],
        out_specs=vmem_spec(),
        scratch_shapes=[
            pltpu.VMEM((model_width // LANES, slot_count + capacity, LANES), jnp.float32)
        ],
        compiler_params=pltpu.CompilerParams(vmem_limit_bytes=16 * mebibyte),
        name="pack_queries",
    )(lengths, groups, queries)


def far_kernel(
    counts_ref,
    arrived_ref,
    keys_ref,
    values_ref,
    out_ref,
    query_ref,
    answer_ref,
    stat_ref,
    score_ref,
    top_ref,
):
    sources, chunk_rows, part_width = arrived_ref.shape
    capacity = chunk_rows - STAT_ROWS
    local_heads = part_width // HD
    key_total = keys_ref.shape[1]
    chunks = key_total // KEY_CHUNK

    def take(source, offset):
        for head in range(local_heads):
            rows = arrived_ref[source, :, head * HD : (head + 1) * HD].astype(jnp.float32)
            query_ref[head, pl.ds(offset, capacity), :] = rows[:capacity]
        return offset + counts_ref[source]

    total = lax.fori_loop(0, sources, take, jnp.int32(0))
    blocks = (total + ROW_BLOCK - 1) // ROW_BLOCK
    lane = lax.broadcasted_iota(jnp.int32, (ROW_BLOCK, LANES), 1)

    def block_rows(block):
        return pl.ds(pl.multiple_of(block * ROW_BLOCK, ROW_BLOCK), ROW_BLOCK)

    def load_queries(block, head):
        return query_ref[head, block_rows(block), :].astype(jnp.bfloat16)

    def score_chunk(rows, head, slot, chunk, part_top):
        columns = slice(chunk * KEY_CHUNK, (chunk + 1) * KEY_CHUNK)
        scores = jnp.dot(
            rows,
            keys_ref[head * HD : (head + 1) * HD, columns],
            preferred_element_type=jnp.float32,
        )
        score_ref[slot, :, columns] = scores
        for piece in range(KEY_CHUNK // LANES):
            part = scores[:, piece * LANES : (piece + 1) * LANES]
            part_top = part if part_top is None else jnp.maximum(part_top, part)
        return part_top

    def finish_top(part_top, slot):
        row_top = jnp.max(part_top, axis=1, keepdims=True) * score_scale
        row_top = row_top.astype(jnp.bfloat16).astype(jnp.float32)
        top_ref[slot] = jnp.broadcast_to(row_top, (ROW_BLOCK, LANES))

    def weigh_chunk(head, slot, chunk, shift):
        columns = slice(chunk * KEY_CHUNK, (chunk + 1) * KEY_CHUNK)
        weights = jnp.exp2(score_ref[slot, :, columns] * (score_scale * log2_e) - shift)
        return jnp.dot(
            weights.astype(jnp.bfloat16),
            values_ref[head, columns, :],
            preferred_element_type=jnp.float32,
        )

    def finish_answer(block, head, slot, mixed):
        rows = block_rows(block)
        row_sum = mixed[:, HD:]
        answer_ref[head, rows, :] = mixed[:, :HD] / row_sum
        top = top_ref[slot]
        if head == 0:
            stat_ref[rows, :] = jnp.where(lane == 0, top, row_sum)
        else:
            before = stat_ref[rows, :]
            with_top = jnp.where(lane == head, top, before)
            stat_ref[rows, :] = jnp.where(lane == local_heads + head, row_sum, with_top)

    def slot_of(block, head):
        return (block * local_heads + head) % 2 if local_heads % 2 else head % 2

    first_rows = load_queries(0, 0)
    part_top = None
    for chunk in range(chunks):
        part_top = score_chunk(first_rows, 0, 0, chunk, part_top)
    finish_top(part_top, 0)

    def one_block(block, carry):
        for head in range(local_heads):
            slot = slot_of(block, head)
            if head + 1 < local_heads:
                next_block, next_head = block, head + 1
            else:
                next_block, next_head = jnp.minimum(block + 1, blocks - 1), 0
            next_slot = 1 - slot
            next_rows = load_queries(next_block, next_head)
            shift = top_ref[slot][:, 0:1] * log2_e
            part_top = None
            mixed = None
            for chunk in range(chunks):
                part_top = score_chunk(next_rows, next_head, next_slot, chunk, part_top)
                part = weigh_chunk(head, slot, chunk, shift)
                mixed = part if mixed is None else mixed + part
            finish_answer(block, head, slot, mixed)
            finish_top(part_top, next_slot)
        return carry

    lax.fori_loop(0, blocks, one_block, 0)

    def give(source, offset):
        rows = [answer_ref[head, pl.ds(offset, capacity), :] for head in range(local_heads)]
        turned = jnp.transpose(stat_ref[pl.ds(offset, LANES), :])[:STAT_ROWS, :]
        if part_width > LANES:
            turned = jnp.concatenate(
                [turned, jnp.zeros((STAT_ROWS, part_width - LANES), jnp.float32)], axis=1
            )
        rows = jnp.concatenate(rows, axis=1)
        out_ref[source] = jnp.concatenate([rows, turned], axis=0).astype(jnp.bfloat16)
        return offset + counts_ref[source]

    lax.fori_loop(0, sources, give, jnp.int32(0))


def attend_prefix(counts, arrived, turned_keys, wide_values):
    sources, chunk_rows, part_width = arrived.shape
    capacity = chunk_rows - STAT_ROWS
    local_heads = part_width // HD
    key_total = turned_keys.shape[1]
    row_total = -(-sources * capacity // ROW_BLOCK) * ROW_BLOCK + LANES
    return pl.pallas_call(
        far_kernel,
        out_shape=jax.ShapeDtypeStruct((sources, capacity + STAT_ROWS, part_width), jnp.bfloat16),
        in_specs=[smem_spec(), vmem_spec(), vmem_spec(), vmem_spec()],
        out_specs=vmem_spec(),
        scratch_shapes=[
            pltpu.VMEM((local_heads, row_total, HD), jnp.float32),
            pltpu.VMEM((local_heads, row_total, HD), jnp.float32),
            pltpu.VMEM((row_total, LANES), jnp.float32),
            pltpu.VMEM((2, ROW_BLOCK, key_total), jnp.float32),
            pltpu.VMEM((2, ROW_BLOCK, LANES), jnp.float32),
        ],
        compiler_params=pltpu.CompilerParams(vmem_limit_bytes=40 * mebibyte),
        cost_estimate=pl.CostEstimate(
            flops=4 * sources * capacity * key_total * part_width,
            bytes_accessed=8 * key_total * part_width,
            transcendentals=sources * capacity * key_total * local_heads,
        ),
        name="attend_prefix",
    )(counts, arrived, turned_keys, wide_values)


def stat_lane(head, local_heads):
    return (head // local_heads) * STAT_ROWS + head % local_heads


def own_kernel(local_heads, lengths_ref, query_ref, key_ref, value_ref, mixed_ref, top_ref, sum_ref):
    slot_count, model_width = query_ref.shape
    head_count = model_width // HD
    row = lax.broadcasted_iota(jnp.int32, (slot_count, slot_count), 0)
    column = lax.broadcasted_iota(jnp.int32, (slot_count, slot_count), 1)
    row_segment = jnp.zeros((slot_count, slot_count), jnp.int32)
    column_segment = jnp.zeros((slot_count, slot_count), jnp.int32)
    start = 0
    for request in range(lengths_ref.shape[1]):
        start = start + lengths_ref[0, request]
        row_segment = row_segment + (row >= start).astype(jnp.int32)
        column_segment = column_segment + (column >= start).astype(jnp.int32)
    visible = (row_segment == column_segment) & (column <= row)
    lane = lax.broadcasted_iota(jnp.int32, (slot_count, LANES), 1)
    tops = jnp.zeros((slot_count, LANES), jnp.float32)
    sums = jnp.ones((slot_count, LANES), jnp.float32)
    for head in range(head_count):
        columns = slice(head * HD, (head + 1) * HD)
        scores = (
            lax.dot_general(
                query_ref[:, columns],
                key_ref[:, columns],
                (((1,), (1,)), ((), ())),
                preferred_element_type=jnp.float32,
            )
            * score_scale
        )
        top = jnp.max(jnp.where(visible, scores, -jnp.inf), axis=1, keepdims=True)
        weights = jnp.where(visible, jnp.exp(scores - top), 0.0)
        mixed_ref[:, columns] = jnp.dot(
            weights.astype(jnp.bfloat16),
            value_ref[:, columns],
            preferred_element_type=jnp.float32,
        )
        at = stat_lane(head, local_heads)
        tops = jnp.where(lane == at, top, tops)
        sums = jnp.where(lane == at, jnp.sum(weights, axis=1, keepdims=True), sums)
    top_ref[...] = tops
    sum_ref[...] = sums


def attend_suffix(lengths, queries, keys, values, local_heads):
    slot_count, model_width = queries.shape
    stats = jax.ShapeDtypeStruct((slot_count, LANES), jnp.float32)
    return pl.pallas_call(
        functools.partial(own_kernel, local_heads),
        out_shape=(jax.ShapeDtypeStruct((slot_count, model_width), jnp.float32), stats, stats),
        in_specs=[smem_spec()] + [vmem_spec()] * 3,
        out_specs=(vmem_spec(), vmem_spec(), vmem_spec()),
        compiler_params=pltpu.CompilerParams(vmem_limit_bytes=16 * mebibyte),
        cost_estimate=pl.CostEstimate(
            flops=40 * slot_count * slot_count * model_width,
            bytes_accessed=8 * slot_count * model_width,
            transcendentals=slot_count * model_width,
        ),
        name="attend_suffix",
    )(lengths, queries, keys, values)


def merge_kernel(
    lengths_ref,
    groups_ref,
    arrived_ref,
    own_mixed_ref,
    own_top_ref,
    own_sum_ref,
    input_ref,
    gain_ref,
    shift_ref,
    first_ref,
    second_ref,
    far_ref,
    stat_ref,
):
    _, column_count, chunk_rows, part_width = arrived_ref.shape
    slot_count, model_width = input_ref.shape
    capacity = chunk_rows - STAT_ROWS
    local_heads = part_width // HD
    head_count = model_width // HD
    start = 0
    for request in range(lengths_ref.shape[1]):
        group = groups_ref[0, request]
        pieces = []
        for column in range(column_count):
            block = arrived_ref[group, column].astype(jnp.float32)
            for head in range(local_heads):
                far_ref[column * local_heads + head, pl.ds(start, capacity), :] = block[
                    :capacity, head * HD : (head + 1) * HD
                ]
            pieces.append(block[capacity:, :LANES])
        if column_count * STAT_ROWS < LANES:
            pieces.append(jnp.zeros((LANES - column_count * STAT_ROWS, LANES), jnp.float32))
        turned = jnp.transpose(jnp.concatenate(pieces, axis=0))
        stat_ref[pl.ds(start, capacity), :] = turned[:capacity]
        start = start + lengths_ref[0, request]
    far_top = stat_ref[:slot_count, :]
    far_sum = pltpu.roll(far_top, LANES - local_heads, 1)
    own_top = own_top_ref[...]
    joint_top = jnp.maximum(far_top, own_top)
    far_weight = jnp.exp(far_top - joint_top) * far_sum
    own_weight = jnp.exp(own_top - joint_top)
    bottom = far_weight + own_weight * own_sum_ref[...]
    far_weight = far_weight / bottom
    own_weight = own_weight / bottom
    total = jnp.zeros((slot_count, LANES), jnp.float32)
    for head in range(head_count):
        columns = slice(head * HD, (head + 1) * HD)
        at = stat_lane(head, local_heads)
        summed = (
            input_ref[:, columns].astype(jnp.float32)
            + far_weight[:, at : at + 1] * far_ref[head, :slot_count, :]
            + own_weight[:, at : at + 1] * own_mixed_ref[:, columns]
        )
        far_ref[head, :slot_count, :] = summed
        total = total + summed
    row_mean = jnp.sum(total, axis=1, keepdims=True) * (1.0 / model_width)
    total = jnp.zeros((slot_count, LANES), jnp.float32)
    for head in range(head_count):
        centred = far_ref[head, :slot_count, :] - row_mean
        total = total + centred * centred
    spread = jnp.sum(total, axis=1, keepdims=True) * (1.0 / model_width)
    factor = lax.rsqrt(spread + norm_eps)
    for head in range(head_count):
        columns = slice(head * HD, (head + 1) * HD)
        centred = far_ref[head, :slot_count, :] - row_mean
        hidden = (centred * factor * gain_ref[:, columns] + shift_ref[:, columns]).astype(
            jnp.bfloat16
        )
        first_ref[:, columns] = hidden[: slot_count // 2]
        second_ref[:, columns] = hidden[slot_count // 2 :]


def merge_parts(lengths, groups, arrived, own_mixed, own_top, own_sum, layer_input, gain, shift):
    slot_count, model_width = layer_input.shape
    capacity = arrived.shape[2] - STAT_ROWS
    half = jax.ShapeDtypeStruct((slot_count // 2, model_width), jnp.bfloat16)
    return pl.pallas_call(
        merge_kernel,
        out_shape=(half, half),
        in_specs=[smem_spec(), smem_spec()] + [vmem_spec()] * 7,
        out_specs=(vmem_spec(), vmem_spec()),
        scratch_shapes=[
            pltpu.VMEM((model_width // HD, slot_count + capacity, HD), jnp.float32),
            pltpu.VMEM((slot_count + capacity, LANES), jnp.float32),
        ],
        compiler_params=pltpu.CompilerParams(vmem_limit_bytes=16 * mebibyte),
        name="merge_parts",
    )(
        lengths,
        groups,
        arrived,
        own_mixed,
        own_top,
        own_sum,
        layer_input,
        gain.reshape(1, model_width),
        shift.reshape(1, model_width),
    )


def swap(value, mask):
    total = lax.axis_size("grp") * lax.axis_size("dev")
    return lax.ppermute(value, ("grp", "dev"), [(here, here ^ mask) for here in range(total)])


def complete(held, masks):
    held = dict(held)
    for mask in masks:
        for at in list(held):
            if mask ^ at not in held:
                held[mask ^ at] = swap(held[at], mask)
    return held


def tie(values, after):
    return lax.optimization_barrier((values, after))[0]


def mlp_kernel(pieces, parts, *refs):
    row_refs, refs = refs[:pieces], refs[pieces:]
    ups, refs = refs[:parts], refs[parts:]
    downs, refs = refs[:parts], refs[parts:]
    out_refs, (up_ref, down_ref, sems) = refs[:pieces], refs[pieces:]
    model_width = row_refs[0].shape[1]
    units = downs[0].shape[0]
    up_copies = [
        pltpu.make_async_copy(ups[part], up_ref.at[part], sems.at[part, 0])
        for part in range(parts)
    ]
    down_copies = [
        pltpu.make_async_copy(
            downs[part], down_ref.at[pl.ds(part * units, units)], sems.at[part, 1]
        )
        for part in range(parts)
    ]
    copies = up_copies + down_copies
    ahead = 4
    for copy in copies[:ahead]:
        copy.start()
    rows = jnp.concatenate([ref[...] for ref in row_refs], axis=0)
    activations = []
    for part in range(parts):
        copies[part].wait()
        if part + ahead < len(copies):
            copies[part + ahead].start()
        product = jnp.dot(
            rows, up_ref[part, :model_width, :], preferred_element_type=jnp.float32
        )
        offset = up_ref[part, model_width:, :].astype(jnp.float32)[0:1]
        activations.append(jax.nn.gelu(product + offset, approximate=True).astype(jnp.bfloat16))
    for part in range(parts, 2 * parts):
        copies[part].wait()
        if part + ahead < len(copies):
            copies[part + ahead].start()
    total = jnp.dot(
        jnp.concatenate(activations, axis=1), down_ref[...], preferred_element_type=jnp.float32
    ).astype(jnp.bfloat16)
    height = row_refs[0].shape[0]
    for piece in range(pieces):
        out_refs[piece][...] = total[piece * height : (piece + 1) * height]


def feed_forward(rows, ups, downs):
    pieces, parts = len(rows), len(ups)
    height, model_width = rows[0].shape
    up_rows, units = ups[0].shape
    return pl.pallas_call(
        functools.partial(mlp_kernel, pieces, parts),
        out_shape=tuple(jax.ShapeDtypeStruct(piece.shape, jnp.bfloat16) for piece in rows),
        in_specs=[vmem_spec()] * pieces + [pl.BlockSpec(memory_space=pl.ANY)] * (2 * parts),
        out_specs=tuple(vmem_spec() for _ in rows),
        scratch_shapes=[
            pltpu.VMEM((parts, up_rows, units), jnp.bfloat16),
            pltpu.VMEM((parts * units, model_width), jnp.bfloat16),
            pltpu.SemaphoreType.DMA((parts, 2)),
        ],
        compiler_params=pltpu.CompilerParams(vmem_limit_bytes=32 * mebibyte),
        cost_estimate=pl.CostEstimate(
            flops=4 * pieces * height * model_width * parts * units,
            bytes_accessed=4 * parts * model_width * units,
            transcendentals=pieces * height * parts * units,
        ),
        name="feed_forward",
    )(*rows, *ups, *downs)


def add_kernel(here_ref, there_ref, out_ref):
    out_ref[...] = (
        here_ref[...].astype(jnp.float32) + there_ref[...].astype(jnp.float32)
    ).astype(jnp.bfloat16)


def add_rows(here, there):
    return pl.pallas_call(
        add_kernel,
        out_shape=jax.ShapeDtypeStruct(here.shape, jnp.bfloat16),
        in_specs=[vmem_spec(), vmem_spec()],
        out_specs=vmem_spec(),
        name="add_rows",
    )(here, there)


def finish_kernel(pieces, *refs):
    bias_ref, gain_ref, shift_ref, out_ref = refs[4 * pieces :]
    height = out_ref.shape[0] // pieces
    for piece in range(pieces):
        hidden, own, near, far = (
            refs[kind * pieces + piece][...].astype(jnp.float32) for kind in range(4)
        )
        summed = hidden + (own + near + far) + bias_ref[...]
        out_ref[piece * height : (piece + 1) * height, :] = layer_norm(
            summed, gain_ref[...], shift_ref[...]
        ).astype(jnp.bfloat16)


def finish_rows(hidden, own, near, far, bias, gain, shift):
    pieces = len(hidden)
    height, model_width = hidden[0].shape
    return pl.pallas_call(
        functools.partial(finish_kernel, pieces),
        out_shape=jax.ShapeDtypeStruct((pieces * height, model_width), jnp.bfloat16),
        in_specs=[vmem_spec()] * (4 * pieces + 3),
        out_specs=vmem_spec(),
        compiler_params=pltpu.CompilerParams(vmem_limit_bytes=16 * mebibyte),
        name="finish_rows",
    )(
        *hidden,
        *own,
        *near,
        *far,
        bias.reshape(1, model_width),
        gain.reshape(1, model_width),
        shift.reshape(1, model_width),
    )


def on_device(
    suffix_queries,
    suffix_keys,
    suffix_values,
    layer_input,
    suffix_lengths,
    request_group,
    prefix_keys,
    prefix_values,
    up_weight,
    up_bias,
    down_weight,
    down_bias,
    attn_gain,
    attn_shift,
    out_gain,
    out_shift,
):
    slot_count, model_width = suffix_queries.shape
    group_count = lax.axis_size("grp")
    column_count = lax.axis_size("dev")
    part_width = model_width // column_count
    local_heads = part_width // HD
    capacity = 2 * slot_count // group_count
    sources = group_count * column_count

    near_mask = group_count // 2 * column_count
    far_mask = column_count // 2
    column_masks = [1 << bit for bit in range(far_mask.bit_length() - 1)]
    group_masks = [column_count << bit for bit in range((group_count // 2).bit_length() - 1)]

    outgoing = pack_queries(
        suffix_lengths, request_group, suffix_queries, group_count, column_count, capacity
    )
    bias_rows = jnp.broadcast_to(up_bias[None, :], (16, up_bias.shape[0]))
    ups = {0: jnp.concatenate([up_weight, bias_rows], axis=0)}
    downs = {0: down_weight}

    arrived = lax.all_to_all(
        outgoing.reshape(sources, capacity + STAT_ROWS, part_width),
        ("grp", "dev"),
        split_axis=0,
        concat_axis=0,
        tiled=True,
    )
    for mask in column_masks:
        ups[mask] = swap(ups[0], mask)
    turned_keys = prefix_keys[0].T
    value_heads = prefix_values[0].reshape(-1, local_heads, HD).transpose(1, 0, 2)
    wide_values = jnp.concatenate([value_heads, jnp.ones_like(value_heads)], axis=2)
    own = attend_suffix(
        suffix_lengths, suffix_queries, suffix_keys, suffix_values, local_heads
    )
    arrived, ups, downs, turned_keys, wide_values, own = lax.optimization_barrier(
        (arrived, ups, downs, turned_keys, wide_values, own)
    )

    counts = arrived[:, capacity, 0].astype(jnp.int32)
    answer_part = attend_prefix(counts, arrived, turned_keys, wide_values)
    for mask in column_masks:
        downs[mask] = swap(downs[0], mask)
    answer_part, ups, downs = lax.optimization_barrier((answer_part, ups, downs))

    answer = lax.all_to_all(
        answer_part, ("grp", "dev"), split_axis=0, concat_axis=0, tiled=True
    ).reshape(group_count, column_count, capacity + STAT_ROWS, part_width)
    core_mask = group_masks[0]
    early_ups = {core_mask ^ at: swap(block, core_mask) for at, block in ups.items()}
    early_downs = {core_mask ^ at: swap(block, core_mask) for at, block in downs.items()}
    ups = complete(ups, column_masks[::-1])
    downs = complete(downs, column_masks)
    ups.update(early_ups)
    downs.update(early_downs)
    answer, ups, downs = lax.optimization_barrier((answer, ups, downs))

    hidden = merge_parts(
        suffix_lengths, request_group, answer, *own, layer_input, attn_gain, attn_shift
    )

    hidden, ups, downs = lax.optimization_barrier((hidden, ups, downs))
    far_a = swap(hidden[0], far_mask)
    near = [swap(piece, near_mask) for piece in hidden]
    ups = complete(ups, group_masks)
    downs = complete(downs, group_masks)
    order = sorted(ups)
    ups = [ups[mask] for mask in order]
    downs = [downs[mask] for mask in order]
    own_part = feed_forward(hidden, ups, downs)
    far_a, own_part = lax.optimization_barrier((far_a, own_part))
    far_b = swap(tie(hidden[1], far_a), far_mask)
    cross_a = swap(far_a, near_mask)
    near_part = feed_forward(tie(near, far_a), ups, downs)
    far_b, cross_a, near_part = lax.optimization_barrier((far_b, cross_a, near_part))
    cross_b = swap(far_b, near_mask)
    far_part_a, cross_part_a = feed_forward([far_a, cross_a], ups, downs)
    cross_b, far_part_a, cross_part_a = lax.optimization_barrier(
        (cross_b, far_part_a, cross_part_a)
    )
    cross_sum_a = swap(cross_part_a, near_mask)
    far_part_b, cross_part_b = feed_forward([far_b, cross_b], ups, downs)
    cross_sum_a, far_part_b, cross_part_b = lax.optimization_barrier(
        (cross_sum_a, far_part_b, cross_part_b)
    )
    cross_sum_b = swap(cross_part_b, near_mask)
    far_sum_a = swap(add_rows(far_part_a, cross_sum_a), far_mask)
    near_sum = [swap(piece, near_mask) for piece in tie(near_part, cross_sum_b)]
    far_sum_b = swap(add_rows(far_part_b, cross_sum_b), far_mask)
    return finish_rows(
        hidden, own_part, near_sum, [far_sum_a, far_sum_b], down_bias, out_gain, out_shift
    )


def solution(mesh):
    placed = (
        P(("grp", "dev"), None),
        P(("grp", "dev"), None),
        P(("grp", "dev"), None),
        P(("grp", "dev"), None),
        P(("grp", "dev"), None),
        P(("grp", "dev"), None),
        P("grp", None, "dev"),
        P("grp", None, "dev"),
        P(None, ("grp", "dev")),
        P(("grp", "dev")),
        P(("grp", "dev"), None),
        P(),
        P(),
        P(),
        P(),
        P(),
    )
    return jax.shard_map(
        on_device, mesh=mesh, in_specs=placed, out_specs=P(("grp", "dev"), None), check_vma=False
    )
```

```python
import functools
import math

import jax
import jax.numpy as jnp
from jax import lax
from jax.experimental import pallas as pl
from jax.experimental.pallas import tpu as pltpu
from jax.sharding import PartitionSpec as P

HD = 128
LANES = 128
STAT_ROWS = 8
ROW_BLOCK = 256
KEY_CHUNK = 1024

norm_eps = 1e-12
score_scale = HD ** (-0.5)
log2_e = math.log2(math.e)
mebibyte = 1024 * 1024


def layer_norm(summed, norm_gain, norm_shift):
    row_mean = jnp.mean(summed, axis=-1, keepdims=True)
    centred = summed - row_mean
    spread = jnp.mean(centred * centred, axis=-1, keepdims=True)
    return centred * lax.rsqrt(spread + norm_eps) * norm_gain + norm_shift


def vmem_spec():
    return pl.BlockSpec(memory_space=pltpu.VMEM)


def hbm_spec():
    return pl.BlockSpec(memory_space=pltpu.HBM)


def smem_spec():
    return pl.BlockSpec(memory_space=pltpu.SMEM)


def pack_kernel(lengths_ref, groups_ref, query_ref, out_ref, wide_ref):
    request_total = lengths_ref.shape[1]
    _, column_count, chunk_rows, part_width = out_ref.shape
    capacity = chunk_rows - STAT_ROWS
    slot_count = query_ref.shape[0]
    tiles = part_width // LANES
    for tile in range(wide_ref.shape[0]):
        wide_ref[tile, 0:slot_count, :] = query_ref[
            :, tile * LANES : (tile + 1) * LANES
        ].astype(jnp.float32)
        wide_ref[tile, slot_count : slot_count + capacity, :] = jnp.zeros(
            (capacity, LANES), jnp.float32
        )
    start = 0
    for request in range(request_total):
        group = groups_ref[0, request]
        count = jnp.full((STAT_ROWS, LANES), lengths_ref[0, request], jnp.int32).astype(jnp.float32)
        for column in range(column_count):
            for tile in range(tiles):
                rows = wide_ref[column * tiles + tile, pl.ds(start, capacity), :]
                rows = jnp.concatenate([rows, count], axis=0)
                out_ref[group, column, :, tile * LANES : (tile + 1) * LANES] = rows.astype(
                    jnp.bfloat16
                )
        start = start + lengths_ref[0, request]


def pack_queries(lengths, groups, queries, group_count, column_count, capacity):
    slot_count, model_width = queries.shape
    part_width = model_width // column_count
    return pl.pallas_call(
        pack_kernel,
        out_shape=jax.ShapeDtypeStruct(
            (group_count, column_count, capacity + STAT_ROWS, part_width), jnp.bfloat16
        ),
        in_specs=[smem_spec(), smem_spec(), vmem_spec()],
        out_specs=vmem_spec(),
        scratch_shapes=[
            pltpu.VMEM((model_width // LANES, slot_count + capacity, LANES), jnp.float32)
        ],
        compiler_params=pltpu.CompilerParams(vmem_limit_bytes=16 * mebibyte),
        name="pack_queries",
    )(lengths, groups, queries)


def far_kernel(
    counts_ref,
    arrived_ref,
    keys_hbm,
    values_hbm,
    out_ref,
    query_ref,
    answer_ref,
    stat_ref,
    score_ref,
    top_ref,
    keys_ref,
    values_ref,
    sems,
):
    copies = [
        pltpu.make_async_copy(keys_hbm, keys_ref, sems.at[0]),
        pltpu.make_async_copy(values_hbm, values_ref, sems.at[1]),
    ]
    for copy in copies:
        copy.start()
    sources, chunk_rows, part_width = arrived_ref.shape
    capacity = chunk_rows - STAT_ROWS
    local_heads = part_width // HD
    key_total = keys_ref.shape[1]
    chunks = key_total // KEY_CHUNK

    def take(source, offset):
        for head in range(local_heads):
            rows = arrived_ref[source, :, head * HD : (head + 1) * HD].astype(jnp.float32)
            query_ref[head, pl.ds(offset, capacity), :] = rows[:capacity]
        return offset + counts_ref[source]

    total = lax.fori_loop(0, sources, take, jnp.int32(0))
    blocks = (total + ROW_BLOCK - 1) // ROW_BLOCK
    lane = lax.broadcasted_iota(jnp.int32, (ROW_BLOCK, LANES), 1)

    def block_rows(block):
        return pl.ds(pl.multiple_of(block * ROW_BLOCK, ROW_BLOCK), ROW_BLOCK)

    def load_queries(block, head):
        return query_ref[head, block_rows(block), :].astype(jnp.bfloat16)

    def score_chunk(rows, head, slot, chunk, part_top):
        columns = slice(chunk * KEY_CHUNK, (chunk + 1) * KEY_CHUNK)
        scores = jnp.dot(
            rows,
            keys_ref[head * HD : (head + 1) * HD, columns],
            preferred_element_type=jnp.float32,
        )
        score_ref[slot, :, columns] = scores
        for piece in range(KEY_CHUNK // LANES):
            part = scores[:, piece * LANES : (piece + 1) * LANES]
            part_top = part if part_top is None else jnp.maximum(part_top, part)
        return part_top

    def finish_top(part_top, slot):
        row_top = jnp.max(part_top, axis=1, keepdims=True) * score_scale
        row_top = row_top.astype(jnp.bfloat16).astype(jnp.float32)
        top_ref[slot] = jnp.broadcast_to(row_top, (ROW_BLOCK, LANES))

    def weigh_chunk(head, slot, chunk, shift):
        columns = slice(chunk * KEY_CHUNK, (chunk + 1) * KEY_CHUNK)
        weights = jnp.exp2(score_ref[slot, :, columns] * (score_scale * log2_e) - shift)
        return jnp.dot(
            weights.astype(jnp.bfloat16),
            values_ref[head, columns, :],
            preferred_element_type=jnp.float32,
        )

    def finish_answer(block, head, slot, mixed):
        rows = block_rows(block)
        row_sum = mixed[:, HD:]
        answer_ref[head, rows, :] = mixed[:, :HD] / row_sum
        top = top_ref[slot]
        if head == 0:
            stat_ref[rows, :] = jnp.where(lane == 0, top, row_sum)
        else:
            before = stat_ref[rows, :]
            with_top = jnp.where(lane == head, top, before)
            stat_ref[rows, :] = jnp.where(lane == local_heads + head, row_sum, with_top)

    def slot_of(block, head):
        return (block * local_heads + head) % 2 if local_heads % 2 else head % 2

    for copy in copies:
        copy.wait()
    first_rows = load_queries(0, 0)
    part_top = None
    for chunk in range(chunks):
        part_top = score_chunk(first_rows, 0, 0, chunk, part_top)
    finish_top(part_top, 0)

    def one_block(block, carry):
        for head in range(local_heads):
            slot = slot_of(block, head)
            if head + 1 < local_heads:
                next_block, next_head = block, head + 1
            else:
                next_block, next_head = jnp.minimum(block + 1, blocks - 1), 0
            next_slot = 1 - slot
            next_rows = load_queries(next_block, next_head)
            shift = top_ref[slot][:, 0:1] * log2_e
            part_top = None
            mixed = None
            for chunk in range(chunks):
                part_top = score_chunk(next_rows, next_head, next_slot, chunk, part_top)
                part = weigh_chunk(head, slot, chunk, shift)
                mixed = part if mixed is None else mixed + part
            finish_answer(block, head, slot, mixed)
            finish_top(part_top, next_slot)
        return carry

    lax.fori_loop(0, blocks, one_block, 0)

    def give(source, offset):
        rows = [answer_ref[head, pl.ds(offset, capacity), :] for head in range(local_heads)]
        turned = jnp.transpose(stat_ref[pl.ds(offset, LANES), :])[:STAT_ROWS, :]
        if part_width > LANES:
            turned = jnp.concatenate(
                [turned, jnp.zeros((STAT_ROWS, part_width - LANES), jnp.float32)], axis=1
            )
        rows = jnp.concatenate(rows, axis=1)
        out_ref[source] = jnp.concatenate([rows, turned], axis=0).astype(jnp.bfloat16)
        return offset + counts_ref[source]

    lax.fori_loop(0, sources, give, jnp.int32(0))


def attend_prefix(counts, arrived, turned_keys, wide_values):
    sources, chunk_rows, part_width = arrived.shape
    capacity = chunk_rows - STAT_ROWS
    local_heads = part_width // HD
    key_total = turned_keys.shape[1]
    row_total = -(-sources * capacity // ROW_BLOCK) * ROW_BLOCK + LANES
    return pl.pallas_call(
        far_kernel,
        out_shape=jax.ShapeDtypeStruct((sources, capacity + STAT_ROWS, part_width), jnp.bfloat16),
        in_specs=[smem_spec(), vmem_spec(), hbm_spec(), hbm_spec()],
        out_specs=vmem_spec(),
        scratch_shapes=[
            pltpu.VMEM((local_heads, row_total, HD), jnp.float32),
            pltpu.VMEM((local_heads, row_total, HD), jnp.float32),
            pltpu.VMEM((row_total, LANES), jnp.float32),
            pltpu.VMEM((2, ROW_BLOCK, key_total), jnp.float32),
            pltpu.VMEM((2, ROW_BLOCK, LANES), jnp.float32),
            pltpu.VMEM(turned_keys.shape, jnp.bfloat16),
            pltpu.VMEM(wide_values.shape, jnp.bfloat16),
            pltpu.SemaphoreType.DMA((2,)),
        ],
        compiler_params=pltpu.CompilerParams(vmem_limit_bytes=40 * mebibyte),
        cost_estimate=pl.CostEstimate(
            flops=4 * sources * capacity * key_total * part_width,
            bytes_accessed=8 * key_total * part_width,
            transcendentals=sources * capacity * key_total * local_heads,
        ),
        name="attend_prefix",
    )(counts, arrived, turned_keys, wide_values)


def stat_lane(head, local_heads):
    return (head // local_heads) * STAT_ROWS + head % local_heads


def own_kernel(local_heads, lengths_ref, query_ref, key_ref, value_ref, mixed_ref, top_ref, sum_ref):
    slot_count, model_width = query_ref.shape
    head_count = model_width // HD
    row = lax.broadcasted_iota(jnp.int32, (slot_count, slot_count), 0)
    column = lax.broadcasted_iota(jnp.int32, (slot_count, slot_count), 1)
    row_segment = jnp.zeros((slot_count, slot_count), jnp.int32)
    column_segment = jnp.zeros((slot_count, slot_count), jnp.int32)
    start = 0
    for request in range(lengths_ref.shape[1]):
        start = start + lengths_ref[0, request]
        row_segment = row_segment + (row >= start).astype(jnp.int32)
        column_segment = column_segment + (column >= start).astype(jnp.int32)
    visible = (row_segment == column_segment) & (column <= row)
    lane = lax.broadcasted_iota(jnp.int32, (slot_count, LANES), 1)
    tops = jnp.zeros((slot_count, LANES), jnp.float32)
    sums = jnp.ones((slot_count, LANES), jnp.float32)
    for head in range(head_count):
        columns = slice(head * HD, (head + 1) * HD)
        scores = (
            lax.dot_general(
                query_ref[:, columns],
                key_ref[:, columns],
                (((1,), (1,)), ((), ())),
                preferred_element_type=jnp.float32,
            )
            * score_scale
        )
        top = jnp.max(jnp.where(visible, scores, -jnp.inf), axis=1, keepdims=True)
        weights = jnp.where(visible, jnp.exp(scores - top), 0.0)
        mixed_ref[:, columns] = jnp.dot(
            weights.astype(jnp.bfloat16),
            value_ref[:, columns],
            preferred_element_type=jnp.float32,
        )
        at = stat_lane(head, local_heads)
        tops = jnp.where(lane == at, top, tops)
        sums = jnp.where(lane == at, jnp.sum(weights, axis=1, keepdims=True), sums)
    top_ref[...] = tops
    sum_ref[...] = sums


def attend_suffix(lengths, queries, keys, values, local_heads):
    slot_count, model_width = queries.shape
    stats = jax.ShapeDtypeStruct((slot_count, LANES), jnp.float32)
    return pl.pallas_call(
        functools.partial(own_kernel, local_heads),
        out_shape=(jax.ShapeDtypeStruct((slot_count, model_width), jnp.float32), stats, stats),
        in_specs=[smem_spec()] + [vmem_spec()] * 3,
        out_specs=(vmem_spec(), vmem_spec(), vmem_spec()),
        compiler_params=pltpu.CompilerParams(vmem_limit_bytes=16 * mebibyte),
        cost_estimate=pl.CostEstimate(
            flops=40 * slot_count * slot_count * model_width,
            bytes_accessed=8 * slot_count * model_width,
            transcendentals=slot_count * model_width,
        ),
        name="attend_suffix",
    )(lengths, queries, keys, values)


def merge_kernel(
    lengths_ref,
    groups_ref,
    arrived_ref,
    own_mixed_ref,
    own_top_ref,
    own_sum_ref,
    input_ref,
    gain_ref,
    shift_ref,
    first_ref,
    second_ref,
    hidden_ref,
    far_ref,
    stat_ref,
):
    _, column_count, chunk_rows, part_width = arrived_ref.shape
    slot_count, model_width = input_ref.shape
    capacity = chunk_rows - STAT_ROWS
    local_heads = part_width // HD
    head_count = model_width // HD
    start = 0
    for request in range(lengths_ref.shape[1]):
        group = groups_ref[0, request]
        pieces = []
        for column in range(column_count):
            block = arrived_ref[group, column].astype(jnp.float32)
            for head in range(local_heads):
                far_ref[column * local_heads + head, pl.ds(start, capacity), :] = block[
                    :capacity, head * HD : (head + 1) * HD
                ]
            pieces.append(block[capacity:, :LANES])
        if column_count * STAT_ROWS < LANES:
            pieces.append(jnp.zeros((LANES - column_count * STAT_ROWS, LANES), jnp.float32))
        turned = jnp.transpose(jnp.concatenate(pieces, axis=0))
        stat_ref[pl.ds(start, capacity), :] = turned[:capacity]
        start = start + lengths_ref[0, request]
    far_top = stat_ref[:slot_count, :]
    far_sum = pltpu.roll(far_top, LANES - local_heads, 1)
    own_top = own_top_ref[...]
    joint_top = jnp.maximum(far_top, own_top)
    far_weight = jnp.exp(far_top - joint_top) * far_sum
    own_weight = jnp.exp(own_top - joint_top)
    bottom = far_weight + own_weight * own_sum_ref[...]
    far_weight = far_weight / bottom
    own_weight = own_weight / bottom
    total = jnp.zeros((slot_count, LANES), jnp.float32)
    for head in range(head_count):
        columns = slice(head * HD, (head + 1) * HD)
        at = stat_lane(head, local_heads)
        summed = (
            input_ref[:, columns].astype(jnp.float32)
            + far_weight[:, at : at + 1] * far_ref[head, :slot_count, :]
            + own_weight[:, at : at + 1] * own_mixed_ref[:, columns]
        )
        far_ref[head, :slot_count, :] = summed
        total = total + summed
    row_mean = jnp.sum(total, axis=1, keepdims=True) * (1.0 / model_width)
    total = jnp.zeros((slot_count, LANES), jnp.float32)
    for head in range(head_count):
        centred = far_ref[head, :slot_count, :] - row_mean
        total = total + centred * centred
    spread = jnp.sum(total, axis=1, keepdims=True) * (1.0 / model_width)
    factor = lax.rsqrt(spread + norm_eps)
    for head in range(head_count):
        columns = slice(head * HD, (head + 1) * HD)
        centred = far_ref[head, :slot_count, :] - row_mean
        hidden = (centred * factor * gain_ref[:, columns] + shift_ref[:, columns]).astype(
            jnp.bfloat16
        )
        first_ref[:, columns] = hidden[: slot_count // 2]
        second_ref[:, columns] = hidden[slot_count // 2 :]
        hidden_ref[:, columns] = hidden


def merge_parts(lengths, groups, arrived, own_mixed, own_top, own_sum, layer_input, gain, shift):
    slot_count, model_width = layer_input.shape
    capacity = arrived.shape[2] - STAT_ROWS
    half = jax.ShapeDtypeStruct((slot_count // 2, model_width), jnp.bfloat16)
    return pl.pallas_call(
        merge_kernel,
        out_shape=(half, half, jax.ShapeDtypeStruct(layer_input.shape, jnp.bfloat16)),
        in_specs=[smem_spec(), smem_spec()] + [vmem_spec()] * 7,
        out_specs=(vmem_spec(), vmem_spec(), vmem_spec()),
        scratch_shapes=[
            pltpu.VMEM((model_width // HD, slot_count + capacity, HD), jnp.float32),
            pltpu.VMEM((slot_count + capacity, LANES), jnp.float32),
        ],
        compiler_params=pltpu.CompilerParams(vmem_limit_bytes=16 * mebibyte),
        name="merge_parts",
    )(
        lengths,
        groups,
        arrived,
        own_mixed,
        own_top,
        own_sum,
        layer_input,
        gain.reshape(1, model_width),
        shift.reshape(1, model_width),
    )


def swap(value, mask):
    total = lax.axis_size("grp") * lax.axis_size("dev")
    pairs = [(here, here ^ mask) for here in range(total)]
    return jax.tree.map(lambda leaf: lax.ppermute(leaf, ("grp", "dev"), pairs), value)


def complete(held, masks):
    held = dict(held)
    for mask in masks:
        for at in list(held):
            if mask ^ at not in held:
                held[mask ^ at] = swap(held[at], mask)
    return held


def tie(values, after):
    return lax.optimization_barrier((values, after))[0]


def mlp_kernel(pieces, up_plan, down_plan, *refs):
    parts = len(up_plan)
    row_refs, refs = refs[:pieces], refs[pieces:]
    up_total, down_total = sum(map(len, up_plan)), sum(map(len, down_plan))
    ups, refs = list(refs[:up_total]), refs[up_total:]
    downs, refs = list(refs[:down_total]), refs[down_total:]
    out_refs, (up_ref, down_ref, sems) = refs[:pieces], refs[pieces:]
    model_width = row_refs[0].shape[1]
    copies = []
    for part, heights in enumerate(up_plan):
        begin, held = 0, []
        for piece, height in enumerate(heights):
            target = up_ref.at[part, pl.ds(begin, height)]
            held.append(pltpu.make_async_copy(ups.pop(0), target, sems.at[part, 0, piece]))
            begin += height
        copies.append(held)
    begin = 0
    for part, heights in enumerate(down_plan):
        held = []
        for piece, height in enumerate(heights):
            target = down_ref.at[pl.ds(begin, height)]
            held.append(pltpu.make_async_copy(downs.pop(0), target, sems.at[part, 1, piece]))
            begin += height
        copies.append(held)
    ahead = 4

    def start(at):
        if at < len(copies):
            for copy in copies[at]:
                copy.start()

    def arrive(at):
        for copy in copies[at]:
            copy.wait()
        start(at + ahead)

    for at in range(ahead):
        start(at)
    rows = jnp.concatenate([ref[...] for ref in row_refs], axis=0)
    activations = []
    for part in range(parts):
        arrive(part)
        product = jnp.dot(
            rows, up_ref[part, :model_width, :], preferred_element_type=jnp.float32
        )
        offset = up_ref[part, model_width:, :].astype(jnp.float32)[0:1]
        activations.append(jax.nn.gelu(product + offset, approximate=True).astype(jnp.bfloat16))
    for part in range(parts):
        arrive(parts + part)
    total = jnp.dot(
        jnp.concatenate(activations, axis=1), down_ref[...], preferred_element_type=jnp.float32
    ).astype(jnp.bfloat16)
    height = row_refs[0].shape[0]
    for piece in range(pieces):
        out_refs[piece][...] = total[piece * height : (piece + 1) * height]


def feed_forward(rows, ups, downs):
    pieces, parts = len(rows), len(ups)
    height, model_width = rows[0].shape
    up_plan = [[piece.shape[0] for piece in block] for block in ups]
    down_plan = [[piece.shape[0] for piece in block] for block in downs]
    up_rows, down_rows = sum(up_plan[0]), sum(down_plan[0])
    units = ups[0][0].shape[1]
    flat = [piece for block in ups + downs for piece in block]
    most = max(map(len, up_plan + down_plan))
    return pl.pallas_call(
        functools.partial(mlp_kernel, pieces, up_plan, down_plan),
        out_shape=tuple(jax.ShapeDtypeStruct(piece.shape, jnp.bfloat16) for piece in rows),
        in_specs=[vmem_spec()] * pieces + [hbm_spec()] * len(flat),
        out_specs=tuple(vmem_spec() for _ in rows),
        scratch_shapes=[
            pltpu.VMEM((parts, up_rows, units), jnp.bfloat16),
            pltpu.VMEM((parts * down_rows, model_width), jnp.bfloat16),
            pltpu.SemaphoreType.DMA((parts, 2, most)),
        ],
        compiler_params=pltpu.CompilerParams(vmem_limit_bytes=32 * mebibyte),
        cost_estimate=pl.CostEstimate(
            flops=4 * pieces * height * model_width * parts * units,
            bytes_accessed=4 * parts * model_width * units,
            transcendentals=pieces * height * parts * units,
        ),
        name="feed_forward",
    )(*rows, *flat)


def add_kernel(here_ref, there_ref, out_ref):
    out_ref[...] = (
        here_ref[...].astype(jnp.float32) + there_ref[...].astype(jnp.float32)
    ).astype(jnp.bfloat16)


def add_rows(here, there):
    return pl.pallas_call(
        add_kernel,
        out_shape=jax.ShapeDtypeStruct(here.shape, jnp.bfloat16),
        in_specs=[vmem_spec(), vmem_spec()],
        out_specs=vmem_spec(),
        name="add_rows",
    )(here, there)


def finish_kernel(
    hidden_ref, own_ref, near_ref, far_a_ref, far_b_ref, bias_ref, gain_ref, shift_ref, out_ref
):
    height = far_a_ref.shape[0]
    for begin, far_ref in ((0, far_a_ref), (height, far_b_ref)):
        rows = slice(begin, begin + height)
        summed = hidden_ref[rows, :].astype(jnp.float32) + (
            own_ref[rows, :].astype(jnp.float32)
            + near_ref[rows, :].astype(jnp.float32)
            + far_ref[...].astype(jnp.float32)
        )
        out_ref[rows, :] = layer_norm(
            summed + bias_ref[...], gain_ref[...], shift_ref[...]
        ).astype(jnp.bfloat16)


def finish_rows(hidden, own, near, far_a, far_b, bias, gain, shift):
    model_width = hidden.shape[1]
    return pl.pallas_call(
        finish_kernel,
        out_shape=jax.ShapeDtypeStruct(hidden.shape, jnp.bfloat16),
        in_specs=[vmem_spec()] * 8,
        out_specs=vmem_spec(),
        compiler_params=pltpu.CompilerParams(vmem_limit_bytes=16 * mebibyte),
        name="finish_rows",
    )(
        hidden,
        own,
        near,
        far_a,
        far_b,
        bias.reshape(1, model_width),
        gain.reshape(1, model_width),
        shift.reshape(1, model_width),
    )


def on_device(
    suffix_queries,
    suffix_keys,
    suffix_values,
    layer_input,
    suffix_lengths,
    request_group,
    prefix_keys,
    prefix_values,
    up_weight,
    up_bias,
    down_weight,
    down_bias,
    attn_gain,
    attn_shift,
    out_gain,
    out_shift,
):
    slot_count, model_width = suffix_queries.shape
    group_count = lax.axis_size("grp")
    column_count = lax.axis_size("dev")
    part_width = model_width // column_count
    local_heads = part_width // HD
    capacity = 2 * slot_count // group_count
    sources = group_count * column_count

    near_mask = group_count // 2 * column_count
    far_mask = column_count // 2
    column_masks = [1 << bit for bit in range(far_mask.bit_length() - 1)]
    group_masks = [column_count << bit for bit in range((group_count // 2).bit_length() - 1)]

    low_mask, high_masks = column_masks[0], column_masks[1:]
    core_mask = group_masks[0]

    outgoing = pack_queries(
        suffix_lengths, request_group, suffix_queries, group_count, column_count, capacity
    )
    bias_rows = jnp.broadcast_to(up_bias[None, :], (16, up_bias.shape[0]))
    up_block = jnp.concatenate([up_weight, bias_rows], axis=0)
    up_cut, down_cut = up_weight.shape[0] // 2, down_weight.shape[0] // 2
    up_pieces = (up_block[:up_cut], up_block[up_cut:])
    down_pieces = (down_weight[:down_cut], down_weight[down_cut:])
    ups, downs = {0: (up_block,)}, {0: (down_weight,)}
    high_mask = high_masks[0]

    arrived = lax.all_to_all(
        outgoing.reshape(sources, capacity + STAT_ROWS, part_width),
        ("grp", "dev"),
        split_axis=0,
        concat_axis=0,
        tiled=True,
    )
    ups[low_mask] = swap(ups[0], low_mask)
    up_first = swap(up_pieces[0], high_mask)
    turned_keys = prefix_keys[0].T
    value_heads = prefix_values[0].reshape(-1, local_heads, HD).transpose(1, 0, 2)
    wide_values = jnp.concatenate([value_heads, jnp.ones_like(value_heads)], axis=2)
    own = attend_suffix(
        suffix_lengths, suffix_queries, suffix_keys, suffix_values, local_heads
    )
    arrived, ups, up_first, up_pieces, downs, down_pieces, turned_keys, wide_values, own = (
        lax.optimization_barrier(
            (arrived, ups, up_first, up_pieces, downs, down_pieces, turned_keys, wide_values, own)
        )
    )

    counts = arrived[:, capacity, 0].astype(jnp.int32)
    answer_part = attend_prefix(counts, arrived, turned_keys, wide_values)
    downs[low_mask] = swap(downs[0], low_mask)
    up_second = swap(up_pieces[1], high_mask)
    down_first = swap(down_pieces[0], high_mask)
    answer_part, ups, up_first, up_second, downs, down_first, down_pieces = (
        lax.optimization_barrier(
            (answer_part, ups, up_first, up_second, downs, down_first, down_pieces)
        )
    )

    answer = lax.all_to_all(
        answer_part, ("grp", "dev"), split_axis=0, concat_axis=0, tiled=True
    ).reshape(group_count, column_count, capacity + STAT_ROWS, part_width)
    ups[high_mask] = (jnp.concatenate([up_first, up_second], axis=0),)
    early_ups = {core_mask ^ at: swap(block, core_mask) for at, block in ups.items()}
    early_downs = {core_mask ^ at: swap(block, core_mask) for at, block in downs.items()}
    down_second = swap(down_pieces[1], high_mask)
    downs[high_mask] = (jnp.concatenate([down_first, down_second], axis=0),)
    ups[low_mask ^ high_mask] = swap(ups[high_mask], low_mask)
    ups.update(early_ups)
    downs.update(early_downs)
    answer, ups, downs = lax.optimization_barrier((answer, ups, downs))

    hidden_a, hidden_b, hidden = merge_parts(
        suffix_lengths, request_group, answer, *own, layer_input, attn_gain, attn_shift
    )

    (hidden_a, hidden_b, hidden), ups, downs = lax.optimization_barrier(
        ((hidden_a, hidden_b, hidden), ups, downs)
    )
    far_a = swap(hidden_a, far_mask)
    near = swap(hidden, near_mask)
    downs[low_mask ^ high_mask] = swap(downs[high_mask], low_mask)
    ups = complete(ups, group_masks + column_masks)
    far_b = swap(tie(hidden_b, far_a), far_mask)
    cross_a = swap(far_a, near_mask)
    far_b, cross_a, near, ups, downs = lax.optimization_barrier(
        (far_b, cross_a, near, ups, downs)
    )
    cross_b = swap(far_b, near_mask)
    downs = complete(downs, group_masks + column_masks)
    order = sorted(ups)
    ups = [ups[mask] for mask in order]
    downs = [downs[mask] for mask in order]
    far_part_a, cross_part_a = feed_forward([far_a, cross_a], ups, downs)
    cross_b, far_part_a, cross_part_a = lax.optimization_barrier(
        (cross_b, far_part_a, cross_part_a)
    )
    cross_sum_a = swap(cross_part_a, near_mask)
    far_part_b, cross_part_b = feed_forward([far_b, cross_b], ups, downs)
    cross_sum_a, far_part_b, cross_part_b = lax.optimization_barrier(
        (cross_sum_a, far_part_b, cross_part_b)
    )
    far_sum_a = swap(add_rows(far_part_a, cross_sum_a), far_mask)
    cross_sum_b = swap(cross_part_b, near_mask)
    (near_part,) = feed_forward([tie(near, cross_part_b)], ups, downs)
    near_sum = swap(near_part, near_mask)
    cross_sum_b, near_part = lax.optimization_barrier((cross_sum_b, near_part))
    far_sum_b = swap(add_rows(far_part_b, cross_sum_b), far_mask)
    (own_part,) = feed_forward([tie(hidden, near_part)], ups, downs)
    return finish_rows(
        hidden, own_part, near_sum, far_sum_a, far_sum_b, down_bias, out_gain, out_shift
    )


def solution(mesh):
    placed = (
        P(("grp", "dev"), None),
        P(("grp", "dev"), None),
        P(("grp", "dev"), None),
        P(("grp", "dev"), None),
        P(("grp", "dev"), None),
        P(("grp", "dev"), None),
        P("grp", None, "dev"),
        P("grp", None, "dev"),
        P(None, ("grp", "dev")),
        P(("grp", "dev")),
        P(("grp", "dev"), None),
        P(),
        P(),
        P(),
        P(),
        P(),
    )
    return jax.shard_map(
        on_device, mesh=mesh, in_specs=placed, out_specs=P(("grp", "dev"), None), check_vma=False
    )
```

```python
import functools
import math

import jax
import jax.numpy as jnp
from jax import lax
from jax.experimental import pallas as pl
from jax.experimental.pallas import tpu as pltpu
from jax.sharding import PartitionSpec as P

HD = 128
LANES = 128
STAT_ROWS = 8
ROW_BLOCK = 256
KEY_CHUNK = 1024

norm_eps = 1e-12
score_scale = HD ** (-0.5)
log2_e = math.log2(math.e)
mebibyte = 1024 * 1024


def layer_norm(summed, norm_gain, norm_shift):
    row_mean = jnp.mean(summed, axis=-1, keepdims=True)
    centred = summed - row_mean
    spread = jnp.mean(centred * centred, axis=-1, keepdims=True)
    return centred * lax.rsqrt(spread + norm_eps) * norm_gain + norm_shift


def vmem_spec():
    return pl.BlockSpec(memory_space=pltpu.VMEM)


def hbm_spec():
    return pl.BlockSpec(memory_space=pltpu.HBM)


def smem_spec():
    return pl.BlockSpec(memory_space=pltpu.SMEM)


def pack_kernel(lengths_ref, groups_ref, query_ref, out_ref, wide_ref):
    request_total = lengths_ref.shape[1]
    _, column_count, chunk_rows, part_width = out_ref.shape
    capacity = chunk_rows - STAT_ROWS
    slot_count = query_ref.shape[0]
    tiles = part_width // LANES
    for tile in range(wide_ref.shape[0]):
        wide_ref[tile, 0:slot_count, :] = query_ref[
            :, tile * LANES : (tile + 1) * LANES
        ].astype(jnp.float32)
        wide_ref[tile, slot_count : slot_count + capacity, :] = jnp.zeros(
            (capacity, LANES), jnp.float32
        )
    start = 0
    for request in range(request_total):
        group = groups_ref[0, request]
        count = jnp.full((STAT_ROWS, LANES), lengths_ref[0, request], jnp.int32).astype(jnp.float32)
        for column in range(column_count):
            for tile in range(tiles):
                rows = wide_ref[column * tiles + tile, pl.ds(start, capacity), :]
                rows = jnp.concatenate([rows, count], axis=0)
                out_ref[group, column, :, tile * LANES : (tile + 1) * LANES] = rows.astype(
                    jnp.bfloat16
                )
        start = start + lengths_ref[0, request]


def pack_queries(lengths, groups, queries, group_count, column_count, capacity):
    slot_count, model_width = queries.shape
    part_width = model_width // column_count
    return pl.pallas_call(
        pack_kernel,
        out_shape=jax.ShapeDtypeStruct(
            (group_count, column_count, capacity + STAT_ROWS, part_width), jnp.bfloat16
        ),
        in_specs=[smem_spec(), smem_spec(), vmem_spec()],
        out_specs=vmem_spec(),
        scratch_shapes=[
            pltpu.VMEM((model_width // LANES, slot_count + capacity, LANES), jnp.float32)
        ],
        compiler_params=pltpu.CompilerParams(vmem_limit_bytes=16 * mebibyte),
        name="pack_queries",
    )(lengths, groups, queries)


def far_kernel(
    counts_ref,
    arrived_ref,
    keys_hbm,
    values_hbm,
    out_ref,
    query_ref,
    answer_ref,
    stat_ref,
    score_ref,
    top_ref,
    keys_ref,
    values_ref,
    sems,
):
    copies = [
        pltpu.make_async_copy(keys_hbm, keys_ref, sems.at[0]),
        pltpu.make_async_copy(values_hbm, values_ref, sems.at[1]),
    ]
    for copy in copies:
        copy.start()
    sources, chunk_rows, part_width = arrived_ref.shape
    capacity = chunk_rows - STAT_ROWS
    local_heads = part_width // HD
    key_total = keys_ref.shape[1]
    chunks = key_total // KEY_CHUNK

    def take(source, offset):
        for head in range(local_heads):
            rows = arrived_ref[source, :, head * HD : (head + 1) * HD].astype(jnp.float32)
            query_ref[head, pl.ds(offset, capacity), :] = rows[:capacity]
        return offset + counts_ref[source]

    total = lax.fori_loop(0, sources, take, jnp.int32(0))
    blocks = (total + ROW_BLOCK - 1) // ROW_BLOCK
    lane = lax.broadcasted_iota(jnp.int32, (ROW_BLOCK, LANES), 1)

    def block_rows(block):
        return pl.ds(pl.multiple_of(block * ROW_BLOCK, ROW_BLOCK), ROW_BLOCK)

    def load_queries(block, head):
        return query_ref[head, block_rows(block), :].astype(jnp.bfloat16)

    def score_chunk(rows, head, slot, chunk, part_top):
        columns = slice(chunk * KEY_CHUNK, (chunk + 1) * KEY_CHUNK)
        scores = jnp.dot(
            rows,
            keys_ref[head * HD : (head + 1) * HD, columns],
            preferred_element_type=jnp.float32,
        )
        score_ref[slot, :, columns] = scores
        for piece in range(KEY_CHUNK // LANES):
            part = scores[:, piece * LANES : (piece + 1) * LANES]
            part_top = part if part_top is None else jnp.maximum(part_top, part)
        return part_top

    def finish_top(part_top, slot):
        row_top = jnp.max(part_top, axis=1, keepdims=True) * score_scale
        row_top = row_top.astype(jnp.bfloat16).astype(jnp.float32)
        top_ref[slot] = jnp.broadcast_to(row_top, (ROW_BLOCK, LANES))

    def weigh_chunk(head, slot, chunk, shift):
        columns = slice(chunk * KEY_CHUNK, (chunk + 1) * KEY_CHUNK)
        weights = jnp.exp2(score_ref[slot, :, columns] * (score_scale * log2_e) - shift)
        return jnp.dot(
            weights.astype(jnp.bfloat16),
            values_ref[head, columns, :],
            preferred_element_type=jnp.float32,
        )

    def finish_answer(block, head, slot, mixed):
        rows = block_rows(block)
        row_sum = mixed[:, HD:]
        answer_ref[head, rows, :] = mixed[:, :HD] / row_sum
        top = top_ref[slot]
        if head == 0:
            stat_ref[rows, :] = jnp.where(lane == 0, top, row_sum)
        else:
            before = stat_ref[rows, :]
            with_top = jnp.where(lane == head, top, before)
            stat_ref[rows, :] = jnp.where(lane == local_heads + head, row_sum, with_top)

    def slot_of(block, head):
        return (block * local_heads + head) % 2 if local_heads % 2 else head % 2

    for copy in copies:
        copy.wait()
    first_rows = load_queries(0, 0)
    part_top = None
    for chunk in range(chunks):
        part_top = score_chunk(first_rows, 0, 0, chunk, part_top)
    finish_top(part_top, 0)

    def one_block(block, carry):
        for head in range(local_heads):
            slot = slot_of(block, head)
            if head + 1 < local_heads:
                next_block, next_head = block, head + 1
            else:
                next_block, next_head = jnp.minimum(block + 1, blocks - 1), 0
            next_slot = 1 - slot
            next_rows = load_queries(next_block, next_head)
            shift = top_ref[slot][:, 0:1] * log2_e
            part_top = None
            mixed = None
            for chunk in range(chunks):
                part_top = score_chunk(next_rows, next_head, next_slot, chunk, part_top)
                part = weigh_chunk(head, slot, chunk, shift)
                mixed = part if mixed is None else mixed + part
            finish_answer(block, head, slot, mixed)
            finish_top(part_top, next_slot)
        return carry

    lax.fori_loop(0, blocks, one_block, 0)

    def give(source, offset):
        rows = [answer_ref[head, pl.ds(offset, capacity), :] for head in range(local_heads)]
        turned = jnp.transpose(stat_ref[pl.ds(offset, LANES), :])[:STAT_ROWS, :]
        if part_width > LANES:
            turned = jnp.concatenate(
                [turned, jnp.zeros((STAT_ROWS, part_width - LANES), jnp.float32)], axis=1
            )
        rows = jnp.concatenate(rows, axis=1)
        out_ref[source] = jnp.concatenate([rows, turned], axis=0).astype(jnp.bfloat16)
        return offset + counts_ref[source]

    lax.fori_loop(0, sources, give, jnp.int32(0))


def attend_prefix(counts, arrived, turned_keys, wide_values):
    sources, chunk_rows, part_width = arrived.shape
    capacity = chunk_rows - STAT_ROWS
    local_heads = part_width // HD
    key_total = turned_keys.shape[1]
    row_total = -(-sources * capacity // ROW_BLOCK) * ROW_BLOCK + LANES
    return pl.pallas_call(
        far_kernel,
        out_shape=jax.ShapeDtypeStruct((sources, capacity + STAT_ROWS, part_width), jnp.bfloat16),
        in_specs=[smem_spec(), vmem_spec(), hbm_spec(), hbm_spec()],
        out_specs=vmem_spec(),
        scratch_shapes=[
            pltpu.VMEM((local_heads, row_total, HD), jnp.float32),
            pltpu.VMEM((local_heads, row_total, HD), jnp.float32),
            pltpu.VMEM((row_total, LANES), jnp.float32),
            pltpu.VMEM((2, ROW_BLOCK, key_total), jnp.float32),
            pltpu.VMEM((2, ROW_BLOCK, LANES), jnp.float32),
            pltpu.VMEM(turned_keys.shape, jnp.bfloat16),
            pltpu.VMEM(wide_values.shape, jnp.bfloat16),
            pltpu.SemaphoreType.DMA((2,)),
        ],
        compiler_params=pltpu.CompilerParams(vmem_limit_bytes=58 * mebibyte),
        cost_estimate=pl.CostEstimate(
            flops=4 * sources * capacity * key_total * part_width,
            bytes_accessed=8 * key_total * part_width,
            transcendentals=sources * capacity * key_total * local_heads,
        ),
        name="attend_prefix",
    )(counts, arrived, turned_keys, wide_values)


def stat_lane(head, local_heads):
    return (head // local_heads) * STAT_ROWS + head % local_heads


def own_kernel(local_heads, lengths_ref, query_ref, key_ref, value_ref, mixed_ref, top_ref, sum_ref):
    slot_count, model_width = query_ref.shape
    head_count = model_width // HD
    row = lax.broadcasted_iota(jnp.int32, (slot_count, slot_count), 0)
    column = lax.broadcasted_iota(jnp.int32, (slot_count, slot_count), 1)
    row_segment = jnp.zeros((slot_count, slot_count), jnp.int32)
    column_segment = jnp.zeros((slot_count, slot_count), jnp.int32)
    start = 0
    for request in range(lengths_ref.shape[1]):
        start = start + lengths_ref[0, request]
        row_segment = row_segment + (row >= start).astype(jnp.int32)
        column_segment = column_segment + (column >= start).astype(jnp.int32)
    visible = (row_segment == column_segment) & (column <= row)
    lane = lax.broadcasted_iota(jnp.int32, (slot_count, LANES), 1)
    tops = jnp.zeros((slot_count, LANES), jnp.float32)
    sums = jnp.ones((slot_count, LANES), jnp.float32)
    for head in range(head_count):
        columns = slice(head * HD, (head + 1) * HD)
        scores = (
            lax.dot_general(
                query_ref[:, columns],
                key_ref[:, columns],
                (((1,), (1,)), ((), ())),
                preferred_element_type=jnp.float32,
            )
            * score_scale
        )
        top = jnp.max(jnp.where(visible, scores, -jnp.inf), axis=1, keepdims=True)
        weights = jnp.where(visible, jnp.exp(scores - top), 0.0)
        mixed_ref[:, columns] = jnp.dot(
            weights.astype(jnp.bfloat16),
            value_ref[:, columns],
            preferred_element_type=jnp.float32,
        )
        at = stat_lane(head, local_heads)
        tops = jnp.where(lane == at, top, tops)
        sums = jnp.where(lane == at, jnp.sum(weights, axis=1, keepdims=True), sums)
    top_ref[...] = tops
    sum_ref[...] = sums


def attend_suffix(lengths, queries, keys, values, local_heads):
    slot_count, model_width = queries.shape
    stats = jax.ShapeDtypeStruct((slot_count, LANES), jnp.float32)
    return pl.pallas_call(
        functools.partial(own_kernel, local_heads),
        out_shape=(jax.ShapeDtypeStruct((slot_count, model_width), jnp.float32), stats, stats),
        in_specs=[smem_spec()] + [vmem_spec()] * 3,
        out_specs=(vmem_spec(), vmem_spec(), vmem_spec()),
        compiler_params=pltpu.CompilerParams(vmem_limit_bytes=16 * mebibyte),
        cost_estimate=pl.CostEstimate(
            flops=40 * slot_count * slot_count * model_width,
            bytes_accessed=8 * slot_count * model_width,
            transcendentals=slot_count * model_width,
        ),
        name="attend_suffix",
    )(lengths, queries, keys, values)


def merge_kernel(
    lengths_ref,
    groups_ref,
    arrived_ref,
    own_mixed_ref,
    own_top_ref,
    own_sum_ref,
    input_ref,
    gain_ref,
    shift_ref,
    first_ref,
    second_ref,
    hidden_ref,
    far_ref,
    stat_ref,
):
    _, column_count, chunk_rows, part_width = arrived_ref.shape
    slot_count, model_width = input_ref.shape
    capacity = chunk_rows - STAT_ROWS
    local_heads = part_width // HD
    head_count = model_width // HD
    start = 0
    for request in range(lengths_ref.shape[1]):
        group = groups_ref[0, request]
        pieces = []
        for column in range(column_count):
            block = arrived_ref[group, column].astype(jnp.float32)
            for head in range(local_heads):
                far_ref[column * local_heads + head, pl.ds(start, capacity), :] = block[
                    :capacity, head * HD : (head + 1) * HD
                ]
            pieces.append(block[capacity:, :LANES])
        if column_count * STAT_ROWS < LANES:
            pieces.append(jnp.zeros((LANES - column_count * STAT_ROWS, LANES), jnp.float32))
        turned = jnp.transpose(jnp.concatenate(pieces, axis=0))
        stat_ref[pl.ds(start, capacity), :] = turned[:capacity]
        start = start + lengths_ref[0, request]
    far_top = stat_ref[:slot_count, :]
    far_sum = pltpu.roll(far_top, LANES - local_heads, 1)
    own_top = own_top_ref[...]
    joint_top = jnp.maximum(far_top, own_top)
    far_weight = jnp.exp(far_top - joint_top) * far_sum
    own_weight = jnp.exp(own_top - joint_top)
    bottom = far_weight + own_weight * own_sum_ref[...]
    far_weight = far_weight / bottom
    own_weight = own_weight / bottom
    total = jnp.zeros((slot_count, LANES), jnp.float32)
    for head in range(head_count):
        columns = slice(head * HD, (head + 1) * HD)
        at = stat_lane(head, local_heads)
        summed = (
            input_ref[:, columns].astype(jnp.float32)
            + far_weight[:, at : at + 1] * far_ref[head, :slot_count, :]
            + own_weight[:, at : at + 1] * own_mixed_ref[:, columns]
        )
        far_ref[head, :slot_count, :] = summed
        total = total + summed
    row_mean = jnp.sum(total, axis=1, keepdims=True) * (1.0 / model_width)
    total = jnp.zeros((slot_count, LANES), jnp.float32)
    for head in range(head_count):
        centred = far_ref[head, :slot_count, :] - row_mean
        total = total + centred * centred
    spread = jnp.sum(total, axis=1, keepdims=True) * (1.0 / model_width)
    factor = lax.rsqrt(spread + norm_eps)
    for head in range(head_count):
        columns = slice(head * HD, (head + 1) * HD)
        centred = far_ref[head, :slot_count, :] - row_mean
        hidden = (centred * factor * gain_ref[:, columns] + shift_ref[:, columns]).astype(
            jnp.bfloat16
        )
        first_ref[:, columns] = hidden[: slot_count // 2]
        second_ref[:, columns] = hidden[slot_count // 2 :]
        hidden_ref[:, columns] = hidden


def merge_parts(lengths, groups, arrived, own_mixed, own_top, own_sum, layer_input, gain, shift):
    slot_count, model_width = layer_input.shape
    capacity = arrived.shape[2] - STAT_ROWS
    half = jax.ShapeDtypeStruct((slot_count // 2, model_width), jnp.bfloat16)
    return pl.pallas_call(
        merge_kernel,
        out_shape=(half, half, jax.ShapeDtypeStruct(layer_input.shape, jnp.bfloat16)),
        in_specs=[smem_spec(), smem_spec()] + [vmem_spec()] * 7,
        out_specs=(vmem_spec(), vmem_spec(), vmem_spec()),
        scratch_shapes=[
            pltpu.VMEM((model_width // HD, slot_count + capacity, HD), jnp.float32),
            pltpu.VMEM((slot_count + capacity, LANES), jnp.float32),
        ],
        compiler_params=pltpu.CompilerParams(vmem_limit_bytes=16 * mebibyte),
        name="merge_parts",
    )(
        lengths,
        groups,
        arrived,
        own_mixed,
        own_top,
        own_sum,
        layer_input,
        gain.reshape(1, model_width),
        shift.reshape(1, model_width),
    )


def swap(value, mask):
    total = lax.axis_size("grp") * lax.axis_size("dev")
    pairs = [(here, here ^ mask) for here in range(total)]
    return jax.tree.map(lambda leaf: lax.ppermute(leaf, ("grp", "dev"), pairs), value)


def complete(held, masks):
    held = dict(held)
    for mask in masks:
        for at in list(held):
            if mask ^ at not in held:
                held[mask ^ at] = swap(held[at], mask)
    return held


def tie(values, after):
    return lax.optimization_barrier((values, after))[0]


def mlp_kernel(pieces, up_plan, down_plan, *refs):
    parts = len(up_plan)
    row_refs, refs = refs[:pieces], refs[pieces:]
    up_total, down_total = sum(map(len, up_plan)), sum(map(len, down_plan))
    ups, refs = list(refs[:up_total]), refs[up_total:]
    downs, refs = list(refs[:down_total]), refs[down_total:]
    out_refs, (up_ref, down_ref, sems) = refs[:pieces], refs[pieces:]
    model_width = row_refs[0].shape[1]
    copies = []
    for part, heights in enumerate(up_plan):
        begin, held = 0, []
        for piece, height in enumerate(heights):
            target = up_ref.at[part, pl.ds(begin, height)]
            held.append(pltpu.make_async_copy(ups.pop(0), target, sems.at[part, 0, piece]))
            begin += height
        copies.append(held)
    begin = 0
    for part, heights in enumerate(down_plan):
        held = []
        for piece, height in enumerate(heights):
            target = down_ref.at[pl.ds(begin, height)]
            held.append(pltpu.make_async_copy(downs.pop(0), target, sems.at[part, 1, piece]))
            begin += height
        copies.append(held)
    ahead = 4

    def start(at):
        if at < len(copies):
            for copy in copies[at]:
                copy.start()

    def arrive(at):
        for copy in copies[at]:
            copy.wait()
        start(at + ahead)

    for at in range(ahead):
        start(at)
    rows = jnp.concatenate([ref[...] for ref in row_refs], axis=0)
    activations = []
    for part in range(parts):
        arrive(part)
        product = jnp.dot(
            rows, up_ref[part, :model_width, :], preferred_element_type=jnp.float32
        )
        offset = up_ref[part, model_width:, :].astype(jnp.float32)[0:1]
        activations.append(jax.nn.gelu(product + offset, approximate=True).astype(jnp.bfloat16))
    for part in range(parts):
        arrive(parts + part)
    total = jnp.dot(
        jnp.concatenate(activations, axis=1), down_ref[...], preferred_element_type=jnp.float32
    ).astype(jnp.bfloat16)
    height = row_refs[0].shape[0]
    for piece in range(pieces):
        out_refs[piece][...] = total[piece * height : (piece + 1) * height]


def feed_forward(rows, ups, downs):
    pieces, parts = len(rows), len(ups)
    height, model_width = rows[0].shape
    up_plan = [[piece.shape[0] for piece in block] for block in ups]
    down_plan = [[piece.shape[0] for piece in block] for block in downs]
    up_rows, down_rows = sum(up_plan[0]), sum(down_plan[0])
    units = ups[0][0].shape[1]
    flat = [piece for block in ups + downs for piece in block]
    most = max(map(len, up_plan + down_plan))
    return pl.pallas_call(
        functools.partial(mlp_kernel, pieces, up_plan, down_plan),
        out_shape=tuple(jax.ShapeDtypeStruct(piece.shape, jnp.bfloat16) for piece in rows),
        in_specs=[vmem_spec()] * pieces + [hbm_spec()] * len(flat),
        out_specs=tuple(vmem_spec() for _ in rows),
        scratch_shapes=[
            pltpu.VMEM((parts, up_rows, units), jnp.bfloat16),
            pltpu.VMEM((parts * down_rows, model_width), jnp.bfloat16),
            pltpu.SemaphoreType.DMA((parts, 2, most)),
        ],
        compiler_params=pltpu.CompilerParams(vmem_limit_bytes=58 * mebibyte),
        cost_estimate=pl.CostEstimate(
            flops=4 * pieces * height * model_width * parts * units,
            bytes_accessed=4 * parts * model_width * units,
            transcendentals=pieces * height * parts * units,
        ),
        name="feed_forward",
    )(*rows, *flat)


def add_kernel(here_ref, there_ref, out_ref):
    out_ref[...] = (
        here_ref[...].astype(jnp.float32) + there_ref[...].astype(jnp.float32)
    ).astype(jnp.bfloat16)


def add_rows(here, there):
    return pl.pallas_call(
        add_kernel,
        out_shape=jax.ShapeDtypeStruct(here.shape, jnp.bfloat16),
        in_specs=[vmem_spec(), vmem_spec()],
        out_specs=vmem_spec(),
        name="add_rows",
    )(here, there)


def finish_kernel(
    hidden_ref, own_ref, near_ref, far_a_ref, far_b_ref, bias_ref, gain_ref, shift_ref, out_ref
):
    height = far_a_ref.shape[0]
    for begin, far_ref in ((0, far_a_ref), (height, far_b_ref)):
        rows = slice(begin, begin + height)
        summed = hidden_ref[rows, :].astype(jnp.float32) + (
            own_ref[rows, :].astype(jnp.float32)
            + near_ref[rows, :].astype(jnp.float32)
            + far_ref[...].astype(jnp.float32)
        )
        out_ref[rows, :] = layer_norm(
            summed + bias_ref[...], gain_ref[...], shift_ref[...]
        ).astype(jnp.bfloat16)


def finish_rows(hidden, own, near, far_a, far_b, bias, gain, shift):
    model_width = hidden.shape[1]
    return pl.pallas_call(
        finish_kernel,
        out_shape=jax.ShapeDtypeStruct(hidden.shape, jnp.bfloat16),
        in_specs=[vmem_spec()] * 8,
        out_specs=vmem_spec(),
        compiler_params=pltpu.CompilerParams(vmem_limit_bytes=16 * mebibyte),
        name="finish_rows",
    )(
        hidden,
        own,
        near,
        far_a,
        far_b,
        bias.reshape(1, model_width),
        gain.reshape(1, model_width),
        shift.reshape(1, model_width),
    )


def on_device(
    suffix_queries,
    suffix_keys,
    suffix_values,
    layer_input,
    suffix_lengths,
    request_group,
    prefix_keys,
    prefix_values,
    up_weight,
    up_bias,
    down_weight,
    down_bias,
    attn_gain,
    attn_shift,
    out_gain,
    out_shift,
):
    slot_count, model_width = suffix_queries.shape
    group_count = lax.axis_size("grp")
    column_count = lax.axis_size("dev")
    part_width = model_width // column_count
    local_heads = part_width // HD
    capacity = 2 * slot_count // group_count
    sources = group_count * column_count

    near_mask = group_count // 2 * column_count
    far_mask = column_count // 2
    column_masks = [1 << bit for bit in range(far_mask.bit_length() - 1)]
    group_masks = [column_count << bit for bit in range((group_count // 2).bit_length() - 1)]

    low_mask, high_masks = column_masks[0], column_masks[1:]
    core_mask = group_masks[0]

    outgoing = pack_queries(
        suffix_lengths, request_group, suffix_queries, group_count, column_count, capacity
    )
    bias_rows = jnp.broadcast_to(up_bias[None, :], (16, up_bias.shape[0]))
    up_block = jnp.concatenate([up_weight, bias_rows], axis=0)
    up_cut, down_cut = up_weight.shape[0] // 2, down_weight.shape[0] // 2
    up_pieces = (up_block[:up_cut], up_block[up_cut:])
    down_pieces = (down_weight[:down_cut], down_weight[down_cut:])
    ups, downs = {0: (up_block,)}, {0: (down_weight,)}
    high_mask = high_masks[0]

    arrived = lax.all_to_all(
        outgoing.reshape(sources, capacity + STAT_ROWS, part_width),
        ("grp", "dev"),
        split_axis=0,
        concat_axis=0,
        tiled=True,
    )
    ups[low_mask] = swap(ups[0], low_mask)
    up_first = swap(up_pieces[0], high_mask)
    ups[core_mask] = swap(ups[0], core_mask)
    downs[core_mask] = swap(downs[0], core_mask)
    turned_keys = prefix_keys[0].T
    value_heads = prefix_values[0].reshape(-1, local_heads, HD).transpose(1, 0, 2)
    wide_values = jnp.concatenate([value_heads, jnp.ones_like(value_heads)], axis=2)
    own = attend_suffix(
        suffix_lengths, suffix_queries, suffix_keys, suffix_values, local_heads
    )
    arrived, ups, up_first, up_pieces, downs, down_pieces, turned_keys, wide_values, own = (
        lax.optimization_barrier(
            (arrived, ups, up_first, up_pieces, downs, down_pieces, turned_keys, wide_values, own)
        )
    )

    counts = arrived[:, capacity, 0].astype(jnp.int32)
    answer_part = attend_prefix(counts, arrived, turned_keys, wide_values)
    downs[low_mask] = swap(downs[0], low_mask)
    up_second = swap(up_pieces[1], high_mask)
    down_first = swap(down_pieces[0], high_mask)
    ups[core_mask ^ low_mask] = swap(ups[low_mask], core_mask)
    answer_part, ups, up_first, up_second, downs, down_first, down_pieces = (
        lax.optimization_barrier(
            (answer_part, ups, up_first, up_second, downs, down_first, down_pieces)
        )
    )

    answer = lax.all_to_all(
        answer_part, ("grp", "dev"), split_axis=0, concat_axis=0, tiled=True
    ).reshape(group_count, column_count, capacity + STAT_ROWS, part_width)
    ups[high_mask] = (jnp.concatenate([up_first, up_second], axis=0),)
    ups[core_mask ^ high_mask] = swap(ups[high_mask], core_mask)
    downs[core_mask ^ low_mask] = swap(downs[low_mask], core_mask)
    down_second = swap(down_pieces[1], high_mask)
    downs[high_mask] = (jnp.concatenate([down_first, down_second], axis=0),)
    ups[low_mask ^ high_mask] = swap(ups[high_mask], low_mask)
    answer, ups, downs = lax.optimization_barrier((answer, ups, downs))

    hidden_a, hidden_b, hidden = merge_parts(
        suffix_lengths, request_group, answer, *own, layer_input, attn_gain, attn_shift
    )

    (hidden_a, hidden_b, hidden), ups, downs = lax.optimization_barrier(
        ((hidden_a, hidden_b, hidden), ups, downs)
    )
    far_a = swap(hidden_a, far_mask)
    near = swap(tie(hidden, far_a), near_mask)
    downs[low_mask ^ high_mask] = swap(downs[high_mask], low_mask)
    downs[core_mask ^ high_mask] = swap(downs[high_mask], core_mask)
    ups = complete(ups, group_masks + column_masks)
    far_b = swap(tie(hidden_b, far_a), far_mask)
    cross_a = swap(far_a, near_mask)
    far_b, cross_a, near, ups, downs = lax.optimization_barrier(
        (far_b, cross_a, near, ups, downs)
    )
    cross_b = swap(far_b, near_mask)
    downs = complete(downs, group_masks + column_masks)
    order = sorted(ups)
    ups = [ups[mask] for mask in order]
    downs = [downs[mask] for mask in order]
    far_part_a, cross_part_a = feed_forward([far_a, cross_a], ups, downs)
    cross_b, far_part_a, cross_part_a = lax.optimization_barrier(
        (cross_b, far_part_a, cross_part_a)
    )
    cross_sum_a = swap(cross_part_a, near_mask)
    far_part_b, cross_part_b = feed_forward([far_b, cross_b], ups, downs)
    cross_sum_a, far_part_b, cross_part_b = lax.optimization_barrier(
        (cross_sum_a, far_part_b, cross_part_b)
    )
    far_sum_a = swap(add_rows(far_part_a, cross_sum_a), far_mask)
    cross_sum_b = swap(cross_part_b, near_mask)
    (near_part,) = feed_forward([tie(near, cross_part_b)], ups, downs)
    near_sum = swap(near_part, near_mask)
    cross_sum_b, near_part = lax.optimization_barrier((cross_sum_b, near_part))
    far_sum_b = swap(add_rows(far_part_b, cross_sum_b), far_mask)
    (own_part,) = feed_forward([tie(hidden, near_part)], ups, downs)
    return finish_rows(
        hidden, own_part, near_sum, far_sum_a, far_sum_b, down_bias, out_gain, out_shift
    )


def solution(mesh):
    placed = (
        P(("grp", "dev"), None),
        P(("grp", "dev"), None),
        P(("grp", "dev"), None),
        P(("grp", "dev"), None),
        P(("grp", "dev"), None),
        P(("grp", "dev"), None),
        P("grp", None, "dev"),
        P("grp", None, "dev"),
        P(None, ("grp", "dev")),
        P(("grp", "dev")),
        P(("grp", "dev"), None),
        P(),
        P(),
        P(),
        P(),
        P(),
    )
    return jax.shard_map(
        on_device, mesh=mesh, in_specs=placed, out_specs=P(("grp", "dev"), None), check_vma=False
    )
```

```python
import functools
import math

import jax
import jax.numpy as jnp
from jax import lax
from jax.experimental import pallas as pl
from jax.experimental.pallas import tpu as pltpu
from jax.sharding import PartitionSpec as P

HD = 128
LANES = 128
STAT_ROWS = 8
ROW_BLOCK = 256
KEY_CHUNK = 1024

norm_eps = 1e-12
score_scale = HD ** (-0.5)
log2_e = math.log2(math.e)
mebibyte = 1024 * 1024


def layer_norm(summed, norm_gain, norm_shift):
    row_mean = jnp.mean(summed, axis=-1, keepdims=True)
    centred = summed - row_mean
    spread = jnp.mean(centred * centred, axis=-1, keepdims=True)
    return centred * lax.rsqrt(spread + norm_eps) * norm_gain + norm_shift


def vmem_spec():
    return pl.BlockSpec(memory_space=pltpu.VMEM)


def hbm_spec():
    return pl.BlockSpec(memory_space=pltpu.HBM)


def smem_spec():
    return pl.BlockSpec(memory_space=pltpu.SMEM)


def pack_kernel(lengths_ref, groups_ref, query_ref, out_ref, wide_ref):
    request_total = lengths_ref.shape[1]
    _, column_count, chunk_rows, part_width = out_ref.shape
    capacity = chunk_rows - STAT_ROWS
    slot_count = query_ref.shape[0]
    tiles = part_width // LANES
    for tile in range(wide_ref.shape[0]):
        wide_ref[tile, 0:slot_count, :] = query_ref[
            :, tile * LANES : (tile + 1) * LANES
        ].astype(jnp.float32)
        wide_ref[tile, slot_count : slot_count + capacity, :] = jnp.zeros(
            (capacity, LANES), jnp.float32
        )
    start = 0
    for request in range(request_total):
        group = groups_ref[0, request]
        count = jnp.full((STAT_ROWS, LANES), lengths_ref[0, request], jnp.int32).astype(jnp.float32)
        for column in range(column_count):
            for tile in range(tiles):
                rows = wide_ref[column * tiles + tile, pl.ds(start, capacity), :]
                rows = jnp.concatenate([rows, count], axis=0)
                out_ref[group, column, :, tile * LANES : (tile + 1) * LANES] = rows.astype(
                    jnp.bfloat16
                )
        start = start + lengths_ref[0, request]


def pack_queries(lengths, groups, queries, group_count, column_count, capacity):
    slot_count, model_width = queries.shape
    part_width = model_width // column_count
    return pl.pallas_call(
        pack_kernel,
        out_shape=jax.ShapeDtypeStruct(
            (group_count, column_count, capacity + STAT_ROWS, part_width), jnp.bfloat16
        ),
        in_specs=[smem_spec(), smem_spec(), vmem_spec()],
        out_specs=vmem_spec(),
        scratch_shapes=[
            pltpu.VMEM((model_width // LANES, slot_count + capacity, LANES), jnp.float32)
        ],
        compiler_params=pltpu.CompilerParams(vmem_limit_bytes=16 * mebibyte),
        name="pack_queries",
    )(lengths, groups, queries)


def far_kernel(
    counts_ref,
    arrived_ref,
    keys_hbm,
    values_hbm,
    out_ref,
    query_ref,
    answer_ref,
    stat_ref,
    score_ref,
    top_ref,
    keys_ref,
    values_ref,
    sems,
):
    copies = [
        pltpu.make_async_copy(keys_hbm, keys_ref, sems.at[0]),
        pltpu.make_async_copy(values_hbm, values_ref, sems.at[1]),
    ]
    for copy in copies:
        copy.start()
    sources, chunk_rows, part_width = arrived_ref.shape
    capacity = chunk_rows - STAT_ROWS
    local_heads = part_width // HD
    key_total = keys_ref.shape[1]
    chunks = key_total // KEY_CHUNK

    def take(source, offset):
        for head in range(local_heads):
            rows = arrived_ref[source, :, head * HD : (head + 1) * HD].astype(jnp.float32)
            query_ref[head, pl.ds(offset, capacity), :] = rows[:capacity]
        return offset + counts_ref[source]

    total = lax.fori_loop(0, sources, take, jnp.int32(0))
    blocks = (total + ROW_BLOCK - 1) // ROW_BLOCK
    lane = lax.broadcasted_iota(jnp.int32, (ROW_BLOCK, LANES), 1)

    def block_rows(block):
        return pl.ds(pl.multiple_of(block * ROW_BLOCK, ROW_BLOCK), ROW_BLOCK)

    def load_queries(block, head):
        return query_ref[head, block_rows(block), :].astype(jnp.bfloat16)

    def score_chunk(rows, head, slot, chunk, part_top):
        columns = slice(chunk * KEY_CHUNK, (chunk + 1) * KEY_CHUNK)
        scores = jnp.dot(
            rows,
            keys_ref[head * HD : (head + 1) * HD, columns],
            preferred_element_type=jnp.float32,
        )
        score_ref[slot, :, columns] = scores
        for piece in range(KEY_CHUNK // LANES):
            part = scores[:, piece * LANES : (piece + 1) * LANES]
            part_top = part if part_top is None else jnp.maximum(part_top, part)
        return part_top

    def finish_top(part_top, slot):
        row_top = jnp.max(part_top, axis=1, keepdims=True) * score_scale
        row_top = row_top.astype(jnp.bfloat16).astype(jnp.float32)
        top_ref[slot] = jnp.broadcast_to(row_top, (ROW_BLOCK, LANES))

    def weigh_chunk(head, slot, chunk, shift):
        columns = slice(chunk * KEY_CHUNK, (chunk + 1) * KEY_CHUNK)
        weights = jnp.exp2(score_ref[slot, :, columns] * (score_scale * log2_e) - shift)
        return jnp.dot(
            weights.astype(jnp.bfloat16),
            values_ref[head, columns, :],
            preferred_element_type=jnp.float32,
        )

    def finish_answer(block, head, slot, mixed):
        rows = block_rows(block)
        row_sum = mixed[:, HD:]
        answer_ref[head, rows, :] = mixed[:, :HD] / row_sum
        top = top_ref[slot]
        if head == 0:
            stat_ref[rows, :] = jnp.where(lane == 0, top, row_sum)
        else:
            before = stat_ref[rows, :]
            with_top = jnp.where(lane == head, top, before)
            stat_ref[rows, :] = jnp.where(lane == local_heads + head, row_sum, with_top)

    def slot_of(block, head):
        return (block * local_heads + head) % 2 if local_heads % 2 else head % 2

    for copy in copies:
        copy.wait()
    first_rows = load_queries(0, 0)
    part_top = None
    for chunk in range(chunks):
        part_top = score_chunk(first_rows, 0, 0, chunk, part_top)
    finish_top(part_top, 0)

    def one_block(block, carry):
        for head in range(local_heads):
            slot = slot_of(block, head)
            if head + 1 < local_heads:
                next_block, next_head = block, head + 1
            else:
                next_block, next_head = jnp.minimum(block + 1, blocks - 1), 0
            next_slot = 1 - slot
            next_rows = load_queries(next_block, next_head)
            shift = top_ref[slot][:, 0:1] * log2_e
            part_top = None
            mixed = None
            for chunk in range(chunks):
                part_top = score_chunk(next_rows, next_head, next_slot, chunk, part_top)
                part = weigh_chunk(head, slot, chunk, shift)
                mixed = part if mixed is None else mixed + part
            finish_answer(block, head, slot, mixed)
            finish_top(part_top, next_slot)
        return carry

    lax.fori_loop(0, blocks, one_block, 0)

    def give(source, offset):
        rows = [answer_ref[head, pl.ds(offset, capacity), :] for head in range(local_heads)]
        turned = jnp.transpose(stat_ref[pl.ds(offset, LANES), :])[:STAT_ROWS, :]
        if part_width > LANES:
            turned = jnp.concatenate(
                [turned, jnp.zeros((STAT_ROWS, part_width - LANES), jnp.float32)], axis=1
            )
        rows = jnp.concatenate(rows, axis=1)
        out_ref[source] = jnp.concatenate([rows, turned], axis=0).astype(jnp.bfloat16)
        return offset + counts_ref[source]

    lax.fori_loop(0, sources, give, jnp.int32(0))


def attend_prefix(counts, arrived, turned_keys, wide_values):
    sources, chunk_rows, part_width = arrived.shape
    capacity = chunk_rows - STAT_ROWS
    local_heads = part_width // HD
    key_total = turned_keys.shape[1]
    row_total = -(-sources * capacity // ROW_BLOCK) * ROW_BLOCK + LANES
    return pl.pallas_call(
        far_kernel,
        out_shape=jax.ShapeDtypeStruct((sources, capacity + STAT_ROWS, part_width), jnp.bfloat16),
        in_specs=[smem_spec(), vmem_spec(), hbm_spec(), hbm_spec()],
        out_specs=vmem_spec(),
        scratch_shapes=[
            pltpu.VMEM((local_heads, row_total, HD), jnp.float32),
            pltpu.VMEM((local_heads, row_total, HD), jnp.float32),
            pltpu.VMEM((row_total, LANES), jnp.float32),
            pltpu.VMEM((2, ROW_BLOCK, key_total), jnp.float32),
            pltpu.VMEM((2, ROW_BLOCK, LANES), jnp.float32),
            pltpu.VMEM(turned_keys.shape, jnp.bfloat16),
            pltpu.VMEM(wide_values.shape, jnp.bfloat16),
            pltpu.SemaphoreType.DMA((2,)),
        ],
        compiler_params=pltpu.CompilerParams(vmem_limit_bytes=58 * mebibyte),
        cost_estimate=pl.CostEstimate(
            flops=4 * sources * capacity * key_total * part_width,
            bytes_accessed=8 * key_total * part_width,
            transcendentals=sources * capacity * key_total * local_heads,
        ),
        name="attend_prefix",
    )(counts, arrived, turned_keys, wide_values)


def stat_lane(head, local_heads):
    return (head // local_heads) * STAT_ROWS + head % local_heads


def own_kernel(local_heads, lengths_ref, query_ref, key_ref, value_ref, mixed_ref, top_ref, sum_ref):
    slot_count, model_width = query_ref.shape
    head_count = model_width // HD
    row = lax.broadcasted_iota(jnp.int32, (slot_count, slot_count), 0)
    column = lax.broadcasted_iota(jnp.int32, (slot_count, slot_count), 1)
    row_segment = jnp.zeros((slot_count, slot_count), jnp.int32)
    column_segment = jnp.zeros((slot_count, slot_count), jnp.int32)
    start = 0
    for request in range(lengths_ref.shape[1]):
        start = start + lengths_ref[0, request]
        row_segment = row_segment + (row >= start).astype(jnp.int32)
        column_segment = column_segment + (column >= start).astype(jnp.int32)
    visible = (row_segment == column_segment) & (column <= row)
    lane = lax.broadcasted_iota(jnp.int32, (slot_count, LANES), 1)
    tops = jnp.zeros((slot_count, LANES), jnp.float32)
    sums = jnp.ones((slot_count, LANES), jnp.float32)
    for head in range(head_count):
        columns = slice(head * HD, (head + 1) * HD)
        scores = (
            lax.dot_general(
                query_ref[:, columns],
                key_ref[:, columns],
                (((1,), (1,)), ((), ())),
                preferred_element_type=jnp.float32,
            )
            * score_scale
        )
        top = jnp.max(jnp.where(visible, scores, -jnp.inf), axis=1, keepdims=True)
        weights = jnp.where(visible, jnp.exp(scores - top), 0.0)
        mixed_ref[:, columns] = jnp.dot(
            weights.astype(jnp.bfloat16),
            value_ref[:, columns],
            preferred_element_type=jnp.float32,
        )
        at = stat_lane(head, local_heads)
        tops = jnp.where(lane == at, top, tops)
        sums = jnp.where(lane == at, jnp.sum(weights, axis=1, keepdims=True), sums)
    top_ref[...] = tops
    sum_ref[...] = sums


def attend_suffix(lengths, queries, keys, values, local_heads):
    slot_count, model_width = queries.shape
    stats = jax.ShapeDtypeStruct((slot_count, LANES), jnp.float32)
    return pl.pallas_call(
        functools.partial(own_kernel, local_heads),
        out_shape=(jax.ShapeDtypeStruct((slot_count, model_width), jnp.float32), stats, stats),
        in_specs=[smem_spec()] + [vmem_spec()] * 3,
        out_specs=(vmem_spec(), vmem_spec(), vmem_spec()),
        compiler_params=pltpu.CompilerParams(vmem_limit_bytes=16 * mebibyte),
        cost_estimate=pl.CostEstimate(
            flops=40 * slot_count * slot_count * model_width,
            bytes_accessed=8 * slot_count * model_width,
            transcendentals=slot_count * model_width,
        ),
        name="attend_suffix",
    )(lengths, queries, keys, values)


def merge_kernel(
    lengths_ref,
    groups_ref,
    arrived_ref,
    own_mixed_ref,
    own_top_ref,
    own_sum_ref,
    input_ref,
    gain_ref,
    shift_ref,
    first_ref,
    second_ref,
    hidden_ref,
    far_ref,
    stat_ref,
):
    _, column_count, chunk_rows, part_width = arrived_ref.shape
    slot_count, model_width = input_ref.shape
    capacity = chunk_rows - STAT_ROWS
    local_heads = part_width // HD
    head_count = model_width // HD
    start = 0
    for request in range(lengths_ref.shape[1]):
        group = groups_ref[0, request]
        pieces = []
        for column in range(column_count):
            block = arrived_ref[group, column].astype(jnp.float32)
            for head in range(local_heads):
                far_ref[column * local_heads + head, pl.ds(start, capacity), :] = block[
                    :capacity, head * HD : (head + 1) * HD
                ]
            pieces.append(block[capacity:, :LANES])
        if column_count * STAT_ROWS < LANES:
            pieces.append(jnp.zeros((LANES - column_count * STAT_ROWS, LANES), jnp.float32))
        turned = jnp.transpose(jnp.concatenate(pieces, axis=0))
        stat_ref[pl.ds(start, capacity), :] = turned[:capacity]
        start = start + lengths_ref[0, request]
    far_top = stat_ref[:slot_count, :]
    far_sum = pltpu.roll(far_top, LANES - local_heads, 1)
    own_top = own_top_ref[...]
    joint_top = jnp.maximum(far_top, own_top)
    far_weight = jnp.exp(far_top - joint_top) * far_sum
    own_weight = jnp.exp(own_top - joint_top)
    bottom = far_weight + own_weight * own_sum_ref[...]
    far_weight = far_weight / bottom
    own_weight = own_weight / bottom
    total = jnp.zeros((slot_count, LANES), jnp.float32)
    for head in range(head_count):
        columns = slice(head * HD, (head + 1) * HD)
        at = stat_lane(head, local_heads)
        summed = (
            input_ref[:, columns].astype(jnp.float32)
            + far_weight[:, at : at + 1] * far_ref[head, :slot_count, :]
            + own_weight[:, at : at + 1] * own_mixed_ref[:, columns]
        )
        far_ref[head, :slot_count, :] = summed
        total = total + summed
    row_mean = jnp.sum(total, axis=1, keepdims=True) * (1.0 / model_width)
    total = jnp.zeros((slot_count, LANES), jnp.float32)
    for head in range(head_count):
        centred = far_ref[head, :slot_count, :] - row_mean
        total = total + centred * centred
    spread = jnp.sum(total, axis=1, keepdims=True) * (1.0 / model_width)
    factor = lax.rsqrt(spread + norm_eps)
    for head in range(head_count):
        columns = slice(head * HD, (head + 1) * HD)
        centred = far_ref[head, :slot_count, :] - row_mean
        hidden = (centred * factor * gain_ref[:, columns] + shift_ref[:, columns]).astype(
            jnp.bfloat16
        )
        first_ref[:, columns] = hidden[: slot_count // 2]
        second_ref[:, columns] = hidden[slot_count // 2 :]
        hidden_ref[:, columns] = hidden


def merge_parts(lengths, groups, arrived, own_mixed, own_top, own_sum, layer_input, gain, shift):
    slot_count, model_width = layer_input.shape
    capacity = arrived.shape[2] - STAT_ROWS
    half = jax.ShapeDtypeStruct((slot_count // 2, model_width), jnp.bfloat16)
    return pl.pallas_call(
        merge_kernel,
        out_shape=(half, half, jax.ShapeDtypeStruct(layer_input.shape, jnp.bfloat16)),
        in_specs=[smem_spec(), smem_spec()] + [vmem_spec()] * 7,
        out_specs=(vmem_spec(), vmem_spec(), vmem_spec()),
        scratch_shapes=[
            pltpu.VMEM((model_width // HD, slot_count + capacity, HD), jnp.float32),
            pltpu.VMEM((slot_count + capacity, LANES), jnp.float32),
        ],
        compiler_params=pltpu.CompilerParams(vmem_limit_bytes=16 * mebibyte),
        name="merge_parts",
    )(
        lengths,
        groups,
        arrived,
        own_mixed,
        own_top,
        own_sum,
        layer_input,
        gain.reshape(1, model_width),
        shift.reshape(1, model_width),
    )


def swap(value, mask):
    total = lax.axis_size("grp") * lax.axis_size("dev")
    pairs = [(here, here ^ mask) for here in range(total)]
    return jax.tree.map(lambda leaf: lax.ppermute(leaf, ("grp", "dev"), pairs), value)


def complete(held, masks):
    held = dict(held)
    for mask in masks:
        for at in list(held):
            if mask ^ at not in held:
                held[mask ^ at] = swap(held[at], mask)
    return held


def tie(values, after):
    return lax.optimization_barrier((values, after))[0]


def mlp_kernel(pieces, up_plan, down_plan, *refs):
    parts = len(up_plan)
    row_refs, refs = refs[:pieces], refs[pieces:]
    up_total, down_total = sum(map(len, up_plan)), sum(map(len, down_plan))
    ups, refs = list(refs[:up_total]), refs[up_total:]
    downs, refs = list(refs[:down_total]), refs[down_total:]
    out_refs, (up_ref, down_ref, sems) = refs[:pieces], refs[pieces:]
    model_width = row_refs[0].shape[1]
    copies = []
    for part, heights in enumerate(up_plan):
        begin, held = 0, []
        for piece, height in enumerate(heights):
            target = up_ref.at[part, pl.ds(begin, height)]
            held.append(pltpu.make_async_copy(ups.pop(0), target, sems.at[part, 0, piece]))
            begin += height
        copies.append(held)
    begin = 0
    for part, heights in enumerate(down_plan):
        held = []
        for piece, height in enumerate(heights):
            target = down_ref.at[pl.ds(begin, height)]
            held.append(pltpu.make_async_copy(downs.pop(0), target, sems.at[part, 1, piece]))
            begin += height
        copies.append(held)
    for held in copies:
        for copy in held:
            copy.start()
    rows = jnp.concatenate([ref[...] for ref in row_refs], axis=0)
    activations = []
    for part in range(parts):
        for copy in copies[part]:
            copy.wait()
        product = jnp.dot(
            rows, up_ref[part, :model_width, :], preferred_element_type=jnp.float32
        )
        offset = up_ref[part, model_width:, :].astype(jnp.float32)[0:1]
        activations.append(jax.nn.gelu(product + offset, approximate=True).astype(jnp.bfloat16))
    for held in copies[parts:]:
        for copy in held:
            copy.wait()
    total = jnp.dot(
        jnp.concatenate(activations, axis=1), down_ref[...], preferred_element_type=jnp.float32
    ).astype(jnp.bfloat16)
    begin = 0
    for out_ref in out_refs:
        height = out_ref.shape[0]
        out_ref[...] = total[begin : begin + height]
        begin += height


def feed_forward(rows, ups, downs):
    pieces, parts = len(rows), len(ups)
    row_total, model_width = sum(piece.shape[0] for piece in rows), rows[0].shape[1]
    up_plan = [[piece.shape[0] for piece in block] for block in ups]
    down_plan = [[piece.shape[0] for piece in block] for block in downs]
    up_rows, down_rows = sum(up_plan[0]), sum(down_plan[0])
    units = ups[0][0].shape[1]
    flat = [piece for block in ups + downs for piece in block]
    most = max(map(len, up_plan + down_plan))
    return pl.pallas_call(
        functools.partial(mlp_kernel, pieces, up_plan, down_plan),
        out_shape=tuple(jax.ShapeDtypeStruct(piece.shape, jnp.bfloat16) for piece in rows),
        in_specs=[vmem_spec()] * pieces + [hbm_spec()] * len(flat),
        out_specs=tuple(vmem_spec() for _ in rows),
        scratch_shapes=[
            pltpu.VMEM((parts, up_rows, units), jnp.bfloat16),
            pltpu.VMEM((parts * down_rows, model_width), jnp.bfloat16),
            pltpu.SemaphoreType.DMA((parts, 2, most)),
        ],
        compiler_params=pltpu.CompilerParams(vmem_limit_bytes=58 * mebibyte),
        cost_estimate=pl.CostEstimate(
            flops=4 * row_total * model_width * parts * units,
            bytes_accessed=4 * parts * model_width * units,
            transcendentals=row_total * parts * units,
        ),
        name="feed_forward",
    )(*rows, *flat)


def add_kernel(here_ref, there_ref, out_ref):
    out_ref[...] = (
        here_ref[...].astype(jnp.float32) + there_ref[...].astype(jnp.float32)
    ).astype(jnp.bfloat16)


def add_rows(here, there):
    return pl.pallas_call(
        add_kernel,
        out_shape=jax.ShapeDtypeStruct(here.shape, jnp.bfloat16),
        in_specs=[vmem_spec(), vmem_spec()],
        out_specs=vmem_spec(),
        name="add_rows",
    )(here, there)


def finish_kernel(
    hidden_ref, own_ref, near_ref, far_a_ref, far_b_ref, bias_ref, gain_ref, shift_ref, out_ref
):
    height = far_a_ref.shape[0]
    for begin, far_ref in ((0, far_a_ref), (height, far_b_ref)):
        rows = slice(begin, begin + height)
        summed = hidden_ref[rows, :].astype(jnp.float32) + (
            own_ref[rows, :].astype(jnp.float32)
            + near_ref[rows, :].astype(jnp.float32)
            + far_ref[...].astype(jnp.float32)
        )
        out_ref[rows, :] = layer_norm(
            summed + bias_ref[...], gain_ref[...], shift_ref[...]
        ).astype(jnp.bfloat16)


def finish_rows(hidden, own, near, far_a, far_b, bias, gain, shift):
    model_width = hidden.shape[1]
    return pl.pallas_call(
        finish_kernel,
        out_shape=jax.ShapeDtypeStruct(hidden.shape, jnp.bfloat16),
        in_specs=[vmem_spec()] * 8,
        out_specs=vmem_spec(),
        compiler_params=pltpu.CompilerParams(vmem_limit_bytes=16 * mebibyte),
        name="finish_rows",
    )(
        hidden,
        own,
        near,
        far_a,
        far_b,
        bias.reshape(1, model_width),
        gain.reshape(1, model_width),
        shift.reshape(1, model_width),
    )


def on_device(
    suffix_queries,
    suffix_keys,
    suffix_values,
    layer_input,
    suffix_lengths,
    request_group,
    prefix_keys,
    prefix_values,
    up_weight,
    up_bias,
    down_weight,
    down_bias,
    attn_gain,
    attn_shift,
    out_gain,
    out_shift,
):
    slot_count, model_width = suffix_queries.shape
    group_count = lax.axis_size("grp")
    column_count = lax.axis_size("dev")
    part_width = model_width // column_count
    local_heads = part_width // HD
    capacity = 2 * slot_count // group_count
    sources = group_count * column_count

    near_mask = group_count // 2 * column_count
    far_mask = column_count // 2
    column_masks = [1 << bit for bit in range(far_mask.bit_length() - 1)]
    group_masks = [column_count << bit for bit in range((group_count // 2).bit_length() - 1)]

    low_mask, high_masks = column_masks[0], column_masks[1:]
    core_mask = group_masks[0]

    outgoing = pack_queries(
        suffix_lengths, request_group, suffix_queries, group_count, column_count, capacity
    )
    bias_rows = jnp.broadcast_to(up_bias[None, :], (16, up_bias.shape[0]))
    up_block = jnp.concatenate([up_weight, bias_rows], axis=0)
    up_cut, down_cut = up_weight.shape[0] // 2, down_weight.shape[0] // 2
    up_pieces = (up_block[:up_cut], up_block[up_cut:])
    down_pieces = (down_weight[:down_cut], down_weight[down_cut:])
    ups, downs = {0: (up_block,)}, {0: (down_weight,)}
    high_mask = high_masks[0]

    arrived = lax.all_to_all(
        outgoing.reshape(sources, capacity + STAT_ROWS, part_width),
        ("grp", "dev"),
        split_axis=0,
        concat_axis=0,
        tiled=True,
    )
    ups[low_mask] = swap(ups[0], low_mask)
    up_first = swap(up_pieces[0], high_mask)
    ups[core_mask] = swap(ups[0], core_mask)
    downs[core_mask] = swap(downs[0], core_mask)
    turned_keys = prefix_keys[0].T
    value_heads = prefix_values[0].reshape(-1, local_heads, HD).transpose(1, 0, 2)
    wide_values = jnp.concatenate([value_heads, jnp.ones_like(value_heads)], axis=2)
    own = attend_suffix(
        suffix_lengths, suffix_queries, suffix_keys, suffix_values, local_heads
    )
    arrived, ups, up_first, up_pieces, downs, down_pieces, turned_keys, wide_values, own = (
        lax.optimization_barrier(
            (arrived, ups, up_first, up_pieces, downs, down_pieces, turned_keys, wide_values, own)
        )
    )

    counts = arrived[:, capacity, 0].astype(jnp.int32)
    answer_part = attend_prefix(counts, arrived, turned_keys, wide_values)
    downs[low_mask] = swap(downs[0], low_mask)
    up_second = swap(up_pieces[1], high_mask)
    down_first = swap(down_pieces[0], high_mask)
    ups[core_mask ^ low_mask] = swap(ups[low_mask], core_mask)
    answer_part, ups, up_first, up_second, downs, down_first, down_pieces = (
        lax.optimization_barrier(
            (answer_part, ups, up_first, up_second, downs, down_first, down_pieces)
        )
    )

    answer = lax.all_to_all(
        answer_part, ("grp", "dev"), split_axis=0, concat_axis=0, tiled=True
    ).reshape(group_count, column_count, capacity + STAT_ROWS, part_width)
    ups[high_mask] = (jnp.concatenate([up_first, up_second], axis=0),)
    ups[core_mask ^ high_mask] = swap(ups[high_mask], core_mask)
    downs[core_mask ^ low_mask] = swap(downs[low_mask], core_mask)
    down_second = swap(down_pieces[1], high_mask)
    downs[high_mask] = (jnp.concatenate([down_first, down_second], axis=0),)
    downs[core_mask ^ high_mask] = swap(downs[high_mask], core_mask)
    ups[low_mask ^ high_mask] = swap(ups[high_mask], low_mask)
    answer, ups, downs = lax.optimization_barrier((answer, ups, downs))

    hidden_a, hidden_b, hidden = merge_parts(
        suffix_lengths, request_group, answer, *own, layer_input, attn_gain, attn_shift
    )

    (hidden_a, hidden_b, hidden), ups, downs = lax.optimization_barrier(
        ((hidden_a, hidden_b, hidden), ups, downs)
    )
    far_a = swap(hidden_a, far_mask)
    near = swap(hidden, near_mask)
    downs[low_mask ^ high_mask] = swap(downs[high_mask], low_mask)
    ups = complete(ups, group_masks + column_masks)
    far_b = swap(tie(hidden_b, far_a), far_mask)
    cross_a = swap(far_a, near_mask)
    far_b, cross_a, near, ups, downs = lax.optimization_barrier(
        (far_b, cross_a, near, ups, downs)
    )
    cross_b = swap(far_b, near_mask)
    downs = complete(downs, group_masks + column_masks)
    order = sorted(ups)
    ups = [ups[mask] for mask in order]
    downs = [downs[mask] for mask in order]
    far_part_a, cross_part_a = feed_forward([far_a, cross_a], ups, downs)
    cross_b, far_part_a, cross_part_a = lax.optimization_barrier(
        (cross_b, far_part_a, cross_part_a)
    )
    cross_sum_a = swap(cross_part_a, near_mask)
    far_part_b, cross_part_b = feed_forward([far_b, cross_b], ups, downs)
    cross_sum_a, far_part_b, cross_part_b = lax.optimization_barrier(
        (cross_sum_a, far_part_b, cross_part_b)
    )
    cross_sum_b = swap(cross_part_b, near_mask)
    joined_a = add_rows(far_part_a, cross_sum_a)
    far_sum_a = swap(joined_a, far_mask)
    near, hidden = tie((near, hidden), joined_a)
    near_part, own_part = feed_forward([near, hidden], ups, downs)
    near_sum = swap(near_part, near_mask)
    cross_sum_b, near_part = lax.optimization_barrier((cross_sum_b, near_part))
    far_sum_b = swap(add_rows(far_part_b, cross_sum_b), far_mask)
    return finish_rows(
        hidden, own_part, near_sum, far_sum_a, far_sum_b, down_bias, out_gain, out_shift
    )


def solution(mesh):
    placed = (
        P(("grp", "dev"), None),
        P(("grp", "dev"), None),
        P(("grp", "dev"), None),
        P(("grp", "dev"), None),
        P(("grp", "dev"), None),
        P(("grp", "dev"), None),
        P("grp", None, "dev"),
        P("grp", None, "dev"),
        P(None, ("grp", "dev")),
        P(("grp", "dev")),
        P(("grp", "dev"), None),
        P(),
        P(),
        P(),
        P(),
        P(),
    )
    return jax.shard_map(
        on_device, mesh=mesh, in_specs=placed, out_specs=P(("grp", "dev"), None), check_vma=False
    )
```

```python
import functools
import math

import jax
import jax.numpy as jnp
from jax import lax
from jax.experimental import pallas as pl
from jax.experimental.pallas import tpu as pltpu
from jax.sharding import PartitionSpec as P

HD = 128
LANES = 128
STAT_ROWS = 8
ROW_BLOCK = 256
KEY_CHUNK = 1024

norm_eps = 1e-12
score_scale = HD ** (-0.5)
log2_e = math.log2(math.e)
mebibyte = 1024 * 1024


def layer_norm(summed, norm_gain, norm_shift):
    row_mean = jnp.mean(summed, axis=-1, keepdims=True)
    centred = summed - row_mean
    spread = jnp.mean(centred * centred, axis=-1, keepdims=True)
    return centred * lax.rsqrt(spread + norm_eps) * norm_gain + norm_shift


def vmem_spec():
    return pl.BlockSpec(memory_space=pltpu.VMEM)


def hbm_spec():
    return pl.BlockSpec(memory_space=pltpu.HBM)


def smem_spec():
    return pl.BlockSpec(memory_space=pltpu.SMEM)


def pack_kernel(lengths_ref, groups_ref, query_ref, out_ref, wide_ref):
    request_total = lengths_ref.shape[1]
    _, column_count, chunk_rows, part_width = out_ref.shape
    capacity = chunk_rows - STAT_ROWS
    slot_count = query_ref.shape[0]
    tiles = part_width // LANES
    for tile in range(wide_ref.shape[0]):
        wide_ref[tile, 0:slot_count, :] = query_ref[
            :, tile * LANES : (tile + 1) * LANES
        ].astype(jnp.float32)
        wide_ref[tile, slot_count : slot_count + capacity, :] = jnp.zeros(
            (capacity, LANES), jnp.float32
        )
    start = 0
    for request in range(request_total):
        group = groups_ref[0, request]
        count = jnp.full((STAT_ROWS, LANES), lengths_ref[0, request], jnp.int32).astype(jnp.float32)
        for column in range(column_count):
            for tile in range(tiles):
                rows = wide_ref[column * tiles + tile, pl.ds(start, capacity), :]
                rows = jnp.concatenate([rows, count], axis=0)
                out_ref[group, column, :, tile * LANES : (tile + 1) * LANES] = rows.astype(
                    jnp.bfloat16
                )
        start = start + lengths_ref[0, request]


def pack_queries(lengths, groups, queries, group_count, column_count, capacity):
    slot_count, model_width = queries.shape
    part_width = model_width // column_count
    return pl.pallas_call(
        pack_kernel,
        out_shape=jax.ShapeDtypeStruct(
            (group_count, column_count, capacity + STAT_ROWS, part_width), jnp.bfloat16
        ),
        in_specs=[smem_spec(), smem_spec(), vmem_spec()],
        out_specs=vmem_spec(),
        scratch_shapes=[
            pltpu.VMEM((model_width // LANES, slot_count + capacity, LANES), jnp.float32)
        ],
        compiler_params=pltpu.CompilerParams(vmem_limit_bytes=16 * mebibyte),
        name="pack_queries",
    )(lengths, groups, queries)


def far_kernel(
    counts_ref,
    arrived_ref,
    keys_hbm,
    values_hbm,
    out_ref,
    query_ref,
    answer_ref,
    stat_ref,
    score_ref,
    top_ref,
    keys_ref,
    values_ref,
    sems,
):
    copies = [
        pltpu.make_async_copy(keys_hbm, keys_ref, sems.at[0]),
        pltpu.make_async_copy(values_hbm, values_ref, sems.at[1]),
    ]
    for copy in copies:
        copy.start()
    sources, chunk_rows, part_width = arrived_ref.shape
    capacity = chunk_rows - STAT_ROWS
    local_heads = part_width // HD
    key_total = keys_ref.shape[1]
    chunks = key_total // KEY_CHUNK

    def take(source, offset):
        for head in range(local_heads):
            rows = arrived_ref[source, :, head * HD : (head + 1) * HD].astype(jnp.float32)
            query_ref[head, pl.ds(offset, capacity), :] = rows[:capacity]
        return offset + counts_ref[source]

    total = lax.fori_loop(0, sources, take, jnp.int32(0))
    blocks = (total + ROW_BLOCK - 1) // ROW_BLOCK
    lane = lax.broadcasted_iota(jnp.int32, (ROW_BLOCK, LANES), 1)

    def block_rows(block):
        return pl.ds(pl.multiple_of(block * ROW_BLOCK, ROW_BLOCK), ROW_BLOCK)

    def load_queries(block, head):
        return query_ref[head, block_rows(block), :].astype(jnp.bfloat16)

    def score_chunk(rows, head, slot, chunk, part_top):
        columns = slice(chunk * KEY_CHUNK, (chunk + 1) * KEY_CHUNK)
        scores = jnp.dot(
            rows,
            keys_ref[head * HD : (head + 1) * HD, columns],
            preferred_element_type=jnp.float32,
        )
        score_ref[slot, :, columns] = scores
        for piece in range(KEY_CHUNK // LANES):
            part = scores[:, piece * LANES : (piece + 1) * LANES]
            part_top = part if part_top is None else jnp.maximum(part_top, part)
        return part_top

    def finish_top(part_top, slot):
        row_top = jnp.max(part_top, axis=1, keepdims=True) * score_scale
        row_top = row_top.astype(jnp.bfloat16).astype(jnp.float32)
        top_ref[slot] = jnp.broadcast_to(row_top, (ROW_BLOCK, LANES))

    def weigh_chunk(head, slot, chunk, shift):
        columns = slice(chunk * KEY_CHUNK, (chunk + 1) * KEY_CHUNK)
        weights = jnp.exp2(score_ref[slot, :, columns] * (score_scale * log2_e) - shift)
        return jnp.dot(
            weights.astype(jnp.bfloat16),
            values_ref[head, columns, :],
            preferred_element_type=jnp.float32,
        )

    def finish_answer(block, head, slot, mixed):
        rows = block_rows(block)
        row_sum = mixed[:, HD:]
        answer_ref[head, rows, :] = mixed[:, :HD] / row_sum
        top = top_ref[slot]
        if head == 0:
            stat_ref[rows, :] = jnp.where(lane == 0, top, row_sum)
        else:
            before = stat_ref[rows, :]
            with_top = jnp.where(lane == head, top, before)
            stat_ref[rows, :] = jnp.where(lane == local_heads + head, row_sum, with_top)

    def slot_of(block, head):
        return (block * local_heads + head) % 2 if local_heads % 2 else head % 2

    for copy in copies:
        copy.wait()
    first_rows = load_queries(0, 0)
    part_top = None
    for chunk in range(chunks):
        part_top = score_chunk(first_rows, 0, 0, chunk, part_top)
    finish_top(part_top, 0)

    def one_block(block, carry):
        for head in range(local_heads):
            slot = slot_of(block, head)
            if head + 1 < local_heads:
                next_block, next_head = block, head + 1
            else:
                next_block, next_head = jnp.minimum(block + 1, blocks - 1), 0
            next_slot = 1 - slot
            next_rows = load_queries(next_block, next_head)
            shift = top_ref[slot][:, 0:1] * log2_e
            part_top = None
            mixed = None
            for chunk in range(chunks):
                part_top = score_chunk(next_rows, next_head, next_slot, chunk, part_top)
                part = weigh_chunk(head, slot, chunk, shift)
                mixed = part if mixed is None else mixed + part
            finish_answer(block, head, slot, mixed)
            finish_top(part_top, next_slot)
        return carry

    lax.fori_loop(0, blocks, one_block, 0)

    def give(source, offset):
        rows = [answer_ref[head, pl.ds(offset, capacity), :] for head in range(local_heads)]
        turned = jnp.transpose(stat_ref[pl.ds(offset, LANES), :])[:STAT_ROWS, :]
        if part_width > LANES:
            turned = jnp.concatenate(
                [turned, jnp.zeros((STAT_ROWS, part_width - LANES), jnp.float32)], axis=1
            )
        rows = jnp.concatenate(rows, axis=1)
        out_ref[source] = jnp.concatenate([rows, turned], axis=0).astype(jnp.bfloat16)
        return offset + counts_ref[source]

    lax.fori_loop(0, sources, give, jnp.int32(0))


def attend_prefix(counts, arrived, turned_keys, wide_values):
    sources, chunk_rows, part_width = arrived.shape
    capacity = chunk_rows - STAT_ROWS
    local_heads = part_width // HD
    key_total = turned_keys.shape[1]
    row_total = -(-sources * capacity // ROW_BLOCK) * ROW_BLOCK + LANES
    return pl.pallas_call(
        far_kernel,
        out_shape=jax.ShapeDtypeStruct((sources, capacity + STAT_ROWS, part_width), jnp.bfloat16),
        in_specs=[smem_spec(), vmem_spec(), hbm_spec(), hbm_spec()],
        out_specs=vmem_spec(),
        scratch_shapes=[
            pltpu.VMEM((local_heads, row_total, HD), jnp.float32),
            pltpu.VMEM((local_heads, row_total, HD), jnp.float32),
            pltpu.VMEM((row_total, LANES), jnp.float32),
            pltpu.VMEM((2, ROW_BLOCK, key_total), jnp.float32),
            pltpu.VMEM((2, ROW_BLOCK, LANES), jnp.float32),
            pltpu.VMEM(turned_keys.shape, jnp.bfloat16),
            pltpu.VMEM(wide_values.shape, jnp.bfloat16),
            pltpu.SemaphoreType.DMA((2,)),
        ],
        compiler_params=pltpu.CompilerParams(vmem_limit_bytes=40 * mebibyte),
        cost_estimate=pl.CostEstimate(
            flops=4 * sources * capacity * key_total * part_width,
            bytes_accessed=8 * key_total * part_width,
            transcendentals=sources * capacity * key_total * local_heads,
        ),
        name="attend_prefix",
    )(counts, arrived, turned_keys, wide_values)


def stat_lane(head, local_heads):
    return (head // local_heads) * STAT_ROWS + head % local_heads


def own_kernel(local_heads, lengths_ref, query_ref, key_ref, value_ref, mixed_ref, top_ref, sum_ref):
    slot_count, model_width = query_ref.shape
    head_count = model_width // HD
    row = lax.broadcasted_iota(jnp.int32, (slot_count, slot_count), 0)
    column = lax.broadcasted_iota(jnp.int32, (slot_count, slot_count), 1)
    row_segment = jnp.zeros((slot_count, slot_count), jnp.int32)
    column_segment = jnp.zeros((slot_count, slot_count), jnp.int32)
    start = 0
    for request in range(lengths_ref.shape[1]):
        start = start + lengths_ref[0, request]
        row_segment = row_segment + (row >= start).astype(jnp.int32)
        column_segment = column_segment + (column >= start).astype(jnp.int32)
    visible = (row_segment == column_segment) & (column <= row)
    lane = lax.broadcasted_iota(jnp.int32, (slot_count, LANES), 1)
    tops = jnp.zeros((slot_count, LANES), jnp.float32)
    sums = jnp.ones((slot_count, LANES), jnp.float32)
    for head in range(head_count):
        columns = slice(head * HD, (head + 1) * HD)
        scores = (
            lax.dot_general(
                query_ref[:, columns],
                key_ref[:, columns],
                (((1,), (1,)), ((), ())),
                preferred_element_type=jnp.float32,
            )
            * score_scale
        )
        top = jnp.max(jnp.where(visible, scores, -jnp.inf), axis=1, keepdims=True)
        weights = jnp.where(visible, jnp.exp(scores - top), 0.0)
        mixed_ref[:, columns] = jnp.dot(
            weights.astype(jnp.bfloat16),
            value_ref[:, columns],
            preferred_element_type=jnp.float32,
        )
        at = stat_lane(head, local_heads)
        tops = jnp.where(lane == at, top, tops)
        sums = jnp.where(lane == at, jnp.sum(weights, axis=1, keepdims=True), sums)
    top_ref[...] = tops
    sum_ref[...] = sums


def attend_suffix(lengths, queries, keys, values, local_heads):
    slot_count, model_width = queries.shape
    stats = jax.ShapeDtypeStruct((slot_count, LANES), jnp.float32)
    return pl.pallas_call(
        functools.partial(own_kernel, local_heads),
        out_shape=(jax.ShapeDtypeStruct((slot_count, model_width), jnp.float32), stats, stats),
        in_specs=[smem_spec()] + [vmem_spec()] * 3,
        out_specs=(vmem_spec(), vmem_spec(), vmem_spec()),
        compiler_params=pltpu.CompilerParams(vmem_limit_bytes=16 * mebibyte),
        cost_estimate=pl.CostEstimate(
            flops=40 * slot_count * slot_count * model_width,
            bytes_accessed=8 * slot_count * model_width,
            transcendentals=slot_count * model_width,
        ),
        name="attend_suffix",
    )(lengths, queries, keys, values)


def merge_kernel(
    lengths_ref,
    groups_ref,
    arrived_ref,
    own_mixed_ref,
    own_top_ref,
    own_sum_ref,
    input_ref,
    gain_ref,
    shift_ref,
    first_ref,
    second_ref,
    hidden_ref,
    far_ref,
    stat_ref,
):
    _, column_count, chunk_rows, part_width = arrived_ref.shape
    slot_count, model_width = input_ref.shape
    capacity = chunk_rows - STAT_ROWS
    local_heads = part_width // HD
    head_count = model_width // HD
    start = 0
    for request in range(lengths_ref.shape[1]):
        group = groups_ref[0, request]
        pieces = []
        for column in range(column_count):
            block = arrived_ref[group, column].astype(jnp.float32)
            for head in range(local_heads):
                far_ref[column * local_heads + head, pl.ds(start, capacity), :] = block[
                    :capacity, head * HD : (head + 1) * HD
                ]
            pieces.append(block[capacity:, :LANES])
        if column_count * STAT_ROWS < LANES:
            pieces.append(jnp.zeros((LANES - column_count * STAT_ROWS, LANES), jnp.float32))
        turned = jnp.transpose(jnp.concatenate(pieces, axis=0))
        stat_ref[pl.ds(start, capacity), :] = turned[:capacity]
        start = start + lengths_ref[0, request]
    far_top = stat_ref[:slot_count, :]
    far_sum = pltpu.roll(far_top, LANES - local_heads, 1)
    own_top = own_top_ref[...]
    joint_top = jnp.maximum(far_top, own_top)
    far_weight = jnp.exp(far_top - joint_top) * far_sum
    own_weight = jnp.exp(own_top - joint_top)
    bottom = far_weight + own_weight * own_sum_ref[...]
    far_weight = far_weight / bottom
    own_weight = own_weight / bottom
    total = jnp.zeros((slot_count, LANES), jnp.float32)
    for head in range(head_count):
        columns = slice(head * HD, (head + 1) * HD)
        at = stat_lane(head, local_heads)
        summed = (
            input_ref[:, columns].astype(jnp.float32)
            + far_weight[:, at : at + 1] * far_ref[head, :slot_count, :]
            + own_weight[:, at : at + 1] * own_mixed_ref[:, columns]
        )
        far_ref[head, :slot_count, :] = summed
        total = total + summed
    row_mean = jnp.sum(total, axis=1, keepdims=True) * (1.0 / model_width)
    total = jnp.zeros((slot_count, LANES), jnp.float32)
    for head in range(head_count):
        centred = far_ref[head, :slot_count, :] - row_mean
        total = total + centred * centred
    spread = jnp.sum(total, axis=1, keepdims=True) * (1.0 / model_width)
    factor = lax.rsqrt(spread + norm_eps)
    for head in range(head_count):
        columns = slice(head * HD, (head + 1) * HD)
        centred = far_ref[head, :slot_count, :] - row_mean
        hidden = (centred * factor * gain_ref[:, columns] + shift_ref[:, columns]).astype(
            jnp.bfloat16
        )
        first_ref[:, columns] = hidden[: slot_count // 2]
        second_ref[:, columns] = hidden[slot_count // 2 :]
        hidden_ref[:, columns] = hidden


def merge_parts(lengths, groups, arrived, own_mixed, own_top, own_sum, layer_input, gain, shift):
    slot_count, model_width = layer_input.shape
    capacity = arrived.shape[2] - STAT_ROWS
    half = jax.ShapeDtypeStruct((slot_count // 2, model_width), jnp.bfloat16)
    return pl.pallas_call(
        merge_kernel,
        out_shape=(half, half, jax.ShapeDtypeStruct(layer_input.shape, jnp.bfloat16)),
        in_specs=[smem_spec(), smem_spec()] + [vmem_spec()] * 7,
        out_specs=(vmem_spec(), vmem_spec(), vmem_spec()),
        scratch_shapes=[
            pltpu.VMEM((model_width // HD, slot_count + capacity, HD), jnp.float32),
            pltpu.VMEM((slot_count + capacity, LANES), jnp.float32),
        ],
        compiler_params=pltpu.CompilerParams(vmem_limit_bytes=16 * mebibyte),
        name="merge_parts",
    )(
        lengths,
        groups,
        arrived,
        own_mixed,
        own_top,
        own_sum,
        layer_input,
        gain.reshape(1, model_width),
        shift.reshape(1, model_width),
    )


def swap(value, mask):
    total = lax.axis_size("grp") * lax.axis_size("dev")
    pairs = [(here, here ^ mask) for here in range(total)]
    return jax.tree.map(lambda leaf: lax.ppermute(leaf, ("grp", "dev"), pairs), value)


def complete(held, masks):
    held = dict(held)
    for mask in masks:
        for at in list(held):
            if mask ^ at not in held:
                held[mask ^ at] = swap(held[at], mask)
    return held


def tie(values, after):
    return lax.optimization_barrier((values, after))[0]


def mlp_kernel(pieces, parts, *refs):
    row_refs, refs = refs[:pieces], refs[pieces:]
    ups, downs, out_refs = refs[:parts], refs[parts : 2 * parts], refs[2 * parts :]
    model_width = row_refs[0].shape[1]
    rows = jnp.concatenate([ref[...] for ref in row_refs], axis=0)
    total = None
    for up_ref, down_ref in zip(ups, downs):
        product = jnp.dot(
            rows, up_ref[:model_width, :], preferred_element_type=jnp.float32
        )
        offset = up_ref[model_width:, :].astype(jnp.float32)[0:1]
        activation = jax.nn.gelu(product + offset, approximate=True).astype(jnp.bfloat16)
        term = jnp.dot(activation, down_ref[...], preferred_element_type=jnp.float32)
        total = term if total is None else total + term
    total = total.astype(jnp.bfloat16)
    begin = 0
    for out_ref in out_refs:
        height = out_ref.shape[0]
        out_ref[...] = total[begin : begin + height]
        begin += height


def feed_forward(rows, ups, downs):
    pieces, parts = len(rows), len(ups)
    row_total, model_width = sum(piece.shape[0] for piece in rows), rows[0].shape[1]
    units = ups[0].shape[1]
    return pl.pallas_call(
        functools.partial(mlp_kernel, pieces, parts),
        out_shape=tuple(jax.ShapeDtypeStruct(piece.shape, jnp.bfloat16) for piece in rows),
        in_specs=[vmem_spec()] * (pieces + 2 * parts),
        out_specs=tuple(vmem_spec() for _ in rows),
        compiler_params=pltpu.CompilerParams(vmem_limit_bytes=34 * mebibyte),
        cost_estimate=pl.CostEstimate(
            flops=4 * row_total * model_width * parts * units,
            bytes_accessed=4 * parts * model_width * units,
            transcendentals=row_total * parts * units,
        ),
        name="feed_forward",
    )(*rows, *ups, *downs)


def add_kernel(here_ref, there_ref, out_ref):
    out_ref[...] = (
        here_ref[...].astype(jnp.float32) + there_ref[...].astype(jnp.float32)
    ).astype(jnp.bfloat16)


def add_rows(here, there):
    return pl.pallas_call(
        add_kernel,
        out_shape=jax.ShapeDtypeStruct(here.shape, jnp.bfloat16),
        in_specs=[vmem_spec(), vmem_spec()],
        out_specs=vmem_spec(),
        name="add_rows",
    )(here, there)


def finish_kernel(
    hidden_ref, own_ref, near_ref, far_a_ref, far_b_ref, bias_ref, gain_ref, shift_ref, out_ref
):
    height = far_a_ref.shape[0]
    for begin, far_ref in ((0, far_a_ref), (height, far_b_ref)):
        rows = slice(begin, begin + height)
        summed = hidden_ref[rows, :].astype(jnp.float32) + (
            own_ref[rows, :].astype(jnp.float32)
            + near_ref[rows, :].astype(jnp.float32)
            + far_ref[...].astype(jnp.float32)
        )
        out_ref[rows, :] = layer_norm(
            summed + bias_ref[...], gain_ref[...], shift_ref[...]
        ).astype(jnp.bfloat16)


def finish_rows(hidden, own, near, far_a, far_b, bias, gain, shift):
    model_width = hidden.shape[1]
    return pl.pallas_call(
        finish_kernel,
        out_shape=jax.ShapeDtypeStruct(hidden.shape, jnp.bfloat16),
        in_specs=[vmem_spec()] * 8,
        out_specs=vmem_spec(),
        compiler_params=pltpu.CompilerParams(vmem_limit_bytes=16 * mebibyte),
        name="finish_rows",
    )(
        hidden,
        own,
        near,
        far_a,
        far_b,
        bias.reshape(1, model_width),
        gain.reshape(1, model_width),
        shift.reshape(1, model_width),
    )


def on_device(
    suffix_queries,
    suffix_keys,
    suffix_values,
    layer_input,
    suffix_lengths,
    request_group,
    prefix_keys,
    prefix_values,
    up_weight,
    up_bias,
    down_weight,
    down_bias,
    attn_gain,
    attn_shift,
    out_gain,
    out_shift,
):
    slot_count, model_width = suffix_queries.shape
    group_count = lax.axis_size("grp")
    column_count = lax.axis_size("dev")
    part_width = model_width // column_count
    local_heads = part_width // HD
    capacity = 2 * slot_count // group_count
    sources = group_count * column_count

    near_mask = group_count // 2 * column_count
    far_mask = column_count // 2
    column_masks = [1 << bit for bit in range(far_mask.bit_length() - 1)]
    group_masks = [column_count << bit for bit in range((group_count // 2).bit_length() - 1)]

    low_mask, high_masks = column_masks[0], column_masks[1:]
    core_mask = group_masks[0]

    outgoing = pack_queries(
        suffix_lengths, request_group, suffix_queries, group_count, column_count, capacity
    )
    bias_rows = jnp.broadcast_to(up_bias[None, :], (16, up_bias.shape[0]))
    up_block = jnp.concatenate([up_weight, bias_rows], axis=0)
    up_cut, down_cut = up_weight.shape[0] // 2, down_weight.shape[0] // 2
    up_pieces = (up_block[:up_cut], up_block[up_cut:])
    down_pieces = (down_weight[:down_cut], down_weight[down_cut:])
    ups, downs = {0: (up_block,)}, {0: (down_weight,)}
    high_mask = high_masks[0]

    arrived = lax.all_to_all(
        outgoing.reshape(sources, capacity + STAT_ROWS, part_width),
        ("grp", "dev"),
        split_axis=0,
        concat_axis=0,
        tiled=True,
    )
    ups[low_mask] = swap(ups[0], low_mask)
    up_first = swap(up_pieces[0], high_mask)
    ups[core_mask] = swap(ups[0], core_mask)
    downs[core_mask] = swap(downs[0], core_mask)
    turned_keys = prefix_keys[0].T
    value_heads = prefix_values[0].reshape(-1, local_heads, HD).transpose(1, 0, 2)
    wide_values = jnp.concatenate([value_heads, jnp.ones_like(value_heads)], axis=2)
    own = attend_suffix(
        suffix_lengths, suffix_queries, suffix_keys, suffix_values, local_heads
    )
    arrived, ups, up_first, up_pieces, downs, down_pieces, turned_keys, wide_values, own = (
        lax.optimization_barrier(
            (arrived, ups, up_first, up_pieces, downs, down_pieces, turned_keys, wide_values, own)
        )
    )

    counts = arrived[:, capacity, 0].astype(jnp.int32)
    answer_part = attend_prefix(counts, arrived, turned_keys, wide_values)
    downs[low_mask] = swap(downs[0], low_mask)
    up_second = swap(up_pieces[1], high_mask)
    down_first = swap(down_pieces[0], high_mask)
    ups[core_mask ^ low_mask] = swap(ups[low_mask], core_mask)
    answer_part, ups, up_first, up_second, downs, down_first, down_pieces = (
        lax.optimization_barrier(
            (answer_part, ups, up_first, up_second, downs, down_first, down_pieces)
        )
    )

    answer = lax.all_to_all(
        answer_part, ("grp", "dev"), split_axis=0, concat_axis=0, tiled=True
    ).reshape(group_count, column_count, capacity + STAT_ROWS, part_width)
    ups[high_mask] = (jnp.concatenate([up_first, up_second], axis=0),)
    ups[core_mask ^ high_mask] = swap(ups[high_mask], core_mask)
    downs[core_mask ^ low_mask] = swap(downs[low_mask], core_mask)
    down_second = swap(down_pieces[1], high_mask)
    downs[high_mask] = (jnp.concatenate([down_first, down_second], axis=0),)
    downs[core_mask ^ high_mask] = swap(downs[high_mask], core_mask)
    ups[low_mask ^ high_mask] = swap(ups[high_mask], low_mask)
    answer, ups, downs = lax.optimization_barrier((answer, ups, downs))

    hidden_a, hidden_b, hidden = merge_parts(
        suffix_lengths, request_group, answer, *own, layer_input, attn_gain, attn_shift
    )

    (hidden_a, hidden_b, hidden), ups, downs = lax.optimization_barrier(
        ((hidden_a, hidden_b, hidden), ups, downs)
    )
    far_a = swap(hidden_a, far_mask)
    near = swap(hidden, near_mask)
    downs[low_mask ^ high_mask] = swap(downs[high_mask], low_mask)
    ups = complete(ups, group_masks + column_masks)
    far_b = swap(tie(hidden_b, far_a), far_mask)
    cross_a = swap(far_a, near_mask)
    far_b, cross_a, near, ups, downs = lax.optimization_barrier(
        (far_b, cross_a, near, ups, downs)
    )
    cross_b = swap(far_b, near_mask)
    downs = complete(downs, group_masks + column_masks)
    order = sorted(ups)
    ups = [ups[mask][0] for mask in order]
    downs = [downs[mask][0] for mask in order]
    far_part_a, cross_part_a = feed_forward([far_a, cross_a], ups, downs)
    cross_b, far_part_a, cross_part_a = lax.optimization_barrier(
        (cross_b, far_part_a, cross_part_a)
    )
    cross_sum_a = swap(cross_part_a, near_mask)
    far_part_b, cross_part_b = feed_forward([far_b, cross_b], ups, downs)
    cross_sum_a, far_part_b, cross_part_b = lax.optimization_barrier(
        (cross_sum_a, far_part_b, cross_part_b)
    )
    cross_sum_b = swap(cross_part_b, near_mask)
    joined_a = add_rows(far_part_a, cross_sum_a)
    far_sum_a = swap(joined_a, far_mask)
    near, hidden = tie((near, hidden), joined_a)
    near_part, own_part = feed_forward([near, hidden], ups, downs)
    near_sum = swap(near_part, near_mask)
    cross_sum_b, near_part, far_sum_a = lax.optimization_barrier(
        (cross_sum_b, near_part, far_sum_a)
    )
    far_sum_b = swap(add_rows(far_part_b, cross_sum_b), far_mask)
    return finish_rows(
        hidden, own_part, near_sum, far_sum_a, far_sum_b, down_bias, out_gain, out_shift
    )


def solution(mesh):
    placed = (
        P(("grp", "dev"), None),
        P(("grp", "dev"), None),
        P(("grp", "dev"), None),
        P(("grp", "dev"), None),
        P(("grp", "dev"), None),
        P(("grp", "dev"), None),
        P("grp", None, "dev"),
        P("grp", None, "dev"),
        P(None, ("grp", "dev")),
        P(("grp", "dev")),
        P(("grp", "dev"), None),
        P(),
        P(),
        P(),
        P(),
        P(),
    )
    return jax.shard_map(
        on_device, mesh=mesh, in_specs=placed, out_specs=P(("grp", "dev"), None), check_vma=False
    )
```

```python
import functools
import math

import jax
import jax.numpy as jnp
from jax import lax
from jax.experimental import pallas as pl
from jax.experimental.pallas import tpu as pltpu
from jax.sharding import PartitionSpec as P

HD = 128
LANES = 128
STAT_ROWS = 8
STREAMS = 4
EMPTY = 64.0
ROW_BLOCK = 256
KEY_CHUNK = 1024

norm_eps = 1e-12
score_scale = HD ** (-0.5)
log2_e = math.log2(math.e)
mebibyte = 1024 * 1024


def layer_norm(summed, norm_gain, norm_shift):
    row_mean = jnp.mean(summed, axis=-1, keepdims=True)
    centred = summed - row_mean
    spread = jnp.mean(centred * centred, axis=-1, keepdims=True)
    return centred * lax.rsqrt(spread + norm_eps) * norm_gain + norm_shift


def vmem_spec():
    return pl.BlockSpec(memory_space=pltpu.VMEM)


def hbm_spec():
    return pl.BlockSpec(memory_space=pltpu.HBM)


def smem_spec():
    return pl.BlockSpec(memory_space=pltpu.SMEM)


def pack_kernel(lengths_ref, groups_ref, query_ref, out_ref, wide_ref):
    request_total = lengths_ref.shape[1]
    _, column_count, capacity, part_width = out_ref.shape
    slot_count = query_ref.shape[0]
    slot = lax.broadcasted_iota(jnp.int32, (capacity, LANES), 0)
    tiles = part_width // LANES
    for tile in range(wide_ref.shape[0]):
        wide_ref[tile, 0:slot_count, :] = query_ref[
            :, tile * LANES : (tile + 1) * LANES
        ].astype(jnp.float32)
        wide_ref[tile, slot_count : slot_count + capacity, :] = jnp.zeros(
            (capacity, LANES), jnp.float32
        )
    start = 0
    for request in range(request_total):
        group = groups_ref[0, request]
        filled = slot < lengths_ref[0, request]
        for column in range(column_count):
            for tile in range(tiles):
                rows = wide_ref[column * tiles + tile, pl.ds(start, capacity), :]
                rows = jnp.where(filled, rows, EMPTY)
                out_ref[group, column, :, tile * LANES : (tile + 1) * LANES] = rows.astype(
                    jnp.bfloat16
                )
        start = start + lengths_ref[0, request]


def pack_queries(lengths, groups, queries, group_count, column_count, capacity):
    slot_count, model_width = queries.shape
    part_width = model_width // column_count
    return pl.pallas_call(
        pack_kernel,
        out_shape=jax.ShapeDtypeStruct(
            (group_count, column_count, capacity, part_width), jnp.bfloat16
        ),
        in_specs=[smem_spec(), smem_spec(), vmem_spec()],
        out_specs=vmem_spec(),
        scratch_shapes=[
            pltpu.VMEM((model_width // LANES, slot_count + capacity, LANES), jnp.float32)
        ],
        compiler_params=pltpu.CompilerParams(vmem_limit_bytes=58 * mebibyte),
        name="pack_queries",
    )(lengths, groups, queries)


def far_kernel(
    counts_ref,
    arrived_ref,
    keys_hbm,
    values_hbm,
    out_ref,
    query_ref,
    answer_ref,
    stat_ref,
    score_ref,
    top_ref,
    keys_ref,
    values_ref,
    sems,
):
    copies = [
        pltpu.make_async_copy(keys_hbm, keys_ref, sems.at[0]),
        pltpu.make_async_copy(values_hbm, values_ref, sems.at[1]),
    ]
    for copy in copies:
        copy.start()
    sources, capacity, part_width = arrived_ref.shape
    local_heads = part_width // HD
    key_total = keys_ref.shape[1]
    chunks = key_total // KEY_CHUNK

    def take(source, offset):
        for head in range(local_heads):
            rows = arrived_ref[source, :, head * HD : (head + 1) * HD].astype(jnp.float32)
            query_ref[head, pl.ds(offset, capacity), :] = rows
        return offset + counts_ref[source]

    total = lax.fori_loop(0, sources, take, jnp.int32(0))
    blocks = (total + ROW_BLOCK - 1) // ROW_BLOCK
    lane = lax.broadcasted_iota(jnp.int32, (ROW_BLOCK, LANES), 1)

    def block_rows(block):
        return pl.ds(pl.multiple_of(block * ROW_BLOCK, ROW_BLOCK), ROW_BLOCK)

    def load_queries(block, head):
        return query_ref[head, block_rows(block), :].astype(jnp.bfloat16)

    def score_chunk(rows, head, slot, chunk, part_top):
        columns = slice(chunk * KEY_CHUNK, (chunk + 1) * KEY_CHUNK)
        scores = jnp.dot(
            rows,
            keys_ref[head * HD : (head + 1) * HD, columns],
            preferred_element_type=jnp.float32,
        )
        score_ref[slot, :, columns] = scores
        for piece in range(KEY_CHUNK // LANES):
            part = scores[:, piece * LANES : (piece + 1) * LANES]
            part_top = part if part_top is None else jnp.maximum(part_top, part)
        return part_top

    def finish_top(part_top, slot):
        row_top = jnp.max(part_top, axis=1, keepdims=True) * score_scale
        row_top = row_top.astype(jnp.bfloat16).astype(jnp.float32)
        top_ref[slot] = jnp.broadcast_to(row_top, (ROW_BLOCK, LANES))

    def weigh_chunk(head, slot, chunk, shift):
        columns = slice(chunk * KEY_CHUNK, (chunk + 1) * KEY_CHUNK)
        weights = jnp.exp2(score_ref[slot, :, columns] * (score_scale * log2_e) - shift)
        return jnp.dot(
            weights.astype(jnp.bfloat16),
            values_ref[head, columns, :],
            preferred_element_type=jnp.float32,
        )

    def finish_answer(block, head, slot, mixed):
        rows = block_rows(block)
        row_sum = mixed[:, HD:]
        answer_ref[head, rows, :] = mixed[:, :HD] / row_sum
        top = top_ref[slot]
        if head == 0:
            stat_ref[rows, :] = jnp.where(lane == 0, top, row_sum)
        else:
            before = stat_ref[rows, :]
            with_top = jnp.where(lane == head, top, before)
            stat_ref[rows, :] = jnp.where(lane == local_heads + head, row_sum, with_top)

    def slot_of(block, head):
        return (block * local_heads + head) % 2 if local_heads % 2 else head % 2

    for copy in copies:
        copy.wait()
    first_rows = load_queries(0, 0)
    part_top = None
    for chunk in range(chunks):
        part_top = score_chunk(first_rows, 0, 0, chunk, part_top)
    finish_top(part_top, 0)

    def one_block(block, carry):
        for head in range(local_heads):
            slot = slot_of(block, head)
            if head + 1 < local_heads:
                next_block, next_head = block, head + 1
            else:
                next_block, next_head = jnp.minimum(block + 1, blocks - 1), 0
            next_slot = 1 - slot
            next_rows = load_queries(next_block, next_head)
            shift = top_ref[slot][:, 0:1] * log2_e
            part_top = None
            mixed = None
            for chunk in range(chunks):
                part_top = score_chunk(next_rows, next_head, next_slot, chunk, part_top)
                part = weigh_chunk(head, slot, chunk, shift)
                mixed = part if mixed is None else mixed + part
            finish_answer(block, head, slot, mixed)
            finish_top(part_top, next_slot)
        return carry

    lax.fori_loop(0, blocks, one_block, 0)

    def give(source, offset):
        rows = [answer_ref[head, pl.ds(offset, capacity), :] for head in range(local_heads)]
        turned = jnp.transpose(stat_ref[pl.ds(offset, LANES), :])[:STAT_ROWS, :]
        if part_width > LANES:
            turned = jnp.concatenate(
                [turned, jnp.zeros((STAT_ROWS, part_width - LANES), jnp.float32)], axis=1
            )
        rows = jnp.concatenate(rows, axis=1)
        out_ref[source] = jnp.concatenate([rows, turned], axis=0).astype(jnp.bfloat16)
        return offset + counts_ref[source]

    lax.fori_loop(0, sources, give, jnp.int32(0))


def attend_prefix(counts, arrived, turned_keys, wide_values):
    sources, capacity, part_width = arrived.shape
    local_heads = part_width // HD
    key_total = turned_keys.shape[1]
    row_total = -(-sources * capacity // ROW_BLOCK) * ROW_BLOCK + LANES
    return pl.pallas_call(
        far_kernel,
        out_shape=jax.ShapeDtypeStruct((sources, capacity + STAT_ROWS, part_width), jnp.bfloat16),
        in_specs=[smem_spec(), vmem_spec(), hbm_spec(), hbm_spec()],
        out_specs=vmem_spec(),
        scratch_shapes=[
            pltpu.VMEM((local_heads, row_total, HD), jnp.float32),
            pltpu.VMEM((local_heads, row_total, HD), jnp.float32),
            pltpu.VMEM((row_total, LANES), jnp.float32),
            pltpu.VMEM((2, ROW_BLOCK, key_total), jnp.float32),
            pltpu.VMEM((2, ROW_BLOCK, LANES), jnp.float32),
            pltpu.VMEM(turned_keys.shape, jnp.bfloat16),
            pltpu.VMEM(wide_values.shape, jnp.bfloat16),
            pltpu.SemaphoreType.DMA((2,)),
        ],
        compiler_params=pltpu.CompilerParams(vmem_limit_bytes=58 * mebibyte),
        cost_estimate=pl.CostEstimate(
            flops=4 * sources * capacity * key_total * part_width,
            bytes_accessed=8 * key_total * part_width,
            transcendentals=sources * capacity * key_total * local_heads,
        ),
        name="attend_prefix",
    )(counts, arrived, turned_keys, wide_values)


def stat_lane(head, local_heads):
    return (head // local_heads) * STAT_ROWS + head % local_heads


def own_kernel(local_heads, lengths_ref, query_ref, key_ref, value_ref, mixed_ref, top_ref, sum_ref):
    slot_count, model_width = query_ref.shape
    head_count = model_width // HD
    row = lax.broadcasted_iota(jnp.int32, (slot_count, slot_count), 0)
    column = lax.broadcasted_iota(jnp.int32, (slot_count, slot_count), 1)
    row_segment = jnp.zeros((slot_count, slot_count), jnp.int32)
    column_segment = jnp.zeros((slot_count, slot_count), jnp.int32)
    start = 0
    for request in range(lengths_ref.shape[1]):
        start = start + lengths_ref[0, request]
        row_segment = row_segment + (row >= start).astype(jnp.int32)
        column_segment = column_segment + (column >= start).astype(jnp.int32)
    visible = (row_segment == column_segment) & (column <= row)
    lane = lax.broadcasted_iota(jnp.int32, (slot_count, LANES), 1)
    tops = jnp.zeros((slot_count, LANES), jnp.float32)
    sums = jnp.ones((slot_count, LANES), jnp.float32)
    for head in range(head_count):
        columns = slice(head * HD, (head + 1) * HD)
        scores = (
            lax.dot_general(
                query_ref[:, columns],
                key_ref[:, columns],
                (((1,), (1,)), ((), ())),
                preferred_element_type=jnp.float32,
            )
            * score_scale
        )
        top = jnp.max(jnp.where(visible, scores, -jnp.inf), axis=1, keepdims=True)
        weights = jnp.where(visible, jnp.exp(scores - top), 0.0)
        mixed_ref[:, columns] = jnp.dot(
            weights.astype(jnp.bfloat16),
            value_ref[:, columns],
            preferred_element_type=jnp.float32,
        )
        at = stat_lane(head, local_heads)
        tops = jnp.where(lane == at, top, tops)
        sums = jnp.where(lane == at, jnp.sum(weights, axis=1, keepdims=True), sums)
    top_ref[...] = tops
    sum_ref[...] = sums


def attend_suffix(lengths, queries, keys, values, local_heads):
    slot_count, model_width = queries.shape
    stats = jax.ShapeDtypeStruct((slot_count, LANES), jnp.float32)
    return pl.pallas_call(
        functools.partial(own_kernel, local_heads),
        out_shape=(jax.ShapeDtypeStruct((slot_count, model_width), jnp.float32), stats, stats),
        in_specs=[smem_spec()] + [vmem_spec()] * 3,
        out_specs=(vmem_spec(), vmem_spec(), vmem_spec()),
        compiler_params=pltpu.CompilerParams(vmem_limit_bytes=16 * mebibyte),
        cost_estimate=pl.CostEstimate(
            flops=40 * slot_count * slot_count * model_width,
            bytes_accessed=8 * slot_count * model_width,
            transcendentals=slot_count * model_width,
        ),
        name="attend_suffix",
    )(lengths, queries, keys, values)


def merge_kernel(
    lengths_ref,
    groups_ref,
    arrived_ref,
    own_mixed_ref,
    own_top_ref,
    own_sum_ref,
    input_ref,
    gain_ref,
    shift_ref,
    first_ref,
    second_ref,
    hidden_ref,
    far_ref,
    stat_ref,
):
    _, column_count, chunk_rows, part_width = arrived_ref.shape
    slot_count, model_width = input_ref.shape
    capacity = chunk_rows - STAT_ROWS
    local_heads = part_width // HD
    head_count = model_width // HD
    start = 0
    for request in range(lengths_ref.shape[1]):
        group = groups_ref[0, request]
        pieces = []
        for column in range(column_count):
            block = arrived_ref[group, column].astype(jnp.float32)
            for head in range(local_heads):
                far_ref[column * local_heads + head, pl.ds(start, capacity), :] = block[
                    :capacity, head * HD : (head + 1) * HD
                ]
            pieces.append(block[capacity:, :LANES])
        if column_count * STAT_ROWS < LANES:
            pieces.append(jnp.zeros((LANES - column_count * STAT_ROWS, LANES), jnp.float32))
        turned = jnp.transpose(jnp.concatenate(pieces, axis=0))
        stat_ref[pl.ds(start, capacity), :] = turned[:capacity]
        start = start + lengths_ref[0, request]
    far_top = stat_ref[:slot_count, :]
    far_sum = pltpu.roll(far_top, LANES - local_heads, 1)
    own_top = own_top_ref[...]
    joint_top = jnp.maximum(far_top, own_top)
    far_weight = jnp.exp(far_top - joint_top) * far_sum
    own_weight = jnp.exp(own_top - joint_top)
    bottom = far_weight + own_weight * own_sum_ref[...]
    far_weight = far_weight / bottom
    own_weight = own_weight / bottom
    total = jnp.zeros((slot_count, LANES), jnp.float32)
    for head in range(head_count):
        columns = slice(head * HD, (head + 1) * HD)
        at = stat_lane(head, local_heads)
        summed = (
            input_ref[:, columns].astype(jnp.float32)
            + far_weight[:, at : at + 1] * far_ref[head, :slot_count, :]
            + own_weight[:, at : at + 1] * own_mixed_ref[:, columns]
        )
        far_ref[head, :slot_count, :] = summed
        total = total + summed
    row_mean = jnp.sum(total, axis=1, keepdims=True) * (1.0 / model_width)
    total = jnp.zeros((slot_count, LANES), jnp.float32)
    for head in range(head_count):
        centred = far_ref[head, :slot_count, :] - row_mean
        total = total + centred * centred
    spread = jnp.sum(total, axis=1, keepdims=True) * (1.0 / model_width)
    factor = lax.rsqrt(spread + norm_eps)
    for head in range(head_count):
        columns = slice(head * HD, (head + 1) * HD)
        centred = far_ref[head, :slot_count, :] - row_mean
        hidden = (centred * factor * gain_ref[:, columns] + shift_ref[:, columns]).astype(
            jnp.bfloat16
        )
        first_ref[:, columns] = hidden[: slot_count // 2]
        second_ref[:, columns] = hidden[slot_count // 2 :]
        hidden_ref[:, columns] = hidden


def merge_parts(lengths, groups, arrived, own_mixed, own_top, own_sum, layer_input, gain, shift):
    slot_count, model_width = layer_input.shape
    capacity = arrived.shape[2] - STAT_ROWS
    half = jax.ShapeDtypeStruct((slot_count // 2, model_width), jnp.bfloat16)
    return pl.pallas_call(
        merge_kernel,
        out_shape=(half, half, jax.ShapeDtypeStruct(layer_input.shape, jnp.bfloat16)),
        in_specs=[smem_spec(), smem_spec()] + [vmem_spec()] * 7,
        out_specs=(vmem_spec(), vmem_spec(), vmem_spec()),
        scratch_shapes=[
            pltpu.VMEM((model_width // HD, slot_count + capacity, HD), jnp.float32),
            pltpu.VMEM((slot_count + capacity, LANES), jnp.float32),
        ],
        compiler_params=pltpu.CompilerParams(vmem_limit_bytes=16 * mebibyte),
        name="merge_parts",
    )(
        lengths,
        groups,
        arrived,
        own_mixed,
        own_top,
        own_sum,
        layer_input,
        gain.reshape(1, model_width),
        shift.reshape(1, model_width),
    )


def swap(value, mask):
    total = lax.axis_size("grp") * lax.axis_size("dev")
    pairs = [(here, here ^ mask) for here in range(total)]
    return jax.tree.map(lambda leaf: lax.ppermute(leaf, ("grp", "dev"), pairs), value)


def complete(held, masks):
    held = dict(held)
    for mask in masks:
        for at in list(held):
            if mask ^ at not in held:
                held[mask ^ at] = swap(held[at], mask)
    return held


def tie(values, after):
    return lax.optimization_barrier((values, after))[0]


def cut(height):
    step = max(height // STREAMS // 16, 1) * 16
    begins = [first for first in range(0, height, step)][:STREAMS]
    return [
        (first, (begins + [height])[at + 1] - first) for at, first in enumerate(begins)
    ]


def mlp_kernel(pieces, up_plan, down_plan, *refs):
    parts = len(up_plan)
    row_refs, refs = refs[:pieces], refs[pieces:]
    up_total, down_total = sum(map(len, up_plan)), sum(map(len, down_plan))
    ups, refs = list(refs[:up_total]), refs[up_total:]
    downs, refs = list(refs[:down_total]), refs[down_total:]
    out_refs, (up_ref, down_ref, sems) = refs[:pieces], refs[pieces:]
    model_width = row_refs[0].shape[1]
    copies = []
    for part, heights in enumerate(up_plan):
        begin, held = 0, []
        for piece, height in enumerate(heights):
            source = ups.pop(0)
            for stream, (first, rows) in enumerate(cut(height)):
                held.append(
                    pltpu.make_async_copy(
                        source.at[pl.ds(first, rows)],
                        up_ref.at[part, pl.ds(begin + first, rows)],
                        sems.at[part, 0, piece * STREAMS + stream],
                    )
                )
            begin += height
        copies.append(held)
    begin = 0
    for part, heights in enumerate(down_plan):
        held = []
        for piece, height in enumerate(heights):
            source = downs.pop(0)
            for stream, (first, rows) in enumerate(cut(height)):
                held.append(
                    pltpu.make_async_copy(
                        source.at[pl.ds(first, rows)],
                        down_ref.at[pl.ds(begin + first, rows)],
                        sems.at[part, 1, piece * STREAMS + stream],
                    )
                )
            begin += height
        copies.append(held)
    for held in copies:
        for copy in held:
            copy.start()
    rows = jnp.concatenate([ref[...] for ref in row_refs], axis=0)
    activations = []
    for part in range(parts):
        for copy in copies[part]:
            copy.wait()
        product = jnp.dot(
            rows, up_ref[part, :model_width, :], preferred_element_type=jnp.float32
        )
        offset = up_ref[part, model_width:, :].astype(jnp.float32)[0:1]
        activations.append(jax.nn.gelu(product + offset, approximate=True).astype(jnp.bfloat16))
    for held in copies[parts:]:
        for copy in held:
            copy.wait()
    total = jnp.dot(
        jnp.concatenate(activations, axis=1), down_ref[...], preferred_element_type=jnp.float32
    ).astype(jnp.bfloat16)
    begin = 0
    for out_ref in out_refs:
        height = out_ref.shape[0]
        out_ref[...] = total[begin : begin + height]
        begin += height


def feed_forward(rows, ups, downs):
    pieces, parts = len(rows), len(ups)
    row_total, model_width = sum(piece.shape[0] for piece in rows), rows[0].shape[1]
    up_plan = [[piece.shape[0] for piece in block] for block in ups]
    down_plan = [[piece.shape[0] for piece in block] for block in downs]
    up_rows, down_rows = sum(up_plan[0]), sum(down_plan[0])
    units = ups[0][0].shape[1]
    flat = [piece for block in ups + downs for piece in block]
    most = max(map(len, up_plan + down_plan))
    return pl.pallas_call(
        functools.partial(mlp_kernel, pieces, up_plan, down_plan),
        out_shape=tuple(jax.ShapeDtypeStruct(piece.shape, jnp.bfloat16) for piece in rows),
        in_specs=[vmem_spec()] * pieces + [hbm_spec()] * len(flat),
        out_specs=tuple(vmem_spec() for _ in rows),
        scratch_shapes=[
            pltpu.VMEM((parts, up_rows, units), jnp.bfloat16),
            pltpu.VMEM((parts * down_rows, model_width), jnp.bfloat16),
            pltpu.SemaphoreType.DMA((parts, 2, most * STREAMS)),
        ],
        compiler_params=pltpu.CompilerParams(vmem_limit_bytes=58 * mebibyte),
        cost_estimate=pl.CostEstimate(
            flops=4 * row_total * model_width * parts * units,
            bytes_accessed=4 * parts * model_width * units,
            transcendentals=row_total * parts * units,
        ),
        name="feed_forward",
    )(*rows, *flat)


def add_rows(here, there):
    return (here.astype(jnp.float32) + there.astype(jnp.float32)).astype(jnp.bfloat16)


def finish_kernel(
    hidden_ref, own_ref, near_ref, far_a_ref, far_b_ref, bias_ref, gain_ref, shift_ref, out_ref
):
    height = far_a_ref.shape[0]
    for begin, far_ref in ((0, far_a_ref), (height, far_b_ref)):
        rows = slice(begin, begin + height)
        summed = hidden_ref[rows, :].astype(jnp.float32) + (
            own_ref[rows, :].astype(jnp.float32)
            + near_ref[rows, :].astype(jnp.float32)
            + far_ref[...].astype(jnp.float32)
        )
        out_ref[rows, :] = layer_norm(
            summed + bias_ref[...], gain_ref[...], shift_ref[...]
        ).astype(jnp.bfloat16)


def finish_rows(hidden, own, near, far_a, far_b, bias, gain, shift):
    model_width = hidden.shape[1]
    return pl.pallas_call(
        finish_kernel,
        out_shape=jax.ShapeDtypeStruct(hidden.shape, jnp.bfloat16),
        in_specs=[vmem_spec()] * 8,
        out_specs=vmem_spec(),
        compiler_params=pltpu.CompilerParams(vmem_limit_bytes=16 * mebibyte),
        name="finish_rows",
    )(
        hidden,
        own,
        near,
        far_a,
        far_b,
        bias.reshape(1, model_width),
        gain.reshape(1, model_width),
        shift.reshape(1, model_width),
    )


def on_device(
    suffix_queries,
    suffix_keys,
    suffix_values,
    layer_input,
    suffix_lengths,
    request_group,
    prefix_keys,
    prefix_values,
    up_weight,
    up_bias,
    down_weight,
    down_bias,
    attn_gain,
    attn_shift,
    out_gain,
    out_shift,
):
    slot_count, model_width = suffix_queries.shape
    group_count = lax.axis_size("grp")
    column_count = lax.axis_size("dev")
    part_width = model_width // column_count
    local_heads = part_width // HD
    capacity = 2 * slot_count // group_count
    sources = group_count * column_count

    near_mask = group_count // 2 * column_count
    far_mask = column_count // 2
    column_masks = [1 << bit for bit in range(far_mask.bit_length() - 1)]
    group_masks = [column_count << bit for bit in range((group_count // 2).bit_length() - 1)]

    low_mask, high_masks = column_masks[0], column_masks[1:]
    core_mask = group_masks[0]

    outgoing = pack_queries(
        suffix_lengths, request_group, suffix_queries, group_count, column_count, capacity
    )
    bias_rows = jnp.broadcast_to(up_bias[None, :], (16, up_bias.shape[0]))
    up_block = jnp.concatenate([up_weight, bias_rows], axis=0)
    up_cut, down_cut = up_weight.shape[0] * 5 // 8, down_weight.shape[0] // 2
    up_pieces = (up_block[:up_cut], up_block[up_cut:])
    down_pieces = (down_weight[:down_cut], down_weight[down_cut:])
    ups, downs = {0: (up_block,)}, {0: (down_weight,)}
    high_mask = high_masks[0]

    arrived = lax.all_to_all(
        outgoing.reshape(sources, capacity, part_width),
        ("grp", "dev"),
        split_axis=0,
        concat_axis=0,
        tiled=True,
    )
    ups[low_mask] = swap(ups[0], low_mask)
    up_first = swap(up_pieces[0], high_mask)
    ups[core_mask] = swap(ups[0], core_mask)
    downs[core_mask] = swap(downs[0], core_mask)
    turned_keys = prefix_keys[0].T
    value_heads = prefix_values[0].reshape(-1, local_heads, HD).transpose(1, 0, 2)
    wide_values = jnp.concatenate([value_heads, jnp.ones_like(value_heads)], axis=2)
    own = attend_suffix(
        suffix_lengths, suffix_queries, suffix_keys, suffix_values, local_heads
    )
    arrived, ups, up_first, up_pieces, downs, down_pieces, turned_keys, wide_values, own = (
        lax.optimization_barrier(
            (arrived, ups, up_first, up_pieces, downs, down_pieces, turned_keys, wide_values, own)
        )
    )

    counts = jnp.sum((arrived[:, :, 0] < EMPTY / 2).astype(jnp.int32), axis=1)
    answer_part = attend_prefix(counts, arrived, turned_keys, wide_values)
    downs[low_mask] = swap(downs[0], low_mask)
    up_second = swap(up_pieces[1], high_mask)
    down_first = swap(down_pieces[0], high_mask)
    ups[core_mask ^ low_mask] = swap(ups[low_mask], core_mask)
    answer_part, ups, up_first, up_second, downs, down_first, down_pieces = (
        lax.optimization_barrier(
            (answer_part, ups, up_first, up_second, downs, down_first, down_pieces)
        )
    )

    answer = lax.all_to_all(
        answer_part, ("grp", "dev"), split_axis=0, concat_axis=0, tiled=True
    ).reshape(group_count, column_count, capacity + STAT_ROWS, part_width)
    ups[high_mask] = (jnp.concatenate([up_first, up_second], axis=0),)
    ups[core_mask ^ high_mask] = swap(ups[high_mask], core_mask)
    downs[core_mask ^ low_mask] = swap(downs[low_mask], core_mask)
    down_second = swap(down_pieces[1], high_mask)
    downs[high_mask] = (jnp.concatenate([down_first, down_second], axis=0),)
    downs[core_mask ^ high_mask] = swap(downs[high_mask], core_mask)
    ups[low_mask ^ high_mask] = swap(ups[high_mask], low_mask)
    answer, ups, downs = lax.optimization_barrier((answer, ups, downs))

    hidden_a, hidden_b, hidden = merge_parts(
        suffix_lengths, request_group, answer, *own, layer_input, attn_gain, attn_shift
    )

    (hidden_a, hidden_b, hidden), ups, downs = lax.optimization_barrier(
        ((hidden_a, hidden_b, hidden), ups, downs)
    )
    far_a = swap(hidden_a, far_mask)
    near = swap(hidden, near_mask)
    downs[low_mask ^ high_mask] = swap(downs[high_mask], low_mask)
    ups = complete(ups, group_masks + column_masks)
    far_b = swap(tie(hidden_b, far_a), far_mask)
    cross_a = swap(far_a, near_mask)
    far_b, cross_a, near, ups, downs = lax.optimization_barrier(
        (far_b, cross_a, near, ups, downs)
    )
    cross_b = swap(far_b, near_mask)
    downs = complete(downs, group_masks + column_masks)
    order = sorted(ups)
    ups = [ups[mask] for mask in order]
    downs = [downs[mask] for mask in order]
    far_part_a, cross_part_a = feed_forward([far_a, cross_a], ups, downs)
    cross_b, far_part_a, cross_part_a = lax.optimization_barrier(
        (cross_b, far_part_a, cross_part_a)
    )
    cross_sum_a = swap(cross_part_a, near_mask)
    far_part_b, cross_part_b = feed_forward([far_b, cross_b], ups, downs)
    cross_sum_a, far_part_b, cross_part_b = lax.optimization_barrier(
        (cross_sum_a, far_part_b, cross_part_b)
    )
    cross_sum_b = swap(cross_part_b, near_mask)
    joined_a = add_rows(far_part_a, cross_sum_a)
    far_sum_a = swap(joined_a, far_mask)
    near, hidden = tie((near, hidden), joined_a)
    near_part, own_part = feed_forward([near, hidden], ups, downs)
    near_sum = swap(near_part, near_mask)
    cross_sum_b, near_part, far_sum_a = lax.optimization_barrier(
        (cross_sum_b, near_part, far_sum_a)
    )
    far_sum_b = swap(add_rows(far_part_b, cross_sum_b), far_mask)
    return finish_rows(
        hidden, own_part, near_sum, far_sum_a, far_sum_b, down_bias, out_gain, out_shift
    )


def solution(mesh):
    placed = (
        P(("grp", "dev"), None),
        P(("grp", "dev"), None),
        P(("grp", "dev"), None),
        P(("grp", "dev"), None),
        P(("grp", "dev"), None),
        P(("grp", "dev"), None),
        P("grp", None, "dev"),
        P("grp", None, "dev"),
        P(None, ("grp", "dev")),
        P(("grp", "dev")),
        P(("grp", "dev"), None),
        P(),
        P(),
        P(),
        P(),
        P(),
    )
    return jax.shard_map(
        on_device, mesh=mesh, in_specs=placed, out_specs=P(("grp", "dev"), None), check_vma=False
    )
```

```python
import functools
import math

import jax
import jax.numpy as jnp
from jax import lax
from jax.experimental import pallas as pl
from jax.experimental.pallas import tpu as pltpu
from jax.sharding import PartitionSpec as P

HD = 128
LANES = 128
STAT_ROWS = 8
STREAMS = 4
FETCHES = 8
EMPTY = 64.0
ROW_BLOCK = 256
KEY_CHUNK = 1024

norm_eps = 1e-12
score_scale = HD ** (-0.5)
log2_e = math.log2(math.e)
mebibyte = 1024 * 1024


def layer_norm(summed, norm_gain, norm_shift):
    row_mean = jnp.mean(summed, axis=-1, keepdims=True)
    centred = summed - row_mean
    spread = jnp.mean(centred * centred, axis=-1, keepdims=True)
    return centred * lax.rsqrt(spread + norm_eps) * norm_gain + norm_shift


def vmem_spec():
    return pl.BlockSpec(memory_space=pltpu.VMEM)


def hbm_spec():
    return pl.BlockSpec(memory_space=pltpu.HBM)


def smem_spec():
    return pl.BlockSpec(memory_space=pltpu.SMEM)


def pack_kernel(lengths_ref, groups_ref, query_ref, out_ref, wide_ref):
    request_total = lengths_ref.shape[1]
    _, column_count, capacity, part_width = out_ref.shape
    slot_count = query_ref.shape[0]
    slot = lax.broadcasted_iota(jnp.int32, (capacity, LANES), 0)
    tiles = part_width // LANES
    for tile in range(wide_ref.shape[0]):
        wide_ref[tile, 0:slot_count, :] = query_ref[
            :, tile * LANES : (tile + 1) * LANES
        ].astype(jnp.float32)
        wide_ref[tile, slot_count : slot_count + capacity, :] = jnp.zeros(
            (capacity, LANES), jnp.float32
        )
    start = 0
    for request in range(request_total):
        group = groups_ref[0, request]
        filled = slot < lengths_ref[0, request]
        for column in range(column_count):
            for tile in range(tiles):
                rows = wide_ref[column * tiles + tile, pl.ds(start, capacity), :]
                rows = jnp.where(filled, rows, EMPTY)
                out_ref[group, column, :, tile * LANES : (tile + 1) * LANES] = rows.astype(
                    jnp.bfloat16
                )
        start = start + lengths_ref[0, request]


def pack_queries(lengths, groups, queries, group_count, column_count, capacity):
    slot_count, model_width = queries.shape
    part_width = model_width // column_count
    return pl.pallas_call(
        pack_kernel,
        out_shape=jax.ShapeDtypeStruct(
            (group_count, column_count, capacity, part_width), jnp.bfloat16
        ),
        in_specs=[smem_spec(), smem_spec(), vmem_spec()],
        out_specs=vmem_spec(),
        scratch_shapes=[
            pltpu.VMEM((model_width // LANES, slot_count + capacity, LANES), jnp.float32)
        ],
        compiler_params=pltpu.CompilerParams(vmem_limit_bytes=58 * mebibyte),
        name="pack_queries",
    )(lengths, groups, queries)


def far_kernel(
    counts_ref,
    arrived_ref,
    keys_hbm,
    values_hbm,
    out_ref,
    query_ref,
    answer_ref,
    stat_ref,
    score_ref,
    top_ref,
    keys_ref,
    values_ref,
    sems,
):
    key_step = keys_ref.shape[0] // FETCHES
    value_step = values_ref.shape[1] // FETCHES
    key_copies, value_copies = [], []
    for fetch in range(FETCHES):
        rows = pl.ds(fetch * key_step, key_step)
        key_copies.append(
            pltpu.make_async_copy(keys_hbm.at[rows], keys_ref.at[rows], sems.at[0, fetch])
        )
        rows = pl.ds(fetch * value_step, value_step)
        for head in range(values_ref.shape[0]):
            value_copies.append(
                pltpu.make_async_copy(
                    values_hbm.at[head, rows], values_ref.at[head, rows], sems.at[1 + head, fetch]
                )
            )
    for copy in key_copies + value_copies:
        copy.start()
    sources, capacity, part_width = arrived_ref.shape
    local_heads = part_width // HD
    key_total = keys_ref.shape[1]
    chunks = key_total // KEY_CHUNK

    def take(source, offset):
        for head in range(local_heads):
            rows = arrived_ref[source, :, head * HD : (head + 1) * HD].astype(jnp.float32)
            query_ref[head, pl.ds(offset, capacity), :] = rows
        return offset + counts_ref[source]

    total = lax.fori_loop(0, sources, take, jnp.int32(0))
    blocks = (total + ROW_BLOCK - 1) // ROW_BLOCK
    lane = lax.broadcasted_iota(jnp.int32, (ROW_BLOCK, LANES), 1)

    def block_rows(block):
        return pl.ds(pl.multiple_of(block * ROW_BLOCK, ROW_BLOCK), ROW_BLOCK)

    def load_queries(block, head):
        return query_ref[head, block_rows(block), :].astype(jnp.bfloat16)

    def score_chunk(rows, head, slot, chunk, part_top):
        columns = slice(chunk * KEY_CHUNK, (chunk + 1) * KEY_CHUNK)
        scores = jnp.dot(
            rows,
            keys_ref[head * HD : (head + 1) * HD, columns],
            preferred_element_type=jnp.float32,
        )
        score_ref[slot, :, columns] = scores
        for piece in range(KEY_CHUNK // LANES):
            part = scores[:, piece * LANES : (piece + 1) * LANES]
            part_top = part if part_top is None else jnp.maximum(part_top, part)
        return part_top

    def finish_top(part_top, slot):
        row_top = jnp.max(part_top, axis=1, keepdims=True) * score_scale
        row_top = row_top.astype(jnp.bfloat16).astype(jnp.float32)
        top_ref[slot] = jnp.broadcast_to(row_top, (ROW_BLOCK, LANES))

    def weigh_chunk(head, slot, chunk, shift):
        columns = slice(chunk * KEY_CHUNK, (chunk + 1) * KEY_CHUNK)
        weights = jnp.exp2(score_ref[slot, :, columns] * (score_scale * log2_e) - shift)
        return jnp.dot(
            weights.astype(jnp.bfloat16),
            values_ref[head, columns, :],
            preferred_element_type=jnp.float32,
        )

    def finish_answer(block, head, slot, mixed):
        rows = block_rows(block)
        row_sum = mixed[:, HD:]
        answer_ref[head, rows, :] = mixed[:, :HD] / row_sum
        top = top_ref[slot]
        if head == 0:
            stat_ref[rows, :] = jnp.where(lane == 0, top, row_sum)
        else:
            before = stat_ref[rows, :]
            with_top = jnp.where(lane == head, top, before)
            stat_ref[rows, :] = jnp.where(lane == local_heads + head, row_sum, with_top)

    def slot_of(block, head):
        return (block * local_heads + head) % 2 if local_heads % 2 else head % 2

    for copy in key_copies:
        copy.wait()
    first_rows = load_queries(0, 0)
    part_top = None
    for chunk in range(chunks):
        part_top = score_chunk(first_rows, 0, 0, chunk, part_top)
    finish_top(part_top, 0)
    for copy in value_copies:
        copy.wait()

    def one_block(block, carry):
        for head in range(local_heads):
            slot = slot_of(block, head)
            if head + 1 < local_heads:
                next_block, next_head = block, head + 1
            else:
                next_block, next_head = jnp.minimum(block + 1, blocks - 1), 0
            next_slot = 1 - slot
            next_rows = load_queries(next_block, next_head)
            shift = top_ref[slot][:, 0:1] * log2_e
            part_top = None
            mixed = None
            for chunk in range(chunks):
                part_top = score_chunk(next_rows, next_head, next_slot, chunk, part_top)
                part = weigh_chunk(head, slot, chunk, shift)
                mixed = part if mixed is None else mixed + part
            finish_answer(block, head, slot, mixed)
            finish_top(part_top, next_slot)
        return carry

    lax.fori_loop(0, blocks, one_block, 0)

    def give(source, offset):
        rows = [answer_ref[head, pl.ds(offset, capacity), :] for head in range(local_heads)]
        turned = jnp.transpose(stat_ref[pl.ds(offset, LANES), :])[:STAT_ROWS, :]
        if part_width > LANES:
            turned = jnp.concatenate(
                [turned, jnp.zeros((STAT_ROWS, part_width - LANES), jnp.float32)], axis=1
            )
        rows = jnp.concatenate(rows, axis=1)
        out_ref[source] = jnp.concatenate([rows, turned], axis=0).astype(jnp.bfloat16)
        return offset + counts_ref[source]

    lax.fori_loop(0, sources, give, jnp.int32(0))


def attend_prefix(counts, arrived, turned_keys, wide_values):
    sources, capacity, part_width = arrived.shape
    local_heads = part_width // HD
    key_total = turned_keys.shape[1]
    row_total = -(-sources * capacity // ROW_BLOCK) * ROW_BLOCK + LANES
    return pl.pallas_call(
        far_kernel,
        out_shape=jax.ShapeDtypeStruct((sources, capacity + STAT_ROWS, part_width), jnp.bfloat16),
        in_specs=[smem_spec(), vmem_spec(), hbm_spec(), hbm_spec()],
        out_specs=vmem_spec(),
        scratch_shapes=[
            pltpu.VMEM((local_heads, row_total, HD), jnp.float32),
            pltpu.VMEM((local_heads, row_total, HD), jnp.float32),
            pltpu.VMEM((row_total, LANES), jnp.float32),
            pltpu.VMEM((2, ROW_BLOCK, key_total), jnp.float32),
            pltpu.VMEM((2, ROW_BLOCK, LANES), jnp.float32),
            pltpu.VMEM(turned_keys.shape, jnp.bfloat16),
            pltpu.VMEM(wide_values.shape, jnp.bfloat16),
            pltpu.SemaphoreType.DMA((1 + local_heads, FETCHES)),
        ],
        compiler_params=pltpu.CompilerParams(vmem_limit_bytes=58 * mebibyte),
        cost_estimate=pl.CostEstimate(
            flops=4 * sources * capacity * key_total * part_width,
            bytes_accessed=8 * key_total * part_width,
            transcendentals=sources * capacity * key_total * local_heads,
        ),
        name="attend_prefix",
    )(counts, arrived, turned_keys, wide_values)


def stat_lane(head, local_heads):
    return (head // local_heads) * STAT_ROWS + head % local_heads


def own_kernel(local_heads, lengths_ref, query_ref, key_ref, value_ref, mixed_ref, top_ref, sum_ref):
    slot_count, model_width = query_ref.shape
    head_count = model_width // HD
    row = lax.broadcasted_iota(jnp.int32, (slot_count, slot_count), 0)
    column = lax.broadcasted_iota(jnp.int32, (slot_count, slot_count), 1)
    row_segment = jnp.zeros((slot_count, slot_count), jnp.int32)
    column_segment = jnp.zeros((slot_count, slot_count), jnp.int32)
    start = 0
    for request in range(lengths_ref.shape[1]):
        start = start + lengths_ref[0, request]
        row_segment = row_segment + (row >= start).astype(jnp.int32)
        column_segment = column_segment + (column >= start).astype(jnp.int32)
    visible = (row_segment == column_segment) & (column <= row)
    lane = lax.broadcasted_iota(jnp.int32, (slot_count, LANES), 1)
    tops = jnp.zeros((slot_count, LANES), jnp.float32)
    sums = jnp.ones((slot_count, LANES), jnp.float32)
    for head in range(head_count):
        columns = slice(head * HD, (head + 1) * HD)
        scores = (
            lax.dot_general(
                query_ref[:, columns],
                key_ref[:, columns],
                (((1,), (1,)), ((), ())),
                preferred_element_type=jnp.float32,
            )
            * score_scale
        )
        top = jnp.max(jnp.where(visible, scores, -jnp.inf), axis=1, keepdims=True)
        weights = jnp.where(visible, jnp.exp(scores - top), 0.0)
        mixed_ref[:, columns] = jnp.dot(
            weights.astype(jnp.bfloat16),
            value_ref[:, columns],
            preferred_element_type=jnp.float32,
        )
        at = stat_lane(head, local_heads)
        tops = jnp.where(lane == at, top, tops)
        sums = jnp.where(lane == at, jnp.sum(weights, axis=1, keepdims=True), sums)
    top_ref[...] = tops
    sum_ref[...] = sums


def attend_suffix(lengths, queries, keys, values, local_heads):
    slot_count, model_width = queries.shape
    stats = jax.ShapeDtypeStruct((slot_count, LANES), jnp.float32)
    return pl.pallas_call(
        functools.partial(own_kernel, local_heads),
        out_shape=(jax.ShapeDtypeStruct((slot_count, model_width), jnp.float32), stats, stats),
        in_specs=[smem_spec()] + [vmem_spec()] * 3,
        out_specs=(vmem_spec(), vmem_spec(), vmem_spec()),
        compiler_params=pltpu.CompilerParams(vmem_limit_bytes=16 * mebibyte),
        cost_estimate=pl.CostEstimate(
            flops=40 * slot_count * slot_count * model_width,
            bytes_accessed=8 * slot_count * model_width,
            transcendentals=slot_count * model_width,
        ),
        name="attend_suffix",
    )(lengths, queries, keys, values)


def merge_kernel(
    lengths_ref,
    groups_ref,
    arrived_ref,
    own_mixed_ref,
    own_top_ref,
    own_sum_ref,
    input_ref,
    gain_ref,
    shift_ref,
    first_ref,
    second_ref,
    hidden_ref,
    far_ref,
    stat_ref,
):
    _, column_count, chunk_rows, part_width = arrived_ref.shape
    slot_count, model_width = input_ref.shape
    capacity = chunk_rows - STAT_ROWS
    local_heads = part_width // HD
    head_count = model_width // HD
    start = 0
    for request in range(lengths_ref.shape[1]):
        group = groups_ref[0, request]
        pieces = []
        for column in range(column_count):
            block = arrived_ref[group, column].astype(jnp.float32)
            for head in range(local_heads):
                far_ref[column * local_heads + head, pl.ds(start, capacity), :] = block[
                    :capacity, head * HD : (head + 1) * HD
                ]
            pieces.append(block[capacity:, :LANES])
        if column_count * STAT_ROWS < LANES:
            pieces.append(jnp.zeros((LANES - column_count * STAT_ROWS, LANES), jnp.float32))
        turned = jnp.transpose(jnp.concatenate(pieces, axis=0))
        stat_ref[pl.ds(start, capacity), :] = turned[:capacity]
        start = start + lengths_ref[0, request]
    far_top = stat_ref[:slot_count, :]
    far_sum = pltpu.roll(far_top, LANES - local_heads, 1)
    own_top = own_top_ref[...]
    joint_top = jnp.maximum(far_top, own_top)
    far_weight = jnp.exp(far_top - joint_top) * far_sum
    own_weight = jnp.exp(own_top - joint_top)
    bottom = far_weight + own_weight * own_sum_ref[...]
    far_weight = far_weight / bottom
    own_weight = own_weight / bottom
    total = jnp.zeros((slot_count, LANES), jnp.float32)
    for head in range(head_count):
        columns = slice(head * HD, (head + 1) * HD)
        at = stat_lane(head, local_heads)
        summed = (
            input_ref[:, columns].astype(jnp.float32)
            + far_weight[:, at : at + 1] * far_ref[head, :slot_count, :]
            + own_weight[:, at : at + 1] * own_mixed_ref[:, columns]
        )
        far_ref[head, :slot_count, :] = summed
        total = total + summed
    row_mean = jnp.sum(total, axis=1, keepdims=True) * (1.0 / model_width)
    total = jnp.zeros((slot_count, LANES), jnp.float32)
    for head in range(head_count):
        centred = far_ref[head, :slot_count, :] - row_mean
        total = total + centred * centred
    spread = jnp.sum(total, axis=1, keepdims=True) * (1.0 / model_width)
    factor = lax.rsqrt(spread + norm_eps)
    for head in range(head_count):
        columns = slice(head * HD, (head + 1) * HD)
        centred = far_ref[head, :slot_count, :] - row_mean
        hidden = (centred * factor * gain_ref[:, columns] + shift_ref[:, columns]).astype(
            jnp.bfloat16
        )
        first_ref[:, columns] = hidden[: slot_count // 2]
        second_ref[:, columns] = hidden[slot_count // 2 :]
        hidden_ref[:, columns] = hidden


def merge_parts(lengths, groups, arrived, own_mixed, own_top, own_sum, layer_input, gain, shift):
    slot_count, model_width = layer_input.shape
    capacity = arrived.shape[2] - STAT_ROWS
    half = jax.ShapeDtypeStruct((slot_count // 2, model_width), jnp.bfloat16)
    return pl.pallas_call(
        merge_kernel,
        out_shape=(half, half, jax.ShapeDtypeStruct(layer_input.shape, jnp.bfloat16)),
        in_specs=[smem_spec(), smem_spec()] + [vmem_spec()] * 7,
        out_specs=(vmem_spec(), vmem_spec(), vmem_spec()),
        scratch_shapes=[
            pltpu.VMEM((model_width // HD, slot_count + capacity, HD), jnp.float32),
            pltpu.VMEM((slot_count + capacity, LANES), jnp.float32),
        ],
        compiler_params=pltpu.CompilerParams(vmem_limit_bytes=16 * mebibyte),
        name="merge_parts",
    )(
        lengths,
        groups,
        arrived,
        own_mixed,
        own_top,
        own_sum,
        layer_input,
        gain.reshape(1, model_width),
        shift.reshape(1, model_width),
    )


def swap(value, mask):
    total = lax.axis_size("grp") * lax.axis_size("dev")
    pairs = [(here, here ^ mask) for here in range(total)]
    return jax.tree.map(lambda leaf: lax.ppermute(leaf, ("grp", "dev"), pairs), value)


def complete(held, masks):
    held = dict(held)
    for mask in masks:
        for at in list(held):
            if mask ^ at not in held:
                held[mask ^ at] = swap(held[at], mask)
    return held


def tie(values, after):
    return lax.optimization_barrier((values, after))[0]


def cut(height):
    step = max(height // STREAMS // 16, 1) * 16
    begins = [first for first in range(0, height, step)][:STREAMS]
    return [
        (first, (begins + [height])[at + 1] - first) for at, first in enumerate(begins)
    ]


def mlp_kernel(pieces, up_plan, down_plan, *refs):
    parts = len(up_plan)
    row_refs, refs = refs[:pieces], refs[pieces:]
    up_total, down_total = sum(map(len, up_plan)), sum(map(len, down_plan))
    ups, refs = list(refs[:up_total]), refs[up_total:]
    downs, refs = list(refs[:down_total]), refs[down_total:]
    out_refs, (up_ref, down_ref, sems) = refs[:pieces], refs[pieces:]
    model_width = row_refs[0].shape[1]
    copies = []
    for part, heights in enumerate(up_plan):
        begin, held = 0, []
        for piece, height in enumerate(heights):
            source = ups.pop(0)
            for stream, (first, rows) in enumerate(cut(height)):
                held.append(
                    pltpu.make_async_copy(
                        source.at[pl.ds(first, rows)],
                        up_ref.at[part, pl.ds(begin + first, rows)],
                        sems.at[part, 0, piece * STREAMS + stream],
                    )
                )
            begin += height
        copies.append(held)
    begin = 0
    for part, heights in enumerate(down_plan):
        held = []
        for piece, height in enumerate(heights):
            source = downs.pop(0)
            for stream, (first, rows) in enumerate(cut(height)):
                held.append(
                    pltpu.make_async_copy(
                        source.at[pl.ds(first, rows)],
                        down_ref.at[pl.ds(begin + first, rows)],
                        sems.at[part, 1, piece * STREAMS + stream],
                    )
                )
            begin += height
        copies.append(held)
    ahead = min(4, len(copies))

    def arrive(at):
        for copy in copies[at]:
            copy.wait()
        for copy in copies[at + ahead] if at + ahead < len(copies) else ():
            copy.start()

    for held in copies[:ahead]:
        for copy in held:
            copy.start()
    rows = jnp.concatenate([ref[...] for ref in row_refs], axis=0)
    activations = []
    for part in range(parts):
        arrive(part)
        product = jnp.dot(
            rows, up_ref[part, :model_width, :], preferred_element_type=jnp.float32
        )
        offset = up_ref[part, model_width:, :].astype(jnp.float32)[0:1]
        activations.append(jax.nn.gelu(product + offset, approximate=True).astype(jnp.bfloat16))
    for part in range(parts):
        arrive(parts + part)
    total = jnp.dot(
        jnp.concatenate(activations, axis=1), down_ref[...], preferred_element_type=jnp.float32
    ).astype(jnp.bfloat16)
    begin = 0
    for out_ref in out_refs:
        height = out_ref.shape[0]
        out_ref[...] = total[begin : begin + height]
        begin += height


def feed_forward(rows, ups, downs):
    pieces, parts = len(rows), len(ups)
    row_total, model_width = sum(piece.shape[0] for piece in rows), rows[0].shape[1]
    up_plan = [[piece.shape[0] for piece in block] for block in ups]
    down_plan = [[piece.shape[0] for piece in block] for block in downs]
    up_rows, down_rows = sum(up_plan[0]), sum(down_plan[0])
    units = ups[0][0].shape[1]
    flat = [piece for block in ups + downs for piece in block]
    most = max(map(len, up_plan + down_plan))
    return pl.pallas_call(
        functools.partial(mlp_kernel, pieces, up_plan, down_plan),
        out_shape=tuple(jax.ShapeDtypeStruct(piece.shape, jnp.bfloat16) for piece in rows),
        in_specs=[vmem_spec()] * pieces + [hbm_spec()] * len(flat),
        out_specs=tuple(vmem_spec() for _ in rows),
        scratch_shapes=[
            pltpu.VMEM((parts, up_rows, units), jnp.bfloat16),
            pltpu.VMEM((parts * down_rows, model_width), jnp.bfloat16),
            pltpu.SemaphoreType.DMA((parts, 2, most * STREAMS)),
        ],
        compiler_params=pltpu.CompilerParams(vmem_limit_bytes=58 * mebibyte),
        cost_estimate=pl.CostEstimate(
            flops=4 * row_total * model_width * parts * units,
            bytes_accessed=4 * parts * model_width * units,
            transcendentals=row_total * parts * units,
        ),
        name="feed_forward",
    )(*rows, *flat)


def add_rows(here, there):
    return (here.astype(jnp.float32) + there.astype(jnp.float32)).astype(jnp.bfloat16)


def finish_kernel(
    hidden_ref, own_ref, near_ref, far_a_ref, far_b_ref, bias_ref, gain_ref, shift_ref, out_ref
):
    height = far_a_ref.shape[0]
    for begin, far_ref in ((0, far_a_ref), (height, far_b_ref)):
        rows = slice(begin, begin + height)
        summed = hidden_ref[rows, :].astype(jnp.float32) + (
            own_ref[rows, :].astype(jnp.float32)
            + near_ref[rows, :].astype(jnp.float32)
            + far_ref[...].astype(jnp.float32)
        )
        out_ref[rows, :] = layer_norm(
            summed + bias_ref[...], gain_ref[...], shift_ref[...]
        ).astype(jnp.bfloat16)


def finish_rows(hidden, own, near, far_a, far_b, bias, gain, shift):
    model_width = hidden.shape[1]
    return pl.pallas_call(
        finish_kernel,
        out_shape=jax.ShapeDtypeStruct(hidden.shape, jnp.bfloat16),
        in_specs=[vmem_spec()] * 8,
        out_specs=vmem_spec(),
        compiler_params=pltpu.CompilerParams(vmem_limit_bytes=16 * mebibyte),
        name="finish_rows",
    )(
        hidden,
        own,
        near,
        far_a,
        far_b,
        bias.reshape(1, model_width),
        gain.reshape(1, model_width),
        shift.reshape(1, model_width),
    )


def on_device(
    suffix_queries,
    suffix_keys,
    suffix_values,
    layer_input,
    suffix_lengths,
    request_group,
    prefix_keys,
    prefix_values,
    up_weight,
    up_bias,
    down_weight,
    down_bias,
    attn_gain,
    attn_shift,
    out_gain,
    out_shift,
):
    slot_count, model_width = suffix_queries.shape
    group_count = lax.axis_size("grp")
    column_count = lax.axis_size("dev")
    part_width = model_width // column_count
    local_heads = part_width // HD
    capacity = 2 * slot_count // group_count
    sources = group_count * column_count

    near_mask = group_count // 2 * column_count
    far_mask = column_count // 2
    column_masks = [1 << bit for bit in range(far_mask.bit_length() - 1)]
    group_masks = [column_count << bit for bit in range((group_count // 2).bit_length() - 1)]

    low_mask, high_masks = column_masks[0], column_masks[1:]
    core_mask = group_masks[0]

    outgoing = pack_queries(
        suffix_lengths, request_group, suffix_queries, group_count, column_count, capacity
    )
    bias_rows = jnp.broadcast_to(up_bias[None, :], (16, up_bias.shape[0]))
    up_block = jnp.concatenate([up_weight, bias_rows], axis=0)
    up_cut, down_cut = up_weight.shape[0] * 5 // 8, down_weight.shape[0] // 2
    up_pieces = (up_block[:up_cut], up_block[up_cut:])
    down_pieces = (down_weight[:down_cut], down_weight[down_cut:])
    ups, downs = {0: (up_block,)}, {0: (down_weight,)}
    high_mask = high_masks[0]

    arrived = lax.all_to_all(
        outgoing.reshape(sources, capacity, part_width),
        ("grp", "dev"),
        split_axis=0,
        concat_axis=0,
        tiled=True,
    )
    ups[low_mask] = swap(ups[0], low_mask)
    up_first = swap(up_pieces[0], high_mask)
    ups[core_mask] = swap(ups[0], core_mask)
    downs[core_mask] = swap(downs[0], core_mask)
    turned_keys = prefix_keys[0].T
    value_heads = prefix_values[0].reshape(-1, local_heads, HD).transpose(1, 0, 2)
    wide_values = jnp.concatenate([value_heads, jnp.ones_like(value_heads)], axis=2)
    own = attend_suffix(
        suffix_lengths, suffix_queries, suffix_keys, suffix_values, local_heads
    )
    arrived, ups, up_first, up_pieces, downs, down_pieces, turned_keys, wide_values, own = (
        lax.optimization_barrier(
            (arrived, ups, up_first, up_pieces, downs, down_pieces, turned_keys, wide_values, own)
        )
    )

    counts = jnp.sum((arrived[:, :, 0] < EMPTY / 2).astype(jnp.int32), axis=1)
    answer_part = attend_prefix(counts, arrived, turned_keys, wide_values)
    downs[low_mask] = swap(downs[0], low_mask)
    up_second = swap(up_pieces[1], high_mask)
    down_first = swap(down_pieces[0], high_mask)
    ups[core_mask ^ low_mask] = swap(ups[low_mask], core_mask)
    answer_part, ups, up_first, up_second, downs, down_first, down_pieces = (
        lax.optimization_barrier(
            (answer_part, ups, up_first, up_second, downs, down_first, down_pieces)
        )
    )

    answer = lax.all_to_all(
        answer_part, ("grp", "dev"), split_axis=0, concat_axis=0, tiled=True
    ).reshape(group_count, column_count, capacity + STAT_ROWS, part_width)
    ups[high_mask] = (jnp.concatenate([up_first, up_second], axis=0),)
    ups[core_mask ^ high_mask] = swap(ups[high_mask], core_mask)
    downs[core_mask ^ low_mask] = swap(downs[low_mask], core_mask)
    down_second = swap(down_pieces[1], high_mask)
    downs[high_mask] = (jnp.concatenate([down_first, down_second], axis=0),)
    downs[core_mask ^ high_mask] = swap(downs[high_mask], core_mask)
    ups[low_mask ^ high_mask] = swap(ups[high_mask], low_mask)
    answer, ups, downs = lax.optimization_barrier((answer, ups, downs))

    hidden_a, hidden_b, hidden = merge_parts(
        suffix_lengths, request_group, answer, *own, layer_input, attn_gain, attn_shift
    )

    (hidden_a, hidden_b, hidden), ups, downs = lax.optimization_barrier(
        ((hidden_a, hidden_b, hidden), ups, downs)
    )
    far_a = swap(hidden_a, far_mask)
    near = swap(hidden, near_mask)
    crossing = (
        swap(downs[high_mask][0][:down_cut], low_mask),
        swap(downs[low_mask][0][down_cut:], high_mask),
    )
    far_a, near, crossing, hidden_b, ups = lax.optimization_barrier(
        (far_a, near, crossing, hidden_b, ups)
    )
    far_b = swap(hidden_b, far_mask)
    cross_a = swap(far_a, near_mask)
    downs[low_mask ^ high_mask] = crossing
    ups = complete(ups, group_masks + column_masks)
    downs = complete(downs, group_masks + column_masks)
    order = sorted(ups)
    ups = [ups[mask] for mask in order]
    downs = [downs[mask] for mask in order]
    near_part, own_part = feed_forward([near, hidden], ups, downs)
    far_b, cross_a, near_part = lax.optimization_barrier((far_b, cross_a, near_part))
    cross_b = swap(far_b, near_mask)
    far_part_a, cross_part_a = feed_forward([far_a, cross_a], ups, downs)
    cross_b, far_part_a, cross_part_a = lax.optimization_barrier(
        (cross_b, far_part_a, cross_part_a)
    )
    cross_sum_a = swap(cross_part_a, near_mask)
    far_part_b, cross_part_b = feed_forward([far_b, cross_b], ups, downs)
    cross_sum_a, far_part_b, cross_part_b = lax.optimization_barrier(
        (cross_sum_a, far_part_b, cross_part_b)
    )
    far_sum_a = swap(add_rows(far_part_a, cross_sum_a), far_mask)
    cross_sum_b = swap(cross_part_b, near_mask)
    far_sum_b = swap(add_rows(far_part_b, cross_sum_b), far_mask)
    near_sum = swap(tie(near_part, cross_part_b), near_mask)
    return finish_rows(
        hidden, own_part, near_sum, far_sum_a, far_sum_b, down_bias, out_gain, out_shift
    )


def solution(mesh):
    placed = (
        P(("grp", "dev"), None),
        P(("grp", "dev"), None),
        P(("grp", "dev"), None),
        P(("grp", "dev"), None),
        P(("grp", "dev"), None),
        P(("grp", "dev"), None),
        P("grp", None, "dev"),
        P("grp", None, "dev"),
        P(None, ("grp", "dev")),
        P(("grp", "dev")),
        P(("grp", "dev"), None),
        P(),
        P(),
        P(),
        P(),
        P(),
    )
    return jax.shard_map(
        on_device, mesh=mesh, in_specs=placed, out_specs=P(("grp", "dev"), None), check_vma=False
    )
```

```python
import functools
import math

import jax
import jax.numpy as jnp
from jax import lax
from jax.experimental import pallas as pl
from jax.experimental.pallas import tpu as pltpu
from jax.sharding import PartitionSpec as P

HD = 128
LANES = 128
STAT_ROWS = 8
STREAMS = 4
FETCHES = 8
UNROLL = 4
EMPTY = 64.0
ROW_BLOCK = 256
KEY_CHUNK = 1024

norm_eps = 1e-12
score_scale = HD ** (-0.5)
log2_e = math.log2(math.e)
mebibyte = 1024 * 1024


def layer_norm(summed, norm_gain, norm_shift):
    row_mean = jnp.mean(summed, axis=-1, keepdims=True)
    centred = summed - row_mean
    spread = jnp.mean(centred * centred, axis=-1, keepdims=True)
    return centred * lax.rsqrt(spread + norm_eps) * norm_gain + norm_shift


def vmem_spec():
    return pl.BlockSpec(memory_space=pltpu.VMEM)


def hbm_spec():
    return pl.BlockSpec(memory_space=pltpu.HBM)


def smem_spec():
    return pl.BlockSpec(memory_space=pltpu.SMEM)


def pack_kernel(lengths_ref, groups_ref, query_ref, out_ref, wide_ref):
    request_total = lengths_ref.shape[1]
    _, column_count, capacity, part_width = out_ref.shape
    slot_count = query_ref.shape[0]
    slot = lax.broadcasted_iota(jnp.int32, (capacity, LANES), 0)
    tiles = part_width // LANES
    for tile in range(wide_ref.shape[0]):
        wide_ref[tile, 0:slot_count, :] = query_ref[
            :, tile * LANES : (tile + 1) * LANES
        ].astype(jnp.float32)
        wide_ref[tile, slot_count : slot_count + capacity, :] = jnp.zeros(
            (capacity, LANES), jnp.float32
        )
    start = 0
    for request in range(request_total):
        group = groups_ref[0, request]
        filled = slot < lengths_ref[0, request]
        for column in range(column_count):
            for tile in range(tiles):
                rows = wide_ref[column * tiles + tile, pl.ds(start, capacity), :]
                rows = jnp.where(filled, rows, EMPTY)
                out_ref[group, column, :, tile * LANES : (tile + 1) * LANES] = rows.astype(
                    jnp.bfloat16
                )
        start = start + lengths_ref[0, request]


def pack_queries(lengths, groups, queries, group_count, column_count, capacity):
    slot_count, model_width = queries.shape
    part_width = model_width // column_count
    return pl.pallas_call(
        pack_kernel,
        out_shape=jax.ShapeDtypeStruct(
            (group_count, column_count, capacity, part_width), jnp.bfloat16
        ),
        in_specs=[smem_spec(), smem_spec(), vmem_spec()],
        out_specs=vmem_spec(),
        scratch_shapes=[
            pltpu.VMEM((model_width // LANES, slot_count + capacity, LANES), jnp.float32)
        ],
        compiler_params=pltpu.CompilerParams(vmem_limit_bytes=58 * mebibyte),
        name="pack_queries",
    )(lengths, groups, queries)


def far_kernel(
    counts_ref,
    arrived_ref,
    keys_hbm,
    values_hbm,
    out_ref,
    query_ref,
    answer_ref,
    stat_ref,
    turned_ref,
    score_ref,
    top_ref,
    keys_ref,
    values_ref,
    sems,
):
    key_step = keys_ref.shape[0] // FETCHES
    value_step = values_ref.shape[1] // FETCHES
    key_copies, value_copies = [], []
    for fetch in range(FETCHES):
        rows = pl.ds(fetch * key_step, key_step)
        key_copies.append(
            pltpu.make_async_copy(keys_hbm.at[rows], keys_ref.at[rows], sems.at[0, fetch])
        )
        rows = pl.ds(fetch * value_step, value_step)
        for head in range(values_ref.shape[0]):
            value_copies.append(
                pltpu.make_async_copy(
                    values_hbm.at[head, rows], values_ref.at[head, rows], sems.at[1 + head, fetch]
                )
            )
    for copy in key_copies + value_copies:
        copy.start()
    sources, capacity, part_width = arrived_ref.shape
    local_heads = part_width // HD
    key_total = keys_ref.shape[1]
    chunks = key_total // KEY_CHUNK

    def take(source, offset):
        for head in range(local_heads):
            rows = arrived_ref[source, :, head * HD : (head + 1) * HD].astype(jnp.float32)
            query_ref[head, pl.ds(offset, capacity), :] = rows
        return offset + counts_ref[source]

    total = lax.fori_loop(0, sources, take, jnp.int32(0), unroll=UNROLL)
    blocks = (total + ROW_BLOCK - 1) // ROW_BLOCK
    lane = lax.broadcasted_iota(jnp.int32, (ROW_BLOCK, LANES), 1)

    def block_rows(block):
        return pl.ds(pl.multiple_of(block * ROW_BLOCK, ROW_BLOCK), ROW_BLOCK)

    def load_queries(block, head):
        return query_ref[head, block_rows(block), :].astype(jnp.bfloat16)

    def score_chunk(rows, head, slot, chunk, part_top):
        columns = slice(chunk * KEY_CHUNK, (chunk + 1) * KEY_CHUNK)
        scores = jnp.dot(
            rows,
            keys_ref[head * HD : (head + 1) * HD, columns],
            preferred_element_type=jnp.float32,
        )
        score_ref[slot, :, columns] = scores
        for piece in range(KEY_CHUNK // LANES):
            part = scores[:, piece * LANES : (piece + 1) * LANES]
            part_top = part if part_top is None else jnp.maximum(part_top, part)
        return part_top

    def finish_top(part_top, slot):
        row_top = jnp.max(part_top, axis=1, keepdims=True) * score_scale
        row_top = row_top.astype(jnp.bfloat16).astype(jnp.float32)
        top_ref[slot] = jnp.broadcast_to(row_top, (ROW_BLOCK, LANES))

    def weigh_chunk(head, slot, chunk, shift):
        columns = slice(chunk * KEY_CHUNK, (chunk + 1) * KEY_CHUNK)
        weights = jnp.exp2(score_ref[slot, :, columns] * (score_scale * log2_e) - shift)
        return jnp.dot(
            weights.astype(jnp.bfloat16),
            values_ref[head, columns, :],
            preferred_element_type=jnp.float32,
        )

    def finish_answer(block, head, slot, mixed):
        rows = block_rows(block)
        row_sum = mixed[:, HD:]
        answer_ref[head, rows, :] = mixed[:, :HD] / row_sum
        top = top_ref[slot]
        if head == 0:
            stats = jnp.where(lane == 0, top, row_sum)
        else:
            stats = jnp.where(lane == head, top, stat_ref[...])
            stats = jnp.where(lane == local_heads + head, row_sum, stats)
        if head + 1 < local_heads:
            stat_ref[...] = stats
        else:
            for half in range(ROW_BLOCK // LANES):
                turned_ref[block * (ROW_BLOCK // LANES) + half] = jnp.transpose(
                    stats[half * LANES : (half + 1) * LANES]
                )[:STAT_ROWS, :]

    def slot_of(block, head):
        return (block * local_heads + head) % 2 if local_heads % 2 else head % 2

    for copy in key_copies:
        copy.wait()
    first_rows = load_queries(0, 0)
    part_top = None
    for chunk in range(chunks):
        part_top = score_chunk(first_rows, 0, 0, chunk, part_top)
    finish_top(part_top, 0)
    for copy in value_copies:
        copy.wait()

    def one_block(block, carry):
        for head in range(local_heads):
            slot = slot_of(block, head)
            if head + 1 < local_heads:
                next_block, next_head = block, head + 1
            else:
                next_block, next_head = jnp.minimum(block + 1, blocks - 1), 0
            next_slot = 1 - slot
            next_rows = load_queries(next_block, next_head)
            shift = top_ref[slot][:, 0:1] * log2_e
            part_top = None
            mixed = None
            for chunk in range(chunks):
                part_top = score_chunk(next_rows, next_head, next_slot, chunk, part_top)
                part = weigh_chunk(head, slot, chunk, shift)
                mixed = part if mixed is None else mixed + part
            finish_answer(block, head, slot, mixed)
            finish_top(part_top, next_slot)
        return carry

    lax.fori_loop(0, blocks, one_block, 0)

    def give(source, offset):
        rows = [answer_ref[head, pl.ds(offset, capacity), :] for head in range(local_heads)]
        tile = offset // LANES
        window = jnp.concatenate([turned_ref[tile], turned_ref[tile + 1]], axis=1)
        turned = pltpu.roll(window, (2 * LANES - offset % LANES) % (2 * LANES), 1)[:, :LANES]
        if part_width > LANES:
            turned = jnp.concatenate(
                [turned, jnp.zeros((STAT_ROWS, part_width - LANES), jnp.float32)], axis=1
            )
        rows = jnp.concatenate(rows, axis=1)
        out_ref[source] = jnp.concatenate([rows, turned], axis=0).astype(jnp.bfloat16)
        return offset + counts_ref[source]

    lax.fori_loop(0, sources, give, jnp.int32(0), unroll=UNROLL)


def attend_prefix(counts, arrived, turned_keys, wide_values):
    sources, capacity, part_width = arrived.shape
    local_heads = part_width // HD
    key_total = turned_keys.shape[1]
    row_total = -(-sources * capacity // ROW_BLOCK) * ROW_BLOCK + LANES
    return pl.pallas_call(
        far_kernel,
        out_shape=jax.ShapeDtypeStruct((sources, capacity + STAT_ROWS, part_width), jnp.bfloat16),
        in_specs=[smem_spec(), vmem_spec(), hbm_spec(), hbm_spec()],
        out_specs=vmem_spec(),
        scratch_shapes=[
            pltpu.VMEM((local_heads, row_total, HD), jnp.float32),
            pltpu.VMEM((local_heads, row_total, HD), jnp.float32),
            pltpu.VMEM((ROW_BLOCK, LANES), jnp.float32),
            pltpu.VMEM((row_total // LANES + 1, STAT_ROWS, LANES), jnp.float32),
            pltpu.VMEM((2, ROW_BLOCK, key_total), jnp.float32),
            pltpu.VMEM((2, ROW_BLOCK, LANES), jnp.float32),
            pltpu.VMEM(turned_keys.shape, jnp.bfloat16),
            pltpu.VMEM(wide_values.shape, jnp.bfloat16),
            pltpu.SemaphoreType.DMA((1 + local_heads, FETCHES)),
        ],
        compiler_params=pltpu.CompilerParams(vmem_limit_bytes=58 * mebibyte),
        cost_estimate=pl.CostEstimate(
            flops=4 * sources * capacity * key_total * part_width,
            bytes_accessed=8 * key_total * part_width,
            transcendentals=sources * capacity * key_total * local_heads,
        ),
        name="attend_prefix",
    )(counts, arrived, turned_keys, wide_values)


def stat_lane(head, local_heads):
    return (head // local_heads) * STAT_ROWS + head % local_heads


def own_kernel(local_heads, lengths_ref, query_ref, key_ref, value_ref, mixed_ref, top_ref, sum_ref):
    slot_count, model_width = query_ref.shape
    head_count = model_width // HD
    row = lax.broadcasted_iota(jnp.int32, (slot_count, slot_count), 0)
    column = lax.broadcasted_iota(jnp.int32, (slot_count, slot_count), 1)
    row_segment = jnp.zeros((slot_count, slot_count), jnp.int32)
    column_segment = jnp.zeros((slot_count, slot_count), jnp.int32)
    start = 0
    for request in range(lengths_ref.shape[1]):
        start = start + lengths_ref[0, request]
        row_segment = row_segment + (row >= start).astype(jnp.int32)
        column_segment = column_segment + (column >= start).astype(jnp.int32)
    visible = (row_segment == column_segment) & (column <= row)
    lane = lax.broadcasted_iota(jnp.int32, (slot_count, LANES), 1)
    tops = jnp.zeros((slot_count, LANES), jnp.float32)
    sums = jnp.ones((slot_count, LANES), jnp.float32)
    for head in range(head_count):
        columns = slice(head * HD, (head + 1) * HD)
        scores = (
            lax.dot_general(
                query_ref[:, columns],
                key_ref[:, columns],
                (((1,), (1,)), ((), ())),
                preferred_element_type=jnp.float32,
            )
            * score_scale
        )
        top = jnp.max(jnp.where(visible, scores, -jnp.inf), axis=1, keepdims=True)
        weights = jnp.where(visible, jnp.exp(scores - top), 0.0)
        mixed_ref[:, columns] = jnp.dot(
            weights.astype(jnp.bfloat16),
            value_ref[:, columns],
            preferred_element_type=jnp.float32,
        )
        at = stat_lane(head, local_heads)
        tops = jnp.where(lane == at, top, tops)
        sums = jnp.where(lane == at, jnp.sum(weights, axis=1, keepdims=True), sums)
    top_ref[...] = tops
    sum_ref[...] = sums


def attend_suffix(lengths, queries, keys, values, local_heads):
    slot_count, model_width = queries.shape
    stats = jax.ShapeDtypeStruct((slot_count, LANES), jnp.float32)
    return pl.pallas_call(
        functools.partial(own_kernel, local_heads),
        out_shape=(jax.ShapeDtypeStruct((slot_count, model_width), jnp.float32), stats, stats),
        in_specs=[smem_spec()] + [vmem_spec()] * 3,
        out_specs=(vmem_spec(), vmem_spec(), vmem_spec()),
        compiler_params=pltpu.CompilerParams(vmem_limit_bytes=16 * mebibyte),
        cost_estimate=pl.CostEstimate(
            flops=40 * slot_count * slot_count * model_width,
            bytes_accessed=8 * slot_count * model_width,
            transcendentals=slot_count * model_width,
        ),
        name="attend_suffix",
    )(lengths, queries, keys, values)


def merge_kernel(
    lengths_ref,
    groups_ref,
    arrived_ref,
    own_mixed_ref,
    own_top_ref,
    own_sum_ref,
    input_ref,
    gain_ref,
    shift_ref,
    first_ref,
    second_ref,
    hidden_ref,
    far_ref,
    stat_ref,
):
    _, column_count, chunk_rows, part_width = arrived_ref.shape
    slot_count, model_width = input_ref.shape
    capacity = chunk_rows - STAT_ROWS
    local_heads = part_width // HD
    head_count = model_width // HD
    start = 0
    for request in range(lengths_ref.shape[1]):
        group = groups_ref[0, request]
        pieces = []
        for column in range(column_count):
            block = arrived_ref[group, column].astype(jnp.float32)
            for head in range(local_heads):
                far_ref[column * local_heads + head, pl.ds(start, capacity), :] = block[
                    :capacity, head * HD : (head + 1) * HD
                ]
            pieces.append(block[capacity:, :LANES])
        if column_count * STAT_ROWS < LANES:
            pieces.append(jnp.zeros((LANES - column_count * STAT_ROWS, LANES), jnp.float32))
        turned = jnp.transpose(jnp.concatenate(pieces, axis=0))
        stat_ref[pl.ds(start, capacity), :] = turned[:capacity]
        start = start + lengths_ref[0, request]
    far_top = stat_ref[:slot_count, :]
    far_sum = pltpu.roll(far_top, LANES - local_heads, 1)
    own_top = own_top_ref[...]
    joint_top = jnp.maximum(far_top, own_top)
    far_weight = jnp.exp(far_top - joint_top) * far_sum
    own_weight = jnp.exp(own_top - joint_top)
    bottom = far_weight + own_weight * own_sum_ref[...]
    far_weight = far_weight / bottom
    own_weight = own_weight / bottom
    total = jnp.zeros((slot_count, LANES), jnp.float32)
    for head in range(head_count):
        columns = slice(head * HD, (head + 1) * HD)
        at = stat_lane(head, local_heads)
        summed = (
            input_ref[:, columns].astype(jnp.float32)
            + far_weight[:, at : at + 1] * far_ref[head, :slot_count, :]
            + own_weight[:, at : at + 1] * own_mixed_ref[:, columns]
        )
        far_ref[head, :slot_count, :] = summed
        total = total + summed
    row_mean = jnp.sum(total, axis=1, keepdims=True) * (1.0 / model_width)
    total = jnp.zeros((slot_count, LANES), jnp.float32)
    for head in range(head_count):
        centred = far_ref[head, :slot_count, :] - row_mean
        total = total + centred * centred
    spread = jnp.sum(total, axis=1, keepdims=True) * (1.0 / model_width)
    factor = lax.rsqrt(spread + norm_eps)
    for head in range(head_count):
        columns = slice(head * HD, (head + 1) * HD)
        centred = far_ref[head, :slot_count, :] - row_mean
        hidden = (centred * factor * gain_ref[:, columns] + shift_ref[:, columns]).astype(
            jnp.bfloat16
        )
        first_ref[:, columns] = hidden[: slot_count // 2]
        second_ref[:, columns] = hidden[slot_count // 2 :]
        hidden_ref[:, columns] = hidden


def merge_parts(lengths, groups, arrived, own_mixed, own_top, own_sum, layer_input, gain, shift):
    slot_count, model_width = layer_input.shape
    capacity = arrived.shape[2] - STAT_ROWS
    half = jax.ShapeDtypeStruct((slot_count // 2, model_width), jnp.bfloat16)
    return pl.pallas_call(
        merge_kernel,
        out_shape=(half, half, jax.ShapeDtypeStruct(layer_input.shape, jnp.bfloat16)),
        in_specs=[smem_spec(), smem_spec()] + [vmem_spec()] * 7,
        out_specs=(vmem_spec(), vmem_spec(), vmem_spec()),
        scratch_shapes=[
            pltpu.VMEM((model_width // HD, slot_count + capacity, HD), jnp.float32),
            pltpu.VMEM((slot_count + capacity, LANES), jnp.float32),
        ],
        compiler_params=pltpu.CompilerParams(vmem_limit_bytes=16 * mebibyte),
        name="merge_parts",
    )(
        lengths,
        groups,
        arrived,
        own_mixed,
        own_top,
        own_sum,
        layer_input,
        gain.reshape(1, model_width),
        shift.reshape(1, model_width),
    )


def swap(value, mask):
    total = lax.axis_size("grp") * lax.axis_size("dev")
    pairs = [(here, here ^ mask) for here in range(total)]
    return jax.tree.map(lambda leaf: lax.ppermute(leaf, ("grp", "dev"), pairs), value)


def complete(held, masks):
    held = dict(held)
    for mask in masks:
        for at in list(held):
            if mask ^ at not in held:
                held[mask ^ at] = swap(held[at], mask)
    return held


def tie(values, after):
    return lax.optimization_barrier((values, after))[0]


def cut(height):
    step = max(height // STREAMS // 16, 1) * 16
    begins = [first for first in range(0, height, step)][:STREAMS]
    return [
        (first, (begins + [height])[at + 1] - first) for at, first in enumerate(begins)
    ]


def mlp_kernel(pieces, up_plan, down_plan, *refs):
    parts = len(up_plan)
    row_refs, refs = refs[:pieces], refs[pieces:]
    up_total, down_total = sum(map(len, up_plan)), sum(map(len, down_plan))
    ups, refs = list(refs[:up_total]), refs[up_total:]
    downs, refs = list(refs[:down_total]), refs[down_total:]
    out_refs, (up_ref, down_ref, sems) = refs[:pieces], refs[pieces:]
    model_width = row_refs[0].shape[1]
    copies = []
    for part, heights in enumerate(up_plan):
        begin, held = 0, []
        for piece, height in enumerate(heights):
            source = ups.pop(0)
            for stream, (first, rows) in enumerate(cut(height)):
                held.append(
                    pltpu.make_async_copy(
                        source.at[pl.ds(first, rows)],
                        up_ref.at[part, pl.ds(begin + first, rows)],
                        sems.at[part, 0, piece * STREAMS + stream],
                    )
                )
            begin += height
        copies.append(held)
    begin = 0
    for part, heights in enumerate(down_plan):
        held = []
        for piece, height in enumerate(heights):
            source = downs.pop(0)
            for stream, (first, rows) in enumerate(cut(height)):
                held.append(
                    pltpu.make_async_copy(
                        source.at[pl.ds(first, rows)],
                        down_ref.at[pl.ds(begin + first, rows)],
                        sems.at[part, 1, piece * STREAMS + stream],
                    )
                )
            begin += height
        copies.append(held)
    for held in copies:
        for copy in held:
            copy.start()
    rows = jnp.concatenate([ref[...] for ref in row_refs], axis=0)
    activations = []
    for part in range(parts):
        for copy in copies[part]:
            copy.wait()
        product = jnp.dot(
            rows, up_ref[part, :model_width, :], preferred_element_type=jnp.float32
        )
        offset = up_ref[part, model_width:, :].astype(jnp.float32)[0:1]
        activations.append(jax.nn.gelu(product + offset, approximate=True).astype(jnp.bfloat16))
    for held in copies[parts:]:
        for copy in held:
            copy.wait()
    total = jnp.dot(
        jnp.concatenate(activations, axis=1), down_ref[...], preferred_element_type=jnp.float32
    ).astype(jnp.bfloat16)
    begin = 0
    for out_ref in out_refs:
        height = out_ref.shape[0]
        out_ref[...] = total[begin : begin + height]
        begin += height


def feed_forward(rows, ups, downs):
    pieces, parts = len(rows), len(ups)
    row_total, model_width = sum(piece.shape[0] for piece in rows), rows[0].shape[1]
    up_plan = [[piece.shape[0] for piece in block] for block in ups]
    down_plan = [[piece.shape[0] for piece in block] for block in downs]
    up_rows, down_rows = sum(up_plan[0]), sum(down_plan[0])
    units = ups[0][0].shape[1]
    flat = [piece for block in ups + downs for piece in block]
    most = max(map(len, up_plan + down_plan))
    return pl.pallas_call(
        functools.partial(mlp_kernel, pieces, up_plan, down_plan),
        out_shape=tuple(jax.ShapeDtypeStruct(piece.shape, jnp.bfloat16) for piece in rows),
        in_specs=[vmem_spec()] * pieces + [hbm_spec()] * len(flat),
        out_specs=tuple(vmem_spec() for _ in rows),
        scratch_shapes=[
            pltpu.VMEM((parts, up_rows, units), jnp.bfloat16),
            pltpu.VMEM((parts * down_rows, model_width), jnp.bfloat16),
            pltpu.SemaphoreType.DMA((parts, 2, most * STREAMS)),
        ],
        compiler_params=pltpu.CompilerParams(vmem_limit_bytes=58 * mebibyte),
        cost_estimate=pl.CostEstimate(
            flops=4 * row_total * model_width * parts * units,
            bytes_accessed=4 * parts * model_width * units,
            transcendentals=row_total * parts * units,
        ),
        name="feed_forward",
    )(*rows, *flat)


def add_rows(here, there):
    return (here.astype(jnp.float32) + there.astype(jnp.float32)).astype(jnp.bfloat16)


def finish_kernel(
    hidden_ref, own_ref, near_ref, far_a_ref, far_b_ref, bias_ref, gain_ref, shift_ref, out_ref
):
    height = far_a_ref.shape[0]
    for begin, far_ref in ((0, far_a_ref), (height, far_b_ref)):
        rows = slice(begin, begin + height)
        summed = hidden_ref[rows, :].astype(jnp.float32) + (
            own_ref[rows, :].astype(jnp.float32)
            + near_ref[rows, :].astype(jnp.float32)
            + far_ref[...].astype(jnp.float32)
        )
        out_ref[rows, :] = layer_norm(
            summed + bias_ref[...], gain_ref[...], shift_ref[...]
        ).astype(jnp.bfloat16)


def finish_rows(hidden, own, near, far_a, far_b, bias, gain, shift):
    model_width = hidden.shape[1]
    return pl.pallas_call(
        finish_kernel,
        out_shape=jax.ShapeDtypeStruct(hidden.shape, jnp.bfloat16),
        in_specs=[vmem_spec()] * 8,
        out_specs=vmem_spec(),
        compiler_params=pltpu.CompilerParams(vmem_limit_bytes=16 * mebibyte),
        name="finish_rows",
    )(
        hidden,
        own,
        near,
        far_a,
        far_b,
        bias.reshape(1, model_width),
        gain.reshape(1, model_width),
        shift.reshape(1, model_width),
    )


def on_device(
    suffix_queries,
    suffix_keys,
    suffix_values,
    layer_input,
    suffix_lengths,
    request_group,
    prefix_keys,
    prefix_values,
    up_weight,
    up_bias,
    down_weight,
    down_bias,
    attn_gain,
    attn_shift,
    out_gain,
    out_shift,
):
    slot_count, model_width = suffix_queries.shape
    group_count = lax.axis_size("grp")
    column_count = lax.axis_size("dev")
    part_width = model_width // column_count
    local_heads = part_width // HD
    capacity = 2 * slot_count // group_count
    sources = group_count * column_count

    near_mask = group_count // 2 * column_count
    far_mask = column_count // 2
    column_masks = [1 << bit for bit in range(far_mask.bit_length() - 1)]
    group_masks = [column_count << bit for bit in range((group_count // 2).bit_length() - 1)]

    low_mask, high_masks = column_masks[0], column_masks[1:]
    core_mask = group_masks[0]

    outgoing = pack_queries(
        suffix_lengths, request_group, suffix_queries, group_count, column_count, capacity
    )
    bias_rows = jnp.broadcast_to(up_bias[None, :], (16, up_bias.shape[0]))
    up_block = jnp.concatenate([up_weight, bias_rows], axis=0)
    up_cut, down_cut = up_weight.shape[0] * 5 // 8, down_weight.shape[0] // 2
    up_pieces = (up_block[:up_cut], up_block[up_cut:])
    down_pieces = (down_weight[:down_cut], down_weight[down_cut:])
    ups, downs = {0: (up_block,)}, {0: (down_weight,)}
    high_mask = high_masks[0]

    arrived = lax.all_to_all(
        outgoing.reshape(sources, capacity, part_width),
        ("grp", "dev"),
        split_axis=0,
        concat_axis=0,
        tiled=True,
    )
    ups[low_mask] = swap(ups[0], low_mask)
    up_first = swap(up_pieces[0], high_mask)
    ups[core_mask] = swap(ups[0], core_mask)
    downs[core_mask] = swap(downs[0], core_mask)
    turned_keys = prefix_keys[0].T
    value_heads = prefix_values[0].reshape(-1, local_heads, HD).transpose(1, 0, 2)
    wide_values = jnp.concatenate([value_heads, jnp.ones_like(value_heads)], axis=2)
    own = attend_suffix(
        suffix_lengths, suffix_queries, suffix_keys, suffix_values, local_heads
    )
    arrived, ups, up_first, up_pieces, downs, down_pieces, turned_keys, wide_values, own = (
        lax.optimization_barrier(
            (arrived, ups, up_first, up_pieces, downs, down_pieces, turned_keys, wide_values, own)
        )
    )

    counts = jnp.sum((arrived[:, :, 0] < EMPTY / 2).astype(jnp.int32), axis=1)
    answer_part = attend_prefix(counts, arrived, turned_keys, wide_values)
    downs[low_mask] = swap(downs[0], low_mask)
    up_second = swap(up_pieces[1], high_mask)
    down_first = swap(down_pieces[0], high_mask)
    ups[core_mask ^ low_mask] = swap(ups[low_mask], core_mask)
    answer_part, ups, up_first, up_second, downs, down_first, down_pieces = (
        lax.optimization_barrier(
            (answer_part, ups, up_first, up_second, downs, down_first, down_pieces)
        )
    )

    answer = lax.all_to_all(
        answer_part, ("grp", "dev"), split_axis=0, concat_axis=0, tiled=True
    ).reshape(group_count, column_count, capacity + STAT_ROWS, part_width)
    ups[high_mask] = (jnp.concatenate([up_first, up_second], axis=0),)
    ups[core_mask ^ high_mask] = swap(ups[high_mask], core_mask)
    downs[core_mask ^ low_mask] = swap(downs[low_mask], core_mask)
    down_second = swap(down_pieces[1], high_mask)
    downs[high_mask] = (jnp.concatenate([down_first, down_second], axis=0),)
    downs[core_mask ^ high_mask] = swap(downs[high_mask], core_mask)
    ups[low_mask ^ high_mask] = swap(ups[high_mask], low_mask)
    answer, ups, downs = lax.optimization_barrier((answer, ups, downs))

    hidden_a, hidden_b, hidden = merge_parts(
        suffix_lengths, request_group, answer, *own, layer_input, attn_gain, attn_shift
    )

    (hidden_a, hidden_b, hidden), ups, downs = lax.optimization_barrier(
        ((hidden_a, hidden_b, hidden), ups, downs)
    )
    far_a = swap(hidden_a, far_mask)
    near = swap(hidden, near_mask)
    downs[low_mask ^ high_mask] = swap(downs[high_mask], low_mask)
    ups = complete(ups, group_masks + column_masks)
    far_b = swap(tie(hidden_b, far_a), far_mask)
    cross_a = swap(far_a, near_mask)
    far_b, cross_a, near, ups, downs = lax.optimization_barrier(
        (far_b, cross_a, near, ups, downs)
    )
    cross_b = swap(far_b, near_mask)
    downs = complete(downs, group_masks + column_masks)
    order = sorted(ups)
    ups = [ups[mask] for mask in order]
    downs = [downs[mask] for mask in order]
    far_part_a, cross_part_a = feed_forward([far_a, cross_a], ups, downs)
    cross_b, far_part_a, cross_part_a = lax.optimization_barrier(
        (cross_b, far_part_a, cross_part_a)
    )
    cross_sum_a = swap(cross_part_a, near_mask)
    far_part_b, cross_part_b = feed_forward([far_b, cross_b], ups, downs)
    cross_sum_a, far_part_b, cross_part_b = lax.optimization_barrier(
        (cross_sum_a, far_part_b, cross_part_b)
    )
    cross_sum_b = swap(cross_part_b, near_mask)
    joined_a = add_rows(far_part_a, cross_sum_a)
    far_sum_a = swap(joined_a, far_mask)
    near, hidden = tie((near, hidden), joined_a)
    near_part, own_part = feed_forward([near, hidden], ups, downs)
    near_sum = swap(near_part, near_mask)
    cross_sum_b, near_part, far_sum_a = lax.optimization_barrier(
        (cross_sum_b, near_part, far_sum_a)
    )
    far_sum_b = swap(add_rows(far_part_b, cross_sum_b), far_mask)
    return finish_rows(
        hidden, own_part, near_sum, far_sum_a, far_sum_b, down_bias, out_gain, out_shift
    )


def solution(mesh):
    placed = (
        P(("grp", "dev"), None),
        P(("grp", "dev"), None),
        P(("grp", "dev"), None),
        P(("grp", "dev"), None),
        P(("grp", "dev"), None),
        P(("grp", "dev"), None),
        P("grp", None, "dev"),
        P("grp", None, "dev"),
        P(None, ("grp", "dev")),
        P(("grp", "dev")),
        P(("grp", "dev"), None),
        P(),
        P(),
        P(),
        P(),
        P(),
    )
    return jax.shard_map(
        on_device, mesh=mesh, in_specs=placed, out_specs=P(("grp", "dev"), None), check_vma=False
    )
```

```python
import functools
import math

import jax
import jax.numpy as jnp
from jax import lax
from jax.experimental import pallas as pl
from jax.experimental.pallas import tpu as pltpu
from jax.sharding import PartitionSpec as P

HD = 128
LANES = 128
STAT_ROWS = 8
STREAMS = 4
FETCHES = 8
UNROLL = 4
EMPTY = 64.0
ROW_BLOCK = 256
KEY_CHUNK = 1024

norm_eps = 1e-12
score_scale = HD ** (-0.5)
log2_e = math.log2(math.e)
mebibyte = 1024 * 1024


def layer_norm(summed, norm_gain, norm_shift):
    row_mean = jnp.mean(summed, axis=-1, keepdims=True)
    centred = summed - row_mean
    spread = jnp.mean(centred * centred, axis=-1, keepdims=True)
    return centred * lax.rsqrt(spread + norm_eps) * norm_gain + norm_shift


def vmem_spec():
    return pl.BlockSpec(memory_space=pltpu.VMEM)


def hbm_spec():
    return pl.BlockSpec(memory_space=pltpu.HBM)


def smem_spec():
    return pl.BlockSpec(memory_space=pltpu.SMEM)


def pack_kernel(lengths_ref, groups_ref, query_ref, out_ref, wide_ref):
    request_total = lengths_ref.shape[1]
    _, column_count, capacity, part_width = out_ref.shape
    slot_count = query_ref.shape[0]
    slot = lax.broadcasted_iota(jnp.int32, (capacity, LANES), 0)
    tiles = part_width // LANES
    for tile in range(wide_ref.shape[0]):
        wide_ref[tile, 0:slot_count, :] = query_ref[
            :, tile * LANES : (tile + 1) * LANES
        ].astype(jnp.float32)
        wide_ref[tile, slot_count : slot_count + capacity, :] = jnp.zeros(
            (capacity, LANES), jnp.float32
        )
    start = 0
    for request in range(request_total):
        group = groups_ref[0, request]
        filled = slot < lengths_ref[0, request]
        for column in range(column_count):
            for tile in range(tiles):
                rows = wide_ref[column * tiles + tile, pl.ds(start, capacity), :]
                rows = jnp.where(filled, rows, EMPTY)
                out_ref[group, column, :, tile * LANES : (tile + 1) * LANES] = rows.astype(
                    jnp.bfloat16
                )
        start = start + lengths_ref[0, request]


def pack_queries(lengths, groups, queries, group_count, column_count, capacity):
    slot_count, model_width = queries.shape
    part_width = model_width // column_count
    return pl.pallas_call(
        pack_kernel,
        out_shape=jax.ShapeDtypeStruct(
            (group_count, column_count, capacity, part_width), jnp.bfloat16
        ),
        in_specs=[smem_spec(), smem_spec(), vmem_spec()],
        out_specs=vmem_spec(),
        scratch_shapes=[
            pltpu.VMEM((model_width // LANES, slot_count + capacity, LANES), jnp.float32)
        ],
        compiler_params=pltpu.CompilerParams(vmem_limit_bytes=58 * mebibyte),
        name="pack_queries",
    )(lengths, groups, queries)


def far_kernel(
    counts_ref,
    arrived_ref,
    keys_hbm,
    values_hbm,
    out_ref,
    query_ref,
    answer_ref,
    stat_ref,
    turned_ref,
    score_ref,
    top_ref,
    keys_ref,
    values_ref,
    sems,
):
    key_step = keys_ref.shape[0] // FETCHES
    value_step = values_ref.shape[1] // FETCHES
    key_copies, value_copies = [], []
    for fetch in range(FETCHES):
        rows = pl.ds(fetch * key_step, key_step)
        key_copies.append(
            pltpu.make_async_copy(keys_hbm.at[rows], keys_ref.at[rows], sems.at[0, fetch])
        )
        rows = pl.ds(fetch * value_step, value_step)
        for head in range(values_ref.shape[0]):
            value_copies.append(
                pltpu.make_async_copy(
                    values_hbm.at[head, rows], values_ref.at[head, rows], sems.at[1 + head, fetch]
                )
            )
    for copy in key_copies + value_copies:
        copy.start()
    sources, capacity, part_width = arrived_ref.shape
    local_heads = part_width // HD
    key_total = keys_ref.shape[1]
    chunks = key_total // KEY_CHUNK

    def take(source, offset):
        for head in range(local_heads):
            rows = arrived_ref[source, :, head * HD : (head + 1) * HD].astype(jnp.float32)
            query_ref[head, pl.ds(offset, capacity), :] = rows
        return offset + counts_ref[source]

    total = lax.fori_loop(0, sources, take, jnp.int32(0), unroll=UNROLL)
    blocks = (total + ROW_BLOCK - 1) // ROW_BLOCK
    lane = lax.broadcasted_iota(jnp.int32, (ROW_BLOCK, LANES), 1)

    def block_rows(block):
        return pl.ds(pl.multiple_of(block * ROW_BLOCK, ROW_BLOCK), ROW_BLOCK)

    def load_queries(block, head):
        return query_ref[head, block_rows(block), :].astype(jnp.bfloat16)

    def score_chunk(rows, head, slot, chunk, part_top):
        columns = slice(chunk * KEY_CHUNK, (chunk + 1) * KEY_CHUNK)
        scores = jnp.dot(
            rows,
            keys_ref[head * HD : (head + 1) * HD, columns],
            preferred_element_type=jnp.float32,
        )
        score_ref[slot, :, columns] = scores
        for piece in range(KEY_CHUNK // LANES):
            part = scores[:, piece * LANES : (piece + 1) * LANES]
            part_top = part if part_top is None else jnp.maximum(part_top, part)
        return part_top

    def finish_top(part_top, slot):
        row_top = jnp.max(part_top, axis=1, keepdims=True) * score_scale
        row_top = row_top.astype(jnp.bfloat16).astype(jnp.float32)
        top_ref[slot] = jnp.broadcast_to(row_top, (ROW_BLOCK, LANES))

    def weigh_chunk(head, slot, chunk, shift):
        columns = slice(chunk * KEY_CHUNK, (chunk + 1) * KEY_CHUNK)
        weights = jnp.exp2(score_ref[slot, :, columns] * (score_scale * log2_e) - shift)
        return jnp.dot(
            weights.astype(jnp.bfloat16),
            values_ref[head, columns, :],
            preferred_element_type=jnp.float32,
        )

    def finish_answer(block, head, slot, mixed):
        rows = block_rows(block)
        row_sum = mixed[:, HD:]
        answer_ref[head, rows, :] = mixed[:, :HD] / row_sum
        top = top_ref[slot]
        if head == 0:
            stats = jnp.where(lane == 0, top, row_sum)
        else:
            stats = jnp.where(lane == head, top, stat_ref[...])
            stats = jnp.where(lane == local_heads + head, row_sum, stats)
        if head + 1 < local_heads:
            stat_ref[...] = stats
        else:
            for half in range(ROW_BLOCK // LANES):
                turned_ref[block * (ROW_BLOCK // LANES) + half] = jnp.transpose(
                    stats[half * LANES : (half + 1) * LANES]
                )[:STAT_ROWS, :]

    def slot_of(block, head):
        return (block * local_heads + head) % 2 if local_heads % 2 else head % 2

    for copy in key_copies:
        copy.wait()
    first_rows = load_queries(0, 0)
    part_top = None
    for chunk in range(chunks):
        part_top = score_chunk(first_rows, 0, 0, chunk, part_top)
    finish_top(part_top, 0)
    for copy in value_copies:
        copy.wait()

    def one_block(block, carry):
        for head in range(local_heads):
            slot = slot_of(block, head)
            if head + 1 < local_heads:
                next_block, next_head = block, head + 1
            else:
                next_block, next_head = jnp.minimum(block + 1, blocks - 1), 0
            next_slot = 1 - slot
            next_rows = load_queries(next_block, next_head)
            shift = top_ref[slot][:, 0:1] * log2_e
            part_top = None
            mixed = None
            for chunk in range(chunks):
                part_top = score_chunk(next_rows, next_head, next_slot, chunk, part_top)
                part = weigh_chunk(head, slot, chunk, shift)
                mixed = part if mixed is None else mixed + part
            finish_answer(block, head, slot, mixed)
            finish_top(part_top, next_slot)
        return carry

    lax.fori_loop(0, blocks, one_block, 0)

    def give(source, offset):
        rows = [answer_ref[head, pl.ds(offset, capacity), :] for head in range(local_heads)]
        tile = offset // LANES
        window = jnp.concatenate([turned_ref[tile], turned_ref[tile + 1]], axis=1)
        turned = pltpu.roll(window, (2 * LANES - offset % LANES) % (2 * LANES), 1)[:, :LANES]
        if part_width > LANES:
            turned = jnp.concatenate(
                [turned, jnp.zeros((STAT_ROWS, part_width - LANES), jnp.float32)], axis=1
            )
        rows = jnp.concatenate(rows, axis=1)
        out_ref[source] = jnp.concatenate([rows, turned], axis=0).astype(jnp.bfloat16)
        return offset + counts_ref[source]

    lax.fori_loop(0, sources, give, jnp.int32(0), unroll=UNROLL)


def attend_prefix(counts, arrived, turned_keys, wide_values):
    sources, capacity, part_width = arrived.shape
    local_heads = part_width // HD
    key_total = turned_keys.shape[1]
    row_total = -(-sources * capacity // ROW_BLOCK) * ROW_BLOCK + LANES
    return pl.pallas_call(
        far_kernel,
        out_shape=jax.ShapeDtypeStruct((sources, capacity + STAT_ROWS, part_width), jnp.bfloat16),
        in_specs=[smem_spec(), vmem_spec(), hbm_spec(), hbm_spec()],
        out_specs=vmem_spec(),
        scratch_shapes=[
            pltpu.VMEM((local_heads, row_total, HD), jnp.float32),
            pltpu.VMEM((local_heads, row_total, HD), jnp.float32),
            pltpu.VMEM((ROW_BLOCK, LANES), jnp.float32),
            pltpu.VMEM((row_total // LANES + 1, STAT_ROWS, LANES), jnp.float32),
            pltpu.VMEM((2, ROW_BLOCK, key_total), jnp.float32),
            pltpu.VMEM((2, ROW_BLOCK, LANES), jnp.float32),
            pltpu.VMEM(turned_keys.shape, jnp.bfloat16),
            pltpu.VMEM(wide_values.shape, jnp.bfloat16),
            pltpu.SemaphoreType.DMA((1 + local_heads, FETCHES)),
        ],
        compiler_params=pltpu.CompilerParams(vmem_limit_bytes=58 * mebibyte),
        cost_estimate=pl.CostEstimate(
            flops=4 * sources * capacity * key_total * part_width,
            bytes_accessed=8 * key_total * part_width,
            transcendentals=sources * capacity * key_total * local_heads,
        ),
        name="attend_prefix",
    )(counts, arrived, turned_keys, wide_values)


def stat_lane(head, local_heads):
    return (head // local_heads) * STAT_ROWS + head % local_heads


def own_kernel(local_heads, lengths_ref, query_ref, key_ref, value_ref, mixed_ref, top_ref, sum_ref):
    slot_count, model_width = query_ref.shape
    head_count = model_width // HD
    row = lax.broadcasted_iota(jnp.int32, (slot_count, slot_count), 0)
    column = lax.broadcasted_iota(jnp.int32, (slot_count, slot_count), 1)
    row_segment = jnp.zeros((slot_count, slot_count), jnp.int32)
    column_segment = jnp.zeros((slot_count, slot_count), jnp.int32)
    start = 0
    for request in range(lengths_ref.shape[1]):
        start = start + lengths_ref[0, request]
        row_segment = row_segment + (row >= start).astype(jnp.int32)
        column_segment = column_segment + (column >= start).astype(jnp.int32)
    visible = (row_segment == column_segment) & (column <= row)
    lane = lax.broadcasted_iota(jnp.int32, (slot_count, LANES), 1)
    tops = jnp.zeros((slot_count, LANES), jnp.float32)
    sums = jnp.ones((slot_count, LANES), jnp.float32)
    for head in range(head_count):
        columns = slice(head * HD, (head + 1) * HD)
        scores = (
            lax.dot_general(
                query_ref[:, columns],
                key_ref[:, columns],
                (((1,), (1,)), ((), ())),
                preferred_element_type=jnp.float32,
            )
            * score_scale
        )
        top = jnp.max(jnp.where(visible, scores, -jnp.inf), axis=1, keepdims=True)
        weights = jnp.where(visible, jnp.exp(scores - top), 0.0)
        mixed_ref[:, columns] = jnp.dot(
            weights.astype(jnp.bfloat16),
            value_ref[:, columns],
            preferred_element_type=jnp.float32,
        )
        at = stat_lane(head, local_heads)
        tops = jnp.where(lane == at, top, tops)
        sums = jnp.where(lane == at, jnp.sum(weights, axis=1, keepdims=True), sums)
    top_ref[...] = tops
    sum_ref[...] = sums


def attend_suffix(lengths, queries, keys, values, local_heads):
    slot_count, model_width = queries.shape
    stats = jax.ShapeDtypeStruct((slot_count, LANES), jnp.float32)
    return pl.pallas_call(
        functools.partial(own_kernel, local_heads),
        out_shape=(jax.ShapeDtypeStruct((slot_count, model_width), jnp.float32), stats, stats),
        in_specs=[smem_spec()] + [vmem_spec()] * 3,
        out_specs=(vmem_spec(), vmem_spec(), vmem_spec()),
        compiler_params=pltpu.CompilerParams(vmem_limit_bytes=16 * mebibyte),
        cost_estimate=pl.CostEstimate(
            flops=40 * slot_count * slot_count * model_width,
            bytes_accessed=8 * slot_count * model_width,
            transcendentals=slot_count * model_width,
        ),
        name="attend_suffix",
    )(lengths, queries, keys, values)


def merge_kernel(
    lengths_ref,
    groups_ref,
    arrived_ref,
    own_mixed_ref,
    own_top_ref,
    own_sum_ref,
    input_ref,
    gain_ref,
    shift_ref,
    first_ref,
    second_ref,
    hidden_ref,
    far_ref,
    stat_ref,
):
    _, column_count, chunk_rows, part_width = arrived_ref.shape
    slot_count, model_width = input_ref.shape
    capacity = chunk_rows - STAT_ROWS
    local_heads = part_width // HD
    head_count = model_width // HD
    start = 0
    for request in range(lengths_ref.shape[1]):
        group = groups_ref[0, request]
        pieces = []
        for column in range(column_count):
            block = arrived_ref[group, column].astype(jnp.float32)
            for head in range(local_heads):
                far_ref[column * local_heads + head, pl.ds(start, capacity), :] = block[
                    :capacity, head * HD : (head + 1) * HD
                ]
            pieces.append(block[capacity:, :LANES])
        if column_count * STAT_ROWS < LANES:
            pieces.append(jnp.zeros((LANES - column_count * STAT_ROWS, LANES), jnp.float32))
        turned = jnp.transpose(jnp.concatenate(pieces, axis=0))
        stat_ref[pl.ds(start, capacity), :] = turned[:capacity]
        start = start + lengths_ref[0, request]
    far_top = stat_ref[:slot_count, :]
    far_sum = pltpu.roll(far_top, LANES - local_heads, 1)
    own_top = own_top_ref[...]
    joint_top = jnp.maximum(far_top, own_top)
    far_weight = jnp.exp(far_top - joint_top) * far_sum
    own_weight = jnp.exp(own_top - joint_top)
    bottom = far_weight + own_weight * own_sum_ref[...]
    far_weight = far_weight / bottom
    own_weight = own_weight / bottom
    total = jnp.zeros((slot_count, LANES), jnp.float32)
    for head in range(head_count):
        columns = slice(head * HD, (head + 1) * HD)
        at = stat_lane(head, local_heads)
        summed = (
            input_ref[:, columns].astype(jnp.float32)
            + far_weight[:, at : at + 1] * far_ref[head, :slot_count, :]
            + own_weight[:, at : at + 1] * own_mixed_ref[:, columns]
        )
        far_ref[head, :slot_count, :] = summed
        total = total + summed
    row_mean = jnp.sum(total, axis=1, keepdims=True) * (1.0 / model_width)
    total = jnp.zeros((slot_count, LANES), jnp.float32)
    for head in range(head_count):
        centred = far_ref[head, :slot_count, :] - row_mean
        total = total + centred * centred
    spread = jnp.sum(total, axis=1, keepdims=True) * (1.0 / model_width)
    factor = lax.rsqrt(spread + norm_eps)
    for head in range(head_count):
        columns = slice(head * HD, (head + 1) * HD)
        centred = far_ref[head, :slot_count, :] - row_mean
        hidden = (centred * factor * gain_ref[:, columns] + shift_ref[:, columns]).astype(
            jnp.bfloat16
        )
        first_ref[:, columns] = hidden[: slot_count // 2]
        second_ref[:, columns] = hidden[slot_count // 2 :]
        hidden_ref[:, columns] = hidden


def merge_parts(lengths, groups, arrived, own_mixed, own_top, own_sum, layer_input, gain, shift):
    slot_count, model_width = layer_input.shape
    capacity = arrived.shape[2] - STAT_ROWS
    half = jax.ShapeDtypeStruct((slot_count // 2, model_width), jnp.bfloat16)
    return pl.pallas_call(
        merge_kernel,
        out_shape=(half, half, jax.ShapeDtypeStruct(layer_input.shape, jnp.bfloat16)),
        in_specs=[smem_spec(), smem_spec()] + [vmem_spec()] * 7,
        out_specs=(vmem_spec(), vmem_spec(), vmem_spec()),
        scratch_shapes=[
            pltpu.VMEM((model_width // HD, slot_count + capacity, HD), jnp.float32),
            pltpu.VMEM((slot_count + capacity, LANES), jnp.float32),
        ],
        compiler_params=pltpu.CompilerParams(vmem_limit_bytes=16 * mebibyte),
        name="merge_parts",
    )(
        lengths,
        groups,
        arrived,
        own_mixed,
        own_top,
        own_sum,
        layer_input,
        gain.reshape(1, model_width),
        shift.reshape(1, model_width),
    )


def swap(value, mask):
    total = lax.axis_size("grp") * lax.axis_size("dev")
    pairs = [(here, here ^ mask) for here in range(total)]
    return jax.tree.map(lambda leaf: lax.ppermute(leaf, ("grp", "dev"), pairs), value)


def swap_block(block, mask, sent):
    for array, _, _ in block:
        if (id(array), mask) not in sent:
            sent[id(array), mask] = (array, swap(array, mask))
    return [(sent[id(array), mask][1], begin, rows) for array, begin, rows in block]


def complete(held, masks):
    held, sent = dict(held), {}
    for mask in masks:
        for at in list(held):
            if mask ^ at not in held:
                held[mask ^ at] = swap_block(held[at], mask, sent)
    return held


def tie(values, after):
    return lax.optimization_barrier((values, after))[0]


def cut(height):
    step = max(height // STREAMS // 16, 1) * 16
    begins = [first for first in range(0, height, step)][:STREAMS]
    return [
        (first, (begins + [height])[at + 1] - first) for at, first in enumerate(begins)
    ]


def mlp_kernel(pieces, held_total, up_plan, down_plan, *refs):
    parts = len(up_plan)
    row_refs, refs = refs[:pieces], refs[pieces:]
    held_refs, refs = refs[:held_total], refs[held_total:]
    out_refs, (up_ref, down_ref, sems) = refs[:pieces], refs[pieces:]
    model_width = row_refs[0].shape[1]
    copies = []
    for part, block in enumerate(up_plan):
        begin, held = 0, []
        for piece, (at, skip, height) in enumerate(block):
            source = held_refs[at]
            for stream, (first, rows) in enumerate(cut(height)):
                held.append(
                    pltpu.make_async_copy(
                        source.at[pl.ds(skip + first, rows)],
                        up_ref.at[part, pl.ds(begin + first, rows)],
                        sems.at[part, 0, piece * STREAMS + stream],
                    )
                )
            begin += height
        copies.append(held)
    begin = 0
    for part, block in enumerate(down_plan):
        held = []
        for piece, (at, skip, height) in enumerate(block):
            source = held_refs[at]
            for stream, (first, rows) in enumerate(cut(height)):
                held.append(
                    pltpu.make_async_copy(
                        source.at[pl.ds(skip + first, rows)],
                        down_ref.at[pl.ds(begin + first, rows)],
                        sems.at[part, 1, piece * STREAMS + stream],
                    )
                )
            begin += height
        copies.append(held)
    for held in copies:
        for copy in held:
            copy.start()
    rows = jnp.concatenate([ref[...] for ref in row_refs], axis=0)
    activations = []
    for part in range(parts):
        for copy in copies[part]:
            copy.wait()
        product = jnp.dot(
            rows, up_ref[part, :model_width, :], preferred_element_type=jnp.float32
        )
        offset = up_ref[part, model_width:, :].astype(jnp.float32)[0:1]
        activations.append(jax.nn.gelu(product + offset, approximate=True).astype(jnp.bfloat16))
    for held in copies[parts:]:
        for copy in held:
            copy.wait()
    total = jnp.dot(
        jnp.concatenate(activations, axis=1), down_ref[...], preferred_element_type=jnp.float32
    ).astype(jnp.bfloat16)
    begin = 0
    for out_ref in out_refs:
        height = out_ref.shape[0]
        out_ref[...] = total[begin : begin + height]
        begin += height


def feed_forward(rows, ups, downs):
    pieces, parts = len(rows), len(ups)
    row_total, model_width = sum(piece.shape[0] for piece in rows), rows[0].shape[1]
    flat = []

    def plan(blocks):
        planned = []
        for block in blocks:
            entries = []
            for array, begin, height in block:
                places = [at for at, known in enumerate(flat) if known is array]
                if not places:
                    places = [len(flat)]
                    flat.append(array)
                entries.append((places[0], begin, height))
            planned.append(entries)
        return planned

    up_plan, down_plan = plan(ups), plan(downs)
    up_rows, down_rows = (sum(entry[2] for entry in held[0]) for held in (up_plan, down_plan))
    units = ups[0][0][0].shape[1]
    most = max(map(len, up_plan + down_plan))
    return pl.pallas_call(
        functools.partial(mlp_kernel, pieces, len(flat), up_plan, down_plan),
        out_shape=tuple(jax.ShapeDtypeStruct(piece.shape, jnp.bfloat16) for piece in rows),
        in_specs=[vmem_spec()] * pieces + [hbm_spec()] * len(flat),
        out_specs=tuple(vmem_spec() for _ in rows),
        scratch_shapes=[
            pltpu.VMEM((parts, up_rows, units), jnp.bfloat16),
            pltpu.VMEM((parts * down_rows, model_width), jnp.bfloat16),
            pltpu.SemaphoreType.DMA((parts, 2, most * STREAMS)),
        ],
        compiler_params=pltpu.CompilerParams(vmem_limit_bytes=58 * mebibyte),
        cost_estimate=pl.CostEstimate(
            flops=4 * row_total * model_width * parts * units,
            bytes_accessed=4 * parts * model_width * units,
            transcendentals=row_total * parts * units,
        ),
        name="feed_forward",
    )(*rows, *flat)


def add_rows(here, there):
    return (here.astype(jnp.float32) + there.astype(jnp.float32)).astype(jnp.bfloat16)


def finish_kernel(
    hidden_ref, own_ref, near_ref, far_a_ref, far_b_ref, bias_ref, gain_ref, shift_ref, out_ref
):
    height = far_a_ref.shape[0]
    for begin, far_ref in ((0, far_a_ref), (height, far_b_ref)):
        rows = slice(begin, begin + height)
        summed = hidden_ref[rows, :].astype(jnp.float32) + (
            own_ref[rows, :].astype(jnp.float32)
            + near_ref[rows, :].astype(jnp.float32)
            + far_ref[...].astype(jnp.float32)
        )
        out_ref[rows, :] = layer_norm(
            summed + bias_ref[...], gain_ref[...], shift_ref[...]
        ).astype(jnp.bfloat16)


def finish_rows(hidden, own, near, far_a, far_b, bias, gain, shift):
    model_width = hidden.shape[1]
    return pl.pallas_call(
        finish_kernel,
        out_shape=jax.ShapeDtypeStruct(hidden.shape, jnp.bfloat16),
        in_specs=[vmem_spec()] * 8,
        out_specs=vmem_spec(),
        compiler_params=pltpu.CompilerParams(vmem_limit_bytes=16 * mebibyte),
        name="finish_rows",
    )(
        hidden,
        own,
        near,
        far_a,
        far_b,
        bias.reshape(1, model_width),
        gain.reshape(1, model_width),
        shift.reshape(1, model_width),
    )


def on_device(
    suffix_queries,
    suffix_keys,
    suffix_values,
    layer_input,
    suffix_lengths,
    request_group,
    prefix_keys,
    prefix_values,
    up_weight,
    up_bias,
    down_weight,
    down_bias,
    attn_gain,
    attn_shift,
    out_gain,
    out_shift,
):
    slot_count, model_width = suffix_queries.shape
    group_count = lax.axis_size("grp")
    column_count = lax.axis_size("dev")
    part_width = model_width // column_count
    local_heads = part_width // HD
    capacity = 2 * slot_count // group_count
    sources = group_count * column_count

    near_mask = group_count // 2 * column_count
    far_mask = column_count // 2
    column_masks = [1 << bit for bit in range(far_mask.bit_length() - 1)]
    group_masks = [column_count << bit for bit in range((group_count // 2).bit_length() - 1)]

    low_mask, high_masks = column_masks[0], column_masks[1:]
    core_mask = group_masks[0]

    outgoing = pack_queries(
        suffix_lengths, request_group, suffix_queries, group_count, column_count, capacity
    )
    bias_rows = jnp.broadcast_to(up_bias[None, :], (16, up_bias.shape[0]))
    up_block = jnp.concatenate([up_weight, bias_rows], axis=0)
    up_cut, down_cut = up_weight.shape[0] // 2, down_weight.shape[0] // 2
    up_first, up_second = up_block[:up_cut], up_block[up_cut:]
    down_first, down_second = down_weight[:down_cut], down_weight[down_cut:]
    high_mask = high_masks[0]

    arrived = lax.all_to_all(
        outgoing.reshape(sources, capacity, part_width),
        ("grp", "dev"),
        split_axis=0,
        concat_axis=0,
        tiled=True,
    )
    up_low_first = swap(up_first, low_mask)
    up_high_first = swap(up_first, high_mask)
    up_core = swap(up_block, core_mask)
    down_core = swap(down_weight, core_mask)
    turned_keys = prefix_keys[0].T
    value_heads = prefix_values[0].reshape(-1, local_heads, HD).transpose(1, 0, 2)
    wide_values = jnp.concatenate([value_heads, jnp.ones_like(value_heads)], axis=2)
    own = attend_suffix(
        suffix_lengths, suffix_queries, suffix_keys, suffix_values, local_heads
    )
    (
        arrived,
        up_low_first,
        up_high_first,
        up_core,
        down_core,
        up_second,
        down_first,
        down_second,
        turned_keys,
        wide_values,
        own,
    ) = lax.optimization_barrier(
        (
            arrived,
            up_low_first,
            up_high_first,
            up_core,
            down_core,
            up_second,
            down_first,
            down_second,
            turned_keys,
            wide_values,
            own,
        )
    )

    counts = jnp.sum((arrived[:, :, 0] < EMPTY / 2).astype(jnp.int32), axis=1)
    answer_part = attend_prefix(counts, arrived, turned_keys, wide_values)
    up_low_second = swap(up_second, low_mask)
    up_high_second = swap(up_second, high_mask)
    down_low_first = swap(down_first, low_mask)
    down_high_first = swap(down_first, high_mask)
    (
        answer_part,
        up_low_second,
        up_high_second,
        down_low_first,
        down_high_first,
        down_second,
    ) = lax.optimization_barrier(
        (
            answer_part,
            up_low_second,
            up_high_second,
            down_low_first,
            down_high_first,
            down_second,
        )
    )

    answer = lax.all_to_all(
        answer_part, ("grp", "dev"), split_axis=0, concat_axis=0, tiled=True
    ).reshape(group_count, column_count, capacity + STAT_ROWS, part_width)
    up_high = jnp.concatenate([up_high_first, up_high_second], axis=0)
    up_low = jnp.concatenate([up_low_first, up_low_second], axis=0)
    down_high_second = swap(down_second, high_mask)
    up_cross = swap(up_high, low_mask)
    up_high_core = swap(up_high, core_mask)
    up_low_core = swap(up_low, core_mask)
    down_low_first_core = swap(down_low_first, core_mask)
    down_high = jnp.concatenate([down_high_first, down_high_second], axis=0)
    down_high_core = swap(down_high, core_mask)
    down_late = jnp.concatenate([down_second, down_high_second], axis=0)
    (
        answer,
        up_cross,
        up_high_core,
        up_low_core,
        down_low_first_core,
        down_high,
        down_high_core,
        down_late,
        down_low_first,
    ) = lax.optimization_barrier(
        (
            answer,
            up_cross,
            up_high_core,
            up_low_core,
            down_low_first_core,
            down_high,
            down_high_core,
            down_late,
            down_low_first,
        )
    )

    hidden_a, hidden_b, hidden = merge_parts(
        suffix_lengths, request_group, answer, *own, layer_input, attn_gain, attn_shift
    )

    (hidden_a, hidden_b, hidden), up_cross, down_late, down_low_first = lax.optimization_barrier(
        ((hidden_a, hidden_b, hidden), up_cross, down_late, down_low_first)
    )
    far_a = swap(hidden_a, far_mask)
    down_late = swap(down_late, low_mask)
    down_cross_first = swap(down_low_first, high_mask)
    far_a, hidden_b, hidden, up_cross = lax.optimization_barrier(
        (far_a, hidden_b, hidden, up_cross)
    )
    far_b = swap(hidden_b, far_mask)
    cross_a = swap(far_a, near_mask)
    near = swap(hidden, near_mask)
    up_cross_core = swap(up_cross, core_mask)
    far_b, cross_a, near, up_cross_core, down_late, down_cross_first = lax.optimization_barrier(
        (far_b, cross_a, near, up_cross_core, down_late, down_cross_first)
    )
    cross_b = swap(far_b, near_mask)
    down_late_core = swap(down_late, core_mask)
    down_cross_first_core = swap(down_cross_first, core_mask)

    up_rows, down_rows = up_block.shape[0], down_weight.shape[0]
    rest = down_rows - down_cut

    def whole(array):
        return [(array, 0, array.shape[0])]

    ups = {0: up_block, low_mask: up_low, high_mask: up_high, low_mask ^ high_mask: up_cross}
    up_cores = (up_core, up_low_core, up_high_core, up_cross_core)
    ups.update({core_mask ^ at: array for at, array in zip(list(ups), up_cores)})
    ups = {at: whole(array) for at, array in ups.items()}
    downs = {0: whole(down_weight), high_mask: whole(down_high)}
    downs[low_mask] = [(down_low_first, 0, down_cut), (down_late, 0, rest)]
    downs[low_mask ^ high_mask] = [(down_cross_first, 0, down_cut), (down_late, rest, rest)]
    downs[core_mask] = whole(down_core)
    downs[core_mask ^ high_mask] = whole(down_high_core)
    downs[core_mask ^ low_mask] = [(down_low_first_core, 0, down_cut), (down_late_core, 0, rest)]
    downs[core_mask ^ low_mask ^ high_mask] = [
        (down_cross_first_core, 0, down_cut),
        (down_late_core, rest, rest),
    ]
    ups = complete(ups, group_masks + column_masks)
    downs = complete(downs, group_masks + column_masks)
    order = sorted(ups)
    ups = [ups[mask] for mask in order]
    downs = [downs[mask] for mask in order]
    far_part_a, cross_part_a = feed_forward([far_a, cross_a], ups, downs)
    cross_b, far_part_a, cross_part_a = lax.optimization_barrier(
        (cross_b, far_part_a, cross_part_a)
    )
    cross_sum_a = swap(cross_part_a, near_mask)
    far_part_b, cross_part_b = feed_forward([far_b, cross_b], ups, downs)
    cross_sum_a, far_part_b, cross_part_b = lax.optimization_barrier(
        (cross_sum_a, far_part_b, cross_part_b)
    )
    cross_sum_b = swap(cross_part_b, near_mask)
    joined_a = add_rows(far_part_a, cross_sum_a)
    far_sum_a = swap(joined_a, far_mask)
    near, hidden = tie((near, hidden), joined_a)
    near_part, own_part = feed_forward([near, hidden], ups, downs)
    near_sum = swap(near_part, near_mask)
    cross_sum_b, near_part, far_sum_a = lax.optimization_barrier(
        (cross_sum_b, near_part, far_sum_a)
    )
    far_sum_b = swap(add_rows(far_part_b, cross_sum_b), far_mask)
    return finish_rows(
        hidden, own_part, near_sum, far_sum_a, far_sum_b, down_bias, out_gain, out_shift
    )


def solution(mesh):
    placed = (
        P(("grp", "dev"), None),
        P(("grp", "dev"), None),
        P(("grp", "dev"), None),
        P(("grp", "dev"), None),
        P(("grp", "dev"), None),
        P(("grp", "dev"), None),
        P("grp", None, "dev"),
        P("grp", None, "dev"),
        P(None, ("grp", "dev")),
        P(("grp", "dev")),
        P(("grp", "dev"), None),
        P(),
        P(),
        P(),
        P(),
        P(),
    )
    return jax.shard_map(
        on_device, mesh=mesh, in_specs=placed, out_specs=P(("grp", "dev"), None), check_vma=False
    )
```

```python
import functools
import math

import jax
import jax.numpy as jnp
from jax import lax
from jax.experimental import pallas as pl
from jax.experimental.pallas import tpu as pltpu
from jax.sharding import PartitionSpec as P

HD = 128
LANES = 128
STAT_ROWS = 8
STREAMS = 4
FETCHES = 8
UNROLL = 4
EMPTY = 64.0
ROW_BLOCK = 256
KEY_CHUNK = 1024

norm_eps = 1e-12
score_scale = HD ** (-0.5)
log2_e = math.log2(math.e)
mebibyte = 1024 * 1024


def layer_norm(summed, norm_gain, norm_shift):
    row_mean = jnp.mean(summed, axis=-1, keepdims=True)
    centred = summed - row_mean
    spread = jnp.mean(centred * centred, axis=-1, keepdims=True)
    return centred * lax.rsqrt(spread + norm_eps) * norm_gain + norm_shift


def vmem_spec():
    return pl.BlockSpec(memory_space=pltpu.VMEM)


def hbm_spec():
    return pl.BlockSpec(memory_space=pltpu.HBM)


def smem_spec():
    return pl.BlockSpec(memory_space=pltpu.SMEM)


def pack_kernel(lengths_ref, groups_ref, query_ref, out_ref, wide_ref):
    request_total = lengths_ref.shape[1]
    _, column_count, capacity, part_width = out_ref.shape
    slot_count = query_ref.shape[0]
    slot = lax.broadcasted_iota(jnp.int32, (capacity, LANES), 0)
    tiles = part_width // LANES
    for tile in range(wide_ref.shape[0]):
        wide_ref[tile, 0:slot_count, :] = query_ref[
            :, tile * LANES : (tile + 1) * LANES
        ].astype(jnp.float32)
        wide_ref[tile, slot_count : slot_count + capacity, :] = jnp.zeros(
            (capacity, LANES), jnp.float32
        )
    start = 0
    for request in range(request_total):
        group = groups_ref[0, request]
        filled = slot < lengths_ref[0, request]
        for column in range(column_count):
            for tile in range(tiles):
                rows = wide_ref[column * tiles + tile, pl.ds(start, capacity), :]
                rows = jnp.where(filled, rows, EMPTY)
                out_ref[group, column, :, tile * LANES : (tile + 1) * LANES] = rows.astype(
                    jnp.bfloat16
                )
        start = start + lengths_ref[0, request]


def pack_queries(lengths, groups, queries, group_count, column_count, capacity):
    slot_count, model_width = queries.shape
    part_width = model_width // column_count
    return pl.pallas_call(
        pack_kernel,
        out_shape=jax.ShapeDtypeStruct(
            (group_count, column_count, capacity, part_width), jnp.bfloat16
        ),
        in_specs=[smem_spec(), smem_spec(), vmem_spec()],
        out_specs=vmem_spec(),
        scratch_shapes=[
            pltpu.VMEM((model_width // LANES, slot_count + capacity, LANES), jnp.float32)
        ],
        compiler_params=pltpu.CompilerParams(vmem_limit_bytes=58 * mebibyte),
        name="pack_queries",
    )(lengths, groups, queries)


def far_kernel(
    counts_ref,
    arrived_ref,
    keys_hbm,
    values_hbm,
    out_ref,
    query_ref,
    answer_ref,
    stat_ref,
    turned_ref,
    score_ref,
    top_ref,
    keys_ref,
    values_ref,
    sems,
):
    key_step = keys_ref.shape[0] // FETCHES
    value_step = values_ref.shape[1] // FETCHES
    key_copies, value_copies = [], []
    for fetch in range(FETCHES):
        rows = pl.ds(fetch * key_step, key_step)
        key_copies.append(
            pltpu.make_async_copy(keys_hbm.at[rows], keys_ref.at[rows], sems.at[0, fetch])
        )
        rows = pl.ds(fetch * value_step, value_step)
        for head in range(values_ref.shape[0]):
            value_copies.append(
                pltpu.make_async_copy(
                    values_hbm.at[head, rows], values_ref.at[head, rows], sems.at[1 + head, fetch]
                )
            )
    for copy in key_copies + value_copies:
        copy.start()
    sources, capacity, part_width = arrived_ref.shape
    local_heads = part_width // HD
    key_total = keys_ref.shape[1]
    chunks = key_total // KEY_CHUNK

    def take(source, offset):
        for head in range(local_heads):
            rows = arrived_ref[source, :, head * HD : (head + 1) * HD].astype(jnp.float32)
            query_ref[head, pl.ds(offset, capacity), :] = rows
        return offset + counts_ref[source]

    total = lax.fori_loop(0, sources, take, jnp.int32(0), unroll=UNROLL)
    blocks = (total + ROW_BLOCK - 1) // ROW_BLOCK
    lane = lax.broadcasted_iota(jnp.int32, (ROW_BLOCK, LANES), 1)

    def block_rows(block):
        return pl.ds(pl.multiple_of(block * ROW_BLOCK, ROW_BLOCK), ROW_BLOCK)

    def load_queries(block, head):
        return query_ref[head, block_rows(block), :].astype(jnp.bfloat16)

    def score_chunk(rows, head, slot, chunk, part_top):
        columns = slice(chunk * KEY_CHUNK, (chunk + 1) * KEY_CHUNK)
        scores = jnp.dot(
            rows,
            keys_ref[head * HD : (head + 1) * HD, columns],
            preferred_element_type=jnp.float32,
        )
        score_ref[slot, :, columns] = scores
        for piece in range(KEY_CHUNK // LANES):
            part = scores[:, piece * LANES : (piece + 1) * LANES]
            part_top = part if part_top is None else jnp.maximum(part_top, part)
        return part_top

    def finish_top(part_top, slot):
        row_top = jnp.max(part_top, axis=1, keepdims=True) * score_scale
        row_top = row_top.astype(jnp.bfloat16).astype(jnp.float32)
        top_ref[slot] = jnp.broadcast_to(row_top, (ROW_BLOCK, LANES))

    def weigh_chunk(head, slot, chunk, shift):
        columns = slice(chunk * KEY_CHUNK, (chunk + 1) * KEY_CHUNK)
        weights = jnp.exp2(score_ref[slot, :, columns] * (score_scale * log2_e) - shift)
        return jnp.dot(
            weights.astype(jnp.bfloat16),
            values_ref[head, columns, :],
            preferred_element_type=jnp.float32,
        )

    def finish_answer(block, head, slot, mixed):
        rows = block_rows(block)
        row_sum = mixed[:, HD:]
        answer_ref[head, rows, :] = mixed[:, :HD] / row_sum
        top = top_ref[slot]
        if head == 0:
            stats = jnp.where(lane == 0, top, row_sum)
        else:
            stats = jnp.where(lane == head, top, stat_ref[...])
            stats = jnp.where(lane == local_heads + head, row_sum, stats)
        if head + 1 < local_heads:
            stat_ref[...] = stats
        else:
            for half in range(ROW_BLOCK // LANES):
                turned_ref[block * (ROW_BLOCK // LANES) + half] = jnp.transpose(
                    stats[half * LANES : (half + 1) * LANES]
                )[:STAT_ROWS, :]

    def slot_of(block, head):
        return (block * local_heads + head) % 2 if local_heads % 2 else head % 2

    for copy in key_copies:
        copy.wait()
    first_rows = load_queries(0, 0)
    part_top = None
    for chunk in range(chunks):
        part_top = score_chunk(first_rows, 0, 0, chunk, part_top)
    finish_top(part_top, 0)
    for copy in value_copies:
        copy.wait()

    def one_block(block, carry):
        for head in range(local_heads):
            slot = slot_of(block, head)
            if head + 1 < local_heads:
                next_block, next_head = block, head + 1
            else:
                next_block, next_head = jnp.minimum(block + 1, blocks - 1), 0
            next_slot = 1 - slot
            next_rows = load_queries(next_block, next_head)
            shift = top_ref[slot][:, 0:1] * log2_e
            part_top = None
            mixed = None
            for chunk in range(chunks):
                part_top = score_chunk(next_rows, next_head, next_slot, chunk, part_top)
                part = weigh_chunk(head, slot, chunk, shift)
                mixed = part if mixed is None else mixed + part
            finish_answer(block, head, slot, mixed)
            finish_top(part_top, next_slot)
        return carry

    lax.fori_loop(0, blocks, one_block, 0)

    def give(source, offset):
        rows = [answer_ref[head, pl.ds(offset, capacity), :] for head in range(local_heads)]
        tile = offset // LANES
        window = jnp.concatenate([turned_ref[tile], turned_ref[tile + 1]], axis=1)
        turned = pltpu.roll(window, (2 * LANES - offset % LANES) % (2 * LANES), 1)[:, :LANES]
        if part_width > LANES:
            turned = jnp.concatenate(
                [turned, jnp.zeros((STAT_ROWS, part_width - LANES), jnp.float32)], axis=1
            )
        rows = jnp.concatenate(rows, axis=1)
        out_ref[source] = jnp.concatenate([rows, turned], axis=0).astype(jnp.bfloat16)
        return offset + counts_ref[source]

    lax.fori_loop(0, sources, give, jnp.int32(0), unroll=UNROLL)


def attend_prefix(counts, arrived, turned_keys, wide_values):
    sources, capacity, part_width = arrived.shape
    local_heads = part_width // HD
    key_total = turned_keys.shape[1]
    row_total = -(-sources * capacity // ROW_BLOCK) * ROW_BLOCK + LANES
    return pl.pallas_call(
        far_kernel,
        out_shape=jax.ShapeDtypeStruct((sources, capacity + STAT_ROWS, part_width), jnp.bfloat16),
        in_specs=[smem_spec(), vmem_spec(), hbm_spec(), hbm_spec()],
        out_specs=vmem_spec(),
        scratch_shapes=[
            pltpu.VMEM((local_heads, row_total, HD), jnp.float32),
            pltpu.VMEM((local_heads, row_total, HD), jnp.float32),
            pltpu.VMEM((ROW_BLOCK, LANES), jnp.float32),
            pltpu.VMEM((row_total // LANES + 1, STAT_ROWS, LANES), jnp.float32),
            pltpu.VMEM((2, ROW_BLOCK, key_total), jnp.float32),
            pltpu.VMEM((2, ROW_BLOCK, LANES), jnp.float32),
            pltpu.VMEM(turned_keys.shape, jnp.bfloat16),
            pltpu.VMEM(wide_values.shape, jnp.bfloat16),
            pltpu.SemaphoreType.DMA((1 + local_heads, FETCHES)),
        ],
        compiler_params=pltpu.CompilerParams(vmem_limit_bytes=58 * mebibyte),
        cost_estimate=pl.CostEstimate(
            flops=4 * sources * capacity * key_total * part_width,
            bytes_accessed=8 * key_total * part_width,
            transcendentals=sources * capacity * key_total * local_heads,
        ),
        name="attend_prefix",
    )(counts, arrived, turned_keys, wide_values)


def stat_lane(head, local_heads):
    return (head // local_heads) * STAT_ROWS + head % local_heads


def own_kernel(local_heads, lengths_ref, query_ref, key_ref, value_ref, mixed_ref, top_ref, sum_ref):
    slot_count, model_width = query_ref.shape
    head_count = model_width // HD
    row = lax.broadcasted_iota(jnp.int32, (slot_count, slot_count), 0)
    column = lax.broadcasted_iota(jnp.int32, (slot_count, slot_count), 1)
    row_segment = jnp.zeros((slot_count, slot_count), jnp.int32)
    column_segment = jnp.zeros((slot_count, slot_count), jnp.int32)
    start = 0
    for request in range(lengths_ref.shape[1]):
        start = start + lengths_ref[0, request]
        row_segment = row_segment + (row >= start).astype(jnp.int32)
        column_segment = column_segment + (column >= start).astype(jnp.int32)
    visible = (row_segment == column_segment) & (column <= row)
    lane = lax.broadcasted_iota(jnp.int32, (slot_count, LANES), 1)
    tops = jnp.zeros((slot_count, LANES), jnp.float32)
    sums = jnp.ones((slot_count, LANES), jnp.float32)
    for head in range(head_count):
        columns = slice(head * HD, (head + 1) * HD)
        scores = (
            lax.dot_general(
                query_ref[:, columns],
                key_ref[:, columns],
                (((1,), (1,)), ((), ())),
                preferred_element_type=jnp.float32,
            )
            * score_scale
        )
        top = jnp.max(jnp.where(visible, scores, -jnp.inf), axis=1, keepdims=True)
        weights = jnp.where(visible, jnp.exp(scores - top), 0.0)
        mixed_ref[:, columns] = jnp.dot(
            weights.astype(jnp.bfloat16),
            value_ref[:, columns],
            preferred_element_type=jnp.float32,
        )
        at = stat_lane(head, local_heads)
        tops = jnp.where(lane == at, top, tops)
        sums = jnp.where(lane == at, jnp.sum(weights, axis=1, keepdims=True), sums)
    top_ref[...] = tops
    sum_ref[...] = sums


def attend_suffix(lengths, queries, keys, values, local_heads):
    slot_count, model_width = queries.shape
    stats = jax.ShapeDtypeStruct((slot_count, LANES), jnp.float32)
    return pl.pallas_call(
        functools.partial(own_kernel, local_heads),
        out_shape=(jax.ShapeDtypeStruct((slot_count, model_width), jnp.float32), stats, stats),
        in_specs=[smem_spec()] + [vmem_spec()] * 3,
        out_specs=(vmem_spec(), vmem_spec(), vmem_spec()),
        compiler_params=pltpu.CompilerParams(vmem_limit_bytes=16 * mebibyte),
        cost_estimate=pl.CostEstimate(
            flops=40 * slot_count * slot_count * model_width,
            bytes_accessed=8 * slot_count * model_width,
            transcendentals=slot_count * model_width,
        ),
        name="attend_suffix",
    )(lengths, queries, keys, values)


def merge_kernel(
    lengths_ref,
    groups_ref,
    arrived_ref,
    own_mixed_ref,
    own_top_ref,
    own_sum_ref,
    input_ref,
    gain_ref,
    shift_ref,
    first_ref,
    second_ref,
    hidden_ref,
    far_ref,
    stat_ref,
):
    _, column_count, chunk_rows, part_width = arrived_ref.shape
    slot_count, model_width = input_ref.shape
    capacity = chunk_rows - STAT_ROWS
    local_heads = part_width // HD
    head_count = model_width // HD
    start = 0
    for request in range(lengths_ref.shape[1]):
        group = groups_ref[0, request]
        pieces = []
        for column in range(column_count):
            block = arrived_ref[group, column].astype(jnp.float32)
            for head in range(local_heads):
                far_ref[column * local_heads + head, pl.ds(start, capacity), :] = block[
                    :capacity, head * HD : (head + 1) * HD
                ]
            pieces.append(block[capacity:, :LANES])
        if column_count * STAT_ROWS < LANES:
            pieces.append(jnp.zeros((LANES - column_count * STAT_ROWS, LANES), jnp.float32))
        turned = jnp.transpose(jnp.concatenate(pieces, axis=0))
        stat_ref[pl.ds(start, capacity), :] = turned[:capacity]
        start = start + lengths_ref[0, request]
    far_top = stat_ref[:slot_count, :]
    far_sum = pltpu.roll(far_top, LANES - local_heads, 1)
    own_top = own_top_ref[...]
    joint_top = jnp.maximum(far_top, own_top)
    far_weight = jnp.exp(far_top - joint_top) * far_sum
    own_weight = jnp.exp(own_top - joint_top)
    bottom = far_weight + own_weight * own_sum_ref[...]
    far_weight = far_weight / bottom
    own_weight = own_weight / bottom
    total = jnp.zeros((slot_count, LANES), jnp.float32)
    for head in range(head_count):
        columns = slice(head * HD, (head + 1) * HD)
        at = stat_lane(head, local_heads)
        summed = (
            input_ref[:, columns].astype(jnp.float32)
            + far_weight[:, at : at + 1] * far_ref[head, :slot_count, :]
            + own_weight[:, at : at + 1] * own_mixed_ref[:, columns]
        )
        far_ref[head, :slot_count, :] = summed
        total = total + summed
    row_mean = jnp.sum(total, axis=1, keepdims=True) * (1.0 / model_width)
    total = jnp.zeros((slot_count, LANES), jnp.float32)
    for head in range(head_count):
        centred = far_ref[head, :slot_count, :] - row_mean
        total = total + centred * centred
    spread = jnp.sum(total, axis=1, keepdims=True) * (1.0 / model_width)
    factor = lax.rsqrt(spread + norm_eps)
    for head in range(head_count):
        columns = slice(head * HD, (head + 1) * HD)
        centred = far_ref[head, :slot_count, :] - row_mean
        hidden = (centred * factor * gain_ref[:, columns] + shift_ref[:, columns]).astype(
            jnp.bfloat16
        )
        first_ref[:, columns] = hidden[: slot_count // 2]
        second_ref[:, columns] = hidden[slot_count // 2 :]
        hidden_ref[:, columns] = hidden


def merge_parts(lengths, groups, arrived, own_mixed, own_top, own_sum, layer_input, gain, shift):
    slot_count, model_width = layer_input.shape
    capacity = arrived.shape[2] - STAT_ROWS
    half = jax.ShapeDtypeStruct((slot_count // 2, model_width), jnp.bfloat16)
    return pl.pallas_call(
        merge_kernel,
        out_shape=(half, half, jax.ShapeDtypeStruct(layer_input.shape, jnp.bfloat16)),
        in_specs=[smem_spec(), smem_spec()] + [vmem_spec()] * 7,
        out_specs=(vmem_spec(), vmem_spec(), vmem_spec()),
        scratch_shapes=[
            pltpu.VMEM((model_width // HD, slot_count + capacity, HD), jnp.float32),
            pltpu.VMEM((slot_count + capacity, LANES), jnp.float32),
        ],
        compiler_params=pltpu.CompilerParams(vmem_limit_bytes=16 * mebibyte),
        name="merge_parts",
    )(
        lengths,
        groups,
        arrived,
        own_mixed,
        own_top,
        own_sum,
        layer_input,
        gain.reshape(1, model_width),
        shift.reshape(1, model_width),
    )


def swap(value, mask):
    total = lax.axis_size("grp") * lax.axis_size("dev")
    pairs = [(here, here ^ mask) for here in range(total)]
    return jax.tree.map(lambda leaf: lax.ppermute(leaf, ("grp", "dev"), pairs), value)


def swap_block(block, mask, sent):
    for array, _, _ in block:
        if (id(array), mask) not in sent:
            sent[id(array), mask] = (array, swap(array, mask))
    return [(sent[id(array), mask][1], begin, rows) for array, begin, rows in block]


def complete(held, masks):
    held, sent = dict(held), {}
    for mask in masks:
        for at in list(held):
            if mask ^ at not in held:
                held[mask ^ at] = swap_block(held[at], mask, sent)
    return held


def tie(values, after):
    return lax.optimization_barrier((values, after))[0]


def cut(height):
    step = max(height // STREAMS // 16, 1) * 16
    begins = [first for first in range(0, height, step)][:STREAMS]
    return [
        (first, (begins + [height])[at + 1] - first) for at, first in enumerate(begins)
    ]


def mlp_kernel(pieces, held_total, up_plan, down_plan, *refs):
    parts = len(up_plan)
    row_refs, refs = refs[:pieces], refs[pieces:]
    held_refs, refs = refs[:held_total], refs[held_total:]
    out_refs, (up_ref, down_ref, sems) = refs[:pieces], refs[pieces:]
    model_width = row_refs[0].shape[1]
    copies = []
    for part, block in enumerate(up_plan):
        begin, held = 0, []
        for piece, (at, skip, height) in enumerate(block):
            source = held_refs[at]
            for stream, (first, rows) in enumerate(cut(height)):
                held.append(
                    pltpu.make_async_copy(
                        source.at[pl.ds(skip + first, rows)],
                        up_ref.at[part, pl.ds(begin + first, rows)],
                        sems.at[part, 0, piece * STREAMS + stream],
                    )
                )
            begin += height
        copies.append(held)
    begin = 0
    for part, block in enumerate(down_plan):
        held = []
        for piece, (at, skip, height) in enumerate(block):
            source = held_refs[at]
            for stream, (first, rows) in enumerate(cut(height)):
                held.append(
                    pltpu.make_async_copy(
                        source.at[pl.ds(skip + first, rows)],
                        down_ref.at[pl.ds(begin + first, rows)],
                        sems.at[part, 1, piece * STREAMS + stream],
                    )
                )
            begin += height
        copies.append(held)
    for held in copies:
        for copy in held:
            copy.start()
    rows = jnp.concatenate([ref[...] for ref in row_refs], axis=0)
    activations = []
    for part in range(parts):
        for copy in copies[part]:
            copy.wait()
        product = jnp.dot(
            rows, up_ref[part, :model_width, :], preferred_element_type=jnp.float32
        )
        offset = up_ref[part, model_width:, :].astype(jnp.float32)[0:1]
        activations.append(jax.nn.gelu(product + offset, approximate=True).astype(jnp.bfloat16))
    for held in copies[parts:]:
        for copy in held:
            copy.wait()
    total = jnp.dot(
        jnp.concatenate(activations, axis=1), down_ref[...], preferred_element_type=jnp.float32
    ).astype(jnp.bfloat16)
    begin = 0
    for out_ref in out_refs:
        height = out_ref.shape[0]
        out_ref[...] = total[begin : begin + height]
        begin += height


def feed_forward(rows, ups, downs):
    pieces, parts = len(rows), len(ups)
    row_total, model_width = sum(piece.shape[0] for piece in rows), rows[0].shape[1]
    flat = []

    def plan(blocks):
        planned = []
        for block in blocks:
            entries = []
            for array, begin, height in block:
                places = [at for at, known in enumerate(flat) if known is array]
                if not places:
                    places = [len(flat)]
                    flat.append(array)
                entries.append((places[0], begin, height))
            planned.append(entries)
        return planned

    up_plan, down_plan = plan(ups), plan(downs)
    up_rows, down_rows = (sum(entry[2] for entry in held[0]) for held in (up_plan, down_plan))
    units = ups[0][0][0].shape[1]
    most = max(map(len, up_plan + down_plan))
    return pl.pallas_call(
        functools.partial(mlp_kernel, pieces, len(flat), up_plan, down_plan),
        out_shape=tuple(jax.ShapeDtypeStruct(piece.shape, jnp.bfloat16) for piece in rows),
        in_specs=[vmem_spec()] * pieces + [hbm_spec()] * len(flat),
        out_specs=tuple(vmem_spec() for _ in rows),
        scratch_shapes=[
            pltpu.VMEM((parts, up_rows, units), jnp.bfloat16),
            pltpu.VMEM((parts * down_rows, model_width), jnp.bfloat16),
            pltpu.SemaphoreType.DMA((parts, 2, most * STREAMS)),
        ],
        compiler_params=pltpu.CompilerParams(vmem_limit_bytes=58 * mebibyte),
        cost_estimate=pl.CostEstimate(
            flops=4 * row_total * model_width * parts * units,
            bytes_accessed=4 * parts * model_width * units,
            transcendentals=row_total * parts * units,
        ),
        name="feed_forward",
    )(*rows, *flat)


def add_rows(here, there):
    return (here.astype(jnp.float32) + there.astype(jnp.float32)).astype(jnp.bfloat16)


def finish_kernel(
    hidden_ref, own_ref, near_ref, far_a_ref, far_b_ref, bias_ref, gain_ref, shift_ref, out_ref
):
    height = far_a_ref.shape[0]
    for begin, far_ref in ((0, far_a_ref), (height, far_b_ref)):
        rows = slice(begin, begin + height)
        summed = hidden_ref[rows, :].astype(jnp.float32) + (
            own_ref[rows, :].astype(jnp.float32)
            + near_ref[rows, :].astype(jnp.float32)
            + far_ref[...].astype(jnp.float32)
        )
        out_ref[rows, :] = layer_norm(
            summed + bias_ref[...], gain_ref[...], shift_ref[...]
        ).astype(jnp.bfloat16)


def finish_rows(hidden, own, near, far_a, far_b, bias, gain, shift):
    model_width = hidden.shape[1]
    return pl.pallas_call(
        finish_kernel,
        out_shape=jax.ShapeDtypeStruct(hidden.shape, jnp.bfloat16),
        in_specs=[vmem_spec()] * 8,
        out_specs=vmem_spec(),
        compiler_params=pltpu.CompilerParams(vmem_limit_bytes=16 * mebibyte),
        name="finish_rows",
    )(
        hidden,
        own,
        near,
        far_a,
        far_b,
        bias.reshape(1, model_width),
        gain.reshape(1, model_width),
        shift.reshape(1, model_width),
    )


def on_device(
    suffix_queries,
    suffix_keys,
    suffix_values,
    layer_input,
    suffix_lengths,
    request_group,
    prefix_keys,
    prefix_values,
    up_weight,
    up_bias,
    down_weight,
    down_bias,
    attn_gain,
    attn_shift,
    out_gain,
    out_shift,
):
    slot_count, model_width = suffix_queries.shape
    group_count = lax.axis_size("grp")
    column_count = lax.axis_size("dev")
    part_width = model_width // column_count
    local_heads = part_width // HD
    capacity = 2 * slot_count // group_count
    sources = group_count * column_count

    near_mask = group_count // 2 * column_count
    far_mask = column_count // 2
    column_masks = [1 << bit for bit in range(far_mask.bit_length() - 1)]
    group_masks = [column_count << bit for bit in range((group_count // 2).bit_length() - 1)]

    low_mask, high_masks = column_masks[0], column_masks[1:]
    core_mask = group_masks[0]

    outgoing = pack_queries(
        suffix_lengths, request_group, suffix_queries, group_count, column_count, capacity
    )
    bias_rows = jnp.broadcast_to(up_bias[None, :], (16, up_bias.shape[0]))
    up_block = jnp.concatenate([up_weight, bias_rows], axis=0)
    up_cut, down_cut = up_weight.shape[0] // 2, down_weight.shape[0] // 2
    up_first, up_second = up_block[:up_cut], up_block[up_cut:]
    down_first, down_second = down_weight[:down_cut], down_weight[down_cut:]
    high_mask = high_masks[0]

    arrived = lax.all_to_all(
        outgoing.reshape(sources, capacity, part_width),
        ("grp", "dev"),
        split_axis=0,
        concat_axis=0,
        tiled=True,
    )
    up_low_first = swap(up_first, low_mask)
    up_high_first = swap(up_first, high_mask)
    up_core = swap(up_block, core_mask)
    down_core = swap(down_weight, core_mask)
    turned_keys = prefix_keys[0].T
    value_heads = prefix_values[0].reshape(-1, local_heads, HD).transpose(1, 0, 2)
    wide_values = jnp.concatenate([value_heads, jnp.ones_like(value_heads)], axis=2)
    own = attend_suffix(
        suffix_lengths, suffix_queries, suffix_keys, suffix_values, local_heads
    )
    (
        arrived,
        up_low_first,
        up_high_first,
        up_core,
        down_core,
        up_second,
        down_first,
        down_second,
        turned_keys,
        wide_values,
        own,
    ) = lax.optimization_barrier(
        (
            arrived,
            up_low_first,
            up_high_first,
            up_core,
            down_core,
            up_second,
            down_first,
            down_second,
            turned_keys,
            wide_values,
            own,
        )
    )

    counts = jnp.sum((arrived[:, :, 0] < EMPTY / 2).astype(jnp.int32), axis=1)
    answer_part = attend_prefix(counts, arrived, turned_keys, wide_values)
    up_low_second = swap(up_second, low_mask)
    up_high_second = swap(up_second, high_mask)
    down_low_first = swap(down_first, low_mask)
    down_high_first = swap(down_first, high_mask)
    (
        answer_part,
        up_low_second,
        up_high_second,
        down_low_first,
        down_high_first,
        down_second,
    ) = lax.optimization_barrier(
        (
            answer_part,
            up_low_second,
            up_high_second,
            down_low_first,
            down_high_first,
            down_second,
        )
    )

    answer = lax.all_to_all(
        answer_part, ("grp", "dev"), split_axis=0, concat_axis=0, tiled=True
    ).reshape(group_count, column_count, capacity + STAT_ROWS, part_width)
    up_high = jnp.concatenate([up_high_first, up_high_second], axis=0)
    up_low = jnp.concatenate([up_low_first, up_low_second], axis=0)
    down_high_second = swap(down_second, high_mask)
    up_cross = swap(up_high, low_mask)
    up_high_core = swap(up_high, core_mask)
    up_low_core = swap(up_low, core_mask)
    down_low_first_core = swap(down_low_first, core_mask)
    down_high = jnp.concatenate([down_high_first, down_high_second], axis=0)
    down_high_core = swap(down_high, core_mask)
    down_late = jnp.concatenate([down_second, down_high_second], axis=0)
    (
        answer,
        up_cross,
        up_high_core,
        up_low_core,
        down_low_first_core,
        down_high,
        down_high_core,
        down_late,
        down_low_first,
    ) = lax.optimization_barrier(
        (
            answer,
            up_cross,
            up_high_core,
            up_low_core,
            down_low_first_core,
            down_high,
            down_high_core,
            down_late,
            down_low_first,
        )
    )

    hidden_a, hidden_b, hidden = merge_parts(
        suffix_lengths, request_group, answer, *own, layer_input, attn_gain, attn_shift
    )

    (hidden_a, hidden_b, hidden), up_cross, down_late, down_low_first = lax.optimization_barrier(
        ((hidden_a, hidden_b, hidden), up_cross, down_late, down_low_first)
    )
    far_a = swap(hidden_a, far_mask)
    down_late = swap(down_late, low_mask)
    down_cross_first = swap(down_low_first, high_mask)
    far_b = swap(tie(hidden_b, far_a), far_mask)
    cross_a = swap(far_a, near_mask)
    near = swap(hidden, near_mask)
    up_cross_core = swap(up_cross, core_mask)
    far_b, cross_a, near, up_cross_core, down_late, down_cross_first = lax.optimization_barrier(
        (far_b, cross_a, near, up_cross_core, down_late, down_cross_first)
    )
    cross_b = swap(far_b, near_mask)
    down_late_core = swap(down_late, core_mask)
    down_cross_first_core = swap(down_cross_first, core_mask)

    up_rows, down_rows = up_block.shape[0], down_weight.shape[0]
    rest = down_rows - down_cut

    def whole(array):
        return [(array, 0, array.shape[0])]

    ups = {0: up_block, low_mask: up_low, high_mask: up_high, low_mask ^ high_mask: up_cross}
    up_cores = (up_core, up_low_core, up_high_core, up_cross_core)
    ups.update({core_mask ^ at: array for at, array in zip(list(ups), up_cores)})
    ups = {at: whole(array) for at, array in ups.items()}
    downs = {0: whole(down_weight), high_mask: whole(down_high)}
    downs[low_mask] = [(down_low_first, 0, down_cut), (down_late, 0, rest)]
    downs[low_mask ^ high_mask] = [(down_cross_first, 0, down_cut), (down_late, rest, rest)]
    downs[core_mask] = whole(down_core)
    downs[core_mask ^ high_mask] = whole(down_high_core)
    downs[core_mask ^ low_mask] = [(down_low_first_core, 0, down_cut), (down_late_core, 0, rest)]
    downs[core_mask ^ low_mask ^ high_mask] = [
        (down_cross_first_core, 0, down_cut),
        (down_late_core, rest, rest),
    ]
    ups = complete(ups, group_masks + column_masks)
    downs = complete(downs, group_masks + column_masks)
    order = sorted(ups)
    ups = [ups[mask] for mask in order]
    downs = [downs[mask] for mask in order]
    far_part_a, cross_part_a = feed_forward([far_a, cross_a], ups, downs)
    cross_b, far_part_a, cross_part_a = lax.optimization_barrier(
        (cross_b, far_part_a, cross_part_a)
    )
    cross_sum_a = swap(cross_part_a, near_mask)
    far_part_b, cross_part_b = feed_forward([far_b, cross_b], ups, downs)
    cross_sum_a, far_part_b, cross_part_b = lax.optimization_barrier(
        (cross_sum_a, far_part_b, cross_part_b)
    )
    cross_sum_b = swap(cross_part_b, near_mask)
    joined_a = add_rows(far_part_a, cross_sum_a)
    far_sum_a = swap(joined_a, far_mask)
    near, hidden = tie((near, hidden), joined_a)
    near_part, own_part = feed_forward([near, hidden], ups, downs)
    near_sum = swap(near_part, near_mask)
    cross_sum_b, near_part, far_sum_a = lax.optimization_barrier(
        (cross_sum_b, near_part, far_sum_a)
    )
    far_sum_b = swap(add_rows(far_part_b, cross_sum_b), far_mask)
    return finish_rows(
        hidden, own_part, near_sum, far_sum_a, far_sum_b, down_bias, out_gain, out_shift
    )


def solution(mesh):
    placed = (
        P(("grp", "dev"), None),
        P(("grp", "dev"), None),
        P(("grp", "dev"), None),
        P(("grp", "dev"), None),
        P(("grp", "dev"), None),
        P(("grp", "dev"), None),
        P("grp", None, "dev"),
        P("grp", None, "dev"),
        P(None, ("grp", "dev")),
        P(("grp", "dev")),
        P(("grp", "dev"), None),
        P(),
        P(),
        P(),
        P(),
        P(),
    )
    return jax.shard_map(
        on_device, mesh=mesh, in_specs=placed, out_specs=P(("grp", "dev"), None), check_vma=False
    )
```

```python
import functools
import math

import jax
import jax.numpy as jnp
from jax import lax
from jax.experimental import pallas as pl
from jax.experimental.pallas import tpu as pltpu
from jax.sharding import PartitionSpec as P

HD = 128
LANES = 128
STAT_ROWS = 8
STREAMS = 1
FETCHES = 8
UNROLL = 4
EMPTY = 64.0
ROW_BLOCK = 256
KEY_CHUNK = 1024

norm_eps = 1e-12
score_scale = HD ** (-0.5)
log2_e = math.log2(math.e)
mebibyte = 1024 * 1024


def layer_norm(summed, norm_gain, norm_shift):
    row_mean = jnp.mean(summed, axis=-1, keepdims=True)
    centred = summed - row_mean
    spread = jnp.mean(centred * centred, axis=-1, keepdims=True)
    return centred * lax.rsqrt(spread + norm_eps) * norm_gain + norm_shift


def vmem_spec():
    return pl.BlockSpec(memory_space=pltpu.VMEM)


def hbm_spec():
    return pl.BlockSpec(memory_space=pltpu.HBM)


def smem_spec():
    return pl.BlockSpec(memory_space=pltpu.SMEM)


def pack_kernel(lengths_ref, groups_ref, query_ref, out_ref, wide_ref):
    request_total = lengths_ref.shape[1]
    _, column_count, capacity, part_width = out_ref.shape
    slot_count = query_ref.shape[0]
    slot = lax.broadcasted_iota(jnp.int32, (capacity, LANES), 0)
    tiles = part_width // LANES
    for tile in range(wide_ref.shape[0]):
        wide_ref[tile, 0:slot_count, :] = query_ref[
            :, tile * LANES : (tile + 1) * LANES
        ].astype(jnp.float32)
        wide_ref[tile, slot_count : slot_count + capacity, :] = jnp.zeros(
            (capacity, LANES), jnp.float32
        )
    start = 0
    for request in range(request_total):
        group = groups_ref[0, request]
        filled = slot < lengths_ref[0, request]
        for column in range(column_count):
            for tile in range(tiles):
                rows = wide_ref[column * tiles + tile, pl.ds(start, capacity), :]
                rows = jnp.where(filled, rows, EMPTY)
                out_ref[group, column, :, tile * LANES : (tile + 1) * LANES] = rows.astype(
                    jnp.bfloat16
                )
        start = start + lengths_ref[0, request]


def pack_queries(lengths, groups, queries, group_count, column_count, capacity):
    slot_count, model_width = queries.shape
    part_width = model_width // column_count
    return pl.pallas_call(
        pack_kernel,
        out_shape=jax.ShapeDtypeStruct(
            (group_count, column_count, capacity, part_width), jnp.bfloat16
        ),
        in_specs=[smem_spec(), smem_spec(), vmem_spec()],
        out_specs=vmem_spec(),
        scratch_shapes=[
            pltpu.VMEM((model_width // LANES, slot_count + capacity, LANES), jnp.float32)
        ],
        compiler_params=pltpu.CompilerParams(vmem_limit_bytes=58 * mebibyte),
        name="pack_queries",
    )(lengths, groups, queries)


def far_kernel(
    counts_ref,
    arrived_ref,
    keys_hbm,
    values_hbm,
    out_ref,
    query_ref,
    answer_ref,
    stat_ref,
    turned_ref,
    score_ref,
    top_ref,
    keys_ref,
    values_ref,
    sems,
):
    key_step = keys_ref.shape[0] // FETCHES
    value_step = values_ref.shape[1] // FETCHES
    key_copies, value_copies = [], []
    for fetch in range(FETCHES):
        rows = pl.ds(fetch * key_step, key_step)
        key_copies.append(
            pltpu.make_async_copy(keys_hbm.at[rows], keys_ref.at[rows], sems.at[0, fetch])
        )
        rows = pl.ds(fetch * value_step, value_step)
        for head in range(values_ref.shape[0]):
            value_copies.append(
                pltpu.make_async_copy(
                    values_hbm.at[head, rows], values_ref.at[head, rows], sems.at[1 + head, fetch]
                )
            )
    for copy in key_copies + value_copies:
        copy.start()
    sources, capacity, part_width = arrived_ref.shape
    local_heads = part_width // HD
    key_total = keys_ref.shape[1]
    chunks = key_total // KEY_CHUNK

    def take(source, offset):
        for head in range(local_heads):
            rows = arrived_ref[source, :, head * HD : (head + 1) * HD].astype(jnp.float32)
            query_ref[head, pl.ds(offset, capacity), :] = rows
        return offset + counts_ref[source]

    total = lax.fori_loop(0, sources, take, jnp.int32(0), unroll=UNROLL)
    blocks = (total + ROW_BLOCK - 1) // ROW_BLOCK
    lane = lax.broadcasted_iota(jnp.int32, (ROW_BLOCK, LANES), 1)

    def block_rows(block):
        return pl.ds(pl.multiple_of(block * ROW_BLOCK, ROW_BLOCK), ROW_BLOCK)

    def load_queries(block, head):
        return query_ref[head, block_rows(block), :].astype(jnp.bfloat16)

    def score_chunk(rows, head, slot, chunk, part_top):
        columns = slice(chunk * KEY_CHUNK, (chunk + 1) * KEY_CHUNK)
        scores = jnp.dot(
            rows,
            keys_ref[head * HD : (head + 1) * HD, columns],
            preferred_element_type=jnp.float32,
        )
        score_ref[slot, :, columns] = scores
        for piece in range(KEY_CHUNK // LANES):
            part = scores[:, piece * LANES : (piece + 1) * LANES]
            part_top = part if part_top is None else jnp.maximum(part_top, part)
        return part_top

    def finish_top(part_top, slot):
        row_top = jnp.max(part_top, axis=1, keepdims=True) * score_scale
        row_top = row_top.astype(jnp.bfloat16).astype(jnp.float32)
        top_ref[slot] = jnp.broadcast_to(row_top, (ROW_BLOCK, LANES))

    def weigh_chunk(head, slot, chunk, shift):
        columns = slice(chunk * KEY_CHUNK, (chunk + 1) * KEY_CHUNK)
        weights = jnp.exp2(score_ref[slot, :, columns] * (score_scale * log2_e) - shift)
        return jnp.dot(
            weights.astype(jnp.bfloat16),
            values_ref[head, columns, :],
            preferred_element_type=jnp.float32,
        )

    def finish_answer(block, head, slot, mixed):
        rows = block_rows(block)
        row_sum = mixed[:, HD:]
        answer_ref[head, rows, :] = mixed[:, :HD] / row_sum
        top = top_ref[slot]
        if head == 0:
            stats = jnp.where(lane == 0, top, row_sum)
        else:
            stats = jnp.where(lane == head, top, stat_ref[...])
            stats = jnp.where(lane == local_heads + head, row_sum, stats)
        if head + 1 < local_heads:
            stat_ref[...] = stats
        else:
            for half in range(ROW_BLOCK // LANES):
                turned_ref[block * (ROW_BLOCK // LANES) + half] = jnp.transpose(
                    stats[half * LANES : (half + 1) * LANES]
                )[:STAT_ROWS, :]

    def slot_of(block, head):
        return (block * local_heads + head) % 2 if local_heads % 2 else head % 2

    for copy in key_copies:
        copy.wait()
    first_rows = load_queries(0, 0)
    part_top = None
    for chunk in range(chunks):
        part_top = score_chunk(first_rows, 0, 0, chunk, part_top)
    finish_top(part_top, 0)
    for copy in value_copies:
        copy.wait()

    def one_block(block, carry):
        for head in range(local_heads):
            slot = slot_of(block, head)
            if head + 1 < local_heads:
                next_block, next_head = block, head + 1
            else:
                next_block, next_head = jnp.minimum(block + 1, blocks - 1), 0
            next_slot = 1 - slot
            next_rows = load_queries(next_block, next_head)
            shift = top_ref[slot][:, 0:1] * log2_e
            part_top = None
            mixed = None
            for chunk in range(chunks):
                part_top = score_chunk(next_rows, next_head, next_slot, chunk, part_top)
                part = weigh_chunk(head, slot, chunk, shift)
                mixed = part if mixed is None else mixed + part
            finish_answer(block, head, slot, mixed)
            finish_top(part_top, next_slot)
        return carry

    lax.fori_loop(0, blocks, one_block, 0)

    def give(source, offset):
        rows = [answer_ref[head, pl.ds(offset, capacity), :] for head in range(local_heads)]
        tile = offset // LANES
        window = jnp.concatenate([turned_ref[tile], turned_ref[tile + 1]], axis=1)
        turned = pltpu.roll(window, (2 * LANES - offset % LANES) % (2 * LANES), 1)[:, :LANES]
        if part_width > LANES:
            turned = jnp.concatenate(
                [turned, jnp.zeros((STAT_ROWS, part_width - LANES), jnp.float32)], axis=1
            )
        rows = jnp.concatenate(rows, axis=1)
        out_ref[source] = jnp.concatenate([rows, turned], axis=0).astype(jnp.bfloat16)
        return offset + counts_ref[source]

    lax.fori_loop(0, sources, give, jnp.int32(0), unroll=UNROLL)


def attend_prefix(counts, arrived, turned_keys, wide_values):
    sources, capacity, part_width = arrived.shape
    local_heads = part_width // HD
    key_total = turned_keys.shape[1]
    row_total = -(-sources * capacity // ROW_BLOCK) * ROW_BLOCK + LANES
    return pl.pallas_call(
        far_kernel,
        out_shape=jax.ShapeDtypeStruct((sources, capacity + STAT_ROWS, part_width), jnp.bfloat16),
        in_specs=[smem_spec(), vmem_spec(), hbm_spec(), hbm_spec()],
        out_specs=vmem_spec(),
        scratch_shapes=[
            pltpu.VMEM((local_heads, row_total, HD), jnp.float32),
            pltpu.VMEM((local_heads, row_total, HD), jnp.float32),
            pltpu.VMEM((ROW_BLOCK, LANES), jnp.float32),
            pltpu.VMEM((row_total // LANES + 1, STAT_ROWS, LANES), jnp.float32),
            pltpu.VMEM((2, ROW_BLOCK, key_total), jnp.float32),
            pltpu.VMEM((2, ROW_BLOCK, LANES), jnp.float32),
            pltpu.VMEM(turned_keys.shape, jnp.bfloat16),
            pltpu.VMEM(wide_values.shape, jnp.bfloat16),
            pltpu.SemaphoreType.DMA((1 + local_heads, FETCHES)),
        ],
        compiler_params=pltpu.CompilerParams(vmem_limit_bytes=58 * mebibyte),
        cost_estimate=pl.CostEstimate(
            flops=4 * sources * capacity * key_total * part_width,
            bytes_accessed=8 * key_total * part_width,
            transcendentals=sources * capacity * key_total * local_heads,
        ),
        name="attend_prefix",
    )(counts, arrived, turned_keys, wide_values)


def stat_lane(head, local_heads):
    return (head // local_heads) * STAT_ROWS + head % local_heads


def own_kernel(local_heads, lengths_ref, query_ref, key_ref, value_ref, mixed_ref, top_ref, sum_ref):
    slot_count, model_width = query_ref.shape
    head_count = model_width // HD
    row = lax.broadcasted_iota(jnp.int32, (slot_count, slot_count), 0)
    column = lax.broadcasted_iota(jnp.int32, (slot_count, slot_count), 1)
    row_segment = jnp.zeros((slot_count, slot_count), jnp.int32)
    column_segment = jnp.zeros((slot_count, slot_count), jnp.int32)
    start = 0
    for request in range(lengths_ref.shape[1]):
        start = start + lengths_ref[0, request]
        row_segment = row_segment + (row >= start).astype(jnp.int32)
        column_segment = column_segment + (column >= start).astype(jnp.int32)
    visible = (row_segment == column_segment) & (column <= row)
    lane = lax.broadcasted_iota(jnp.int32, (slot_count, LANES), 1)
    tops = jnp.zeros((slot_count, LANES), jnp.float32)
    sums = jnp.ones((slot_count, LANES), jnp.float32)
    for head in range(head_count):
        columns = slice(head * HD, (head + 1) * HD)
        scores = (
            lax.dot_general(
                query_ref[:, columns],
                key_ref[:, columns],
                (((1,), (1,)), ((), ())),
                preferred_element_type=jnp.float32,
            )
            * score_scale
        )
        top = jnp.max(jnp.where(visible, scores, -jnp.inf), axis=1, keepdims=True)
        weights = jnp.where(visible, jnp.exp(scores - top), 0.0)
        mixed_ref[:, columns] = jnp.dot(
            weights.astype(jnp.bfloat16),
            value_ref[:, columns],
            preferred_element_type=jnp.float32,
        )
        at = stat_lane(head, local_heads)
        tops = jnp.where(lane == at, top, tops)
        sums = jnp.where(lane == at, jnp.sum(weights, axis=1, keepdims=True), sums)
    top_ref[...] = tops
    sum_ref[...] = sums


def attend_suffix(lengths, queries, keys, values, local_heads):
    slot_count, model_width = queries.shape
    stats = jax.ShapeDtypeStruct((slot_count, LANES), jnp.float32)
    return pl.pallas_call(
        functools.partial(own_kernel, local_heads),
        out_shape=(jax.ShapeDtypeStruct((slot_count, model_width), jnp.float32), stats, stats),
        in_specs=[smem_spec()] + [vmem_spec()] * 3,
        out_specs=(vmem_spec(), vmem_spec(), vmem_spec()),
        compiler_params=pltpu.CompilerParams(vmem_limit_bytes=16 * mebibyte),
        cost_estimate=pl.CostEstimate(
            flops=40 * slot_count * slot_count * model_width,
            bytes_accessed=8 * slot_count * model_width,
            transcendentals=slot_count * model_width,
        ),
        name="attend_suffix",
    )(lengths, queries, keys, values)


def merge_kernel(
    lengths_ref,
    groups_ref,
    arrived_ref,
    own_mixed_ref,
    own_top_ref,
    own_sum_ref,
    input_ref,
    gain_ref,
    shift_ref,
    first_ref,
    second_ref,
    hidden_ref,
    far_ref,
    stat_ref,
):
    _, column_count, chunk_rows, part_width = arrived_ref.shape
    slot_count, model_width = input_ref.shape
    capacity = chunk_rows - STAT_ROWS
    local_heads = part_width // HD
    head_count = model_width // HD
    start = 0
    for request in range(lengths_ref.shape[1]):
        group = groups_ref[0, request]
        pieces = []
        for column in range(column_count):
            block = arrived_ref[group, column].astype(jnp.float32)
            for head in range(local_heads):
                far_ref[column * local_heads + head, pl.ds(start, capacity), :] = block[
                    :capacity, head * HD : (head + 1) * HD
                ]
            pieces.append(block[capacity:, :LANES])
        if column_count * STAT_ROWS < LANES:
            pieces.append(jnp.zeros((LANES - column_count * STAT_ROWS, LANES), jnp.float32))
        turned = jnp.transpose(jnp.concatenate(pieces, axis=0))
        stat_ref[pl.ds(start, capacity), :] = turned[:capacity]
        start = start + lengths_ref[0, request]
    far_top = stat_ref[:slot_count, :]
    far_sum = pltpu.roll(far_top, LANES - local_heads, 1)
    own_top = own_top_ref[...]
    joint_top = jnp.maximum(far_top, own_top)
    far_weight = jnp.exp(far_top - joint_top) * far_sum
    own_weight = jnp.exp(own_top - joint_top)
    bottom = far_weight + own_weight * own_sum_ref[...]
    far_weight = far_weight / bottom
    own_weight = own_weight / bottom
    total = jnp.zeros((slot_count, LANES), jnp.float32)
    for head in range(head_count):
        columns = slice(head * HD, (head + 1) * HD)
        at = stat_lane(head, local_heads)
        summed = (
            input_ref[:, columns].astype(jnp.float32)
            + far_weight[:, at : at + 1] * far_ref[head, :slot_count, :]
            + own_weight[:, at : at + 1] * own_mixed_ref[:, columns]
        )
        far_ref[head, :slot_count, :] = summed
        total = total + summed
    row_mean = jnp.sum(total, axis=1, keepdims=True) * (1.0 / model_width)
    total = jnp.zeros((slot_count, LANES), jnp.float32)
    for head in range(head_count):
        centred = far_ref[head, :slot_count, :] - row_mean
        total = total + centred * centred
    spread = jnp.sum(total, axis=1, keepdims=True) * (1.0 / model_width)
    factor = lax.rsqrt(spread + norm_eps)
    for head in range(head_count):
        columns = slice(head * HD, (head + 1) * HD)
        centred = far_ref[head, :slot_count, :] - row_mean
        hidden = (centred * factor * gain_ref[:, columns] + shift_ref[:, columns]).astype(
            jnp.bfloat16
        )
        first_ref[:, columns] = hidden[: slot_count // 2]
        second_ref[:, columns] = hidden[slot_count // 2 :]
        hidden_ref[:, columns] = hidden


def merge_parts(lengths, groups, arrived, own_mixed, own_top, own_sum, layer_input, gain, shift):
    slot_count, model_width = layer_input.shape
    capacity = arrived.shape[2] - STAT_ROWS
    half = jax.ShapeDtypeStruct((slot_count // 2, model_width), jnp.bfloat16)
    return pl.pallas_call(
        merge_kernel,
        out_shape=(half, half, jax.ShapeDtypeStruct(layer_input.shape, jnp.bfloat16)),
        in_specs=[smem_spec(), smem_spec()] + [vmem_spec()] * 7,
        out_specs=(vmem_spec(), vmem_spec(), vmem_spec()),
        scratch_shapes=[
            pltpu.VMEM((model_width // HD, slot_count + capacity, HD), jnp.float32),
            pltpu.VMEM((slot_count + capacity, LANES), jnp.float32),
        ],
        compiler_params=pltpu.CompilerParams(vmem_limit_bytes=16 * mebibyte),
        name="merge_parts",
    )(
        lengths,
        groups,
        arrived,
        own_mixed,
        own_top,
        own_sum,
        layer_input,
        gain.reshape(1, model_width),
        shift.reshape(1, model_width),
    )


def swap(value, mask):
    total = lax.axis_size("grp") * lax.axis_size("dev")
    pairs = [(here, here ^ mask) for here in range(total)]
    return jax.tree.map(lambda leaf: lax.ppermute(leaf, ("grp", "dev"), pairs), value)


def swap_block(block, mask, sent):
    for array, _, _ in block:
        if (id(array), mask) not in sent:
            sent[id(array), mask] = (array, swap(array, mask))
    return [(sent[id(array), mask][1], begin, rows) for array, begin, rows in block]


def complete(held, masks):
    held, sent = dict(held), {}
    for mask in masks:
        for at in list(held):
            if mask ^ at not in held:
                held[mask ^ at] = swap_block(held[at], mask, sent)
    return held


def tie(values, after):
    return lax.optimization_barrier((values, after))[0]


def cut(height):
    step = max(height // STREAMS // 16, 1) * 16
    begins = [first for first in range(0, height, step)][:STREAMS]
    return [
        (first, (begins + [height])[at + 1] - first) for at, first in enumerate(begins)
    ]


def mlp_kernel(pieces, held_total, up_plan, down_plan, *refs):
    parts = len(up_plan)
    row_refs, refs = refs[:pieces], refs[pieces:]
    held_refs, refs = refs[:held_total], refs[held_total:]
    out_refs, (up_ref, down_ref, sems) = refs[:pieces], refs[pieces:]
    model_width = row_refs[0].shape[1]
    copies = []
    for part, block in enumerate(up_plan):
        begin, held = 0, []
        for piece, (at, skip, height) in enumerate(block):
            source = held_refs[at]
            for stream, (first, rows) in enumerate(cut(height)):
                held.append(
                    pltpu.make_async_copy(
                        source.at[pl.ds(skip + first, rows)],
                        up_ref.at[part, pl.ds(begin + first, rows)],
                        sems.at[part, 0, piece * STREAMS + stream],
                    )
                )
            begin += height
        copies.append(held)
    begin = 0
    for part, block in enumerate(down_plan):
        held = []
        for piece, (at, skip, height) in enumerate(block):
            source = held_refs[at]
            for stream, (first, rows) in enumerate(cut(height)):
                held.append(
                    pltpu.make_async_copy(
                        source.at[pl.ds(skip + first, rows)],
                        down_ref.at[pl.ds(begin + first, rows)],
                        sems.at[part, 1, piece * STREAMS + stream],
                    )
                )
            begin += height
        copies.append(held)
    for held in copies[:parts]:
        for copy in held:
            copy.start()
    rows = jnp.concatenate([ref[...] for ref in row_refs], axis=0)
    activations = []
    for part in range(parts):
        for copy in copies[part]:
            copy.wait()
        if part == 0:
            for held in copies[parts:]:
                for copy in held:
                    copy.start()
        product = jnp.dot(
            rows, up_ref[part, :model_width, :], preferred_element_type=jnp.float32
        )
        offset = up_ref[part, model_width:, :].astype(jnp.float32)[0:1]
        activations.append(jax.nn.gelu(product + offset, approximate=True).astype(jnp.bfloat16))
    for held in copies[parts:]:
        for copy in held:
            copy.wait()
    total = jnp.dot(
        jnp.concatenate(activations, axis=1), down_ref[...], preferred_element_type=jnp.float32
    ).astype(jnp.bfloat16)
    begin = 0
    for out_ref in out_refs:
        height = out_ref.shape[0]
        out_ref[...] = total[begin : begin + height]
        begin += height


def feed_forward(rows, ups, downs):
    pieces, parts = len(rows), len(ups)
    row_total, model_width = sum(piece.shape[0] for piece in rows), rows[0].shape[1]
    flat = []

    def plan(blocks):
        planned = []
        for block in blocks:
            entries = []
            for array, begin, height in block:
                places = [at for at, known in enumerate(flat) if known is array]
                if not places:
                    places = [len(flat)]
                    flat.append(array)
                entries.append((places[0], begin, height))
            planned.append(entries)
        return planned

    up_plan, down_plan = plan(ups), plan(downs)
    up_rows, down_rows = (sum(entry[2] for entry in held[0]) for held in (up_plan, down_plan))
    units = ups[0][0][0].shape[1]
    most = max(map(len, up_plan + down_plan))
    return pl.pallas_call(
        functools.partial(mlp_kernel, pieces, len(flat), up_plan, down_plan),
        out_shape=tuple(jax.ShapeDtypeStruct(piece.shape, jnp.bfloat16) for piece in rows),
        in_specs=[vmem_spec()] * pieces + [hbm_spec()] * len(flat),
        out_specs=tuple(vmem_spec() for _ in rows),
        scratch_shapes=[
            pltpu.VMEM((parts, up_rows, units), jnp.bfloat16),
            pltpu.VMEM((parts * down_rows, model_width), jnp.bfloat16),
            pltpu.SemaphoreType.DMA((parts, 2, most * STREAMS)),
        ],
        compiler_params=pltpu.CompilerParams(vmem_limit_bytes=58 * mebibyte),
        cost_estimate=pl.CostEstimate(
            flops=4 * row_total * model_width * parts * units,
            bytes_accessed=4 * parts * model_width * units,
            transcendentals=row_total * parts * units,
        ),
        name="feed_forward",
    )(*rows, *flat)


def add_rows(here, there):
    return (here.astype(jnp.float32) + there.astype(jnp.float32)).astype(jnp.bfloat16)


def finish_kernel(
    hidden_ref, own_ref, near_ref, far_a_ref, far_b_ref, bias_ref, gain_ref, shift_ref, out_ref
):
    height = far_a_ref.shape[0]
    for begin, far_ref in ((0, far_a_ref), (height, far_b_ref)):
        rows = slice(begin, begin + height)
        summed = hidden_ref[rows, :].astype(jnp.float32) + (
            own_ref[rows, :].astype(jnp.float32)
            + near_ref[rows, :].astype(jnp.float32)
            + far_ref[...].astype(jnp.float32)
        )
        out_ref[rows, :] = layer_norm(
            summed + bias_ref[...], gain_ref[...], shift_ref[...]
        ).astype(jnp.bfloat16)


def finish_rows(hidden, own, near, far_a, far_b, bias, gain, shift):
    model_width = hidden.shape[1]
    return pl.pallas_call(
        finish_kernel,
        out_shape=jax.ShapeDtypeStruct(hidden.shape, jnp.bfloat16),
        in_specs=[vmem_spec()] * 8,
        out_specs=vmem_spec(),
        compiler_params=pltpu.CompilerParams(vmem_limit_bytes=16 * mebibyte),
        name="finish_rows",
    )(
        hidden,
        own,
        near,
        far_a,
        far_b,
        bias.reshape(1, model_width),
        gain.reshape(1, model_width),
        shift.reshape(1, model_width),
    )


def on_device(
    suffix_queries,
    suffix_keys,
    suffix_values,
    layer_input,
    suffix_lengths,
    request_group,
    prefix_keys,
    prefix_values,
    up_weight,
    up_bias,
    down_weight,
    down_bias,
    attn_gain,
    attn_shift,
    out_gain,
    out_shift,
):
    slot_count, model_width = suffix_queries.shape
    group_count = lax.axis_size("grp")
    column_count = lax.axis_size("dev")
    part_width = model_width // column_count
    local_heads = part_width // HD
    capacity = 2 * slot_count // group_count
    sources = group_count * column_count

    near_mask = group_count // 2 * column_count
    far_mask = column_count // 2
    column_masks = [1 << bit for bit in range(far_mask.bit_length() - 1)]
    group_masks = [column_count << bit for bit in range((group_count // 2).bit_length() - 1)]

    low_mask, high_masks = column_masks[0], column_masks[1:]
    core_mask = group_masks[0]

    outgoing = pack_queries(
        suffix_lengths, request_group, suffix_queries, group_count, column_count, capacity
    )
    bias_rows = jnp.broadcast_to(up_bias[None, :], (16, up_bias.shape[0]))
    up_block = jnp.concatenate([up_weight, bias_rows], axis=0)
    up_cut, down_cut = up_weight.shape[0] // 2, down_weight.shape[0] // 2
    up_first, up_second = up_block[:up_cut], up_block[up_cut:]
    down_first, down_second = down_weight[:down_cut], down_weight[down_cut:]
    high_mask = high_masks[0]

    arrived = lax.all_to_all(
        outgoing.reshape(sources, capacity, part_width),
        ("grp", "dev"),
        split_axis=0,
        concat_axis=0,
        tiled=True,
    )
    up_low_first = swap(up_first, low_mask)
    up_high_first = swap(up_first, high_mask)
    up_core = swap(up_block, core_mask)
    down_core = swap(down_weight, core_mask)
    turned_keys = prefix_keys[0].T
    value_heads = prefix_values[0].reshape(-1, local_heads, HD).transpose(1, 0, 2)
    wide_values = jnp.concatenate([value_heads, jnp.ones_like(value_heads)], axis=2)
    own = attend_suffix(
        suffix_lengths, suffix_queries, suffix_keys, suffix_values, local_heads
    )
    (
        arrived,
        up_low_first,
        up_high_first,
        up_core,
        down_core,
        up_second,
        down_first,
        down_second,
        turned_keys,
        wide_values,
        own,
    ) = lax.optimization_barrier(
        (
            arrived,
            up_low_first,
            up_high_first,
            up_core,
            down_core,
            up_second,
            down_first,
            down_second,
            turned_keys,
            wide_values,
            own,
        )
    )

    counts = jnp.sum((arrived[:, :, 0] < EMPTY / 2).astype(jnp.int32), axis=1)
    answer_part = attend_prefix(counts, arrived, turned_keys, wide_values)
    up_low_second = swap(up_second, low_mask)
    up_high_second = swap(up_second, high_mask)
    down_low_first = swap(down_first, low_mask)
    down_high_first = swap(down_first, high_mask)
    (
        answer_part,
        up_low_second,
        up_high_second,
        down_low_first,
        down_high_first,
        down_second,
    ) = lax.optimization_barrier(
        (
            answer_part,
            up_low_second,
            up_high_second,
            down_low_first,
            down_high_first,
            down_second,
        )
    )

    answer = lax.all_to_all(
        answer_part, ("grp", "dev"), split_axis=0, concat_axis=0, tiled=True
    ).reshape(group_count, column_count, capacity + STAT_ROWS, part_width)
    up_high = jnp.concatenate([up_high_first, up_high_second], axis=0)
    down_high_second = swap(down_second, high_mask)
    up_low = jnp.concatenate(tie([up_low_first, up_low_second], down_high_second), axis=0)
    up_cross = swap(up_high, low_mask)
    up_high_core = swap(up_high, core_mask)
    up_low_core = swap(up_low, core_mask)
    down_low_first_core = swap(down_low_first, core_mask)
    down_high = jnp.concatenate([down_high_first, down_high_second], axis=0)
    down_high_core = swap(down_high, core_mask)
    down_late = jnp.concatenate([down_second, down_high_second], axis=0)
    (
        answer,
        up_cross,
        up_high_core,
        up_low_core,
        down_low_first_core,
        down_high,
        down_high_core,
        down_late,
        down_low_first,
    ) = lax.optimization_barrier(
        (
            answer,
            up_cross,
            up_high_core,
            up_low_core,
            down_low_first_core,
            down_high,
            down_high_core,
            down_late,
            down_low_first,
        )
    )

    hidden_a, hidden_b, hidden = merge_parts(
        suffix_lengths, request_group, answer, *own, layer_input, attn_gain, attn_shift
    )

    (hidden_a, hidden_b, hidden), up_cross, down_late, down_low_first = lax.optimization_barrier(
        ((hidden_a, hidden_b, hidden), up_cross, down_late, down_low_first)
    )
    far_a = swap(hidden_a, far_mask)
    down_late = swap(down_late, low_mask)
    down_cross_first = swap(down_low_first, high_mask)
    far_b = swap(tie(hidden_b, far_a), far_mask)
    cross_a = swap(far_a, near_mask)
    near = swap(hidden, near_mask)
    up_cross_core = swap(up_cross, core_mask)
    far_b, cross_a, near, up_cross_core, down_late, down_cross_first = lax.optimization_barrier(
        (far_b, cross_a, near, up_cross_core, down_late, down_cross_first)
    )
    cross_b = swap(far_b, near_mask)
    down_late_core = swap(down_late, core_mask)
    down_cross_first_core = swap(down_cross_first, core_mask)

    up_rows, down_rows = up_block.shape[0], down_weight.shape[0]
    rest = down_rows - down_cut

    def whole(array):
        return [(array, 0, array.shape[0])]

    ups = {0: up_block, low_mask: up_low, high_mask: up_high, low_mask ^ high_mask: up_cross}
    up_cores = (up_core, up_low_core, up_high_core, up_cross_core)
    ups.update({core_mask ^ at: array for at, array in zip(list(ups), up_cores)})
    ups = {at: whole(array) for at, array in ups.items()}
    downs = {0: whole(down_weight), high_mask: whole(down_high)}
    downs[low_mask] = [(down_low_first, 0, down_cut), (down_late, 0, rest)]
    downs[low_mask ^ high_mask] = [(down_cross_first, 0, down_cut), (down_late, rest, rest)]
    downs[core_mask] = whole(down_core)
    downs[core_mask ^ high_mask] = whole(down_high_core)
    downs[core_mask ^ low_mask] = [(down_low_first_core, 0, down_cut), (down_late_core, 0, rest)]
    downs[core_mask ^ low_mask ^ high_mask] = [
        (down_cross_first_core, 0, down_cut),
        (down_late_core, rest, rest),
    ]
    ups = complete(ups, group_masks + column_masks)
    downs = complete(downs, group_masks + column_masks)
    order = sorted(ups)
    ups = [ups[mask] for mask in order]
    downs = [downs[mask] for mask in order]
    far_part_a, cross_part_a = feed_forward([far_a, cross_a], ups, downs)
    cross_b, far_part_a, cross_part_a = lax.optimization_barrier(
        (cross_b, far_part_a, cross_part_a)
    )
    cross_sum_a = swap(cross_part_a, near_mask)
    far_part_b, cross_part_b = feed_forward([far_b, cross_b], ups, downs)
    cross_sum_a, far_part_b, cross_part_b = lax.optimization_barrier(
        (cross_sum_a, far_part_b, cross_part_b)
    )
    cross_sum_b = swap(cross_part_b, near_mask)
    joined_a = add_rows(far_part_a, cross_sum_a)
    far_sum_a = swap(joined_a, far_mask)
    near, hidden = tie((near, hidden), joined_a)
    near_part, own_part = feed_forward([near, hidden], ups, downs)
    near_sum = swap(near_part, near_mask)
    cross_sum_b, near_part, far_sum_a = lax.optimization_barrier(
        (cross_sum_b, near_part, far_sum_a)
    )
    far_sum_b = swap(add_rows(far_part_b, cross_sum_b), far_mask)
    return finish_rows(
        hidden, own_part, near_sum, far_sum_a, far_sum_b, down_bias, out_gain, out_shift
    )


def solution(mesh):
    placed = (
        P(("grp", "dev"), None),
        P(("grp", "dev"), None),
        P(("grp", "dev"), None),
        P(("grp", "dev"), None),
        P(("grp", "dev"), None),
        P(("grp", "dev"), None),
        P("grp", None, "dev"),
        P("grp", None, "dev"),
        P(None, ("grp", "dev")),
        P(("grp", "dev")),
        P(("grp", "dev"), None),
        P(),
        P(),
        P(),
        P(),
        P(),
    )
    return jax.shard_map(
        on_device, mesh=mesh, in_specs=placed, out_specs=P(("grp", "dev"), None), check_vma=False
    )
```

```python
import functools
import math

import jax
import jax.numpy as jnp
from jax import lax
from jax.experimental import pallas as pl
from jax.experimental.pallas import tpu as pltpu
from jax.sharding import PartitionSpec as P

HD = 128
LANES = 128
STAT_ROWS = 8
STREAMS = 1
FETCHES = 8
UNROLL = 4
EMPTY = 64.0
ROW_BLOCK = 256
KEY_CHUNK = 1024

norm_eps = 1e-12
score_scale = HD ** (-0.5)
log2_e = math.log2(math.e)
mebibyte = 1024 * 1024


def layer_norm(summed, norm_gain, norm_shift):
    row_mean = jnp.mean(summed, axis=-1, keepdims=True)
    centred = summed - row_mean
    spread = jnp.mean(centred * centred, axis=-1, keepdims=True)
    return centred * lax.rsqrt(spread + norm_eps) * norm_gain + norm_shift


def vmem_spec():
    return pl.BlockSpec(memory_space=pltpu.VMEM)


def hbm_spec():
    return pl.BlockSpec(memory_space=pltpu.HBM)


def smem_spec():
    return pl.BlockSpec(memory_space=pltpu.SMEM)


def pack_kernel(lengths_ref, groups_ref, query_ref, out_ref, wide_ref):
    request_total = lengths_ref.shape[1]
    _, column_count, capacity, part_width = out_ref.shape
    slot_count = query_ref.shape[0]
    slot = lax.broadcasted_iota(jnp.int32, (capacity, LANES), 0)
    tiles = part_width // LANES
    for tile in range(wide_ref.shape[0]):
        wide_ref[tile, 0:slot_count, :] = query_ref[
            :, tile * LANES : (tile + 1) * LANES
        ].astype(jnp.float32)
        wide_ref[tile, slot_count : slot_count + capacity, :] = jnp.zeros(
            (capacity, LANES), jnp.float32
        )
    start = 0
    for request in range(request_total):
        group = groups_ref[0, request]
        filled = slot < lengths_ref[0, request]
        for column in range(column_count):
            for tile in range(tiles):
                rows = wide_ref[column * tiles + tile, pl.ds(start, capacity), :]
                rows = jnp.where(filled, rows, EMPTY)
                out_ref[group, column, :, tile * LANES : (tile + 1) * LANES] = rows.astype(
                    jnp.bfloat16
                )
        start = start + lengths_ref[0, request]


def pack_queries(lengths, groups, queries, group_count, column_count, capacity):
    slot_count, model_width = queries.shape
    part_width = model_width // column_count
    return pl.pallas_call(
        pack_kernel,
        out_shape=jax.ShapeDtypeStruct(
            (group_count, column_count, capacity, part_width), jnp.bfloat16
        ),
        in_specs=[smem_spec(), smem_spec(), vmem_spec()],
        out_specs=vmem_spec(),
        scratch_shapes=[
            pltpu.VMEM((model_width // LANES, slot_count + capacity, LANES), jnp.float32)
        ],
        compiler_params=pltpu.CompilerParams(vmem_limit_bytes=58 * mebibyte),
        name="pack_queries",
    )(lengths, groups, queries)


def far_kernel(
    counts_ref,
    arrived_ref,
    keys_hbm,
    values_hbm,
    out_ref,
    query_ref,
    answer_ref,
    stat_ref,
    turned_ref,
    score_ref,
    top_ref,
    keys_ref,
    values_ref,
    sems,
):
    key_step = keys_ref.shape[0] // FETCHES
    value_step = values_ref.shape[1] // FETCHES
    key_copies, value_copies = [], []
    for fetch in range(FETCHES):
        rows = pl.ds(fetch * key_step, key_step)
        key_copies.append(
            pltpu.make_async_copy(keys_hbm.at[rows], keys_ref.at[rows], sems.at[0, fetch])
        )
        rows = pl.ds(fetch * value_step, value_step)
        for head in range(values_ref.shape[0]):
            value_copies.append(
                pltpu.make_async_copy(
                    values_hbm.at[head, rows], values_ref.at[head, rows], sems.at[1 + head, fetch]
                )
            )
    for copy in key_copies + value_copies:
        copy.start()
    sources, capacity, part_width = arrived_ref.shape
    local_heads = part_width // HD
    key_total = keys_ref.shape[1]
    chunks = key_total // KEY_CHUNK

    def take(source, offset):
        for head in range(local_heads):
            rows = arrived_ref[source, :, head * HD : (head + 1) * HD].astype(jnp.float32)
            query_ref[head, pl.ds(offset, capacity), :] = rows
        return offset + counts_ref[source]

    total = lax.fori_loop(0, sources, take, jnp.int32(0), unroll=UNROLL)
    blocks = (total + ROW_BLOCK - 1) // ROW_BLOCK
    lane = lax.broadcasted_iota(jnp.int32, (ROW_BLOCK, LANES), 1)

    def block_rows(block):
        return pl.ds(pl.multiple_of(block * ROW_BLOCK, ROW_BLOCK), ROW_BLOCK)

    def load_queries(block, head):
        return query_ref[head, block_rows(block), :].astype(jnp.bfloat16)

    def score_chunk(rows, head, slot, chunk, part_top):
        columns = slice(chunk * KEY_CHUNK, (chunk + 1) * KEY_CHUNK)
        scores = jnp.dot(
            rows,
            keys_ref[head * HD : (head + 1) * HD, columns],
            preferred_element_type=jnp.float32,
        )
        score_ref[slot, :, columns] = scores
        for piece in range(KEY_CHUNK // LANES):
            part = scores[:, piece * LANES : (piece + 1) * LANES]
            part_top = part if part_top is None else jnp.maximum(part_top, part)
        return part_top

    def finish_top(part_top, slot):
        row_top = jnp.max(part_top, axis=1, keepdims=True) * score_scale
        row_top = row_top.astype(jnp.bfloat16).astype(jnp.float32)
        top_ref[slot] = jnp.broadcast_to(row_top, (ROW_BLOCK, LANES))

    def weigh_chunk(head, slot, chunk, shift):
        columns = slice(chunk * KEY_CHUNK, (chunk + 1) * KEY_CHUNK)
        weights = jnp.exp2(score_ref[slot, :, columns] * (score_scale * log2_e) - shift)
        return jnp.dot(
            weights.astype(jnp.bfloat16),
            values_ref[head, columns, :],
            preferred_element_type=jnp.float32,
        )

    def finish_answer(block, head, slot, mixed):
        rows = block_rows(block)
        row_sum = mixed[:, HD:]
        answer_ref[head, rows, :] = mixed[:, :HD] / row_sum
        top = top_ref[slot]
        if head == 0:
            stats = jnp.where(lane == 0, top, row_sum)
        else:
            stats = jnp.where(lane == head, top, stat_ref[...])
            stats = jnp.where(lane == local_heads + head, row_sum, stats)
        if head + 1 < local_heads:
            stat_ref[...] = stats
        else:
            for half in range(ROW_BLOCK // LANES):
                turned_ref[block * (ROW_BLOCK // LANES) + half] = jnp.transpose(
                    stats[half * LANES : (half + 1) * LANES]
                )[:STAT_ROWS, :]

    def slot_of(block, head):
        return (block * local_heads + head) % 2 if local_heads % 2 else head % 2

    for copy in key_copies:
        copy.wait()
    first_rows = load_queries(0, 0)
    part_top = None
    for chunk in range(chunks):
        part_top = score_chunk(first_rows, 0, 0, chunk, part_top)
    finish_top(part_top, 0)
    for copy in value_copies:
        copy.wait()

    def one_block(block, carry):
        for head in range(local_heads):
            slot = slot_of(block, head)
            if head + 1 < local_heads:
                next_block, next_head = block, head + 1
            else:
                next_block, next_head = jnp.minimum(block + 1, blocks - 1), 0
            next_slot = 1 - slot
            next_rows = load_queries(next_block, next_head)
            shift = top_ref[slot][:, 0:1] * log2_e
            part_top = None
            mixed = None
            for chunk in range(chunks):
                part_top = score_chunk(next_rows, next_head, next_slot, chunk, part_top)
                part = weigh_chunk(head, slot, chunk, shift)
                mixed = part if mixed is None else mixed + part
            finish_answer(block, head, slot, mixed)
            finish_top(part_top, next_slot)
        return carry

    lax.fori_loop(0, blocks, one_block, 0)

    def give(source, offset):
        rows = [answer_ref[head, pl.ds(offset, capacity), :] for head in range(local_heads)]
        tile = offset // LANES
        window = jnp.concatenate([turned_ref[tile], turned_ref[tile + 1]], axis=1)
        turned = pltpu.roll(window, (2 * LANES - offset % LANES) % (2 * LANES), 1)[:, :LANES]
        if part_width > LANES:
            turned = jnp.concatenate(
                [turned, jnp.zeros((STAT_ROWS, part_width - LANES), jnp.float32)], axis=1
            )
        rows = jnp.concatenate(rows, axis=1)
        out_ref[source] = jnp.concatenate([rows, turned], axis=0).astype(jnp.bfloat16)
        return offset + counts_ref[source]

    lax.fori_loop(0, sources, give, jnp.int32(0), unroll=UNROLL)


def attend_prefix(counts, arrived, turned_keys, wide_values):
    sources, capacity, part_width = arrived.shape
    local_heads = part_width // HD
    key_total = turned_keys.shape[1]
    row_total = -(-sources * capacity // ROW_BLOCK) * ROW_BLOCK + LANES
    return pl.pallas_call(
        far_kernel,
        out_shape=jax.ShapeDtypeStruct((sources, capacity + STAT_ROWS, part_width), jnp.bfloat16),
        in_specs=[smem_spec(), vmem_spec(), hbm_spec(), hbm_spec()],
        out_specs=vmem_spec(),
        scratch_shapes=[
            pltpu.VMEM((local_heads, row_total, HD), jnp.float32),
            pltpu.VMEM((local_heads, row_total, HD), jnp.float32),
            pltpu.VMEM((ROW_BLOCK, LANES), jnp.float32),
            pltpu.VMEM((row_total // LANES + 1, STAT_ROWS, LANES), jnp.float32),
            pltpu.VMEM((2, ROW_BLOCK, key_total), jnp.float32),
            pltpu.VMEM((2, ROW_BLOCK, LANES), jnp.float32),
            pltpu.VMEM(turned_keys.shape, jnp.bfloat16),
            pltpu.VMEM(wide_values.shape, jnp.bfloat16),
            pltpu.SemaphoreType.DMA((1 + local_heads, FETCHES)),
        ],
        compiler_params=pltpu.CompilerParams(vmem_limit_bytes=58 * mebibyte),
        cost_estimate=pl.CostEstimate(
            flops=4 * sources * capacity * key_total * part_width,
            bytes_accessed=8 * key_total * part_width,
            transcendentals=sources * capacity * key_total * local_heads,
        ),
        name="attend_prefix",
    )(counts, arrived, turned_keys, wide_values)


def stat_lane(head, local_heads):
    return (head // local_heads) * STAT_ROWS + head % local_heads


def own_kernel(local_heads, lengths_ref, query_ref, key_ref, value_ref, mixed_ref, top_ref, sum_ref):
    slot_count, model_width = query_ref.shape
    head_count = model_width // HD
    row = lax.broadcasted_iota(jnp.int32, (slot_count, slot_count), 0)
    column = lax.broadcasted_iota(jnp.int32, (slot_count, slot_count), 1)
    row_segment = jnp.zeros((slot_count, slot_count), jnp.int32)
    column_segment = jnp.zeros((slot_count, slot_count), jnp.int32)
    start = 0
    for request in range(lengths_ref.shape[1]):
        start = start + lengths_ref[0, request]
        row_segment = row_segment + (row >= start).astype(jnp.int32)
        column_segment = column_segment + (column >= start).astype(jnp.int32)
    visible = (row_segment == column_segment) & (column <= row)
    lane = lax.broadcasted_iota(jnp.int32, (slot_count, LANES), 1)
    tops = jnp.zeros((slot_count, LANES), jnp.float32)
    sums = jnp.ones((slot_count, LANES), jnp.float32)
    for head in range(head_count):
        columns = slice(head * HD, (head + 1) * HD)
        scores = (
            lax.dot_general(
                query_ref[:, columns],
                key_ref[:, columns],
                (((1,), (1,)), ((), ())),
                preferred_element_type=jnp.float32,
            )
            * score_scale
        )
        top = jnp.max(jnp.where(visible, scores, -jnp.inf), axis=1, keepdims=True)
        weights = jnp.where(visible, jnp.exp(scores - top), 0.0)
        mixed_ref[:, columns] = jnp.dot(
            weights.astype(jnp.bfloat16),
            value_ref[:, columns],
            preferred_element_type=jnp.float32,
        )
        at = stat_lane(head, local_heads)
        tops = jnp.where(lane == at, top, tops)
        sums = jnp.where(lane == at, jnp.sum(weights, axis=1, keepdims=True), sums)
    top_ref[...] = tops
    sum_ref[...] = sums


def attend_suffix(lengths, queries, keys, values, local_heads):
    slot_count, model_width = queries.shape
    stats = jax.ShapeDtypeStruct((slot_count, LANES), jnp.float32)
    return pl.pallas_call(
        functools.partial(own_kernel, local_heads),
        out_shape=(jax.ShapeDtypeStruct((slot_count, model_width), jnp.float32), stats, stats),
        in_specs=[smem_spec()] + [vmem_spec()] * 3,
        out_specs=(vmem_spec(), vmem_spec(), vmem_spec()),
        compiler_params=pltpu.CompilerParams(vmem_limit_bytes=16 * mebibyte),
        cost_estimate=pl.CostEstimate(
            flops=40 * slot_count * slot_count * model_width,
            bytes_accessed=8 * slot_count * model_width,
            transcendentals=slot_count * model_width,
        ),
        name="attend_suffix",
    )(lengths, queries, keys, values)


def merge_kernel(
    lengths_ref,
    groups_ref,
    arrived_ref,
    own_mixed_ref,
    own_top_ref,
    own_sum_ref,
    input_ref,
    gain_ref,
    shift_ref,
    first_ref,
    second_ref,
    hidden_ref,
    far_ref,
    stat_ref,
):
    _, column_count, chunk_rows, part_width = arrived_ref.shape
    slot_count, model_width = input_ref.shape
    capacity = chunk_rows - STAT_ROWS
    local_heads = part_width // HD
    head_count = model_width // HD
    start = 0
    for request in range(lengths_ref.shape[1]):
        group = groups_ref[0, request]
        pieces = []
        for column in range(column_count):
            block = arrived_ref[group, column].astype(jnp.float32)
            for head in range(local_heads):
                far_ref[column * local_heads + head, pl.ds(start, capacity), :] = block[
                    :capacity, head * HD : (head + 1) * HD
                ]
            pieces.append(block[capacity:, :LANES])
        if column_count * STAT_ROWS < LANES:
            pieces.append(jnp.zeros((LANES - column_count * STAT_ROWS, LANES), jnp.float32))
        turned = jnp.transpose(jnp.concatenate(pieces, axis=0))
        stat_ref[pl.ds(start, capacity), :] = turned[:capacity]
        start = start + lengths_ref[0, request]
    far_top = stat_ref[:slot_count, :]
    far_sum = pltpu.roll(far_top, LANES - local_heads, 1)
    own_top = own_top_ref[...]
    joint_top = jnp.maximum(far_top, own_top)
    far_weight = jnp.exp(far_top - joint_top) * far_sum
    own_weight = jnp.exp(own_top - joint_top)
    bottom = far_weight + own_weight * own_sum_ref[...]
    far_weight = far_weight / bottom
    own_weight = own_weight / bottom
    total = jnp.zeros((slot_count, LANES), jnp.float32)
    for head in range(head_count):
        columns = slice(head * HD, (head + 1) * HD)
        at = stat_lane(head, local_heads)
        summed = (
            input_ref[:, columns].astype(jnp.float32)
            + far_weight[:, at : at + 1] * far_ref[head, :slot_count, :]
            + own_weight[:, at : at + 1] * own_mixed_ref[:, columns]
        )
        far_ref[head, :slot_count, :] = summed
        total = total + summed
    row_mean = jnp.sum(total, axis=1, keepdims=True) * (1.0 / model_width)
    total = jnp.zeros((slot_count, LANES), jnp.float32)
    for head in range(head_count):
        centred = far_ref[head, :slot_count, :] - row_mean
        total = total + centred * centred
    spread = jnp.sum(total, axis=1, keepdims=True) * (1.0 / model_width)
    factor = lax.rsqrt(spread + norm_eps)
    for head in range(head_count):
        columns = slice(head * HD, (head + 1) * HD)
        centred = far_ref[head, :slot_count, :] - row_mean
        hidden = (centred * factor * gain_ref[:, columns] + shift_ref[:, columns]).astype(
            jnp.bfloat16
        )
        first_ref[:, columns] = hidden[: slot_count // 2]
        second_ref[:, columns] = hidden[slot_count // 2 :]
        hidden_ref[:, columns] = hidden


def merge_parts(lengths, groups, arrived, own_mixed, own_top, own_sum, layer_input, gain, shift):
    slot_count, model_width = layer_input.shape
    capacity = arrived.shape[2] - STAT_ROWS
    half = jax.ShapeDtypeStruct((slot_count // 2, model_width), jnp.bfloat16)
    return pl.pallas_call(
        merge_kernel,
        out_shape=(half, half, jax.ShapeDtypeStruct(layer_input.shape, jnp.bfloat16)),
        in_specs=[smem_spec(), smem_spec()] + [vmem_spec()] * 7,
        out_specs=(vmem_spec(), vmem_spec(), vmem_spec()),
        scratch_shapes=[
            pltpu.VMEM((model_width // HD, slot_count + capacity, HD), jnp.float32),
            pltpu.VMEM((slot_count + capacity, LANES), jnp.float32),
        ],
        compiler_params=pltpu.CompilerParams(vmem_limit_bytes=16 * mebibyte),
        name="merge_parts",
    )(
        lengths,
        groups,
        arrived,
        own_mixed,
        own_top,
        own_sum,
        layer_input,
        gain.reshape(1, model_width),
        shift.reshape(1, model_width),
    )


def swap(value, mask):
    total = lax.axis_size("grp") * lax.axis_size("dev")
    pairs = [(here, here ^ mask) for here in range(total)]
    return jax.tree.map(lambda leaf: lax.ppermute(leaf, ("grp", "dev"), pairs), value)


def swap_block(block, mask, sent):
    for array, _, _ in block:
        if (id(array), mask) not in sent:
            sent[id(array), mask] = (array, swap(array, mask))
    return [(sent[id(array), mask][1], begin, rows) for array, begin, rows in block]


def complete(held, masks):
    held, sent = dict(held), {}
    for mask in masks:
        for at in list(held):
            if mask ^ at not in held:
                held[mask ^ at] = swap_block(held[at], mask, sent)
    return held


def tie(values, after):
    return lax.optimization_barrier((values, after))[0]


def cut(height):
    step = max(height // STREAMS // 16, 1) * 16
    begins = [first for first in range(0, height, step)][:STREAMS]
    return [
        (first, (begins + [height])[at + 1] - first) for at, first in enumerate(begins)
    ]


def mlp_kernel(pieces, held_total, up_plan, down_plan, *refs):
    parts = len(up_plan)
    row_refs, refs = refs[:pieces], refs[pieces:]
    held_refs, refs = refs[:held_total], refs[held_total:]
    out_refs, (up_ref, down_ref, sems) = refs[:pieces], refs[pieces:]
    model_width = row_refs[0].shape[1]
    copies = []
    for part, block in enumerate(up_plan):
        begin, held = 0, []
        for piece, (at, skip, height) in enumerate(block):
            source = held_refs[at]
            for stream, (first, rows) in enumerate(cut(height)):
                held.append(
                    pltpu.make_async_copy(
                        source.at[pl.ds(skip + first, rows)],
                        up_ref.at[part, pl.ds(begin + first, rows)],
                        sems.at[part, 0, piece * STREAMS + stream],
                    )
                )
            begin += height
        copies.append(held)
    begin = 0
    for part, block in enumerate(down_plan):
        held = []
        for piece, (at, skip, height) in enumerate(block):
            source = held_refs[at]
            for stream, (first, rows) in enumerate(cut(height)):
                held.append(
                    pltpu.make_async_copy(
                        source.at[pl.ds(skip + first, rows)],
                        down_ref.at[pl.ds(begin + first, rows)],
                        sems.at[part, 1, piece * STREAMS + stream],
                    )
                )
            begin += height
        copies.append(held)
    for held in copies[:parts]:
        for copy in held:
            copy.start()
    rows = jnp.concatenate([ref[...] for ref in row_refs], axis=0)
    activations = []
    for part in range(parts):
        for copy in copies[part]:
            copy.wait()
        if part == 0:
            for held in copies[parts:]:
                for copy in held:
                    copy.start()
        product = jnp.dot(
            rows, up_ref[part, :model_width, :], preferred_element_type=jnp.float32
        )
        offset = up_ref[part, model_width:, :].astype(jnp.float32)[0:1]
        activations.append(jax.nn.gelu(product + offset, approximate=True).astype(jnp.bfloat16))
    for held in copies[parts:]:
        for copy in held:
            copy.wait()
    total = jnp.dot(
        jnp.concatenate(activations, axis=1), down_ref[...], preferred_element_type=jnp.float32
    ).astype(jnp.bfloat16)
    begin = 0
    for out_ref in out_refs:
        height = out_ref.shape[0]
        out_ref[...] = total[begin : begin + height]
        begin += height


def feed_forward(rows, ups, downs):
    pieces, parts = len(rows), len(ups)
    row_total, model_width = sum(piece.shape[0] for piece in rows), rows[0].shape[1]
    flat = []

    def plan(blocks):
        planned = []
        for block in blocks:
            entries = []
            for array, begin, height in block:
                places = [at for at, known in enumerate(flat) if known is array]
                if not places:
                    places = [len(flat)]
                    flat.append(array)
                entries.append((places[0], begin, height))
            planned.append(entries)
        return planned

    up_plan, down_plan = plan(ups), plan(downs)
    up_rows, down_rows = (sum(entry[2] for entry in held[0]) for held in (up_plan, down_plan))
    units = ups[0][0][0].shape[1]
    most = max(map(len, up_plan + down_plan))
    return pl.pallas_call(
        functools.partial(mlp_kernel, pieces, len(flat), up_plan, down_plan),
        out_shape=tuple(jax.ShapeDtypeStruct(piece.shape, jnp.bfloat16) for piece in rows),
        in_specs=[vmem_spec()] * pieces + [hbm_spec()] * len(flat),
        out_specs=tuple(vmem_spec() for _ in rows),
        scratch_shapes=[
            pltpu.VMEM((parts, up_rows, units), jnp.bfloat16),
            pltpu.VMEM((parts * down_rows, model_width), jnp.bfloat16),
            pltpu.SemaphoreType.DMA((parts, 2, most * STREAMS)),
        ],
        compiler_params=pltpu.CompilerParams(vmem_limit_bytes=58 * mebibyte),
        cost_estimate=pl.CostEstimate(
            flops=4 * row_total * model_width * parts * units,
            bytes_accessed=4 * parts * model_width * units,
            transcendentals=row_total * parts * units,
        ),
        name="feed_forward",
    )(*rows, *flat)


def add_rows(here, there):
    return (here.astype(jnp.float32) + there.astype(jnp.float32)).astype(jnp.bfloat16)


def finish_kernel(
    hidden_ref, own_ref, near_ref, far_a_ref, far_b_ref, bias_ref, gain_ref, shift_ref, out_ref
):
    height = far_a_ref.shape[0]
    for begin, far_ref in ((0, far_a_ref), (height, far_b_ref)):
        rows = slice(begin, begin + height)
        summed = hidden_ref[rows, :].astype(jnp.float32) + (
            own_ref[rows, :].astype(jnp.float32)
            + near_ref[rows, :].astype(jnp.float32)
            + far_ref[...].astype(jnp.float32)
        )
        out_ref[rows, :] = layer_norm(
            summed + bias_ref[...], gain_ref[...], shift_ref[...]
        ).astype(jnp.bfloat16)


def finish_rows(hidden, own, near, far_a, far_b, bias, gain, shift):
    model_width = hidden.shape[1]
    return pl.pallas_call(
        finish_kernel,
        out_shape=jax.ShapeDtypeStruct(hidden.shape, jnp.bfloat16),
        in_specs=[vmem_spec()] * 8,
        out_specs=vmem_spec(),
        compiler_params=pltpu.CompilerParams(vmem_limit_bytes=16 * mebibyte),
        name="finish_rows",
    )(
        hidden,
        own,
        near,
        far_a,
        far_b,
        bias.reshape(1, model_width),
        gain.reshape(1, model_width),
        shift.reshape(1, model_width),
    )


def on_device(
    suffix_queries,
    suffix_keys,
    suffix_values,
    layer_input,
    suffix_lengths,
    request_group,
    prefix_keys,
    prefix_values,
    up_weight,
    up_bias,
    down_weight,
    down_bias,
    attn_gain,
    attn_shift,
    out_gain,
    out_shift,
):
    slot_count, model_width = suffix_queries.shape
    group_count = lax.axis_size("grp")
    column_count = lax.axis_size("dev")
    part_width = model_width // column_count
    local_heads = part_width // HD
    capacity = 2 * slot_count // group_count
    sources = group_count * column_count

    near_mask = group_count // 2 * column_count
    far_mask = column_count // 2
    column_masks = [1 << bit for bit in range(far_mask.bit_length() - 1)]
    group_masks = [column_count << bit for bit in range((group_count // 2).bit_length() - 1)]

    low_mask, high_masks = column_masks[0], column_masks[1:]
    core_mask = group_masks[0]

    outgoing = pack_queries(
        suffix_lengths, request_group, suffix_queries, group_count, column_count, capacity
    )
    bias_rows = jnp.broadcast_to(up_bias[None, :], (16, up_bias.shape[0]))
    up_block = jnp.concatenate([up_weight, bias_rows], axis=0)
    up_cut, down_cut = up_weight.shape[0] // 2, down_weight.shape[0] // 2
    up_first, up_second = up_block[:up_cut], up_block[up_cut:]
    down_first, down_second = down_weight[:down_cut], down_weight[down_cut:]
    high_mask = high_masks[0]

    arrived = lax.all_to_all(
        outgoing.reshape(sources, capacity, part_width),
        ("grp", "dev"),
        split_axis=0,
        concat_axis=0,
        tiled=True,
    )
    up_low_first = swap(up_first, low_mask)
    up_high_first = swap(up_first, high_mask)
    up_core = swap(up_block, core_mask)
    down_core = swap(down_weight, core_mask)
    turned_keys = prefix_keys[0].T
    value_heads = prefix_values[0].reshape(-1, local_heads, HD).transpose(1, 0, 2)
    wide_values = jnp.concatenate([value_heads, jnp.ones_like(value_heads)], axis=2)
    own = attend_suffix(
        suffix_lengths, suffix_queries, suffix_keys, suffix_values, local_heads
    )
    (
        arrived,
        up_low_first,
        up_high_first,
        up_core,
        down_core,
        up_second,
        down_first,
        down_second,
        turned_keys,
        wide_values,
        own,
    ) = lax.optimization_barrier(
        (
            arrived,
            up_low_first,
            up_high_first,
            up_core,
            down_core,
            up_second,
            down_first,
            down_second,
            turned_keys,
            wide_values,
            own,
        )
    )

    counts = jnp.sum((arrived[:, :, 0] < EMPTY / 2).astype(jnp.int32), axis=1)
    answer_part = attend_prefix(counts, arrived, turned_keys, wide_values)
    up_low_second = swap(up_second, low_mask)
    up_high_second = swap(up_second, high_mask)
    down_low_first = swap(down_first, low_mask)
    down_high_first = swap(down_first, high_mask)
    (
        answer_part,
        up_low_second,
        up_high_second,
        down_low_first,
        down_high_first,
        down_second,
    ) = lax.optimization_barrier(
        (
            answer_part,
            up_low_second,
            up_high_second,
            down_low_first,
            down_high_first,
            down_second,
        )
    )

    answer = lax.all_to_all(
        answer_part, ("grp", "dev"), split_axis=0, concat_axis=0, tiled=True
    ).reshape(group_count, column_count, capacity + STAT_ROWS, part_width)
    up_high = jnp.concatenate([up_high_first, up_high_second], axis=0)
    down_high_second = swap(down_second, high_mask)
    up_low = jnp.concatenate(tie([up_low_first, up_low_second], down_high_second), axis=0)
    up_cross = swap(up_high, low_mask)
    up_high_core = swap(up_high, core_mask)
    up_low_core = swap(up_low, core_mask)
    down_low_first_core = swap(down_low_first, core_mask)
    down_cross_first = swap(tie(down_low_first, down_high_second), high_mask)
    down_high = jnp.concatenate([down_high_first, down_high_second], axis=0)
    down_high_core = swap(down_high, core_mask)
    down_late = jnp.concatenate([down_second, down_high_second], axis=0)
    (
        answer,
        up_cross,
        up_high_core,
        up_low_core,
        down_low_first_core,
        down_high,
        down_high_core,
        down_late,
        down_cross_first,
    ) = lax.optimization_barrier(
        (
            answer,
            up_cross,
            up_high_core,
            up_low_core,
            down_low_first_core,
            down_high,
            down_high_core,
            down_late,
            down_cross_first,
        )
    )

    hidden_a, hidden_b, hidden = merge_parts(
        suffix_lengths, request_group, answer, *own, layer_input, attn_gain, attn_shift
    )

    (hidden_a, hidden_b, hidden), up_cross, down_late = lax.optimization_barrier(
        ((hidden_a, hidden_b, hidden), up_cross, down_late)
    )
    far_a = swap(hidden_a, far_mask)
    down_late = swap(down_late, low_mask)
    far_b = swap(tie(hidden_b, far_a), far_mask)
    cross_a = swap(far_a, near_mask)
    near = swap(hidden, near_mask)
    up_cross_core = swap(up_cross, core_mask)
    far_b, cross_a, near, up_cross_core, down_late, down_cross_first = lax.optimization_barrier(
        (far_b, cross_a, near, up_cross_core, down_late, down_cross_first)
    )
    cross_b = swap(far_b, near_mask)
    down_late_core = swap(down_late, core_mask)
    down_cross_first_core = swap(down_cross_first, core_mask)

    up_rows, down_rows = up_block.shape[0], down_weight.shape[0]
    rest = down_rows - down_cut

    def whole(array):
        return [(array, 0, array.shape[0])]

    ups = {0: up_block, low_mask: up_low, high_mask: up_high, low_mask ^ high_mask: up_cross}
    up_cores = (up_core, up_low_core, up_high_core, up_cross_core)
    ups.update({core_mask ^ at: array for at, array in zip(list(ups), up_cores)})
    ups = {at: whole(array) for at, array in ups.items()}
    downs = {0: whole(down_weight), high_mask: whole(down_high)}
    downs[low_mask] = [(down_low_first, 0, down_cut), (down_late, 0, rest)]
    downs[low_mask ^ high_mask] = [(down_cross_first, 0, down_cut), (down_late, rest, rest)]
    downs[core_mask] = whole(down_core)
    downs[core_mask ^ high_mask] = whole(down_high_core)
    downs[core_mask ^ low_mask] = [(down_low_first_core, 0, down_cut), (down_late_core, 0, rest)]
    downs[core_mask ^ low_mask ^ high_mask] = [
        (down_cross_first_core, 0, down_cut),
        (down_late_core, rest, rest),
    ]
    ups = complete(ups, group_masks + column_masks)
    downs = complete(downs, group_masks + column_masks)
    order = sorted(ups)
    ups = [ups[mask] for mask in order]
    downs = [downs[mask] for mask in order]
    far_part_a, cross_part_a = feed_forward([far_a, cross_a], ups, downs)
    cross_b, far_part_a, cross_part_a = lax.optimization_barrier(
        (cross_b, far_part_a, cross_part_a)
    )
    cross_sum_a = swap(cross_part_a, near_mask)
    far_part_b, cross_part_b = feed_forward([far_b, cross_b], ups, downs)
    cross_sum_a, far_part_b, cross_part_b = lax.optimization_barrier(
        (cross_sum_a, far_part_b, cross_part_b)
    )
    cross_sum_b = swap(cross_part_b, near_mask)
    joined_a = add_rows(far_part_a, cross_sum_a)
    far_sum_a = swap(joined_a, far_mask)
    near, hidden = tie((near, hidden), joined_a)
    near_part, own_part = feed_forward([near, hidden], ups, downs)
    near_sum = swap(near_part, near_mask)
    cross_sum_b, near_part, far_sum_a = lax.optimization_barrier(
        (cross_sum_b, near_part, far_sum_a)
    )
    far_sum_b = swap(add_rows(far_part_b, cross_sum_b), far_mask)
    return finish_rows(
        hidden, own_part, near_sum, far_sum_a, far_sum_b, down_bias, out_gain, out_shift
    )


def solution(mesh):
    placed = (
        P(("grp", "dev"), None),
        P(("grp", "dev"), None),
        P(("grp", "dev"), None),
        P(("grp", "dev"), None),
        P(("grp", "dev"), None),
        P(("grp", "dev"), None),
        P("grp", None, "dev"),
        P("grp", None, "dev"),
        P(None, ("grp", "dev")),
        P(("grp", "dev")),
        P(("grp", "dev"), None),
        P(),
        P(),
        P(),
        P(),
        P(),
    )
    return jax.shard_map(
        on_device, mesh=mesh, in_specs=placed, out_specs=P(("grp", "dev"), None), check_vma=False
    )
```

```python
import functools
import math

import jax
import jax.numpy as jnp
from jax import lax
from jax.experimental import pallas as pl
from jax.experimental.pallas import tpu as pltpu
from jax.sharding import PartitionSpec as P

HD = 128
LANES = 128
STAT_ROWS = 8
STREAMS = 1
FETCHES = 8
UNROLL = 4
EMPTY = 64.0
ROW_BLOCK = 256
KEY_CHUNK = 1024

norm_eps = 1e-12
score_scale = HD ** (-0.5)
log2_e = math.log2(math.e)
mebibyte = 1024 * 1024


def layer_norm(summed, norm_gain, norm_shift):
    row_mean = jnp.mean(summed, axis=-1, keepdims=True)
    centred = summed - row_mean
    spread = jnp.mean(centred * centred, axis=-1, keepdims=True)
    return centred * lax.rsqrt(spread + norm_eps) * norm_gain + norm_shift


def vmem_spec():
    return pl.BlockSpec(memory_space=pltpu.VMEM)


def hbm_spec():
    return pl.BlockSpec(memory_space=pltpu.HBM)


def smem_spec():
    return pl.BlockSpec(memory_space=pltpu.SMEM)


def pack_kernel(lengths_ref, groups_ref, query_ref, out_ref, wide_ref):
    request_total = lengths_ref.shape[1]
    _, column_count, capacity, part_width = out_ref.shape
    slot_count = query_ref.shape[0]
    slot = lax.broadcasted_iota(jnp.int32, (capacity, LANES), 0)
    tiles = part_width // LANES
    for tile in range(wide_ref.shape[0]):
        wide_ref[tile, 0:slot_count, :] = query_ref[
            :, tile * LANES : (tile + 1) * LANES
        ].astype(jnp.float32)
        wide_ref[tile, slot_count : slot_count + capacity, :] = jnp.zeros(
            (capacity, LANES), jnp.float32
        )
    start = 0
    for request in range(request_total):
        group = groups_ref[0, request]
        filled = slot < lengths_ref[0, request]
        for column in range(column_count):
            for tile in range(tiles):
                rows = wide_ref[column * tiles + tile, pl.ds(start, capacity), :]
                rows = jnp.where(filled, rows, EMPTY)
                out_ref[group, column, :, tile * LANES : (tile + 1) * LANES] = rows.astype(
                    jnp.bfloat16
                )
        start = start + lengths_ref[0, request]


def pack_queries(lengths, groups, queries, group_count, column_count, capacity):
    slot_count, model_width = queries.shape
    part_width = model_width // column_count
    return pl.pallas_call(
        pack_kernel,
        out_shape=jax.ShapeDtypeStruct(
            (group_count, column_count, capacity, part_width), jnp.bfloat16
        ),
        in_specs=[smem_spec(), smem_spec(), vmem_spec()],
        out_specs=vmem_spec(),
        scratch_shapes=[
            pltpu.VMEM((model_width // LANES, slot_count + capacity, LANES), jnp.float32)
        ],
        compiler_params=pltpu.CompilerParams(vmem_limit_bytes=58 * mebibyte),
        name="pack_queries",
    )(lengths, groups, queries)


def far_kernel(
    counts_ref,
    arrived_ref,
    keys_hbm,
    values_hbm,
    out_ref,
    query_ref,
    answer_ref,
    stat_ref,
    turned_ref,
    score_ref,
    top_ref,
    keys_ref,
    values_ref,
    sems,
):
    key_step = keys_ref.shape[0] // FETCHES
    value_step = values_ref.shape[1] // FETCHES
    key_copies, value_copies = [], []
    for fetch in range(FETCHES):
        rows = pl.ds(fetch * key_step, key_step)
        key_copies.append(
            pltpu.make_async_copy(keys_hbm.at[rows], keys_ref.at[rows], sems.at[0, fetch])
        )
        rows = pl.ds(fetch * value_step, value_step)
        for head in range(values_ref.shape[0]):
            value_copies.append(
                pltpu.make_async_copy(
                    values_hbm.at[head, rows], values_ref.at[head, rows], sems.at[1 + head, fetch]
                )
            )
    for copy in key_copies + value_copies:
        copy.start()
    sources, capacity, part_width = arrived_ref.shape
    local_heads = part_width // HD
    key_total = keys_ref.shape[1]
    chunks = key_total // KEY_CHUNK

    def take(source, offset):
        for head in range(local_heads):
            rows = arrived_ref[source, :, head * HD : (head + 1) * HD].astype(jnp.float32)
            query_ref[head, pl.ds(offset, capacity), :] = rows
        return offset + counts_ref[source]

    total = lax.fori_loop(0, sources, take, jnp.int32(0), unroll=UNROLL)
    blocks = (total + ROW_BLOCK - 1) // ROW_BLOCK
    lane = lax.broadcasted_iota(jnp.int32, (ROW_BLOCK, LANES), 1)

    def block_rows(block):
        return pl.ds(pl.multiple_of(block * ROW_BLOCK, ROW_BLOCK), ROW_BLOCK)

    def load_queries(block, head):
        return query_ref[head, block_rows(block), :].astype(jnp.bfloat16)

    def score_chunk(rows, head, slot, chunk, part_top):
        columns = slice(chunk * KEY_CHUNK, (chunk + 1) * KEY_CHUNK)
        scores = jnp.dot(
            rows,
            keys_ref[head * HD : (head + 1) * HD, columns],
            preferred_element_type=jnp.float32,
        )
        score_ref[slot, :, columns] = scores
        for piece in range(KEY_CHUNK // LANES):
            part = scores[:, piece * LANES : (piece + 1) * LANES]
            part_top = part if part_top is None else jnp.maximum(part_top, part)
        return part_top

    def finish_top(part_top, slot):
        row_top = jnp.max(part_top, axis=1, keepdims=True) * score_scale
        row_top = row_top.astype(jnp.bfloat16).astype(jnp.float32)
        top_ref[slot] = jnp.broadcast_to(row_top, (ROW_BLOCK, LANES))

    def weigh_chunk(head, slot, chunk, shift):
        columns = slice(chunk * KEY_CHUNK, (chunk + 1) * KEY_CHUNK)
        weights = jnp.exp2(score_ref[slot, :, columns] * (score_scale * log2_e) - shift)
        return jnp.dot(
            weights.astype(jnp.bfloat16),
            values_ref[head, columns, :],
            preferred_element_type=jnp.float32,
        )

    def finish_answer(block, head, slot, mixed):
        rows = block_rows(block)
        row_sum = mixed[:, HD:]
        answer_ref[head, rows, :] = mixed[:, :HD] / row_sum
        top = top_ref[slot]
        if head == 0:
            stats = jnp.where(lane == 0, top, row_sum)
        else:
            stats = jnp.where(lane == head, top, stat_ref[...])
            stats = jnp.where(lane == local_heads + head, row_sum, stats)
        if head + 1 < local_heads:
            stat_ref[...] = stats
        else:
            for half in range(ROW_BLOCK // LANES):
                turned_ref[block * (ROW_BLOCK // LANES) + half] = jnp.transpose(
                    stats[half * LANES : (half + 1) * LANES]
                )[:STAT_ROWS, :]

    def slot_of(block, head):
        return (block * local_heads + head) % 2 if local_heads % 2 else head % 2

    for copy in key_copies:
        copy.wait()
    first_rows = load_queries(0, 0)
    part_top = None
    for chunk in range(chunks):
        part_top = score_chunk(first_rows, 0, 0, chunk, part_top)
    finish_top(part_top, 0)
    for copy in value_copies:
        copy.wait()

    def one_block(block, carry):
        for head in range(local_heads):
            slot = slot_of(block, head)
            if head + 1 < local_heads:
                next_block, next_head = block, head + 1
            else:
                next_block, next_head = jnp.minimum(block + 1, blocks - 1), 0
            next_slot = 1 - slot
            next_rows = load_queries(next_block, next_head)
            shift = top_ref[slot][:, 0:1] * log2_e
            part_top = None
            mixed = None
            for chunk in range(chunks):
                part_top = score_chunk(next_rows, next_head, next_slot, chunk, part_top)
                part = weigh_chunk(head, slot, chunk, shift)
                mixed = part if mixed is None else mixed + part
            finish_answer(block, head, slot, mixed)
            finish_top(part_top, next_slot)
        return carry

    lax.fori_loop(0, blocks, one_block, 0)

    def give(source, offset):
        rows = [answer_ref[head, pl.ds(offset, capacity), :] for head in range(local_heads)]
        tile = offset // LANES
        window = jnp.concatenate([turned_ref[tile], turned_ref[tile + 1]], axis=1)
        turned = pltpu.roll(window, (2 * LANES - offset % LANES) % (2 * LANES), 1)[:, :LANES]
        if part_width > LANES:
            turned = jnp.concatenate(
                [turned, jnp.zeros((STAT_ROWS, part_width - LANES), jnp.float32)], axis=1
            )
        rows = jnp.concatenate(rows, axis=1)
        out_ref[source] = jnp.concatenate([rows, turned], axis=0).astype(jnp.bfloat16)
        return offset + counts_ref[source]

    lax.fori_loop(0, sources, give, jnp.int32(0), unroll=UNROLL)


def attend_prefix(counts, arrived, turned_keys, wide_values):
    sources, capacity, part_width = arrived.shape
    local_heads = part_width // HD
    key_total = turned_keys.shape[1]
    row_total = -(-sources * capacity // ROW_BLOCK) * ROW_BLOCK + LANES
    return pl.pallas_call(
        far_kernel,
        out_shape=jax.ShapeDtypeStruct((sources, capacity + STAT_ROWS, part_width), jnp.bfloat16),
        in_specs=[smem_spec(), vmem_spec(), hbm_spec(), hbm_spec()],
        out_specs=vmem_spec(),
        scratch_shapes=[
            pltpu.VMEM((local_heads, row_total, HD), jnp.float32),
            pltpu.VMEM((local_heads, row_total, HD), jnp.float32),
            pltpu.VMEM((ROW_BLOCK, LANES), jnp.float32),
            pltpu.VMEM((row_total // LANES + 1, STAT_ROWS, LANES), jnp.float32),
            pltpu.VMEM((2, ROW_BLOCK, key_total), jnp.float32),
            pltpu.VMEM((2, ROW_BLOCK, LANES), jnp.float32),
            pltpu.VMEM(turned_keys.shape, jnp.bfloat16),
            pltpu.VMEM(wide_values.shape, jnp.bfloat16),
            pltpu.SemaphoreType.DMA((1 + local_heads, FETCHES)),
        ],
        compiler_params=pltpu.CompilerParams(vmem_limit_bytes=58 * mebibyte),
        cost_estimate=pl.CostEstimate(
            flops=4 * sources * capacity * key_total * part_width,
            bytes_accessed=8 * key_total * part_width,
            transcendentals=sources * capacity * key_total * local_heads,
        ),
        name="attend_prefix",
    )(counts, arrived, turned_keys, wide_values)


def stat_lane(head, local_heads):
    return (head // local_heads) * STAT_ROWS + head % local_heads


def own_kernel(local_heads, lengths_ref, query_ref, key_ref, value_ref, mixed_ref, top_ref, sum_ref):
    slot_count, model_width = query_ref.shape
    head_count = model_width // HD
    row = lax.broadcasted_iota(jnp.int32, (slot_count, slot_count), 0)
    column = lax.broadcasted_iota(jnp.int32, (slot_count, slot_count), 1)
    row_segment = jnp.zeros((slot_count, slot_count), jnp.int32)
    column_segment = jnp.zeros((slot_count, slot_count), jnp.int32)
    start = 0
    for request in range(lengths_ref.shape[1]):
        start = start + lengths_ref[0, request]
        row_segment = row_segment + (row >= start).astype(jnp.int32)
        column_segment = column_segment + (column >= start).astype(jnp.int32)
    visible = (row_segment == column_segment) & (column <= row)
    lane = lax.broadcasted_iota(jnp.int32, (slot_count, LANES), 1)
    tops = jnp.zeros((slot_count, LANES), jnp.float32)
    sums = jnp.ones((slot_count, LANES), jnp.float32)
    for head in range(head_count):
        columns = slice(head * HD, (head + 1) * HD)
        scores = (
            lax.dot_general(
                query_ref[:, columns],
                key_ref[:, columns],
                (((1,), (1,)), ((), ())),
                preferred_element_type=jnp.float32,
            )
            * score_scale
        )
        top = jnp.max(jnp.where(visible, scores, -jnp.inf), axis=1, keepdims=True)
        weights = jnp.where(visible, jnp.exp(scores - top), 0.0)
        mixed_ref[:, columns] = jnp.dot(
            weights.astype(jnp.bfloat16),
            value_ref[:, columns],
            preferred_element_type=jnp.float32,
        )
        at = stat_lane(head, local_heads)
        tops = jnp.where(lane == at, top, tops)
        sums = jnp.where(lane == at, jnp.sum(weights, axis=1, keepdims=True), sums)
    top_ref[...] = tops
    sum_ref[...] = sums


def attend_suffix(lengths, queries, keys, values, local_heads):
    slot_count, model_width = queries.shape
    stats = jax.ShapeDtypeStruct((slot_count, LANES), jnp.float32)
    return pl.pallas_call(
        functools.partial(own_kernel, local_heads),
        out_shape=(jax.ShapeDtypeStruct((slot_count, model_width), jnp.float32), stats, stats),
        in_specs=[smem_spec()] + [vmem_spec()] * 3,
        out_specs=(vmem_spec(), vmem_spec(), vmem_spec()),
        compiler_params=pltpu.CompilerParams(vmem_limit_bytes=16 * mebibyte),
        cost_estimate=pl.CostEstimate(
            flops=40 * slot_count * slot_count * model_width,
            bytes_accessed=8 * slot_count * model_width,
            transcendentals=slot_count * model_width,
        ),
        name="attend_suffix",
    )(lengths, queries, keys, values)


def merge_kernel(
    lengths_ref,
    groups_ref,
    arrived_ref,
    own_mixed_ref,
    own_top_ref,
    own_sum_ref,
    input_ref,
    gain_ref,
    shift_ref,
    first_ref,
    second_ref,
    hidden_ref,
    far_ref,
    stat_ref,
):
    _, column_count, chunk_rows, part_width = arrived_ref.shape
    slot_count, model_width = input_ref.shape
    capacity = chunk_rows - STAT_ROWS
    local_heads = part_width // HD
    head_count = model_width // HD
    start = 0
    for request in range(lengths_ref.shape[1]):
        group = groups_ref[0, request]
        pieces = []
        for column in range(column_count):
            block = arrived_ref[group, column].astype(jnp.float32)
            for head in range(local_heads):
                far_ref[column * local_heads + head, pl.ds(start, capacity), :] = block[
                    :capacity, head * HD : (head + 1) * HD
                ]
            pieces.append(block[capacity:, :LANES])
        if column_count * STAT_ROWS < LANES:
            pieces.append(jnp.zeros((LANES - column_count * STAT_ROWS, LANES), jnp.float32))
        turned = jnp.transpose(jnp.concatenate(pieces, axis=0))
        stat_ref[pl.ds(start, capacity), :] = turned[:capacity]
        start = start + lengths_ref[0, request]
    far_top = stat_ref[:slot_count, :]
    far_sum = pltpu.roll(far_top, LANES - local_heads, 1)
    own_top = own_top_ref[...]
    joint_top = jnp.maximum(far_top, own_top)
    far_weight = jnp.exp(far_top - joint_top) * far_sum
    own_weight = jnp.exp(own_top - joint_top)
    bottom = far_weight + own_weight * own_sum_ref[...]
    far_weight = far_weight / bottom
    own_weight = own_weight / bottom
    total = jnp.zeros((slot_count, LANES), jnp.float32)
    for head in range(head_count):
        columns = slice(head * HD, (head + 1) * HD)
        at = stat_lane(head, local_heads)
        summed = (
            input_ref[:, columns].astype(jnp.float32)
            + far_weight[:, at : at + 1] * far_ref[head, :slot_count, :]
            + own_weight[:, at : at + 1] * own_mixed_ref[:, columns]
        )
        far_ref[head, :slot_count, :] = summed
        total = total + summed
    row_mean = jnp.sum(total, axis=1, keepdims=True) * (1.0 / model_width)
    total = jnp.zeros((slot_count, LANES), jnp.float32)
    for head in range(head_count):
        centred = far_ref[head, :slot_count, :] - row_mean
        total = total + centred * centred
    spread = jnp.sum(total, axis=1, keepdims=True) * (1.0 / model_width)
    factor = lax.rsqrt(spread + norm_eps)
    for head in range(head_count):
        columns = slice(head * HD, (head + 1) * HD)
        centred = far_ref[head, :slot_count, :] - row_mean
        hidden = (centred * factor * gain_ref[:, columns] + shift_ref[:, columns]).astype(
            jnp.bfloat16
        )
        first_ref[:, columns] = hidden[: slot_count // 2]
        second_ref[:, columns] = hidden[slot_count // 2 :]
        hidden_ref[:, columns] = hidden


def merge_parts(lengths, groups, arrived, own_mixed, own_top, own_sum, layer_input, gain, shift):
    slot_count, model_width = layer_input.shape
    capacity = arrived.shape[2] - STAT_ROWS
    half = jax.ShapeDtypeStruct((slot_count // 2, model_width), jnp.bfloat16)
    return pl.pallas_call(
        merge_kernel,
        out_shape=(half, half, jax.ShapeDtypeStruct(layer_input.shape, jnp.bfloat16)),
        in_specs=[smem_spec(), smem_spec()] + [vmem_spec()] * 7,
        out_specs=(vmem_spec(), vmem_spec(), vmem_spec()),
        scratch_shapes=[
            pltpu.VMEM((model_width // HD, slot_count + capacity, HD), jnp.float32),
            pltpu.VMEM((slot_count + capacity, LANES), jnp.float32),
        ],
        compiler_params=pltpu.CompilerParams(vmem_limit_bytes=16 * mebibyte),
        name="merge_parts",
    )(
        lengths,
        groups,
        arrived,
        own_mixed,
        own_top,
        own_sum,
        layer_input,
        gain.reshape(1, model_width),
        shift.reshape(1, model_width),
    )


def swap(value, mask):
    total = lax.axis_size("grp") * lax.axis_size("dev")
    pairs = [(here, here ^ mask) for here in range(total)]
    return jax.tree.map(lambda leaf: lax.ppermute(leaf, ("grp", "dev"), pairs), value)


def complete(held, masks):
    held = dict(held)
    for mask in masks:
        for at in list(held):
            if mask ^ at not in held:
                held[mask ^ at] = swap(held[at], mask)
    return held


def tie(values, after):
    return lax.optimization_barrier((values, after))[0]


def cut(height):
    step = max(height // STREAMS // 16, 1) * 16
    begins = [first for first in range(0, height, step)][:STREAMS]
    return [
        (first, (begins + [height])[at + 1] - first) for at, first in enumerate(begins)
    ]


def mlp_kernel(pieces, up_plan, down_plan, *refs):
    parts = len(up_plan)
    row_refs, refs = refs[:pieces], refs[pieces:]
    up_total, down_total = sum(map(len, up_plan)), sum(map(len, down_plan))
    ups, refs = list(refs[:up_total]), refs[up_total:]
    downs, refs = list(refs[:down_total]), refs[down_total:]
    out_refs, (up_ref, down_ref, sems) = refs[:pieces], refs[pieces:]
    model_width = row_refs[0].shape[1]
    copies = []
    for part, heights in enumerate(up_plan):
        begin, held = 0, []
        for piece, height in enumerate(heights):
            source = ups.pop(0)
            for stream, (first, rows) in enumerate(cut(height)):
                held.append(
                    pltpu.make_async_copy(
                        source.at[pl.ds(first, rows)],
                        up_ref.at[part, pl.ds(begin + first, rows)],
                        sems.at[part, 0, piece * STREAMS + stream],
                    )
                )
            begin += height
        copies.append(held)
    begin = 0
    for part, heights in enumerate(down_plan):
        held = []
        for piece, height in enumerate(heights):
            source = downs.pop(0)
            for stream, (first, rows) in enumerate(cut(height)):
                held.append(
                    pltpu.make_async_copy(
                        source.at[pl.ds(first, rows)],
                        down_ref.at[pl.ds(begin + first, rows)],
                        sems.at[part, 1, piece * STREAMS + stream],
                    )
                )
            begin += height
        copies.append(held)
    for held in copies[:parts]:
        for copy in held:
            copy.start()
    rows = jnp.concatenate([ref[...] for ref in row_refs], axis=0)
    activations = []
    for part in range(parts):
        for copy in copies[part]:
            copy.wait()
        if part == 0:
            for held in copies[parts:]:
                for copy in held:
                    copy.start()
        product = jnp.dot(
            rows, up_ref[part, :model_width, :], preferred_element_type=jnp.float32
        )
        offset = up_ref[part, model_width:, :].astype(jnp.float32)[0:1]
        activations.append(jax.nn.gelu(product + offset, approximate=True).astype(jnp.bfloat16))
    for held in copies[parts:]:
        for copy in held:
            copy.wait()
    total = jnp.dot(
        jnp.concatenate(activations, axis=1), down_ref[...], preferred_element_type=jnp.float32
    ).astype(jnp.bfloat16)
    begin = 0
    for out_ref in out_refs:
        height = out_ref.shape[0]
        out_ref[...] = total[begin : begin + height]
        begin += height


def feed_forward(rows, ups, downs):
    pieces, parts = len(rows), len(ups)
    row_total, model_width = sum(piece.shape[0] for piece in rows), rows[0].shape[1]
    up_plan = [[piece.shape[0] for piece in block] for block in ups]
    down_plan = [[piece.shape[0] for piece in block] for block in downs]
    up_rows, down_rows = sum(up_plan[0]), sum(down_plan[0])
    units = ups[0][0].shape[1]
    flat = [piece for block in ups + downs for piece in block]
    most = max(map(len, up_plan + down_plan))
    return pl.pallas_call(
        functools.partial(mlp_kernel, pieces, up_plan, down_plan),
        out_shape=tuple(jax.ShapeDtypeStruct(piece.shape, jnp.bfloat16) for piece in rows),
        in_specs=[vmem_spec()] * pieces + [hbm_spec()] * len(flat),
        out_specs=tuple(vmem_spec() for _ in rows),
        scratch_shapes=[
            pltpu.VMEM((parts, up_rows, units), jnp.bfloat16),
            pltpu.VMEM((parts * down_rows, model_width), jnp.bfloat16),
            pltpu.SemaphoreType.DMA((parts, 2, most * STREAMS)),
        ],
        compiler_params=pltpu.CompilerParams(vmem_limit_bytes=58 * mebibyte),
        cost_estimate=pl.CostEstimate(
            flops=4 * row_total * model_width * parts * units,
            bytes_accessed=4 * parts * model_width * units,
            transcendentals=row_total * parts * units,
        ),
        name="feed_forward",
    )(*rows, *flat)


def add_rows(here, there):
    return (here.astype(jnp.float32) + there.astype(jnp.float32)).astype(jnp.bfloat16)


def finish_kernel(
    hidden_ref, own_ref, near_ref, far_a_ref, far_b_ref, bias_ref, gain_ref, shift_ref, out_ref
):
    height = far_a_ref.shape[0]
    for begin, far_ref in ((0, far_a_ref), (height, far_b_ref)):
        rows = slice(begin, begin + height)
        summed = hidden_ref[rows, :].astype(jnp.float32) + (
            own_ref[rows, :].astype(jnp.float32)
            + near_ref[rows, :].astype(jnp.float32)
            + far_ref[...].astype(jnp.float32)
        )
        out_ref[rows, :] = layer_norm(
            summed + bias_ref[...], gain_ref[...], shift_ref[...]
        ).astype(jnp.bfloat16)


def finish_rows(hidden, own, near, far_a, far_b, bias, gain, shift):
    model_width = hidden.shape[1]
    return pl.pallas_call(
        finish_kernel,
        out_shape=jax.ShapeDtypeStruct(hidden.shape, jnp.bfloat16),
        in_specs=[vmem_spec()] * 8,
        out_specs=vmem_spec(),
        compiler_params=pltpu.CompilerParams(vmem_limit_bytes=16 * mebibyte),
        name="finish_rows",
    )(
        hidden,
        own,
        near,
        far_a,
        far_b,
        bias.reshape(1, model_width),
        gain.reshape(1, model_width),
        shift.reshape(1, model_width),
    )


def on_device(
    suffix_queries,
    suffix_keys,
    suffix_values,
    layer_input,
    suffix_lengths,
    request_group,
    prefix_keys,
    prefix_values,
    up_weight,
    up_bias,
    down_weight,
    down_bias,
    attn_gain,
    attn_shift,
    out_gain,
    out_shift,
):
    slot_count, model_width = suffix_queries.shape
    group_count = lax.axis_size("grp")
    column_count = lax.axis_size("dev")
    part_width = model_width // column_count
    local_heads = part_width // HD
    capacity = 2 * slot_count // group_count
    sources = group_count * column_count

    near_mask = group_count // 2 * column_count
    far_mask = column_count // 2
    column_masks = [1 << bit for bit in range(far_mask.bit_length() - 1)]
    group_masks = [column_count << bit for bit in range((group_count // 2).bit_length() - 1)]

    low_mask, high_masks = column_masks[0], column_masks[1:]
    core_mask = group_masks[0]

    outgoing = pack_queries(
        suffix_lengths, request_group, suffix_queries, group_count, column_count, capacity
    )
    bias_rows = jnp.broadcast_to(up_bias[None, :], (16, up_bias.shape[0]))
    up_block = jnp.concatenate([up_weight, bias_rows], axis=0)
    up_cut, down_cut = up_weight.shape[0] * 5 // 8, down_weight.shape[0] // 2
    up_pieces = (up_block[:up_cut], up_block[up_cut:])
    down_pieces = (down_weight[:down_cut], down_weight[down_cut:])
    ups, downs = {0: (up_block,)}, {0: (down_weight,)}
    high_mask = high_masks[0]

    arrived = lax.all_to_all(
        outgoing.reshape(sources, capacity, part_width),
        ("grp", "dev"),
        split_axis=0,
        concat_axis=0,
        tiled=True,
    )
    ups[low_mask] = swap(ups[0], low_mask)
    up_first = swap(up_pieces[0], high_mask)
    ups[core_mask] = swap(ups[0], core_mask)
    downs[core_mask] = swap(downs[0], core_mask)
    turned_keys = prefix_keys[0].T
    value_heads = prefix_values[0].reshape(-1, local_heads, HD).transpose(1, 0, 2)
    wide_values = jnp.concatenate([value_heads, jnp.ones_like(value_heads)], axis=2)
    own = attend_suffix(
        suffix_lengths, suffix_queries, suffix_keys, suffix_values, local_heads
    )
    arrived, ups, up_first, up_pieces, downs, down_pieces, turned_keys, wide_values, own = (
        lax.optimization_barrier(
            (arrived, ups, up_first, up_pieces, downs, down_pieces, turned_keys, wide_values, own)
        )
    )

    counts = jnp.sum((arrived[:, :, 0] < EMPTY / 2).astype(jnp.int32), axis=1)
    answer_part = attend_prefix(counts, arrived, turned_keys, wide_values)
    downs[low_mask] = swap(downs[0], low_mask)
    up_second = swap(up_pieces[1], high_mask)
    down_first = swap(down_pieces[0], high_mask)
    ups[core_mask ^ low_mask] = swap(ups[low_mask], core_mask)
    answer_part, ups, up_first, up_second, downs, down_first, down_pieces = (
        lax.optimization_barrier(
            (answer_part, ups, up_first, up_second, downs, down_first, down_pieces)
        )
    )

    answer = lax.all_to_all(
        answer_part, ("grp", "dev"), split_axis=0, concat_axis=0, tiled=True
    ).reshape(group_count, column_count, capacity + STAT_ROWS, part_width)
    ups[high_mask] = (jnp.concatenate([up_first, up_second], axis=0),)
    ups[core_mask ^ high_mask] = swap(ups[high_mask], core_mask)
    downs[core_mask ^ low_mask] = swap(downs[low_mask], core_mask)
    down_second = swap(down_pieces[1], high_mask)
    downs[high_mask] = (jnp.concatenate([down_first, down_second], axis=0),)
    downs[core_mask ^ high_mask] = swap(downs[high_mask], core_mask)
    ups[low_mask ^ high_mask] = swap(ups[high_mask], low_mask)
    answer, ups, downs = lax.optimization_barrier((answer, ups, downs))

    hidden_a, hidden_b, hidden = merge_parts(
        suffix_lengths, request_group, answer, *own, layer_input, attn_gain, attn_shift
    )

    (hidden_a, hidden_b, hidden), ups, downs = lax.optimization_barrier(
        ((hidden_a, hidden_b, hidden), ups, downs)
    )
    far_a = swap(hidden_a, far_mask)
    near = swap(hidden, near_mask)
    downs[low_mask ^ high_mask] = swap(downs[high_mask], low_mask)
    ups = complete(ups, group_masks + column_masks)
    far_b = swap(tie(hidden_b, far_a), far_mask)
    cross_a = swap(far_a, near_mask)
    far_b, cross_a, near, ups, downs = lax.optimization_barrier(
        (far_b, cross_a, near, ups, downs)
    )
    cross_b = swap(far_b, near_mask)
    downs = complete(downs, group_masks + column_masks)
    order = sorted(ups)
    ups = [ups[mask] for mask in order]
    downs = [downs[mask] for mask in order]
    far_part_a, cross_part_a = feed_forward([far_a, cross_a], ups, downs)
    cross_b, far_part_a, cross_part_a = lax.optimization_barrier(
        (cross_b, far_part_a, cross_part_a)
    )
    cross_sum_a = swap(cross_part_a, near_mask)
    far_part_b, cross_part_b = feed_forward([far_b, cross_b], ups, downs)
    cross_sum_a, far_part_b, cross_part_b = lax.optimization_barrier(
        (cross_sum_a, far_part_b, cross_part_b)
    )
    cross_sum_b = swap(cross_part_b, near_mask)
    joined_a = add_rows(far_part_a, cross_sum_a)
    far_sum_a = swap(joined_a, far_mask)
    near, hidden = tie((near, hidden), joined_a)
    near_part, own_part = feed_forward([near, hidden], ups, downs)
    near_sum = swap(near_part, near_mask)
    cross_sum_b, near_part, far_sum_a = lax.optimization_barrier(
        (cross_sum_b, near_part, far_sum_a)
    )
    far_sum_b = swap(add_rows(far_part_b, cross_sum_b), far_mask)
    return finish_rows(
        hidden, own_part, near_sum, far_sum_a, far_sum_b, down_bias, out_gain, out_shift
    )


def solution(mesh):
    placed = (
        P(("grp", "dev"), None),
        P(("grp", "dev"), None),
        P(("grp", "dev"), None),
        P(("grp", "dev"), None),
        P(("grp", "dev"), None),
        P(("grp", "dev"), None),
        P("grp", None, "dev"),
        P("grp", None, "dev"),
        P(None, ("grp", "dev")),
        P(("grp", "dev")),
        P(("grp", "dev"), None),
        P(),
        P(),
        P(),
        P(),
        P(),
    )
    return jax.shard_map(
        on_device, mesh=mesh, in_specs=placed, out_specs=P(("grp", "dev"), None), check_vma=False
    )
```

```python
import functools
import math

import jax
import jax.numpy as jnp
from jax import lax
from jax.experimental import pallas as pl
from jax.experimental.pallas import tpu as pltpu
from jax.sharding import PartitionSpec as P

HD = 128
LANES = 128
STAT_ROWS = 8
STREAMS = 1
FETCHES = 8
UNROLL = 4
EMPTY = 64.0
ROW_BLOCK = 256
KEY_CHUNK = 512

norm_eps = 1e-12
score_scale = HD ** (-0.5)
log2_e = math.log2(math.e)
mebibyte = 1024 * 1024


def layer_norm(summed, norm_gain, norm_shift):
    row_mean = jnp.mean(summed, axis=-1, keepdims=True)
    centred = summed - row_mean
    spread = jnp.mean(centred * centred, axis=-1, keepdims=True)
    return centred * lax.rsqrt(spread + norm_eps) * norm_gain + norm_shift


def vmem_spec():
    return pl.BlockSpec(memory_space=pltpu.VMEM)


def hbm_spec():
    return pl.BlockSpec(memory_space=pltpu.HBM)


def smem_spec():
    return pl.BlockSpec(memory_space=pltpu.SMEM)


def pack_kernel(lengths_ref, groups_ref, query_ref, out_ref, wide_ref):
    request_total = lengths_ref.shape[1]
    _, column_count, capacity, part_width = out_ref.shape
    slot_count = query_ref.shape[0]
    slot = lax.broadcasted_iota(jnp.int32, (capacity, LANES), 0)
    tiles = part_width // LANES
    for tile in range(wide_ref.shape[0]):
        wide_ref[tile, 0:slot_count, :] = query_ref[
            :, tile * LANES : (tile + 1) * LANES
        ].astype(jnp.float32)
        wide_ref[tile, slot_count : slot_count + capacity, :] = jnp.zeros(
            (capacity, LANES), jnp.float32
        )
    start = 0
    for request in range(request_total):
        group = groups_ref[0, request]
        filled = slot < lengths_ref[0, request]
        for column in range(column_count):
            for tile in range(tiles):
                rows = wide_ref[column * tiles + tile, pl.ds(start, capacity), :]
                rows = jnp.where(filled, rows, EMPTY)
                out_ref[group, column, :, tile * LANES : (tile + 1) * LANES] = rows.astype(
                    jnp.bfloat16
                )
        start = start + lengths_ref[0, request]


def pack_queries(lengths, groups, queries, group_count, column_count, capacity):
    slot_count, model_width = queries.shape
    part_width = model_width // column_count
    return pl.pallas_call(
        pack_kernel,
        out_shape=jax.ShapeDtypeStruct(
            (group_count, column_count, capacity, part_width), jnp.bfloat16
        ),
        in_specs=[smem_spec(), smem_spec(), vmem_spec()],
        out_specs=vmem_spec(),
        scratch_shapes=[
            pltpu.VMEM((model_width // LANES, slot_count + capacity, LANES), jnp.float32)
        ],
        compiler_params=pltpu.CompilerParams(vmem_limit_bytes=58 * mebibyte),
        name="pack_queries",
    )(lengths, groups, queries)


def far_kernel(
    counts_ref,
    arrived_ref,
    keys_hbm,
    values_hbm,
    out_ref,
    query_ref,
    answer_ref,
    stat_ref,
    turned_ref,
    score_ref,
    top_ref,
    keys_ref,
    values_ref,
    sems,
):
    key_step = keys_ref.shape[0] // FETCHES
    value_step = values_ref.shape[1] // FETCHES
    key_copies, value_copies = [], []
    for fetch in range(FETCHES):
        rows = pl.ds(fetch * key_step, key_step)
        key_copies.append(
            pltpu.make_async_copy(keys_hbm.at[rows], keys_ref.at[rows], sems.at[0, fetch])
        )
        rows = pl.ds(fetch * value_step, value_step)
        for head in range(values_ref.shape[0]):
            value_copies.append(
                pltpu.make_async_copy(
                    values_hbm.at[head, rows], values_ref.at[head, rows], sems.at[1 + head, fetch]
                )
            )
    for copy in key_copies + value_copies:
        copy.start()
    sources, capacity, part_width = arrived_ref.shape
    local_heads = part_width // HD
    key_total = keys_ref.shape[1]
    chunks = key_total // KEY_CHUNK

    def take(source, offset):
        for head in range(local_heads):
            rows = arrived_ref[source, :, head * HD : (head + 1) * HD].astype(jnp.float32)
            query_ref[head, pl.ds(offset, capacity), :] = rows
        return offset + counts_ref[source]

    total = lax.fori_loop(0, sources, take, jnp.int32(0), unroll=UNROLL)
    blocks = (total + ROW_BLOCK - 1) // ROW_BLOCK
    lane = lax.broadcasted_iota(jnp.int32, (ROW_BLOCK, LANES), 1)

    def block_rows(block):
        return pl.ds(pl.multiple_of(block * ROW_BLOCK, ROW_BLOCK), ROW_BLOCK)

    def load_queries(block, head):
        return query_ref[head, block_rows(block), :].astype(jnp.bfloat16)

    def score_chunk(rows, head, slot, chunk, part_top):
        columns = slice(chunk * KEY_CHUNK, (chunk + 1) * KEY_CHUNK)
        scores = jnp.dot(
            rows,
            keys_ref[head * HD : (head + 1) * HD, columns],
            preferred_element_type=jnp.float32,
        )
        score_ref[slot, :, columns] = scores
        for piece in range(KEY_CHUNK // LANES):
            part = scores[:, piece * LANES : (piece + 1) * LANES]
            part_top = part if part_top is None else jnp.maximum(part_top, part)
        return part_top

    def finish_top(part_top, slot):
        row_top = jnp.max(part_top, axis=1, keepdims=True) * score_scale
        row_top = row_top.astype(jnp.bfloat16).astype(jnp.float32)
        top_ref[slot] = jnp.broadcast_to(row_top, (ROW_BLOCK, LANES))

    def weigh_chunk(head, slot, chunk, shift):
        columns = slice(chunk * KEY_CHUNK, (chunk + 1) * KEY_CHUNK)
        weights = jnp.exp2(score_ref[slot, :, columns] * (score_scale * log2_e) - shift)
        return jnp.dot(
            weights.astype(jnp.bfloat16),
            values_ref[head, columns, :],
            preferred_element_type=jnp.float32,
        )

    def finish_answer(block, head, slot, mixed):
        rows = block_rows(block)
        row_sum = mixed[:, HD:]
        answer_ref[head, rows, :] = mixed[:, :HD] / row_sum
        top = top_ref[slot]
        if head == 0:
            stats = jnp.where(lane == 0, top, row_sum)
        else:
            stats = jnp.where(lane == head, top, stat_ref[...])
            stats = jnp.where(lane == local_heads + head, row_sum, stats)
        if head + 1 < local_heads:
            stat_ref[...] = stats
        else:
            for half in range(ROW_BLOCK // LANES):
                turned_ref[block * (ROW_BLOCK // LANES) + half] = jnp.transpose(
                    stats[half * LANES : (half + 1) * LANES]
                )[:STAT_ROWS, :]

    def slot_of(block, head):
        return (block * local_heads + head) % 2 if local_heads % 2 else head % 2

    for copy in key_copies:
        copy.wait()
    first_rows = load_queries(0, 0)
    part_top = None
    for chunk in range(chunks):
        part_top = score_chunk(first_rows, 0, 0, chunk, part_top)
    finish_top(part_top, 0)
    for copy in value_copies:
        copy.wait()

    def one_block(block, carry):
        for head in range(local_heads):
            slot = slot_of(block, head)
            if head + 1 < local_heads:
                next_block, next_head = block, head + 1
            else:
                next_block, next_head = jnp.minimum(block + 1, blocks - 1), 0
            next_slot = 1 - slot
            next_rows = load_queries(next_block, next_head)
            shift = top_ref[slot][:, 0:1] * log2_e
            part_top = None
            mixed = None
            for chunk in range(chunks):
                part_top = score_chunk(next_rows, next_head, next_slot, chunk, part_top)
                part = weigh_chunk(head, slot, chunk, shift)
                mixed = part if mixed is None else mixed + part
            finish_answer(block, head, slot, mixed)
            finish_top(part_top, next_slot)
        return carry

    lax.fori_loop(0, blocks, one_block, 0)

    def give(source, offset):
        rows = [answer_ref[head, pl.ds(offset, capacity), :] for head in range(local_heads)]
        tile = offset // LANES
        window = jnp.concatenate([turned_ref[tile], turned_ref[tile + 1]], axis=1)
        turned = pltpu.roll(window, (2 * LANES - offset % LANES) % (2 * LANES), 1)[:, :LANES]
        if part_width > LANES:
            turned = jnp.concatenate(
                [turned, jnp.zeros((STAT_ROWS, part_width - LANES), jnp.float32)], axis=1
            )
        rows = jnp.concatenate(rows, axis=1)
        out_ref[source] = jnp.concatenate([rows, turned], axis=0).astype(jnp.bfloat16)
        return offset + counts_ref[source]

    lax.fori_loop(0, sources, give, jnp.int32(0), unroll=UNROLL)


def attend_prefix(counts, arrived, turned_keys, wide_values):
    sources, capacity, part_width = arrived.shape
    local_heads = part_width // HD
    key_total = turned_keys.shape[1]
    row_total = -(-sources * capacity // ROW_BLOCK) * ROW_BLOCK + LANES
    return pl.pallas_call(
        far_kernel,
        out_shape=jax.ShapeDtypeStruct((sources, capacity + STAT_ROWS, part_width), jnp.bfloat16),
        in_specs=[smem_spec(), vmem_spec(), hbm_spec(), hbm_spec()],
        out_specs=vmem_spec(),
        scratch_shapes=[
            pltpu.VMEM((local_heads, row_total, HD), jnp.float32),
            pltpu.VMEM((local_heads, row_total, HD), jnp.float32),
            pltpu.VMEM((ROW_BLOCK, LANES), jnp.float32),
            pltpu.VMEM((row_total // LANES + 1, STAT_ROWS, LANES), jnp.float32),
            pltpu.VMEM((2, ROW_BLOCK, key_total), jnp.float32),
            pltpu.VMEM((2, ROW_BLOCK, LANES), jnp.float32),
            pltpu.VMEM(turned_keys.shape, jnp.bfloat16),
            pltpu.VMEM(wide_values.shape, jnp.bfloat16),
            pltpu.SemaphoreType.DMA((1 + local_heads, FETCHES)),
        ],
        compiler_params=pltpu.CompilerParams(vmem_limit_bytes=58 * mebibyte),
        cost_estimate=pl.CostEstimate(
            flops=4 * sources * capacity * key_total * part_width,
            bytes_accessed=8 * key_total * part_width,
            transcendentals=sources * capacity * key_total * local_heads,
        ),
        name="attend_prefix",
    )(counts, arrived, turned_keys, wide_values)


def stat_lane(head, local_heads):
    return (head // local_heads) * STAT_ROWS + head % local_heads


def own_kernel(local_heads, lengths_ref, query_ref, key_ref, value_ref, mixed_ref, top_ref, sum_ref):
    slot_count, model_width = query_ref.shape
    head_count = model_width // HD
    row = lax.broadcasted_iota(jnp.int32, (slot_count, slot_count), 0)
    column = lax.broadcasted_iota(jnp.int32, (slot_count, slot_count), 1)
    row_segment = jnp.zeros((slot_count, slot_count), jnp.int32)
    column_segment = jnp.zeros((slot_count, slot_count), jnp.int32)
    start = 0
    for request in range(lengths_ref.shape[1]):
        start = start + lengths_ref[0, request]
        row_segment = row_segment + (row >= start).astype(jnp.int32)
        column_segment = column_segment + (column >= start).astype(jnp.int32)
    visible = (row_segment == column_segment) & (column <= row)
    lane = lax.broadcasted_iota(jnp.int32, (slot_count, LANES), 1)
    tops = jnp.zeros((slot_count, LANES), jnp.float32)
    sums = jnp.ones((slot_count, LANES), jnp.float32)
    for head in range(head_count):
        columns = slice(head * HD, (head + 1) * HD)
        scores = (
            lax.dot_general(
                query_ref[:, columns],
                key_ref[:, columns],
                (((1,), (1,)), ((), ())),
                preferred_element_type=jnp.float32,
            )
            * score_scale
        )
        top = jnp.max(jnp.where(visible, scores, -jnp.inf), axis=1, keepdims=True)
        weights = jnp.where(visible, jnp.exp(scores - top), 0.0)
        mixed_ref[:, columns] = jnp.dot(
            weights.astype(jnp.bfloat16),
            value_ref[:, columns],
            preferred_element_type=jnp.float32,
        )
        at = stat_lane(head, local_heads)
        tops = jnp.where(lane == at, top, tops)
        sums = jnp.where(lane == at, jnp.sum(weights, axis=1, keepdims=True), sums)
    top_ref[...] = tops
    sum_ref[...] = sums


def attend_suffix(lengths, queries, keys, values, local_heads):
    slot_count, model_width = queries.shape
    stats = jax.ShapeDtypeStruct((slot_count, LANES), jnp.float32)
    return pl.pallas_call(
        functools.partial(own_kernel, local_heads),
        out_shape=(jax.ShapeDtypeStruct((slot_count, model_width), jnp.float32), stats, stats),
        in_specs=[smem_spec()] + [vmem_spec()] * 3,
        out_specs=(vmem_spec(), vmem_spec(), vmem_spec()),
        compiler_params=pltpu.CompilerParams(vmem_limit_bytes=16 * mebibyte),
        cost_estimate=pl.CostEstimate(
            flops=40 * slot_count * slot_count * model_width,
            bytes_accessed=8 * slot_count * model_width,
            transcendentals=slot_count * model_width,
        ),
        name="attend_suffix",
    )(lengths, queries, keys, values)


def merge_kernel(
    lengths_ref,
    groups_ref,
    arrived_ref,
    own_mixed_ref,
    own_top_ref,
    own_sum_ref,
    input_ref,
    gain_ref,
    shift_ref,
    first_ref,
    second_ref,
    hidden_ref,
    far_ref,
    stat_ref,
):
    _, column_count, chunk_rows, part_width = arrived_ref.shape
    slot_count, model_width = input_ref.shape
    capacity = chunk_rows - STAT_ROWS
    local_heads = part_width // HD
    head_count = model_width // HD
    start = 0
    for request in range(lengths_ref.shape[1]):
        group = groups_ref[0, request]
        pieces = []
        for column in range(column_count):
            block = arrived_ref[group, column].astype(jnp.float32)
            for head in range(local_heads):
                far_ref[column * local_heads + head, pl.ds(start, capacity), :] = block[
                    :capacity, head * HD : (head + 1) * HD
                ]
            pieces.append(block[capacity:, :LANES])
        if column_count * STAT_ROWS < LANES:
            pieces.append(jnp.zeros((LANES - column_count * STAT_ROWS, LANES), jnp.float32))
        turned = jnp.transpose(jnp.concatenate(pieces, axis=0))
        stat_ref[pl.ds(start, capacity), :] = turned[:capacity]
        start = start + lengths_ref[0, request]
    far_top = stat_ref[:slot_count, :]
    far_sum = pltpu.roll(far_top, LANES - local_heads, 1)
    own_top = own_top_ref[...]
    joint_top = jnp.maximum(far_top, own_top)
    far_weight = jnp.exp(far_top - joint_top) * far_sum
    own_weight = jnp.exp(own_top - joint_top)
    bottom = far_weight + own_weight * own_sum_ref[...]
    far_weight = far_weight / bottom
    own_weight = own_weight / bottom
    total = jnp.zeros((slot_count, LANES), jnp.float32)
    for head in range(head_count):
        columns = slice(head * HD, (head + 1) * HD)
        at = stat_lane(head, local_heads)
        summed = (
            input_ref[:, columns].astype(jnp.float32)
            + far_weight[:, at : at + 1] * far_ref[head, :slot_count, :]
            + own_weight[:, at : at + 1] * own_mixed_ref[:, columns]
        )
        far_ref[head, :slot_count, :] = summed
        total = total + summed
    row_mean = jnp.sum(total, axis=1, keepdims=True) * (1.0 / model_width)
    total = jnp.zeros((slot_count, LANES), jnp.float32)
    for head in range(head_count):
        centred = far_ref[head, :slot_count, :] - row_mean
        total = total + centred * centred
    spread = jnp.sum(total, axis=1, keepdims=True) * (1.0 / model_width)
    factor = lax.rsqrt(spread + norm_eps)
    for head in range(head_count):
        columns = slice(head * HD, (head + 1) * HD)
        centred = far_ref[head, :slot_count, :] - row_mean
        hidden = (centred * factor * gain_ref[:, columns] + shift_ref[:, columns]).astype(
            jnp.bfloat16
        )
        first_ref[:, columns] = hidden[: slot_count // 2]
        second_ref[:, columns] = hidden[slot_count // 2 :]
        hidden_ref[:, columns] = hidden


def merge_parts(lengths, groups, arrived, own_mixed, own_top, own_sum, layer_input, gain, shift):
    slot_count, model_width = layer_input.shape
    capacity = arrived.shape[2] - STAT_ROWS
    half = jax.ShapeDtypeStruct((slot_count // 2, model_width), jnp.bfloat16)
    return pl.pallas_call(
        merge_kernel,
        out_shape=(half, half, jax.ShapeDtypeStruct(layer_input.shape, jnp.bfloat16)),
        in_specs=[smem_spec(), smem_spec()] + [vmem_spec()] * 7,
        out_specs=(vmem_spec(), vmem_spec(), vmem_spec()),
        scratch_shapes=[
            pltpu.VMEM((model_width // HD, slot_count + capacity, HD), jnp.float32),
            pltpu.VMEM((slot_count + capacity, LANES), jnp.float32),
        ],
        compiler_params=pltpu.CompilerParams(vmem_limit_bytes=16 * mebibyte),
        name="merge_parts",
    )(
        lengths,
        groups,
        arrived,
        own_mixed,
        own_top,
        own_sum,
        layer_input,
        gain.reshape(1, model_width),
        shift.reshape(1, model_width),
    )


def swap(value, mask):
    total = lax.axis_size("grp") * lax.axis_size("dev")
    pairs = [(here, here ^ mask) for here in range(total)]
    return jax.tree.map(lambda leaf: lax.ppermute(leaf, ("grp", "dev"), pairs), value)


def complete(held, masks):
    held = dict(held)
    for mask in masks:
        for at in list(held):
            if mask ^ at not in held:
                held[mask ^ at] = swap(held[at], mask)
    return held


def tie(values, after):
    return lax.optimization_barrier((values, after))[0]


def cut(height):
    step = max(height // STREAMS // 16, 1) * 16
    begins = [first for first in range(0, height, step)][:STREAMS]
    return [
        (first, (begins + [height])[at + 1] - first) for at, first in enumerate(begins)
    ]


def mlp_kernel(pieces, up_plan, down_plan, *refs):
    parts = len(up_plan)
    row_refs, refs = refs[:pieces], refs[pieces:]
    up_total, down_total = sum(map(len, up_plan)), sum(map(len, down_plan))
    ups, refs = list(refs[:up_total]), refs[up_total:]
    downs, refs = list(refs[:down_total]), refs[down_total:]
    out_refs, (up_ref, down_ref, sems) = refs[:pieces], refs[pieces:]
    model_width = row_refs[0].shape[1]
    copies = []
    for part, heights in enumerate(up_plan):
        begin, held = 0, []
        for piece, height in enumerate(heights):
            source = ups.pop(0)
            for stream, (first, rows) in enumerate(cut(height)):
                held.append(
                    pltpu.make_async_copy(
                        source.at[pl.ds(first, rows)],
                        up_ref.at[part, pl.ds(begin + first, rows)],
                        sems.at[part, 0, piece * STREAMS + stream],
                    )
                )
            begin += height
        copies.append(held)
    begin = 0
    for part, heights in enumerate(down_plan):
        held = []
        for piece, height in enumerate(heights):
            source = downs.pop(0)
            for stream, (first, rows) in enumerate(cut(height)):
                held.append(
                    pltpu.make_async_copy(
                        source.at[pl.ds(first, rows)],
                        down_ref.at[pl.ds(begin + first, rows)],
                        sems.at[part, 1, piece * STREAMS + stream],
                    )
                )
            begin += height
        copies.append(held)
    for held in copies[:parts]:
        for copy in held:
            copy.start()
    rows = jnp.concatenate([ref[...] for ref in row_refs], axis=0)
    activations = []
    for part in range(parts):
        for copy in copies[part]:
            copy.wait()
        if part == 0:
            for held in copies[parts:]:
                for copy in held:
                    copy.start()
        product = jnp.dot(
            rows, up_ref[part, :model_width, :], preferred_element_type=jnp.float32
        )
        offset = up_ref[part, model_width:, :].astype(jnp.float32)[0:1]
        activations.append(jax.nn.gelu(product + offset, approximate=True).astype(jnp.bfloat16))
    for held in copies[parts:]:
        for copy in held:
            copy.wait()
    total = jnp.dot(
        jnp.concatenate(activations, axis=1), down_ref[...], preferred_element_type=jnp.float32
    ).astype(jnp.bfloat16)
    begin = 0
    for out_ref in out_refs:
        height = out_ref.shape[0]
        out_ref[...] = total[begin : begin + height]
        begin += height


def feed_forward(rows, ups, downs):
    pieces, parts = len(rows), len(ups)
    row_total, model_width = sum(piece.shape[0] for piece in rows), rows[0].shape[1]
    up_plan = [[piece.shape[0] for piece in block] for block in ups]
    down_plan = [[piece.shape[0] for piece in block] for block in downs]
    up_rows, down_rows = sum(up_plan[0]), sum(down_plan[0])
    units = ups[0][0].shape[1]
    flat = [piece for block in ups + downs for piece in block]
    most = max(map(len, up_plan + down_plan))
    return pl.pallas_call(
        functools.partial(mlp_kernel, pieces, up_plan, down_plan),
        out_shape=tuple(jax.ShapeDtypeStruct(piece.shape, jnp.bfloat16) for piece in rows),
        in_specs=[vmem_spec()] * pieces + [hbm_spec()] * len(flat),
        out_specs=tuple(vmem_spec() for _ in rows),
        scratch_shapes=[
            pltpu.VMEM((parts, up_rows, units), jnp.bfloat16),
            pltpu.VMEM((parts * down_rows, model_width), jnp.bfloat16),
            pltpu.SemaphoreType.DMA((parts, 2, most * STREAMS)),
        ],
        compiler_params=pltpu.CompilerParams(vmem_limit_bytes=58 * mebibyte),
        cost_estimate=pl.CostEstimate(
            flops=4 * row_total * model_width * parts * units,
            bytes_accessed=4 * parts * model_width * units,
            transcendentals=row_total * parts * units,
        ),
        name="feed_forward",
    )(*rows, *flat)


def add_rows(here, there):
    return (here.astype(jnp.float32) + there.astype(jnp.float32)).astype(jnp.bfloat16)


def finish_kernel(
    hidden_ref, own_ref, near_ref, far_a_ref, far_b_ref, bias_ref, gain_ref, shift_ref, out_ref
):
    height = far_a_ref.shape[0]
    for begin, far_ref in ((0, far_a_ref), (height, far_b_ref)):
        rows = slice(begin, begin + height)
        summed = hidden_ref[rows, :].astype(jnp.float32) + (
            own_ref[rows, :].astype(jnp.float32)
            + near_ref[rows, :].astype(jnp.float32)
            + far_ref[...].astype(jnp.float32)
        )
        out_ref[rows, :] = layer_norm(
            summed + bias_ref[...], gain_ref[...], shift_ref[...]
        ).astype(jnp.bfloat16)


def finish_rows(hidden, own, near, far_a, far_b, bias, gain, shift):
    model_width = hidden.shape[1]
    return pl.pallas_call(
        finish_kernel,
        out_shape=jax.ShapeDtypeStruct(hidden.shape, jnp.bfloat16),
        in_specs=[vmem_spec()] * 8,
        out_specs=vmem_spec(),
        compiler_params=pltpu.CompilerParams(vmem_limit_bytes=16 * mebibyte),
        name="finish_rows",
    )(
        hidden,
        own,
        near,
        far_a,
        far_b,
        bias.reshape(1, model_width),
        gain.reshape(1, model_width),
        shift.reshape(1, model_width),
    )


def on_device(
    suffix_queries,
    suffix_keys,
    suffix_values,
    layer_input,
    suffix_lengths,
    request_group,
    prefix_keys,
    prefix_values,
    up_weight,
    up_bias,
    down_weight,
    down_bias,
    attn_gain,
    attn_shift,
    out_gain,
    out_shift,
):
    slot_count, model_width = suffix_queries.shape
    group_count = lax.axis_size("grp")
    column_count = lax.axis_size("dev")
    part_width = model_width // column_count
    local_heads = part_width // HD
    capacity = 2 * slot_count // group_count
    sources = group_count * column_count

    near_mask = group_count // 2 * column_count
    far_mask = column_count // 2
    column_masks = [1 << bit for bit in range(far_mask.bit_length() - 1)]
    group_masks = [column_count << bit for bit in range((group_count // 2).bit_length() - 1)]

    low_mask, high_masks = column_masks[0], column_masks[1:]
    core_mask = group_masks[0]

    outgoing = pack_queries(
        suffix_lengths, request_group, suffix_queries, group_count, column_count, capacity
    )
    bias_rows = jnp.broadcast_to(up_bias[None, :], (16, up_bias.shape[0]))
    up_block = jnp.concatenate([up_weight, bias_rows], axis=0)
    up_cut, down_cut = up_weight.shape[0] * 5 // 8, down_weight.shape[0] // 2
    up_pieces = (up_block[:up_cut], up_block[up_cut:])
    down_pieces = (down_weight[:down_cut], down_weight[down_cut:])
    ups, downs = {0: (up_block,)}, {0: (down_weight,)}
    high_mask = high_masks[0]

    arrived = lax.all_to_all(
        outgoing.reshape(sources, capacity, part_width),
        ("grp", "dev"),
        split_axis=0,
        concat_axis=0,
        tiled=True,
    )
    ups[low_mask] = swap(ups[0], low_mask)
    up_first = swap(up_pieces[0], high_mask)
    ups[core_mask] = swap(ups[0], core_mask)
    downs[core_mask] = swap(downs[0], core_mask)
    turned_keys = prefix_keys[0].T
    value_heads = prefix_values[0].reshape(-1, local_heads, HD).transpose(1, 0, 2)
    wide_values = jnp.concatenate([value_heads, jnp.ones_like(value_heads)], axis=2)
    own = attend_suffix(
        suffix_lengths, suffix_queries, suffix_keys, suffix_values, local_heads
    )
    arrived, ups, up_first, up_pieces, downs, down_pieces, turned_keys, wide_values, own = (
        lax.optimization_barrier(
            (arrived, ups, up_first, up_pieces, downs, down_pieces, turned_keys, wide_values, own)
        )
    )

    counts = jnp.sum((arrived[:, :, 0] < EMPTY / 2).astype(jnp.int32), axis=1)
    answer_part = attend_prefix(counts, arrived, turned_keys, wide_values)
    downs[low_mask] = swap(downs[0], low_mask)
    up_second = swap(up_pieces[1], high_mask)
    down_first = swap(down_pieces[0], high_mask)
    ups[core_mask ^ low_mask] = swap(ups[low_mask], core_mask)
    answer_part, ups, up_first, up_second, downs, down_first, down_pieces = (
        lax.optimization_barrier(
            (answer_part, ups, up_first, up_second, downs, down_first, down_pieces)
        )
    )

    answer = lax.all_to_all(
        answer_part, ("grp", "dev"), split_axis=0, concat_axis=0, tiled=True
    ).reshape(group_count, column_count, capacity + STAT_ROWS, part_width)
    ups[high_mask] = (jnp.concatenate([up_first, up_second], axis=0),)
    ups[core_mask ^ high_mask] = swap(ups[high_mask], core_mask)
    downs[core_mask ^ low_mask] = swap(downs[low_mask], core_mask)
    down_second = swap(down_pieces[1], high_mask)
    downs[high_mask] = (jnp.concatenate([down_first, down_second], axis=0),)
    downs[core_mask ^ high_mask] = swap(downs[high_mask], core_mask)
    ups[low_mask ^ high_mask] = swap(ups[high_mask], low_mask)
    answer, ups, downs = lax.optimization_barrier((answer, ups, downs))

    hidden_a, hidden_b, hidden = merge_parts(
        suffix_lengths, request_group, answer, *own, layer_input, attn_gain, attn_shift
    )

    (hidden_a, hidden_b, hidden), ups, downs = lax.optimization_barrier(
        ((hidden_a, hidden_b, hidden), ups, downs)
    )
    far_a = swap(hidden_a, far_mask)
    near = swap(hidden, near_mask)
    downs[low_mask ^ high_mask] = swap(downs[high_mask], low_mask)
    ups = complete(ups, group_masks + column_masks)
    far_b = swap(tie(hidden_b, far_a), far_mask)
    cross_a = swap(far_a, near_mask)
    far_b, cross_a, near, ups, downs = lax.optimization_barrier(
        (far_b, cross_a, near, ups, downs)
    )
    cross_b = swap(far_b, near_mask)
    downs = complete(downs, group_masks + column_masks)
    order = sorted(ups)
    ups = [ups[mask] for mask in order]
    downs = [downs[mask] for mask in order]
    far_part_a, cross_part_a = feed_forward([far_a, cross_a], ups, downs)
    cross_b, far_part_a, cross_part_a = lax.optimization_barrier(
        (cross_b, far_part_a, cross_part_a)
    )
    cross_sum_a = swap(cross_part_a, near_mask)
    far_part_b, cross_part_b = feed_forward([far_b, cross_b], ups, downs)
    cross_sum_a, far_part_b, cross_part_b = lax.optimization_barrier(
        (cross_sum_a, far_part_b, cross_part_b)
    )
    cross_sum_b = swap(cross_part_b, near_mask)
    joined_a = add_rows(far_part_a, cross_sum_a)
    far_sum_a = swap(joined_a, far_mask)
    near, hidden = tie((near, hidden), joined_a)
    near_part, own_part = feed_forward([near, hidden], ups, downs)
    near_sum = swap(near_part, near_mask)
    cross_sum_b, near_part, far_sum_a = lax.optimization_barrier(
        (cross_sum_b, near_part, far_sum_a)
    )
    far_sum_b = swap(add_rows(far_part_b, cross_sum_b), far_mask)
    return finish_rows(
        hidden, own_part, near_sum, far_sum_a, far_sum_b, down_bias, out_gain, out_shift
    )


def solution(mesh):
    placed = (
        P(("grp", "dev"), None),
        P(("grp", "dev"), None),
        P(("grp", "dev"), None),
        P(("grp", "dev"), None),
        P(("grp", "dev"), None),
        P(("grp", "dev"), None),
        P("grp", None, "dev"),
        P("grp", None, "dev"),
        P(None, ("grp", "dev")),
        P(("grp", "dev")),
        P(("grp", "dev"), None),
        P(),
        P(),
        P(),
        P(),
        P(),
    )
    return jax.shard_map(
        on_device, mesh=mesh, in_specs=placed, out_specs=P(("grp", "dev"), None), check_vma=False
    )
```
